32 devices in a mesh: dp: 8 (over z, x), tensor: 4 (over y, core).
Axes of the slice: x: 2, y: 2, z: 4, core: 2. Of those that a mesh axis runs over, the one named last changes fastest.
Arguments:
- tokens: bfloat16 [16, 320, 2048], P('dp', 'tensor'), may hold values from -6 to 6
- cotangent: bfloat16 [16, 320, 2048], P('dp', 'tensor'), may hold values from -6 to 6
- project_weight: float32 [3, 2048, 2048], P(None, 'dp', 'tensor'), may hold values from -0.14142136 to 0.14142136
- output_weight: float32 [2048, 2048], P('tensor', 'dp'), may hold values from -0.75 to 0.75
- gate_up_weight: float32 [2, 2048, 5632], P(None, 'dp', 'tensor'), may hold values from -0.125 to 0.125
- down_weight: float32 [5632, 2048], P('tensor', 'dp'), may hold values from -0.078125 to 0.078125
- norm_params: float32 [2, 2048], P(None, 'dp'), may hold values from -0.5 to 2.25
- first_project: float32 [3, 2048, 2048], P(None, 'dp', 'tensor'), may hold values from -6 to 6
- first_output: float32 [2048, 2048], P('tensor', 'dp'), may hold values from -0.4375 to 0.4375
- first_gate_up: float32 [2, 2048, 5632], P(None, 'dp', 'tensor'), may hold values from -1.25 to 1.25
- first_down: float32 [5632, 2048], P('tensor', 'dp'), may hold values from -2 to 2
- first_norm: float32 [2, 2048], P(None, 'dp'), may hold values from -6 to 6
- second_project: float32 [3, 2048, 2048], P(None, 'dp', 'tensor'), may hold values from 0.014848 to 0.06144
- second_output: float32 [2048, 2048], P('tensor', 'dp'), may hold values from 6.656e-05 to 0.00026624
- second_gate_up: float32 [2, 2048, 5632], P(None, 'dp', 'tensor'), may hold values from 0.0007168 to 0.0029696
- second_down: float32 [5632, 2048], P('tensor', 'dp'), may hold values from 0.0016384 to 0.006656
- second_norm: float32 [2, 2048], P(None, 'dp'), may hold values from 0.0512 to 0.2048
Outputs:
- layer_out: bfloat16 [16, 320, 2048], P('dp', 'tensor')
- input_grad: bfloat16 [16, 320, 2048], P('dp', 'tensor')
- grad_project: float32 [3, 2048, 2048], P(None, 'dp', 'tensor')
- grad_output: float32 [2048, 2048], P('tensor', 'dp')
- grad_gate_up: float32 [2, 2048, 5632], P(None, 'dp', 'tensor')
- grad_down: float32 [5632, 2048], P('tensor', 'dp')
- grad_norm_params: float32 [2, 2048], P(None, 'dp')
- norm_total: float32 [], replicated
- new_project: float32 [3, 2048, 2048], P(None, 'dp', 'tensor')
- new_output: float32 [2048, 2048], P('tensor', 'dp')
- new_gate_up: float32 [2, 2048, 5632], P(None, 'dp', 'tensor')
- new_down: float32 [5632, 2048], P('tensor', 'dp')
- new_norm_params: float32 [2, 2048], P(None, 'dp')
- moment_project: float32 [3, 2048, 2048], P(None, 'dp', 'tensor')
- moment_output: float32 [2048, 2048], P('tensor', 'dp')
- moment_gate_up: float32 [2, 2048, 5632], P(None, 'dp', 'tensor')
- moment_down: float32 [5632, 2048], P('tensor', 'dp')
- moment_norm: float32 [2, 2048], P(None, 'dp')
- square_project: float32 [3, 2048, 2048], P(None, 'dp', 'tensor')
- square_output: float32 [2048, 2048], P('tensor', 'dp')
- square_gate_up: float32 [2, 2048, 5632], P(None, 'dp', 'tensor')
- square_down: float32 [5632, 2048], P('tensor', 'dp')
- square_norm: float32 [2, 2048], P(None, 'dp')
The draws below stay inside these ranges and needn't reach their ends.
All inputs are finite; a program needn't handle non-finite values.
Results may differ from the reference program's by a relative error of at most 0.012.
The reference program's roundings to bfloat16 on the way count: a program that leaves them out, or rounds other values in their place, can miss the bound.
Values may be sent and summed in bfloat16 or wider, within the bound.
A program may use at most 256 MiB of HBM per device.

```python
import math
import jax
import jax.numpy as jnp
from jax import lax

D = 2048
HEADS = 32
HEAD_DIM = 64
FF = 5632
SEQ = 320
STEP = 10
ROT = 16
ROWS = 16


def draw_project_weight(key, part):
    scale = 1.0 / math.sqrt(D)
    column = jnp.arange(D, dtype=jnp.float32) / (D - 1)
    base = jax.random.truncated_normal(key, -4.0, 4.0, (3, D, D), jnp.float32)
    ramp = 0.7 + 0.7 * column
    ones_row = jnp.ones((D,), jnp.float32)
    kinds = jnp.stack([ones_row, ones_row, ramp])
    return base * scale * kinds[:, None, :]


def draw_norm_params(key, part):
    first_key, second_key = jax.random.split(key, 2)
    column = jnp.arange(D, dtype=jnp.float32) / (D - 1)
    ramp = 0.6 + column
    rough = jnp.exp(jax.random.uniform(first_key, (D,), jnp.float32, -0.2, 0.2))
    shift = 0.25 * jax.random.truncated_normal(second_key, -2.0, 2.0, (D,), jnp.float32)
    return jnp.stack([ramp * rough, shift])


def shard_levels(own_key, shape, pieces, least, top_value):
    level = 1.0
    for axis_at, shards_of in pieces:
        steps = jax.random.uniform(jax.random.fold_in(jax.random.fold_in(own_key, 6), axis_at), (shards_of,), jnp.float32, least / len(pieces), top_value / len(pieces))
        level = level * jnp.repeat(jnp.exp(steps), shape[axis_at] // shards_of).reshape((-1,) + (1,) * (len(shape) - 1 - axis_at))
    return level


def centred(rng, shape, width, bound, pieces=(), kind=jnp.bfloat16):
    values = jax.random.normal(rng, shape, jnp.float32) * width
    if len(pieces) > 0:
        values = shard_levels(rng, shape, pieces, -0.22, 0.18) * values
    return jnp.clip(values, min=-bound, max=bound).astype(kind)


def setup_inputs(seed: int = 0) -> dict:
    key_list = jax.random.split(jax.random.key(seed), 18)
    tokens = centred(key_list[0], (ROWS, SEQ, D), 1.0, 6.0, ((0, 8), (1, 4)))
    cotangent = centred(key_list[1], (ROWS, SEQ, D), 1.0, 6.0, ((0, 8), (1, 4)))
    project_weight = draw_project_weight(jax.random.fold_in(key_list[17], 71), 0)
    output_weight = centred(key_list[3], (D, D), (D // 32) ** -0.5, 0.75, ((0, 4), (1, 8)), jnp.float32)
    gate_up_weight = centred(key_list[4], (2, D, FF), D ** -0.5, 0.125, ((1, 8), (2, 4)), jnp.float32)
    down_weight = centred(key_list[5], (FF, D), FF ** -0.5, 0.078125, ((0, 4), (1, 8)), jnp.float32)
    norm_params = draw_norm_params(jax.random.fold_in(key_list[17], 71), 0)
    first_project = centred(key_list[7], (3, D, D), (0.006 * (ROWS * SEQ) ** 0.5), 6.0, ((1, 8), (2, 4)), jnp.float32)
    first_output = centred(key_list[8], (D, D), (0.0004 * (ROWS * SEQ) ** 0.5), 0.4375, ((0, 4), (1, 8)), jnp.float32)
    first_gate_up = centred(key_list[9], (2, D, FF), (0.0013 * (ROWS * SEQ) ** 0.5), 1.25, ((1, 8), (2, 4)), jnp.float32)
    first_down = centred(key_list[10], (FF, D), (0.002 * (ROWS * SEQ) ** 0.5), 2.0, ((0, 4), (1, 8)), jnp.float32)
    first_norm = centred(key_list[11], (2, D), (0.011 * (ROWS * SEQ) ** 0.5), 6.0, ((1, 8),), jnp.float32)
    second_project = jnp.clip(jnp.exp(math.log(0.06144) - 1.42019586 * jax.random.uniform(key_list[12], (3, D, D), jnp.float32) ** shard_levels(key_list[12], (3, D, D), ((1, 8), (2, 4)), -0.2, 0.2)), 0.014848, 0.06144)
    second_output = jnp.clip(jnp.exp(math.log(0.00026624) - 1.3862944 * jax.random.uniform(key_list[13], (D, D), jnp.float32) ** shard_levels(key_list[13], (D, D), ((0, 4), (1, 8)), -0.2, 0.2)), 6.656000186922029e-05, 0.00026624)
    second_gate_up = jnp.clip(jnp.exp(math.log(0.0029696) - 1.42138571 * jax.random.uniform(key_list[14], (2, D, FF), jnp.float32) ** shard_levels(key_list[14], (2, D, FF), ((1, 8), (2, 4)), -0.2, 0.2)), 0.0007168, 0.0029696)
    second_down = jnp.clip(jnp.exp(math.log(0.006656) - 1.4017985 * jax.random.uniform(key_list[15], (FF, D), jnp.float32) ** shard_levels(key_list[15], (FF, D), ((0, 4), (1, 8)), -0.2, 0.2)), 0.0016384, 0.006656)
    second_norm = jnp.clip(jnp.exp(math.log(0.2048) - 1.3862944 * jax.random.uniform(key_list[16], (2, D), jnp.float32) ** shard_levels(key_list[16], (2, D), ((1, 8),), -0.2, 0.2)), 0.0512, 0.2048)
    return {"tokens": tokens, "cotangent": cotangent, "project_weight": project_weight, "output_weight": output_weight, "gate_up_weight": gate_up_weight, "down_weight": down_weight, "norm_params": norm_params, "first_project": first_project, "first_output": first_output, "first_gate_up": first_gate_up, "first_down": first_down, "first_norm": first_norm, "second_project": second_project, "second_output": second_output, "second_gate_up": second_gate_up, "second_down": second_down, "second_norm": second_norm}


BETA_ONE = 0.9
BETA_TWO = 0.999
ADAM_EPS = 1e-08
NORM_EPS = 1e-05
MASK_FILL = -1e+30

@jax.custom_vjp
def low(v):
    return lax.optimization_barrier(v.astype(jnp.bfloat16)).astype(jnp.float32)

@jax.custom_vjp
def low_back(v):
    return v

def low_keep(v):
    return (low(v), None)

def low_pass(kept, grad):
    return (grad,)

def back_keep(v):
    return (v, None)

def back_low(kept, grad):
    return (low(grad),)
low.defvjp(low_keep, low_pass)
low_back.defvjp(back_keep, back_low)

def highest_dot(left_side, right_side):
    return jnp.dot(left_side, right_side, preferred_element_type=jnp.float32, precision=lax.Precision.HIGHEST)

def angle_tables(length):
    half_rot = ROT // 2
    inverse = 10000.0 ** (-2.0 * jnp.arange(half_rot, dtype=jnp.float32) / ROT)
    angles = jnp.arange(length, dtype=jnp.float32)[:, None] * inverse[None, :]
    return (jnp.cos(angles)[:, None, :], jnp.sin(angles)[:, None, :])

def rotate(values_in, cosine, sine_table, direction):
    half_rot = ROT // 2
    first_half = values_in[..., :half_rot]
    second_half = values_in[..., half_rot:ROT]
    return jnp.concatenate([first_half * cosine - direction * second_half * sine_table, second_half * cosine + direction * first_half * sine_table, values_in[..., ROT:]], axis=-1)

def layer_forward(weights_all, seq_tokens):
    project_low, output_low, gate_up_low, down_low, norm_low = [low(weight_one) for weight_one in weights_all]
    row_mean = lax.optimization_barrier(jnp.mean(seq_tokens, axis=1, keepdims=True))
    centered = seq_tokens - row_mean
    row_var = lax.optimization_barrier(jnp.mean(centered * centered, axis=1, keepdims=True))
    normed = low(centered * lax.rsqrt(row_var + NORM_EPS) * norm_low[0] + norm_low[1])
    cosine, sine_table = angle_tables(SEQ)
    query_rot = low(rotate(low_back(highest_dot(normed, project_low[0])).reshape(SEQ, HEADS, HEAD_DIM), cosine, sine_table, 1.0))
    key_rot = low(rotate(low_back(highest_dot(normed, project_low[1])).reshape(SEQ, HEADS, HEAD_DIM), cosine, sine_table, 1.0))
    value_low = low(low_back(highest_dot(normed, project_low[2])).reshape(SEQ, HEADS, HEAD_DIM))
    scores = low_back(jnp.einsum('qhd,khd->hqk', query_rot, key_rot, precision=lax.Precision.HIGHEST) * 0.125)
    positions = jnp.arange(SEQ)
    causal = positions[:, None] >= positions[None, :]
    scores = jnp.where(causal[None], scores, MASK_FILL)
    row_top = lax.optimization_barrier(jnp.max(scores, axis=2, keepdims=True))
    exponent = jnp.exp(scores - row_top)
    soft_low = low(exponent / lax.optimization_barrier(jnp.sum(exponent, axis=2, keepdims=True)))
    attended = low_back(low(jnp.einsum('hqk,khd->qhd', soft_low, value_low, precision=lax.Precision.HIGHEST).reshape(SEQ, D)))
    gate_pre = low_back(highest_dot(normed, gate_up_low[0]))
    up_pre = low_back(highest_dot(normed, gate_up_low[1]))
    hidden_low = low_back(low(jax.nn.silu(gate_pre) * up_pre))
    return seq_tokens + highest_dot(attended, output_low) + highest_dot(hidden_low, down_low)

def adam_update(weight_old, gradient, moment_old, square_old, factor, rate, decay):
    clipped = gradient * factor
    moment_new = BETA_ONE * moment_old + (1.0 - BETA_ONE) * clipped
    square_new = BETA_TWO * square_old + (1.0 - BETA_TWO) * clipped * clipped
    moment_hat = moment_new / (1.0 - BETA_ONE ** STEP)
    square_hat = square_new / (1.0 - BETA_TWO ** STEP)
    weight_new = weight_old - rate * (moment_hat / (jnp.sqrt(square_hat) + ADAM_EPS) + decay * weight_old)
    return (weight_new, moment_new, square_new)

def reference(tokens, cotangent, project_weight, output_weight, gate_up_weight, down_weight, norm_params, first_project, first_output, first_gate_up, first_down, first_norm, second_project, second_output, second_gate_up, second_down, second_norm):
    weights_all = (project_weight, output_weight, gate_up_weight, down_weight, norm_params)

    def one_sequence(carried, pair_in):
        seq_tokens, seq_cot = pair_in
        result, pullback = jax.vjp(layer_forward, weights_all, seq_tokens.astype(jnp.float32))
        grads_seq, token_grad = pullback(seq_cot.astype(jnp.float32))
        summed = tuple((earlier + later for earlier, later in zip(carried, grads_seq)))
        return (summed, (result.astype(jnp.bfloat16), token_grad.astype(jnp.bfloat16)))
    start_grads = tuple((jnp.zeros(weight_one.shape, jnp.float32) for weight_one in weights_all))
    grads_all, (layer_out, input_grad) = lax.scan(one_sequence, start_grads, (tokens, cotangent))
    square_sum = jnp.float32(0.0)
    for grad_one in grads_all:
        square_sum = square_sum + jnp.sum(grad_one * grad_one)
    norm_total = jnp.sqrt(square_sum)
    limit = 0.03 * math.sqrt((4 * D * D + 3 * D * FF + 2 * D) * ROWS * SEQ)
    factor = jnp.minimum(1.0, limit / (norm_total + 1e-06))
    rates = (2.0 / math.sqrt(D), 2.0 / math.sqrt(D // 32), 2.0 / math.sqrt(D), 2.0 / math.sqrt(FF), 0.5)
    decays = (0.1, 0.1, 0.1, 0.1, 0.0)
    firsts = (first_project, first_output, first_gate_up, first_down, first_norm)
    seconds = (second_project, second_output, second_gate_up, second_down, second_norm)
    updated = [adam_update(weights_all[index], grads_all[index], firsts[index], seconds[index], factor, rates[index], decays[index]) for index in range(5)]
    return (layer_out, input_grad, grads_all[0], grads_all[1], grads_all[2], grads_all[3], grads_all[4], norm_total, updated[0][0], updated[1][0], updated[2][0], updated[3][0], updated[4][0], updated[0][1], updated[1][1], updated[2][1], updated[3][1], updated[4][1], updated[0][2], updated[1][2], updated[2][2], updated[3][2], updated[4][2])
```

```python
import math

import jax
import jax.numpy as jnp
from jax import lax
from jax.sharding import PartitionSpec as P

D = 2048
HEAD_DIM = 64
FF = 5632
SEQ = 320
STEP = 10
ROT = 16

BETA_ONE = 0.9
BETA_TWO = 0.999
ADAM_EPS = 1e-08
NORM_EPS = 1e-05
MASK_FILL = -1e30

BOTH = ("dp", "tensor")


def swap(values, dp_flip, tensor_flip):
    dp_size, tensor_size = lax.axis_size("dp"), lax.axis_size("tensor")
    pairs = [
        (d * tensor_size + t, (d ^ dp_flip) * tensor_size + (t ^ tensor_flip))
        for d in range(dp_size)
        for t in range(tensor_size)
    ]
    return lax.ppermute(values, BOTH, pairs)


def relative(values, axis, me, count):
    width = values.shape[axis] // count
    return jnp.concatenate(
        [lax.dynamic_slice_in_dim(values, (me ^ r) * width, width, axis) for r in range(count)],
        axis=axis,
    )


def flip_blocks(values, axis, count, flip):
    width = values.shape[axis] // count
    return jnp.concatenate(
        [lax.slice_in_dim(values, (r ^ flip) * width, ((r ^ flip) + 1) * width, axis=axis) for r in range(count)],
        axis=axis,
    )


def gather_blocks(mine, other):
    half = lax.axis_size("dp") // 2
    outer = [mine] + [swap(other if j % 2 else mine, 2 * j, 0) for j in range(1, half)]
    blocks = []
    for block in outer:
        blocks += [block, swap(block, 1, 0)]
    return blocks


def gather_rows(values):
    count = lax.axis_size("dp")
    other = flip_blocks(swap(values, 2, 0), values.ndim - 1, count, 2)
    pair = jnp.concatenate([values, other], axis=0)
    four = jnp.concatenate([pair, swap(pair, 0, 2)], axis=0)
    return jnp.concatenate([four, swap(four, 0, 1)], axis=0)


def scatter_rows(partial):
    count = lax.axis_size("dp")
    quarter = partial.shape[0] // 2
    four = partial[:quarter].astype(jnp.float32) + swap(partial[quarter:].astype(jnp.bfloat16), 0, 1)
    quarter //= 2
    pair = four[:quarter] + swap(four[quarter:].astype(jnp.bfloat16), 0, 2)
    quarter //= 2
    other = swap(pair[quarter:].astype(jnp.bfloat16), 2, 0).astype(jnp.float32)
    return pair[:quarter] + flip_blocks(other, 2, count, 2)


def scatter_blocks(partial_of):
    half = lax.axis_size("dp") // 2
    away = swap(partial_of(1).astype(jnp.bfloat16), 1, 0)
    summed = partial_of(0) + away.astype(jnp.float32)
    low = summed.astype(jnp.bfloat16)
    mine, other = summed[0], None
    for j in range(1, half):
        came = swap(low[j], 2 * j, 0).astype(jnp.float32)
        if j % 2 == 0:
            mine = mine + came
        else:
            other = came if other is None else other + came
    return mine, other


def rotate(values_in, cosine, sine_table, direction):
    half_rot = ROT // 2
    first_half = values_in[..., :half_rot]
    second_half = values_in[..., half_rot:ROT]
    return jnp.concatenate(
        [
            first_half * cosine - direction * second_half * sine_table,
            second_half * cosine + direction * first_half * sine_table,
            values_in[..., ROT:],
        ],
        axis=-1,
    )


def dot_plain(a, b):
    return lax.dot_general(a, b, (((1,), (0,)), ((), ())), preferred_element_type=jnp.float32)


def dot_rows(a, b):
    return lax.dot_general(a, b, (((0,), (0,)), ((), ())), preferred_element_type=jnp.float32)


def dot_cols(a, b):
    return lax.dot_general(a, b, (((1,), (1,)), ((), ())), preferred_element_type=jnp.float32)


def adam_update(weight_old, gradient, moment_old, square_old, factor, rate, decay):
    clipped = gradient * factor
    moment_new = BETA_ONE * moment_old + (1.0 - BETA_ONE) * clipped
    square_new = BETA_TWO * square_old + (1.0 - BETA_TWO) * clipped * clipped
    moment_hat = moment_new / (1.0 - BETA_ONE**STEP)
    square_hat = square_new / (1.0 - BETA_TWO**STEP)
    weight_new = weight_old - rate * (
        moment_hat / (jnp.sqrt(square_hat) + ADAM_EPS) + decay * weight_old
    )
    return (weight_new, moment_new, square_new)


def local(
    tokens,
    cotangent,
    project_weight,
    output_weight,
    gate_up_weight,
    down_weight,
    norm_params,
    first_project,
    first_output,
    first_gate_up,
    first_down,
    first_norm,
    second_project,
    second_output,
    second_gate_up,
    second_down,
    second_norm,
):
    count = lax.axis_size("dp")
    blocks_half = count // 2
    me = lax.axis_index("dp")
    side = (me // 2) % 2
    spot = lax.axis_index("tensor")
    micro_count, piece = tokens.shape[0], tokens.shape[1]
    head_cols = project_weight.shape[2] // 2
    unit_cols = gate_up_weight.shape[2] // 2
    rows_each = project_weight.shape[1]
    heads = head_cols // HEAD_DIM

    def halves(first, second):
        first, second = first.astype(jnp.bfloat16), second.astype(jnp.bfloat16)
        return jnp.where(side == 0, first, second), jnp.where(side == 0, second, first)

    def project_half(s):
        return jnp.concatenate(
            [project_weight[k, :, s * head_cols : (s + 1) * head_cols] for k in range(3)], axis=1
        )

    def gate_up_half(s):
        return jnp.concatenate(
            [gate_up_weight[k, :, s * unit_cols : (s + 1) * unit_cols] for k in range(2)], axis=1
        )

    def out_half(s):
        return jnp.concatenate(
            [
                output_weight[s * head_cols : (s + 1) * head_cols],
                down_weight[s * unit_cols : (s + 1) * unit_cols],
            ],
            axis=0,
        )

    norm_full = relative(
        lax.all_gather(norm_params.astype(jnp.bfloat16), "dp", axis=1, tiled=True), 1, me, count
    ).astype(jnp.float32)
    gain, shift = norm_full[0], norm_full[1]

    w_project = jnp.concatenate(gather_blocks(*halves(project_half(0), project_half(1))), axis=0)
    w_gate_up = jnp.concatenate(gather_blocks(*halves(gate_up_half(0), gate_up_half(1))), axis=0)
    w_out = jnp.concatenate(gather_blocks(*halves(out_half(0), out_half(1))), axis=1)

    tok_rows = relative(tokens, 2, me, count).astype(jnp.float32)
    row_mean = jnp.mean(tok_rows, axis=2, keepdims=True)
    centered = tok_rows - row_mean
    row_scale = lax.rsqrt(jnp.mean(centered * centered, axis=2, keepdims=True) + NORM_EPS)
    unit_rows = centered * row_scale
    normed = (unit_rows * gain + shift).astype(jnp.bfloat16)
    cot_low = relative(cotangent, 2, me, count)

    all_normed = gather_rows(normed)
    all_cot = gather_rows(cot_low)
    blocks_all = all_normed.shape[0]
    rows_all = blocks_all * piece
    all_normed = all_normed.reshape(rows_all, D)
    all_cot = all_cot.reshape(rows_all, D)

    spots = lax.axis_size("tensor")
    order = jnp.array([0, 2, 1, 3])
    positions = ((spot ^ order)[:, None] * piece + jnp.arange(piece)[None, :]).reshape(-1)
    inverse = 10000.0 ** (-2.0 * jnp.arange(ROT // 2, dtype=jnp.float32) / ROT)
    angles = positions.astype(jnp.float32)[:, None] * inverse[None, :]
    cosine, sine_table = jnp.cos(angles)[:, None, :], jnp.sin(angles)[:, None, :]
    causal = (positions[:, None] >= positions[None, :])[None, None]
    seqs = 2 * micro_count
    seq_len = spots * piece

    def to_heads(values):
        return (
            values.reshape(spots, seqs, piece, heads, HEAD_DIM)
            .transpose(1, 0, 2, 3, 4)
            .reshape(seqs, seq_len, heads, HEAD_DIM)
        )

    def from_heads(values):
        return (
            values.reshape(seqs, spots, piece, heads * HEAD_DIM)
            .transpose(1, 0, 2, 3)
            .reshape(rows_all, heads * HEAD_DIM)
        )

    projected = dot_plain(all_normed, w_project)
    query = rotate(to_heads(projected[:, :head_cols]), cosine, sine_table, 1.0).astype(jnp.bfloat16)
    key = rotate(to_heads(projected[:, head_cols : 2 * head_cols]), cosine, sine_table, 1.0).astype(
        jnp.bfloat16
    )
    value = to_heads(projected[:, 2 * head_cols :]).astype(jnp.bfloat16)
    scores = jnp.where(
        causal,
        jnp.einsum("sqhd,skhd->shqk", query, key, preferred_element_type=jnp.float32) * 0.125,
        MASK_FILL,
    )
    row_top = jnp.max(scores, axis=3, keepdims=True)
    exponent = jnp.exp(scores - row_top)
    row_total = jnp.sum(exponent, axis=3, keepdims=True)
    soft = exponent / row_total
    soft_low = soft.astype(jnp.bfloat16)
    attended = from_heads(
        jnp.einsum("shqk,skhd->sqhd", soft_low, value, preferred_element_type=jnp.float32)
    ).astype(jnp.bfloat16)

    gate_up = dot_plain(all_normed, w_gate_up)
    gate_pre, up_pre = gate_up[:, :unit_cols], gate_up[:, unit_cols:]
    sigmoid_gate = jax.nn.sigmoid(gate_pre)
    swish_gate = gate_pre * sigmoid_gate
    hidden = (swish_gate * up_pre).astype(jnp.bfloat16)
    middle = jnp.concatenate([attended, hidden], axis=1)

    def grad_out_part(i):
        cot_part = all_cot.reshape(rows_all, blocks_half, 2, rows_each)[:, :, i].reshape(rows_all, -1)
        return dot_rows(middle, cot_part).reshape(-1, blocks_half, rows_each).transpose(1, 0, 2)

    grad_out_mine, grad_out_other = scatter_blocks(grad_out_part)

    d_middle = dot_cols(all_cot, w_out).astype(jnp.bfloat16)
    d_hid = d_middle[:, head_cols:].astype(jnp.float32)
    d_gate = d_hid * up_pre * (sigmoid_gate * (1.0 + gate_pre * (1.0 - sigmoid_gate)))
    d_up = d_hid * swish_gate
    d_gate_up = jnp.concatenate([d_gate, d_up], axis=1).astype(jnp.bfloat16)

    def normed_part(i):
        return all_normed.reshape(rows_all, blocks_half, 2, rows_each)[:, :, i].reshape(rows_all, -1)

    grad_gu_mine, grad_gu_other = scatter_blocks(
        lambda i: dot_rows(normed_part(i), d_gate_up).reshape(blocks_half, rows_each, -1)
    )

    d_att = to_heads(d_middle[:, :head_cols])
    d_value = jnp.einsum("shqk,sqhd->skhd", soft_low, d_att, preferred_element_type=jnp.float32)
    d_prob = jnp.einsum("sqhd,skhd->shqk", d_att, value, preferred_element_type=jnp.float32)
    d_score = (
        soft * (d_prob - jnp.sum(d_prob * soft, axis=3, keepdims=True))
    ).astype(jnp.bfloat16)
    d_query = rotate(
        0.125 * jnp.einsum("shqk,skhd->sqhd", d_score, key, preferred_element_type=jnp.float32),
        cosine,
        sine_table,
        -1.0,
    )
    d_key = rotate(
        0.125 * jnp.einsum("shqk,sqhd->skhd", d_score, query, preferred_element_type=jnp.float32),
        cosine,
        sine_table,
        -1.0,
    )
    d_project = jnp.concatenate(
        [from_heads(d_query), from_heads(d_key), from_heads(d_value)], axis=1
    ).astype(jnp.bfloat16)

    d_normed = scatter_rows(
        (dot_cols(d_project, w_project) + dot_cols(d_gate_up, w_gate_up)).reshape(
            blocks_all, piece, D
        )
    )
    grad_p_mine, grad_p_other = scatter_blocks(
        lambda i: dot_rows(normed_part(i), d_project).reshape(blocks_half, rows_each, -1)
    )
    summed = scatter_rows(dot_plain(middle, w_out).reshape(blocks_all, piece, D))
    layer_out = relative((tok_rows + summed).astype(jnp.bfloat16), 2, me, count)

    d_unit = d_normed * gain
    d_input = row_scale * (
        d_unit
        - jnp.mean(d_unit, axis=2, keepdims=True)
        - unit_rows * jnp.mean(d_unit * unit_rows, axis=2, keepdims=True)
    )
    input_grad = relative((cot_low.astype(jnp.float32) + d_input).astype(jnp.bfloat16), 2, me, count)

    grad_norm = jnp.stack(
        [jnp.sum(d_normed * unit_rows, axis=(0, 1)), jnp.sum(d_normed, axis=(0, 1))]
    ).reshape(2, blocks_half, 2, rows_each)
    grad_norm = grad_norm[:, :, 0] + swap(grad_norm[:, :, 1], 1, 0)
    own = grad_norm[:, 0]
    for j in range(1, blocks_half):
        own = own + swap(grad_norm[:, j], 2 * j, 0)
    own = own + swap(own, 0, 2)
    norm_grad = own + swap(own, 0, 1)

    def both(mine, other, axis):
        return jnp.concatenate(
            [jnp.where(side == 0, mine, other), jnp.where(side == 0, other, mine)], axis=axis
        )

    def columns(mine, other, k, width):
        span = slice(k * width, (k + 1) * width)
        return both(mine[:, span], other[:, span], 1)

    grads = (
        jnp.stack([columns(grad_p_mine, grad_p_other, k, head_cols) for k in range(3)]),
        both(grad_out_mine[:head_cols], grad_out_other[:head_cols], 0),
        jnp.stack([columns(grad_gu_mine, grad_gu_other, k, unit_cols) for k in range(2)]),
        both(grad_out_mine[head_cols:], grad_out_other[head_cols:], 0),
        norm_grad,
    )
    square_local = sum(jnp.sum(g * g) for g in grads[:4]) + jnp.sum(norm_grad * norm_grad) / spots
    norm_total = jnp.sqrt(lax.psum(square_local, BOTH))
    limit = 0.03 * math.sqrt((4 * D * D + 3 * D * FF + 2 * D) * micro_count * count * SEQ)
    factor = jnp.minimum(1.0, limit / (norm_total + 1e-06))
    rates = (
        2.0 / math.sqrt(D),
        2.0 / math.sqrt(D // 32),
        2.0 / math.sqrt(D),
        2.0 / math.sqrt(FF),
        0.5,
    )
    decays = (0.1, 0.1, 0.1, 0.1, 0.0)
    masters = (project_weight, output_weight, gate_up_weight, down_weight, norm_params)
    firsts = (first_project, first_output, first_gate_up, first_down, first_norm)
    seconds = (second_project, second_output, second_gate_up, second_down, second_norm)
    updated = [
        adam_update(*parts) for parts in zip(masters, grads, firsts, seconds, [factor] * 5, rates, decays)
    ]
    return (
        layer_out,
        input_grad,
        *grads,
        norm_total,
        *[u[0] for u in updated],
        *[u[1] for u in updated],
        *[u[2] for u in updated],
    )


def solution(mesh):
    wide = P("dp", "tensor", None)
    stacked = P(None, "dp", "tensor")
    tall = P("tensor", "dp")
    params = (stacked, tall, stacked, tall, P(None, "dp"))
    return jax.shard_map(
        local,
        mesh=mesh,
        in_specs=(wide, wide, *params, *params, *params),
        out_specs=(wide, wide, *params, P(), *params, *params, *params),
        check_vma=False,
    )
```

```python
import math

import jax
import jax.numpy as jnp
from jax import lax
from jax.experimental import pallas as pl
from jax.experimental.pallas import tpu as pltpu
from jax.sharding import PartitionSpec as P

D = 2048
HEAD_DIM = 64
FF = 5632
SEQ = 320
STEP = 10
ROT = 16

BETA_ONE = 0.9
BETA_TWO = 0.999
ADAM_EPS = 1e-08
NORM_EPS = 1e-05
MASK_FILL = -1e30

BOTH = ("dp", "tensor")


def swap(values, dp_flip, tensor_flip):
    dp_size, tensor_size = lax.axis_size("dp"), lax.axis_size("tensor")
    pairs = [
        (d * tensor_size + t, (d ^ dp_flip) * tensor_size + (t ^ tensor_flip))
        for d in range(dp_size)
        for t in range(tensor_size)
    ]
    return lax.ppermute(values, BOTH, pairs)


def block_order(count):
    return [2 * j + i for i in range(2) for j in range(count // 2)]


def relative(values, axis, me, count):
    width = values.shape[axis] // count
    return jnp.concatenate(
        [lax.dynamic_slice_in_dim(values, (me ^ r) * width, width, axis) for r in block_order(count)],
        axis=axis,
    )


def from_relative(values, axis, me, count):
    width = values.shape[axis] // count
    places = [((me ^ g) % 2) * (count // 2) + (me ^ g) // 2 for g in range(count)]
    return jnp.concatenate(
        [lax.dynamic_slice_in_dim(values, place * width, width, axis) for place in places],
        axis=axis,
    )


def flip_blocks(values, axis, count):
    width = values.shape[axis] // count
    return jnp.concatenate(
        [lax.slice_in_dim(values, (p ^ 1) * width, ((p ^ 1) + 1) * width, axis=axis) for p in range(count)],
        axis=axis,
    )


def gather_blocks(mine, other):
    half = lax.axis_size("dp") // 2
    near = [mine] + [swap(other if j % 2 else mine, 2 * j, 0) for j in range(1, half)]
    return near + [swap(block, 1, 0) for block in near]


def gather_rows(values):
    other = flip_blocks(swap(values, 2, 0), values.ndim - 1, lax.axis_size("dp"))
    pair = jnp.concatenate([values, other], axis=0)
    four = jnp.concatenate([pair, swap(pair, 0, 2)], axis=0)
    return jnp.concatenate([four, swap(four, 0, 1)], axis=0)


def scatter_rows(partial_of):
    away = swap(partial_of(1).astype(jnp.bfloat16), 0, 1)
    four = partial_of(0) + away.astype(jnp.float32)
    half = four.shape[0] // 2
    pair = four[:half] + swap(four[half:].astype(jnp.bfloat16), 0, 2).astype(jnp.float32)
    half //= 2
    other = swap(pair[half:].astype(jnp.bfloat16), 2, 0).astype(jnp.float32)
    return pair[:half] + flip_blocks(other, 2, lax.axis_size("dp"))


def scatter_blocks(partial_of, axis):
    half = lax.axis_size("dp") // 2
    away = swap(partial_of(1).astype(jnp.bfloat16), 1, 0)
    summed = partial_of(0) + away.astype(jnp.float32)
    pieces = jnp.split(summed, half, axis=axis)
    mine, other = pieces[0], None
    for j in range(1, half):
        came = swap(pieces[j].astype(jnp.bfloat16), 2 * j, 0).astype(jnp.float32)
        if j % 2 == 0:
            mine = mine + came
        else:
            other = came if other is None else other + came
    return mine, other


def dot_plain(a, b):
    return lax.dot_general(a, b, (((1,), (0,)), ((), ())), preferred_element_type=jnp.float32)


def dot_rows(a, b):
    return lax.dot_general(a, b, (((0,), (0,)), ((), ())), preferred_element_type=jnp.float32)


def dot_cols(a, b):
    return lax.dot_general(a, b, (((1,), (1,)), ((), ())), preferred_element_type=jnp.float32)


def turn(values, tables, direction):
    cosine, low_sine, high_sine = tables
    lanes = values.shape[1]
    half_rot = ROT // 2
    moved = pltpu.roll(values, lanes - half_rot, 1) * low_sine + pltpu.roll(values, half_rot, 1) * high_sine
    return values * cosine + direction * moved


def head_probabilities(query, key, bias):
    scores = dot_cols(query, key) * 0.125 + bias
    exponent = jnp.exp(scores - jnp.max(scores, axis=1, keepdims=True))
    return exponent / jnp.sum(exponent, axis=1, keepdims=True)


def attention_fore(projected_ref, tables_ref, bias_ref, turned_ref, attended_ref):
    spots, _, piece, width = projected_ref.shape
    rows, third = spots * piece, width // 3
    tables = [tables_ref[k] for k in range(3)]
    first = lax.broadcasted_iota(jnp.int32, (rows, 128), 1) < HEAD_DIM
    for pair in range(third // 128):
        span = [slice(k * third + pair * 128, k * third + pair * 128 + 128) for k in range(3)]
        query, key, value = [projected_ref[:, 0, :, s].reshape(rows, 128) for s in span]
        query = turn(query, tables, 1.0).astype(jnp.bfloat16)
        key = turn(key, tables, 1.0).astype(jnp.bfloat16)
        value = value.astype(jnp.bfloat16)
        for s, part in zip(span, (query, key, value)):
            turned_ref[:, 0, :, s] = part.reshape(spots, piece, 128)
        none = jnp.zeros_like(query)
        outs = [
            dot_plain(head_probabilities(q, key, bias_ref[...]).astype(jnp.bfloat16), value)
            for q in (jnp.where(first, query, none), jnp.where(first, none, query))
        ]
        attended_ref[:, 0, :, span[0]] = (
            jnp.where(first, outs[0], outs[1]).astype(jnp.bfloat16).reshape(spots, piece, 128)
        )


def attention_back(turned_ref, d_att_ref, tables_ref, bias_ref, d_project_ref):
    spots, _, piece, width = turned_ref.shape
    rows, third = spots * piece, width // 3
    tables = [tables_ref[k] for k in range(3)]
    first = lax.broadcasted_iota(jnp.int32, (rows, 128), 1) < HEAD_DIM
    for pair in range(third // 128):
        span = [slice(k * third + pair * 128, k * third + pair * 128 + 128) for k in range(3)]
        query, key, value = [turned_ref[:, 0, :, s].reshape(rows, 128) for s in span]
        d_att = d_att_ref[:, 0, :, span[0]].reshape(rows, 128)
        none = jnp.zeros_like(query)
        parts = []
        for head in range(2):
            keep = first if head == 0 else jnp.logical_not(first)
            one_query = jnp.where(keep, query, none)
            one_d_att = jnp.where(keep, d_att, none)
            prob = head_probabilities(one_query, key, bias_ref[...])
            d_value = dot_rows(prob.astype(jnp.bfloat16), d_att)
            d_prob = dot_cols(one_d_att, value)
            d_score = (prob * (d_prob - jnp.sum(d_prob * prob, axis=1, keepdims=True))).astype(
                jnp.bfloat16
            )
            parts.append((dot_plain(d_score, key), dot_rows(d_score, query), d_value))
        joined = [jnp.where(first, one, two) for one, two in zip(*parts)]
        done = (turn(0.125 * joined[0], tables, -1.0), turn(0.125 * joined[1], tables, -1.0), joined[2])
        for s, part in zip(span, done):
            d_project_ref[:, 0, :, s] = part.astype(jnp.bfloat16).reshape(spots, piece, 128)


def join_gate_up(packed, whole):
    last = packed[:, 2 * whole :]
    gate = jnp.concatenate([packed[:, :whole], last], axis=1)
    up = jnp.concatenate([packed[:, whole : 2 * whole], pltpu.roll(last, 64, 1)], axis=1)
    return gate, up


def units_fore(normed_ref, weight_ref, packed_ref, hidden_ref):
    packed = dot_plain(normed_ref[...], weight_ref[...])
    packed_ref[...] = packed
    units = hidden_ref.shape[1]
    gate, up = join_gate_up(packed, units - 64)
    hidden_ref[...] = (gate * jax.nn.sigmoid(gate) * up).astype(jnp.bfloat16)[:, :units]


def units_back(cot_ref, weight_ref, packed_ref, d_packed_ref):
    units = weight_ref.shape[0]
    whole = units - 64
    d_hid = dot_cols(cot_ref[...], weight_ref[...]).astype(jnp.bfloat16).astype(jnp.float32)
    d_hid = jnp.concatenate([d_hid, jnp.zeros((d_hid.shape[0], 64), jnp.float32)], axis=1)
    gate, up = join_gate_up(packed_ref[...], whole)
    sigmoid_gate = jax.nn.sigmoid(gate)
    d_gate = d_hid * up * (sigmoid_gate * (1.0 + gate * (1.0 - sigmoid_gate)))
    d_up = d_hid * (gate * sigmoid_gate)
    first = lax.broadcasted_iota(jnp.int32, (gate.shape[0], 128), 1) < 64
    last = jnp.where(first, d_gate[:, whole:], pltpu.roll(d_up[:, whole:], 64, 1))
    d_packed_ref[:, :whole] = d_gate[:, :whole].astype(jnp.bfloat16)
    d_packed_ref[:, whole : 2 * whole] = d_up[:, :whole].astype(jnp.bfloat16)
    d_packed_ref[:, 2 * whole :] = last.astype(jnp.bfloat16)


def whole_block(shape):
    return pl.BlockSpec(shape, lambda *_: (0,) * len(shape))


KERNEL_PARAMS = pltpu.CompilerParams(vmem_limit_bytes=40 * 1024 * 1024)


def run_attention_fore(projected, tables, bias):
    spots, seqs, piece, width = projected.shape
    block = lambda w: pl.BlockSpec((spots, 1, piece, w), lambda s: (0, s, 0, 0))
    rows = spots * piece
    return pl.pallas_call(
        attention_fore,
        grid=(seqs,),
        in_specs=[block(width), whole_block(tables.shape), whole_block(bias.shape)],
        out_specs=[block(width), block(width // 3)],
        out_shape=[
            jax.ShapeDtypeStruct((spots, seqs, piece, width), jnp.bfloat16),
            jax.ShapeDtypeStruct((spots, seqs, piece, width // 3), jnp.bfloat16),
        ],
        compiler_params=KERNEL_PARAMS,
        cost_estimate=pl.CostEstimate(
            flops=seqs * rows * rows * width * 2, bytes_accessed=seqs * rows * width * 7, transcendentals=0
        ),
        name="attention_fore",
    )(projected, tables, bias)


def run_attention_back(turned, d_att, tables, bias):
    spots, seqs, piece, width = turned.shape
    block = lambda w: pl.BlockSpec((spots, 1, piece, w), lambda s: (0, s, 0, 0))
    rows = spots * piece
    return pl.pallas_call(
        attention_back,
        grid=(seqs,),
        in_specs=[block(width), block(width // 3), whole_block(tables.shape), whole_block(bias.shape)],
        out_specs=block(width),
        out_shape=jax.ShapeDtypeStruct((spots, seqs, piece, width), jnp.bfloat16),
        compiler_params=KERNEL_PARAMS,
        cost_estimate=pl.CostEstimate(
            flops=seqs * rows * rows * width * 5, bytes_accessed=seqs * rows * width * 5, transcendentals=0
        ),
        name="attention_back",
    )(turned, d_att, tables, bias)


def row_tile(rows):
    return 256 if rows % 256 == 0 else rows // 8


def run_units_fore(normed, weight):
    rows, units = normed.shape[0], weight.shape[1] // 2
    tile = row_tile(rows)
    block = lambda w: pl.BlockSpec((tile, w), lambda r: (r, 0))
    return pl.pallas_call(
        units_fore,
        grid=(rows // tile,),
        in_specs=[block(D), whole_block(weight.shape)],
        out_specs=[block(2 * units), block(units)],
        out_shape=[
            jax.ShapeDtypeStruct((rows, 2 * units), jnp.float32),
            jax.ShapeDtypeStruct((rows, units), jnp.bfloat16),
        ],
        compiler_params=KERNEL_PARAMS,
        cost_estimate=pl.CostEstimate(
            flops=rows * D * units * 4, bytes_accessed=rows * (D * 2 + units * 10), transcendentals=0
        ),
        name="units_fore",
    )(normed, weight)


def run_units_back(cot, weight, packed):
    rows, units = cot.shape[0], weight.shape[0]
    tile = row_tile(rows)
    block = lambda w: pl.BlockSpec((tile, w), lambda r: (r, 0))
    return pl.pallas_call(
        units_back,
        grid=(rows // tile,),
        in_specs=[block(D), whole_block(weight.shape), block(2 * units)],
        out_specs=block(2 * units),
        out_shape=jax.ShapeDtypeStruct((rows, 2 * units), jnp.bfloat16),
        compiler_params=KERNEL_PARAMS,
        cost_estimate=pl.CostEstimate(
            flops=rows * D * units * 2, bytes_accessed=rows * (D * 2 + units * 12), transcendentals=0
        ),
        name="units_back",
    )(cot, weight, packed)


def adam_update(weight_old, gradient, moment_old, square_old, factor, rate, decay):
    clipped = gradient * factor
    moment_new = BETA_ONE * moment_old + (1.0 - BETA_ONE) * clipped
    square_new = BETA_TWO * square_old + (1.0 - BETA_TWO) * clipped * clipped
    moment_hat = moment_new / (1.0 - BETA_ONE**STEP)
    square_hat = square_new / (1.0 - BETA_TWO**STEP)
    weight_new = weight_old - rate * (
        moment_hat / (jnp.sqrt(square_hat) + ADAM_EPS) + decay * weight_old
    )
    return (weight_new, moment_new, square_new)


def local(
    tokens,
    cotangent,
    project_weight,
    output_weight,
    gate_up_weight,
    down_weight,
    norm_params,
    first_project,
    first_output,
    first_gate_up,
    first_down,
    first_norm,
    second_project,
    second_output,
    second_gate_up,
    second_down,
    second_norm,
):
    count = lax.axis_size("dp")
    blocks_half = count // 2
    me = lax.axis_index("dp")
    side = (me // 2) % 2
    spot = lax.axis_index("tensor")
    spots = lax.axis_size("tensor")
    micro_count, piece = tokens.shape[0], tokens.shape[1]
    head_cols = project_weight.shape[2] // 2
    unit_cols = gate_up_weight.shape[2] // 2
    whole = unit_cols - 64
    rows_each = project_weight.shape[1]
    seqs = 2 * micro_count
    rows_all = spots * seqs * piece

    def halves(first, second):
        first, second = first.astype(jnp.bfloat16), second.astype(jnp.bfloat16)
        return jnp.where(side == 0, first, second), jnp.where(side == 0, second, first)

    def project_half(s):
        return jnp.concatenate(
            [project_weight[k, :, s * head_cols : (s + 1) * head_cols] for k in range(3)], axis=1
        )

    def unit_spans(s):
        return slice(s * whole, (s + 1) * whole), slice(2 * whole + 64 * s, 2 * whole + 64 * (s + 1))

    def gate_up_half(s):
        wide, narrow = unit_spans(s)
        return jnp.concatenate(
            [gate_up_weight[k, :, span] for span in (wide, narrow) for k in range(2)], axis=1
        )

    def output_half(s):
        return output_weight[s * head_cols : (s + 1) * head_cols]

    def down_half(s):
        return jnp.concatenate([down_weight[span] for span in unit_spans(s)], axis=0)

    def gather_half(half_of, axis):
        return jnp.concatenate(gather_blocks(*halves(half_of(0), half_of(1))), axis=axis)

    norm_low = norm_params.astype(jnp.bfloat16)
    norm_full = jnp.concatenate(gather_blocks(norm_low, norm_low), axis=1).astype(jnp.float32)
    gain, shift = norm_full[0], norm_full[1]

    w_project = gather_half(project_half, 0)
    w_gate_up = gather_half(gate_up_half, 0)
    w_down = gather_half(down_half, 1)
    w_output = gather_half(output_half, 1)

    tok_rows = relative(tokens, 2, me, count).astype(jnp.float32)
    row_mean = jnp.mean(tok_rows, axis=2, keepdims=True)
    centered = tok_rows - row_mean
    row_scale = lax.rsqrt(jnp.mean(centered * centered, axis=2, keepdims=True) + NORM_EPS)
    unit_rows = centered * row_scale
    normed = (unit_rows * gain + shift).astype(jnp.bfloat16)
    cot_low = relative(cotangent, 2, me, count)

    all_normed = gather_rows(normed).reshape(rows_all, D)
    all_cot = gather_rows(cot_low).reshape(rows_all, D)

    order = jnp.array([0, 2, 1, 3])
    positions = ((spot ^ order)[:, None] * piece + jnp.arange(piece)[None, :]).reshape(-1)
    half_rot = ROT // 2
    inverse = 10000.0 ** (-2.0 * jnp.arange(half_rot, dtype=jnp.float32) / ROT)
    angles = positions.astype(jnp.float32)[:, None] * inverse[None, :]
    cosine, sine = jnp.cos(angles), jnp.sin(angles)
    none = jnp.zeros_like(sine)
    rest = jnp.zeros((angles.shape[0], HEAD_DIM - ROT), jnp.float32)
    tables = jnp.stack(
        [
            jnp.tile(jnp.concatenate(parts, axis=1), (1, 2))
            for parts in ((cosine, cosine, rest + 1.0), (-sine, none, rest), (none, sine, rest))
        ]
    )
    bias = jnp.where(positions[:, None] >= positions[None, :], 0.0, MASK_FILL)

    projected = dot_plain(all_normed, w_project).reshape(spots, seqs, piece, 3 * head_cols)
    turned, attended = run_attention_fore(projected, tables, bias)
    attended = attended.reshape(rows_all, head_cols)
    packed, hidden = run_units_fore(all_normed, w_gate_up)

    half_d = D // 2

    def side_of(values, i):
        return values[:, i * half_d : (i + 1) * half_d]

    def core_of(values, c):
        return values[c * (rows_all // 2) : (c + 1) * (rows_all // 2)]

    grad_down = scatter_blocks(lambda i: dot_rows(hidden, side_of(all_cot, i)), 1)
    grad_output = scatter_blocks(lambda i: dot_rows(attended, side_of(all_cot, i)), 1)

    d_packed = run_units_back(all_cot, w_down, packed)
    grad_gate_up = scatter_blocks(lambda i: dot_rows(side_of(all_normed, i), d_packed), 0)

    d_att = dot_cols(all_cot, w_output).astype(jnp.bfloat16).reshape(spots, seqs, piece, head_cols)
    d_project = run_attention_back(turned, d_att, tables, bias).reshape(rows_all, 3 * head_cols)
    grad_project = scatter_blocks(lambda i: dot_rows(side_of(all_normed, i), d_project), 0)

    def split_rows(values):
        return values.reshape(-1, piece, D)

    d_normed = scatter_rows(
        lambda c: split_rows(
            dot_cols(core_of(d_project, c), w_project) + dot_cols(core_of(d_packed, c), w_gate_up)
        )
    )
    summed = scatter_rows(
        lambda c: split_rows(
            dot_plain(core_of(attended, c), w_output) + dot_plain(core_of(hidden, c), w_down)
        )
    )
    layer_out = from_relative((tok_rows + summed).astype(jnp.bfloat16), 2, me, count)

    d_unit = d_normed * gain
    d_input = row_scale * (
        d_unit
        - jnp.mean(d_unit, axis=2, keepdims=True)
        - unit_rows * jnp.mean(d_unit * unit_rows, axis=2, keepdims=True)
    )
    input_grad = from_relative((cot_low.astype(jnp.float32) + d_input).astype(jnp.bfloat16), 2, me, count)

    grad_norm = jnp.stack(
        [jnp.sum(d_normed * unit_rows, axis=(0, 1)), jnp.sum(d_normed, axis=(0, 1))]
    )
    grad_norm = grad_norm[:, :half_d] + swap(grad_norm[:, half_d:], 1, 0)
    grad_norm = grad_norm.reshape(2, blocks_half, rows_each)
    norm_grad = grad_norm[:, 0]
    for j in range(1, blocks_half):
        norm_grad = norm_grad + swap(grad_norm[:, j], 2 * j, 0)
    norm_grad = norm_grad + swap(norm_grad, 0, 2)
    norm_grad = norm_grad + swap(norm_grad, 0, 1)

    def in_order(pair):
        mine, other = pair
        return jnp.where(side == 0, mine, other), jnp.where(side == 0, other, mine)

    project_pair = in_order(grad_project)
    gate_up_pair = in_order(grad_gate_up)
    down_pair = in_order(grad_down)
    grads = (
        jnp.stack(
            [
                jnp.concatenate([g[:, k * head_cols : (k + 1) * head_cols] for g in project_pair], axis=1)
                for k in range(3)
            ]
        ),
        jnp.concatenate(in_order(grad_output), axis=0),
        jnp.stack(
            [
                jnp.concatenate(
                    [g[:, k * whole : (k + 1) * whole] for g in gate_up_pair]
                    + [g[:, 2 * whole + 64 * k : 2 * whole + 64 * (k + 1)] for g in gate_up_pair],
                    axis=1,
                )
                for k in range(2)
            ]
        ),
        jnp.concatenate([g[:whole] for g in down_pair] + [g[whole:] for g in down_pair], axis=0),
        norm_grad,
    )
    square_local = sum(jnp.sum(g * g) for g in grads[:4]) + jnp.sum(norm_grad * norm_grad) / spots
    norm_total = jnp.sqrt(lax.psum(square_local, BOTH))
    limit = 0.03 * math.sqrt((4 * D * D + 3 * D * FF + 2 * D) * micro_count * count * SEQ)
    factor = jnp.minimum(1.0, limit / (norm_total + 1e-06))
    rates = (
        2.0 / math.sqrt(D),
        2.0 / math.sqrt(D // 32),
        2.0 / math.sqrt(D),
        2.0 / math.sqrt(FF),
        0.5,
    )
    decays = (0.1, 0.1, 0.1, 0.1, 0.0)
    masters = (project_weight, output_weight, gate_up_weight, down_weight, norm_params)
    firsts = (first_project, first_output, first_gate_up, first_down, first_norm)
    seconds = (second_project, second_output, second_gate_up, second_down, second_norm)
    updated = [
        adam_update(*parts) for parts in zip(masters, grads, firsts, seconds, [factor] * 5, rates, decays)
    ]
    return (
        layer_out,
        input_grad,
        *grads,
        norm_total,
        *[u[0] for u in updated],
        *[u[1] for u in updated],
        *[u[2] for u in updated],
    )


def solution(mesh):
    wide = P("dp", "tensor", None)
    stacked = P(None, "dp", "tensor")
    tall = P("tensor", "dp")
    params = (stacked, tall, stacked, tall, P(None, "dp"))
    return jax.shard_map(
        local,
        mesh=mesh,
        in_specs=(wide, wide, *params, *params, *params),
        out_specs=(wide, wide, *params, P(), *params, *params, *params),
        check_vma=False,
    )
```

```python
import functools
import math

import jax
import jax.numpy as jnp
from jax import lax
from jax.experimental import pallas as pl
from jax.experimental.pallas import tpu as pltpu
from jax.sharding import PartitionSpec as P

D = 2048
HEAD_DIM = 64
FF = 5632
SEQ = 320
STEP = 10
ROT = 16

BETA_ONE = 0.9
BETA_TWO = 0.999
ADAM_EPS = 1e-08
NORM_EPS = 1e-05
MASK_FILL = -1e30

BOTH = ("dp", "tensor")
MESH = pl.DeviceIdType.MESH


def swap(values, dp_flip, tensor_flip):
    dp_size, tensor_size = lax.axis_size("dp"), lax.axis_size("tensor")
    pairs = [
        (d * tensor_size + t, (d ^ dp_flip) * tensor_size + (t ^ tensor_flip))
        for d in range(dp_size)
        for t in range(tensor_size)
    ]
    return lax.ppermute(values, BOTH, pairs)


def block_order(count):
    return [2 * j + i for i in range(2) for j in range(count // 2)]


def relative(values, axis, me, count):
    width = values.shape[axis] // count
    return jnp.concatenate(
        [lax.dynamic_slice_in_dim(values, (me ^ r) * width, width, axis) for r in block_order(count)],
        axis=axis,
    )


def from_relative(values, axis, me, count):
    width = values.shape[axis] // count
    places = [((me ^ g) % 2) * (count // 2) + (me ^ g) // 2 for g in range(count)]
    return jnp.concatenate(
        [lax.dynamic_slice_in_dim(values, place * width, width, axis) for place in places],
        axis=axis,
    )


def flip_blocks(values, axis, count):
    width = values.shape[axis] // count
    return jnp.concatenate(
        [lax.slice_in_dim(values, (p ^ 1) * width, ((p ^ 1) + 1) * width, axis=axis) for p in range(count)],
        axis=axis,
    )


def gather_small(block):
    near = [block] + [swap(block, 2 * j, 0) for j in range(1, lax.axis_size("dp") // 2)]
    near = jnp.concatenate(near, axis=1)
    return jnp.concatenate([near, swap(near, 1, 0)], axis=1)


def place(dp_flip, tensor_flip):
    return (lax.axis_index("dp") ^ dp_flip, lax.axis_index("tensor") ^ tensor_flip)


def greet(places):
    barrier = pltpu.get_barrier_semaphore()
    for there in places:
        pl.semaphore_signal(barrier, inc=1, device_id=there, device_id_type=MESH)
    pl.semaphore_wait(barrier, len(places))


def send_to(there, source, target, send_sem, recv_sem):
    return pltpu.make_async_remote_copy(
        src_ref=source,
        dst_ref=target,
        send_sem=send_sem,
        recv_sem=recv_sem,
        device_id=there,
        device_id_type=MESH,
    )


def group_places(half):
    return [place(2 * j, 0) for j in range(1, half)] + [place(1, 0), place(0, 2), place(0, 1)]


def gather_all(half, layout, acts, *refs):
    n = len(layout)
    mine, other = refs[:n], refs[n : 2 * n]
    own_rows = refs[2 * n : 2 * n + acts]
    flipped_rows = refs[2 * n + acts : 2 * n + 2 * acts]
    outs = refs[2 * n + 2 * acts : 3 * n + 2 * acts]
    act_out = refs[3 * n + 2 * acts : 3 * n + 3 * acts]
    z_send, z_recv, x_send, x_recv, a_send, a_recv, own_sem = refs[3 * n + 3 * acts :]
    greet(group_places(half))

    def block(c, p):
        axis, width = layout[c]
        span = pl.ds(p * width, width)
        return outs[c].at[span] if axis == 0 else outs[c].at[:, span]

    def z_copy(c, j):
        source = (other if j % 2 else mine)[c]
        return send_to(place(2 * j, 0), source, block(c, j), z_send.at[c, j], z_recv.at[c, j])

    def x_copy(c, j):
        source = block(c, j) if j else mine[c]
        return send_to(place(1, 0), source, block(c, half + j), x_send.at[c, j], x_recv.at[c, j])

    def own_copy(c):
        return pltpu.make_async_copy(mine[c], block(c, 0), own_sem.at[c])

    def rows(a, index):
        each = act_out[a].shape[0] // 8
        return act_out[a].at[pl.ds(index * each, each)]

    def a_copy(a, k):
        source = (
            flipped_rows[a],
            own_rows[a],
            rows(a, 1),
            own_rows[a],
            rows(a, 1),
            rows(a, 2),
            rows(a, 3),
        )[k]
        there = place(2, 0) if k == 0 else place(0, 2) if k < 3 else place(0, 1)
        return send_to(there, source, rows(a, k + 1), a_send.at[a, k], a_recv.at[a, k])

    def own_act(a):
        return pltpu.make_async_copy(own_rows[a], rows(a, 0), own_sem.at[n + a])

    def act_begin(a):
        for k in (0, 1, 3):
            a_copy(a, k).start()

    far = range(1, half)
    for j in far:
        z_copy(0, j).start()
    for c in range(min(2, n)):
        x_copy(c, 0).start()
    act_begin(0)
    for a in range(acts):
        own_act(a).start()
    for c in range(n):
        own_copy(c).start()
    for c in range(n):
        for j in far:
            z_copy(c, j).wait_recv()
            x_copy(c, j).start()
            if c + 1 < n:
                z_copy(c + 1, j).start()
        if c + 2 < n:
            x_copy(c + 2, 0).start()
        if c < acts:
            a_copy(c, 0).wait_recv()
            a_copy(c, 2).start()
            a_copy(c, 4).start()
            a_copy(c, 1).wait_recv()
            a_copy(c, 5).start()
            if c + 1 < acts:
                act_begin(c + 1)
        if 1 <= c <= acts:
            a_copy(c - 1, 2).wait_recv()
            a_copy(c - 1, 6).start()
    for c in range(n):
        own_copy(c).wait()
        for j in range(half):
            if j:
                z_copy(c, j).wait_send()
            x_copy(c, j).wait()
    for a in range(acts):
        own_act(a).wait()
        for k in range(7):
            a_copy(a, k).wait_send()
            if k >= 3:
                a_copy(a, k).wait_recv()


def run_gather(half, chunks, acts):
    layout, shapes = [], []
    for mine, _, axis in chunks:
        layout.append((axis, mine.shape[axis]))
        shape = list(mine.shape)
        shape[axis] *= 2 * half
        shapes.append(jax.ShapeDtypeStruct(tuple(shape), mine.dtype))
    shapes += [jax.ShapeDtypeStruct((a.shape[0] * 8,) + a.shape[1:], a.dtype) for a in acts]
    n, m = len(chunks), len(acts)
    ins = [c[0] for c in chunks] + [c[1] for c in chunks] + acts
    ins += [flip_blocks(a, a.ndim - 1, 2 * half) for a in acts]
    anywhere = pl.BlockSpec(memory_space=pl.ANY)
    sem = pltpu.SemaphoreType.DMA
    return pl.pallas_call(
        functools.partial(gather_all, half, layout, m),
        out_shape=shapes,
        in_specs=[anywhere] * len(ins),
        out_specs=[anywhere] * len(shapes),
        scratch_shapes=[sem((n, half))] * 4 + [sem((m, 7))] * 2 + [sem((n + m,))],
        compiler_params=pltpu.CompilerParams(collective_id=0, has_side_effects=True),
        name="gather_all",
    )(*ins)


def add_rows(out_ref, *terms):
    rows = out_ref.shape[0]
    step = 32 if rows % 32 == 0 else 16

    def body(i, carry):
        span = pl.ds(pl.multiple_of(i * step, step), step)
        total = terms[0][span].astype(jnp.float32)
        for term in terms[1:]:
            total = total + term[span].astype(jnp.float32)
        out_ref[span] = total.astype(out_ref.dtype)
        return carry

    lax.fori_loop(0, rows // step, body, 0)


def scatter_all(half, axes, acts, window, *refs):
    n = len(axes)

    def take(count):
        nonlocal refs
        head, refs = refs[:count], refs[count:]
        return head

    away, near, act_away, act_close = take(n), take(n), take(acts), take(acts)
    mine, other, act_sum, act_far = take(n), take(n), take(acts), take(acts)
    x_in, x_own, z_in = take(n), take(n), take(n)
    a_near, a_core, a_y, a_out = take(acts), take(acts), take(acts), take(acts)
    x_send, x_recv, z_send, z_recv, own_sem, a_send, a_recv, a_own = refs
    greet(group_places(half))

    def piece(ref, c, j):
        width = ref.shape[axes[c]] // half
        span = pl.ds(j * width, width)
        return ref.at[span] if axes[c] == 0 else ref.at[:, span]

    def x_copy(c, j):
        return send_to(place(1, 0), piece(away[c], c, j), x_in[c].at[j], x_send.at[c, j], x_recv.at[c, j])

    def z_copy(c, j):
        return send_to(place(2 * j, 0), x_in[c].at[j], z_in[c].at[j], z_send.at[c, j], z_recv.at[c, j])

    def own_copy(c, j):
        return pltpu.make_async_copy(piece(near[c], c, j), x_own[c].at[j], own_sem.at[c, j])

    def a_copy(a, s):
        source = (act_away[a], a_out[a].at[pl.ds(0, 4)], a_out[a].at[pl.ds(4, 2)])[s]
        target = (a_core[a], a_y[a], act_far[a])[s]
        there = (place(0, 1), place(0, 2), place(2, 0))[s]
        return send_to(there, source, target, a_send.at[a, s], a_recv.at[a, s])

    def a_load(a):
        return pltpu.make_async_copy(act_close[a], a_near[a], a_own.at[a])

    def a_step(a, s):
        if s == 0:
            a_load(a).wait()
            a_copy(a, 0).wait_recv()
            for i in range(4):
                add_rows(a_out[a].at[i], a_near[a].at[4 + i], a_core[a].at[4 + i])
            a_copy(a, 1).start()
        else:
            a_copy(a, 1).wait_recv()
            for i in range(2):
                add_rows(a_out[a].at[4 + i], *[part[a].at[2 + i] for part in (a_near, a_core, a_y)])
            a_copy(a, 2).start()
            for i in range(2):
                add_rows(act_sum[a].at[i], *[part[a].at[i] for part in (a_near, a_core, a_y)])

    order = [(c, j) for c in range(n) for j in range(half - 1, -1, -1)]
    for c, j in order[:window]:
        x_copy(c, j).start()
    for a in range(acts):
        a_copy(a, 0).start()
        a_load(a).start()
    for c, j in order:
        own_copy(c, j).start()
    steps = [(a, s) for s in range(2) for a in range(acts)]
    for i, (c, j) in enumerate(order):
        x_copy(c, j).wait_recv()
        if i + window < len(order):
            x_copy(*order[i + window]).start()
        own_copy(c, j).wait()
        if j:
            add_rows(x_in[c].at[j], x_in[c].at[j], x_own[c].at[j])
            z_copy(c, j).start()
        else:
            add_rows(mine[c], x_in[c].at[j], x_own[c].at[j])
        if steps and i % 2 == 1:
            a_step(*steps.pop(0))
    for c in range(n):
        for j in range(1, half):
            z_copy(c, j).wait_recv()
        add_rows(other[c], *[z_in[c].at[j] for j in range(1, half, 2)])
        add_rows(mine[c], mine[c], *[z_in[c].at[j] for j in range(2, half, 2)])
    for c in range(n):
        for j in range(half):
            x_copy(c, j).wait_send()
            if j:
                z_copy(c, j).wait_send()
    for a in range(acts):
        for s in range(3):
            a_copy(a, s).wait_send()
        a_copy(a, 2).wait_recv()


def run_scatter(half, chunks, acts, window=2):
    n, m = len(chunks), len(acts)
    axes = [c[2] for c in chunks]
    pieces = []
    for away, _, axis in chunks:
        shape = list(away.shape)
        shape[axis] //= half
        pieces.append(tuple(shape))
    anywhere = pl.BlockSpec(memory_space=pl.ANY)
    vmem = pl.BlockSpec(memory_space=pltpu.VMEM)
    ins = [c[k] for k in range(2) for c in chunks] + [a[k] for k in range(2) for a in acts]
    low = jnp.bfloat16

    def part(a, top, bottom):
        return (a.shape[0] * top // bottom,) + a.shape[1:]

    shapes = [jax.ShapeDtypeStruct(p, jnp.float32) for p in pieces] * 2
    shapes += [jax.ShapeDtypeStruct(part(a, 1, 4), kind) for kind in (jnp.float32, low) for a, _ in acts]
    scratch = [pltpu.VMEM((half,) + p, low) for p in pieces] * 3
    scratch += [pltpu.VMEM(part(a, *share), low) for share in ((1, 1), (1, 1), (1, 2), (3, 4)) for a, _ in acts]
    sem = pltpu.SemaphoreType.DMA
    scratch += [sem((n, half))] * 5 + [sem((m, 3))] * 2 + [sem((m,))]
    outs = pl.pallas_call(
        functools.partial(scatter_all, half, axes, m, window),
        out_shape=shapes,
        in_specs=[anywhere] * len(ins),
        out_specs=[vmem] * (2 * n + m) + [anywhere] * m,
        scratch_shapes=scratch,
        compiler_params=pltpu.CompilerParams(
            collective_id=1, has_side_effects=True, vmem_limit_bytes=60 * 1024 * 1024
        ),
        name="scatter_all",
    )(*ins)
    totals = [
        outs[2 * n + a] + flip_blocks(outs[2 * n + m + a].astype(jnp.float32), 2, 2 * half) for a in range(m)
    ]
    return list(zip(outs[:n], outs[n : 2 * n])), totals


def sum_kernel(rounds, in_ref, out_ref, sent, came, send_sem, recv_sem):
    places = [place(*flips) for flips in rounds]
    greet(places)
    out_ref[...] = in_ref[...]
    for k, there in enumerate(places):
        sent[k] = out_ref[...]
        copy = send_to(there, sent.at[k], came.at[k], send_sem.at[k], recv_sem.at[k])
        copy.start()
        copy.wait()
        out_ref[...] = out_ref[...] + came[k]


def sum_everywhere(value):
    rounds = []
    for axis, size in enumerate((lax.axis_size("dp"), lax.axis_size("tensor"))):
        flip = 1
        while flip < size:
            rounds.append((0, flip) if axis else (flip, 0))
            flip *= 2
    vmem = pl.BlockSpec(memory_space=pltpu.VMEM)
    tile = (8, 128)
    sem = pltpu.SemaphoreType.DMA
    total = pl.pallas_call(
        functools.partial(sum_kernel, rounds),
        out_shape=jax.ShapeDtypeStruct(tile, jnp.float32),
        in_specs=[vmem],
        out_specs=vmem,
        scratch_shapes=[pltpu.VMEM((len(rounds),) + tile, jnp.float32)] * 2 + [sem((len(rounds),))] * 2,
        compiler_params=pltpu.CompilerParams(collective_id=2, has_side_effects=True),
        name="sum_everywhere",
    )(jnp.full(tile, value))
    return total[0, 0]


def dot_plain(a, b):
    return lax.dot_general(a, b, (((1,), (0,)), ((), ())), preferred_element_type=jnp.float32)


def dot_rows(a, b):
    return lax.dot_general(a, b, (((0,), (0,)), ((), ())), preferred_element_type=jnp.float32)


def dot_cols(a, b):
    return lax.dot_general(a, b, (((1,), (1,)), ((), ())), preferred_element_type=jnp.float32)


def turn(values, tables, direction):
    cosine, low_sine, high_sine = tables
    lanes = values.shape[1]
    half_rot = ROT // 2
    moved = pltpu.roll(values, lanes - half_rot, 1) * low_sine + pltpu.roll(values, half_rot, 1) * high_sine
    return values * cosine + direction * moved


def head_probabilities(query, key, bias):
    scores = dot_cols(query, key) * 0.125 + bias
    exponent = jnp.exp(scores - jnp.max(scores, axis=1, keepdims=True))
    return exponent / jnp.sum(exponent, axis=1, keepdims=True)


def attention_fore(projected_ref, tables_ref, bias_ref, turned_ref, attended_ref):
    spots, _, piece, width = projected_ref.shape
    rows, third = spots * piece, width // 3
    tables = [tables_ref[k] for k in range(3)]
    first = lax.broadcasted_iota(jnp.int32, (rows, 128), 1) < HEAD_DIM
    for pair in range(third // 128):
        span = [slice(k * third + pair * 128, k * third + pair * 128 + 128) for k in range(3)]
        query, key, value = [projected_ref[:, 0, :, s].reshape(rows, 128) for s in span]
        query = turn(query, tables, 1.0).astype(jnp.bfloat16)
        key = turn(key, tables, 1.0).astype(jnp.bfloat16)
        value = value.astype(jnp.bfloat16)
        for s, part in zip(span, (query, key, value)):
            turned_ref[:, 0, :, s] = part.reshape(spots, piece, 128)
        none = jnp.zeros_like(query)
        outs = [
            dot_plain(head_probabilities(q, key, bias_ref[...]).astype(jnp.bfloat16), value)
            for q in (jnp.where(first, query, none), jnp.where(first, none, query))
        ]
        attended_ref[:, 0, :, span[0]] = (
            jnp.where(first, outs[0], outs[1]).astype(jnp.bfloat16).reshape(spots, piece, 128)
        )


def attention_back(turned_ref, d_att_ref, tables_ref, bias_ref, d_project_ref):
    spots, _, piece, width = turned_ref.shape
    rows, third = spots * piece, width // 3
    tables = [tables_ref[k] for k in range(3)]
    first = lax.broadcasted_iota(jnp.int32, (rows, 128), 1) < HEAD_DIM
    for pair in range(third // 128):
        span = [slice(k * third + pair * 128, k * third + pair * 128 + 128) for k in range(3)]
        query, key, value = [turned_ref[:, 0, :, s].reshape(rows, 128) for s in span]
        d_att = d_att_ref[:, 0, :, span[0]].reshape(rows, 128)
        none = jnp.zeros_like(query)
        parts = []
        for head in range(2):
            keep = first if head == 0 else jnp.logical_not(first)
            one_query = jnp.where(keep, query, none)
            one_d_att = jnp.where(keep, d_att, none)
            prob = head_probabilities(one_query, key, bias_ref[...])
            d_value = dot_rows(prob.astype(jnp.bfloat16), d_att)
            d_prob = dot_cols(one_d_att, value)
            d_score = (prob * (d_prob - jnp.sum(d_prob * prob, axis=1, keepdims=True))).astype(
                jnp.bfloat16
            )
            parts.append((dot_plain(d_score, key), dot_rows(d_score, query), d_value))
        joined = [jnp.where(first, one, two) for one, two in zip(*parts)]
        done = (turn(0.125 * joined[0], tables, -1.0), turn(0.125 * joined[1], tables, -1.0), joined[2])
        for s, part in zip(span, done):
            d_project_ref[:, 0, :, s] = part.astype(jnp.bfloat16).reshape(spots, piece, 128)


def join_gate_up(packed, whole):
    last = packed[:, 2 * whole :]
    gate = jnp.concatenate([packed[:, :whole], last], axis=1)
    up = jnp.concatenate([packed[:, whole : 2 * whole], pltpu.roll(last, 64, 1)], axis=1)
    return gate, up


def units_fore(normed_ref, weight_ref, packed_ref, hidden_ref):
    packed = dot_plain(normed_ref[...], weight_ref[...])
    packed_ref[...] = packed
    units = hidden_ref.shape[1]
    gate, up = join_gate_up(packed, units - 64)
    hidden_ref[...] = (gate * jax.nn.sigmoid(gate) * up).astype(jnp.bfloat16)[:, :units]


def units_back(cot_ref, weight_ref, packed_ref, d_packed_ref):
    units = weight_ref.shape[0]
    whole = units - 64
    d_hid = dot_cols(cot_ref[...], weight_ref[...]).astype(jnp.bfloat16).astype(jnp.float32)
    d_hid = jnp.concatenate([d_hid, jnp.zeros((d_hid.shape[0], 64), jnp.float32)], axis=1)
    gate, up = join_gate_up(packed_ref[...], whole)
    sigmoid_gate = jax.nn.sigmoid(gate)
    d_gate = d_hid * up * (sigmoid_gate * (1.0 + gate * (1.0 - sigmoid_gate)))
    d_up = d_hid * (gate * sigmoid_gate)
    first = lax.broadcasted_iota(jnp.int32, (gate.shape[0], 128), 1) < 64
    last = jnp.where(first, d_gate[:, whole:], pltpu.roll(d_up[:, whole:], 64, 1))
    d_packed_ref[:, :whole] = d_gate[:, :whole].astype(jnp.bfloat16)
    d_packed_ref[:, whole : 2 * whole] = d_up[:, :whole].astype(jnp.bfloat16)
    d_packed_ref[:, 2 * whole :] = last.astype(jnp.bfloat16)


def whole_block(shape):
    return pl.BlockSpec(shape, lambda *_: (0,) * len(shape))


KERNEL_PARAMS = pltpu.CompilerParams(vmem_limit_bytes=40 * 1024 * 1024)


def run_attention_fore(projected, tables, bias):
    spots, seqs, piece, width = projected.shape
    block = lambda w: pl.BlockSpec((spots, 1, piece, w), lambda s: (0, s, 0, 0))
    rows = spots * piece
    return pl.pallas_call(
        attention_fore,
        grid=(seqs,),
        in_specs=[block(width), whole_block(tables.shape), whole_block(bias.shape)],
        out_specs=[block(width), block(width // 3)],
        out_shape=[
            jax.ShapeDtypeStruct((spots, seqs, piece, width), jnp.bfloat16),
            jax.ShapeDtypeStruct((spots, seqs, piece, width // 3), jnp.bfloat16),
        ],
        compiler_params=KERNEL_PARAMS,
        cost_estimate=pl.CostEstimate(
            flops=seqs * rows * rows * width * 2, bytes_accessed=seqs * rows * width * 7, transcendentals=0
        ),
        name="attention_fore",
    )(projected, tables, bias)


def run_attention_back(turned, d_att, tables, bias):
    spots, seqs, piece, width = turned.shape
    block = lambda w: pl.BlockSpec((spots, 1, piece, w), lambda s: (0, s, 0, 0))
    rows = spots * piece
    return pl.pallas_call(
        attention_back,
        grid=(seqs,),
        in_specs=[block(width), block(width // 3), whole_block(tables.shape), whole_block(bias.shape)],
        out_specs=block(width),
        out_shape=jax.ShapeDtypeStruct((spots, seqs, piece, width), jnp.bfloat16),
        compiler_params=KERNEL_PARAMS,
        cost_estimate=pl.CostEstimate(
            flops=seqs * rows * rows * width * 5, bytes_accessed=seqs * rows * width * 5, transcendentals=0
        ),
        name="attention_back",
    )(turned, d_att, tables, bias)


def row_tile(rows):
    return 256 if rows % 256 == 0 else rows // 8


def run_units_fore(normed, weight):
    rows, units = normed.shape[0], weight.shape[1] // 2
    tile = row_tile(rows)
    block = lambda w: pl.BlockSpec((tile, w), lambda r: (r, 0))
    return pl.pallas_call(
        units_fore,
        grid=(rows // tile,),
        in_specs=[block(D), whole_block(weight.shape)],
        out_specs=[block(2 * units), block(units)],
        out_shape=[
            jax.ShapeDtypeStruct((rows, 2 * units), jnp.float32),
            jax.ShapeDtypeStruct((rows, units), jnp.bfloat16),
        ],
        compiler_params=KERNEL_PARAMS,
        cost_estimate=pl.CostEstimate(
            flops=rows * D * units * 4, bytes_accessed=rows * (D * 2 + units * 10), transcendentals=0
        ),
        name="units_fore",
    )(normed, weight)


def run_units_back(cot, weight, packed):
    rows, units = cot.shape[0], weight.shape[0]
    tile = row_tile(rows)
    block = lambda w: pl.BlockSpec((tile, w), lambda r: (r, 0))
    return pl.pallas_call(
        units_back,
        grid=(rows // tile,),
        in_specs=[block(D), whole_block(weight.shape), block(2 * units)],
        out_specs=block(2 * units),
        out_shape=jax.ShapeDtypeStruct((rows, 2 * units), jnp.bfloat16),
        compiler_params=KERNEL_PARAMS,
        cost_estimate=pl.CostEstimate(
            flops=rows * D * units * 2, bytes_accessed=rows * (D * 2 + units * 12), transcendentals=0
        ),
        name="units_back",
    )(cot, weight, packed)


def adam_update(weight_old, gradient, moment_old, square_old, factor, rate, decay):
    clipped = gradient * factor
    moment_new = BETA_ONE * moment_old + (1.0 - BETA_ONE) * clipped
    square_new = BETA_TWO * square_old + (1.0 - BETA_TWO) * clipped * clipped
    moment_hat = moment_new / (1.0 - BETA_ONE**STEP)
    square_hat = square_new / (1.0 - BETA_TWO**STEP)
    weight_new = weight_old - rate * (
        moment_hat / (jnp.sqrt(square_hat) + ADAM_EPS) + decay * weight_old
    )
    return (weight_new, moment_new, square_new)


def local(
    tokens,
    cotangent,
    project_weight,
    output_weight,
    gate_up_weight,
    down_weight,
    norm_params,
    first_project,
    first_output,
    first_gate_up,
    first_down,
    first_norm,
    second_project,
    second_output,
    second_gate_up,
    second_down,
    second_norm,
):
    count = lax.axis_size("dp")
    blocks_half = count // 2
    me = lax.axis_index("dp")
    side = (me // 2) % 2
    spot = lax.axis_index("tensor")
    spots = lax.axis_size("tensor")
    micro_count, piece = tokens.shape[0], tokens.shape[1]
    head_cols = project_weight.shape[2] // 2
    unit_cols = gate_up_weight.shape[2] // 2
    whole = unit_cols - 64
    rows_each = project_weight.shape[1]
    seqs = 2 * micro_count
    rows_all = spots * seqs * piece

    def halves(first, second):
        first, second = first.astype(jnp.bfloat16), second.astype(jnp.bfloat16)
        return jnp.where(side == 0, first, second), jnp.where(side == 0, second, first)

    def project_half(s):
        return jnp.concatenate(
            [project_weight[k, :, s * head_cols : (s + 1) * head_cols] for k in range(3)], axis=1
        )

    def unit_spans(s):
        return slice(s * whole, (s + 1) * whole), slice(2 * whole + 64 * s, 2 * whole + 64 * (s + 1))

    def gate_up_half(s):
        wide, narrow = unit_spans(s)
        return jnp.concatenate(
            [gate_up_weight[k, :, span] for span in (wide, narrow) for k in range(2)], axis=1
        )

    def output_half(s):
        return output_weight[s * head_cols : (s + 1) * head_cols]

    def down_half(s):
        return jnp.concatenate([down_weight[span] for span in unit_spans(s)], axis=0)

    by_columns = rows_each % 128 == 0

    norm_low = norm_params.astype(jnp.bfloat16)
    norm_full = gather_small(norm_low).astype(jnp.float32)
    gain, shift = norm_full[0], norm_full[1]

    tok_rows = relative(tokens, 2, me, count).astype(jnp.float32)
    row_mean = jnp.mean(tok_rows, axis=2, keepdims=True)
    centered = tok_rows - row_mean
    row_scale = lax.rsqrt(jnp.mean(centered * centered, axis=2, keepdims=True) + NORM_EPS)
    unit_rows = centered * row_scale
    normed = (unit_rows * gain + shift).astype(jnp.bfloat16)
    cot_low = relative(cotangent, 2, me, count)

    def chunk(half_of, columns):
        pair = halves(half_of(0), half_of(1))
        if columns and not by_columns:
            return (pair[0].T, pair[1].T, 0)
        return (*pair, int(columns))

    gathered = run_gather(
        blocks_half,
        [chunk(project_half, False), chunk(gate_up_half, False), chunk(down_half, True), chunk(output_half, True)],
        [normed, cot_low],
    )
    w_project, w_gate_up, w_down, w_output = gathered[:4]
    if not by_columns:
        w_down, w_output = w_down.T, w_output.T
    all_normed, all_cot = [rows.reshape(rows_all, D) for rows in gathered[4:]]

    order = jnp.array([0, 2, 1, 3])
    positions = ((spot ^ order)[:, None] * piece + jnp.arange(piece)[None, :]).reshape(-1)
    half_rot = ROT // 2
    inverse = 10000.0 ** (-2.0 * jnp.arange(half_rot, dtype=jnp.float32) / ROT)
    angles = positions.astype(jnp.float32)[:, None] * inverse[None, :]
    cosine, sine = jnp.cos(angles), jnp.sin(angles)
    none = jnp.zeros_like(sine)
    rest = jnp.zeros((angles.shape[0], HEAD_DIM - ROT), jnp.float32)
    tables = jnp.stack(
        [
            jnp.tile(jnp.concatenate(parts, axis=1), (1, 2))
            for parts in ((cosine, cosine, rest + 1.0), (-sine, none, rest), (none, sine, rest))
        ]
    )
    bias = jnp.where(positions[:, None] >= positions[None, :], 0.0, MASK_FILL)

    projected = dot_plain(all_normed, w_project).reshape(spots, seqs, piece, 3 * head_cols)
    turned, attended = run_attention_fore(projected, tables, bias)
    attended = attended.reshape(rows_all, head_cols)
    packed, hidden = run_units_fore(all_normed, w_gate_up)

    half_d = D // 2

    def side_of(values, i):
        return values[:, i * half_d : (i + 1) * half_d]

    def core_of(values, c):
        return values[c * (rows_all // 2) : (c + 1) * (rows_all // 2)]

    def by_side(left_of, right_of, columns=False):
        def one(i):
            if columns and not by_columns:
                return dot_rows(right_of(i), left_of(i)).astype(jnp.bfloat16)
            return dot_rows(left_of(i), right_of(i)).astype(jnp.bfloat16)

        return (one(1), one(0), int(columns and by_columns))

    def split_rows(values):
        return values.astype(jnp.bfloat16).reshape(-1, piece, D)

    cot_of = functools.partial(side_of, all_cot)
    normed_of = functools.partial(side_of, all_normed)
    down_parts = by_side(lambda i: hidden, cot_of, True)
    output_parts = by_side(lambda i: attended, cot_of, True)

    d_packed = run_units_back(all_cot, w_down, packed)
    gate_up_parts = by_side(normed_of, lambda i: d_packed)

    d_att = dot_cols(all_cot, w_output).astype(jnp.bfloat16).reshape(spots, seqs, piece, head_cols)
    d_project = run_attention_back(turned, d_att, tables, bias).reshape(rows_all, 3 * head_cols)
    project_parts = by_side(normed_of, lambda i: d_project)

    out_parts = [
        split_rows(dot_plain(core_of(attended, c), w_output) + dot_plain(core_of(hidden, c), w_down))
        for c in (1, 0)
    ]
    back_parts = [
        split_rows(dot_cols(core_of(d_project, c), w_project) + dot_cols(core_of(d_packed, c), w_gate_up))
        for c in (1, 0)
    ]
    (grad_down, grad_output, grad_gate_up, grad_project), (d_normed, summed) = run_scatter(
        blocks_half, [down_parts, output_parts, gate_up_parts, project_parts], [back_parts, out_parts]
    )
    if not by_columns:
        grad_down, grad_output = [tuple(g.T for g in pair) for pair in (grad_down, grad_output)]
    layer_out = from_relative((tok_rows + summed).astype(jnp.bfloat16), 2, me, count)

    d_unit = d_normed * gain
    d_input = row_scale * (
        d_unit
        - jnp.mean(d_unit, axis=2, keepdims=True)
        - unit_rows * jnp.mean(d_unit * unit_rows, axis=2, keepdims=True)
    )
    input_grad = from_relative((cot_low.astype(jnp.float32) + d_input).astype(jnp.bfloat16), 2, me, count)

    grad_norm = jnp.stack(
        [jnp.sum(d_normed * unit_rows, axis=(0, 1)), jnp.sum(d_normed, axis=(0, 1))]
    )
    grad_norm = grad_norm[:, :half_d] + swap(grad_norm[:, half_d:], 1, 0)
    grad_norm = grad_norm.reshape(2, blocks_half, rows_each)
    norm_grad = grad_norm[:, 0]
    for j in range(1, blocks_half):
        norm_grad = norm_grad + swap(grad_norm[:, j], 2 * j, 0)
    norm_grad = norm_grad + swap(norm_grad, 0, 2)
    norm_grad = norm_grad + swap(norm_grad, 0, 1)

    def in_order(pair):
        mine, other = pair
        return jnp.where(side == 0, mine, other), jnp.where(side == 0, other, mine)

    project_pair = in_order(grad_project)
    gate_up_pair = in_order(grad_gate_up)
    down_pair = in_order(grad_down)
    grads = (
        jnp.stack(
            [
                jnp.concatenate([g[:, k * head_cols : (k + 1) * head_cols] for g in project_pair], axis=1)
                for k in range(3)
            ]
        ),
        jnp.concatenate(in_order(grad_output), axis=0),
        jnp.stack(
            [
                jnp.concatenate(
                    [g[:, k * whole : (k + 1) * whole] for g in gate_up_pair]
                    + [g[:, 2 * whole + 64 * k : 2 * whole + 64 * (k + 1)] for g in gate_up_pair],
                    axis=1,
                )
                for k in range(2)
            ]
        ),
        jnp.concatenate([g[:whole] for g in down_pair] + [g[whole:] for g in down_pair], axis=0),
        norm_grad,
    )
    square_local = sum(jnp.sum(g * g) for g in grads[:4]) + jnp.sum(norm_grad * norm_grad) / spots
    norm_total = jnp.sqrt(sum_everywhere(square_local))
    limit = 0.03 * math.sqrt((4 * D * D + 3 * D * FF + 2 * D) * micro_count * count * SEQ)
    factor = jnp.minimum(1.0, limit / (norm_total + 1e-06))
    rates = (
        2.0 / math.sqrt(D),
        2.0 / math.sqrt(D // 32),
        2.0 / math.sqrt(D),
        2.0 / math.sqrt(FF),
        0.5,
    )
    decays = (0.1, 0.1, 0.1, 0.1, 0.0)
    masters = (project_weight, output_weight, gate_up_weight, down_weight, norm_params)
    firsts = (first_project, first_output, first_gate_up, first_down, first_norm)
    seconds = (second_project, second_output, second_gate_up, second_down, second_norm)
    updated = [
        adam_update(*parts) for parts in zip(masters, grads, firsts, seconds, [factor] * 5, rates, decays)
    ]
    return (
        layer_out,
        input_grad,
        *grads,
        norm_total,
        *[u[0] for u in updated],
        *[u[1] for u in updated],
        *[u[2] for u in updated],
    )


def solution(mesh):
    wide = P("dp", "tensor", None)
    stacked = P(None, "dp", "tensor")
    tall = P("tensor", "dp")
    params = (stacked, tall, stacked, tall, P(None, "dp"))
    return jax.shard_map(
        local,
        mesh=mesh,
        in_specs=(wide, wide, *params, *params, *params),
        out_specs=(wide, wide, *params, P(), *params, *params, *params),
        check_vma=False,
    )
```

```python
import functools
import math

import jax
import jax.numpy as jnp
from jax import lax
from jax.experimental import pallas as pl
from jax.experimental.pallas import tpu as pltpu
from jax.sharding import PartitionSpec as P

D = 2048
HEAD_DIM = 64
FF = 5632
SEQ = 320
STEP = 10
ROT = 16

BETA_ONE = 0.9
BETA_TWO = 0.999
ADAM_EPS = 1e-08
NORM_EPS = 1e-05
MASK_FILL = -1e30

BOTH = ("dp", "tensor")
MESH = pl.DeviceIdType.MESH


def swap(values, dp_flip, tensor_flip):
    dp_size, tensor_size = lax.axis_size("dp"), lax.axis_size("tensor")
    pairs = [
        (d * tensor_size + t, (d ^ dp_flip) * tensor_size + (t ^ tensor_flip))
        for d in range(dp_size)
        for t in range(tensor_size)
    ]
    return lax.ppermute(values, BOTH, pairs)


def block_order(count):
    return [2 * j + i for i in range(2) for j in range(count // 2)]


def relative(values, axis, me, count):
    width = values.shape[axis] // count
    return jnp.concatenate(
        [lax.dynamic_slice_in_dim(values, (me ^ r) * width, width, axis) for r in block_order(count)],
        axis=axis,
    )


def from_relative(values, axis, me, count):
    width = values.shape[axis] // count
    places = [((me ^ g) % 2) * (count // 2) + (me ^ g) // 2 for g in range(count)]
    return jnp.concatenate(
        [lax.dynamic_slice_in_dim(values, place * width, width, axis) for place in places],
        axis=axis,
    )


def flip_blocks(values, axis, count):
    width = values.shape[axis] // count
    return jnp.concatenate(
        [lax.slice_in_dim(values, (p ^ 1) * width, ((p ^ 1) + 1) * width, axis=axis) for p in range(count)],
        axis=axis,
    )


def gather_small(block):
    near = [block] + [swap(block, 2 * j, 0) for j in range(1, lax.axis_size("dp") // 2)]
    near = jnp.concatenate(near, axis=1)
    return jnp.concatenate([near, swap(near, 1, 0)], axis=1)


def place(dp_flip, tensor_flip):
    return (lax.axis_index("dp") ^ dp_flip, lax.axis_index("tensor") ^ tensor_flip)


def greet(places):
    barrier = pltpu.get_barrier_semaphore()
    for there in places:
        pl.semaphore_signal(barrier, inc=1, device_id=there, device_id_type=MESH)
    pl.semaphore_wait(barrier, len(places))


def send_to(there, source, target, send_sem, recv_sem):
    return pltpu.make_async_remote_copy(
        src_ref=source,
        dst_ref=target,
        send_sem=send_sem,
        recv_sem=recv_sem,
        device_id=there,
        device_id_type=MESH,
    )


def group_places(half):
    return [place(2 * j, 0) for j in range(1, half)] + [place(1, 0), place(0, 2), place(0, 1)]


def gather_all(half, layout, acts, *refs):
    n = len(layout)
    mine, other = refs[:n], refs[n : 2 * n]
    own_rows = refs[2 * n : 2 * n + acts]
    flipped_rows = refs[2 * n + acts : 2 * n + 2 * acts]
    outs = refs[2 * n + 2 * acts : 3 * n + 2 * acts]
    act_out = refs[3 * n + 2 * acts : 3 * n + 3 * acts]
    z_send, z_recv, x_send, x_recv, a_send, a_recv, own_sem = refs[3 * n + 3 * acts :]
    greet(group_places(half))

    def block(c, p):
        axis, width = layout[c]
        span = pl.ds(p * width, width)
        return outs[c].at[span] if axis == 0 else outs[c].at[:, span]

    def z_copy(c, j):
        source = (other if j % 2 else mine)[c]
        return send_to(place(2 * j, 0), source, block(c, j), z_send.at[c, j], z_recv.at[c, j])

    def x_copy(c, j):
        source = block(c, j) if j else mine[c]
        return send_to(place(1, 0), source, block(c, half + j), x_send.at[c, j], x_recv.at[c, j])

    def own_copy(c):
        return pltpu.make_async_copy(mine[c], block(c, 0), own_sem.at[c])

    def rows(a, index):
        each = act_out[a].shape[0] // 8
        return act_out[a].at[pl.ds(index * each, each)]

    def a_copy(a, k):
        source = (
            flipped_rows[a],
            own_rows[a],
            rows(a, 1),
            own_rows[a],
            rows(a, 1),
            rows(a, 2),
            rows(a, 3),
        )[k]
        there = place(2, 0) if k == 0 else place(0, 2) if k < 3 else place(0, 1)
        return send_to(there, source, rows(a, k + 1), a_send.at[a, k], a_recv.at[a, k])

    def own_act(a):
        return pltpu.make_async_copy(own_rows[a], rows(a, 0), own_sem.at[n + a])

    def act_begin(a):
        for k in (0, 1, 3):
            a_copy(a, k).start()

    far = range(1, half)
    for j in far:
        z_copy(0, j).start()
    for c in range(min(2, n)):
        x_copy(c, 0).start()
    act_begin(0)
    for a in range(acts):
        own_act(a).start()
    for c in range(n):
        own_copy(c).start()
    for c in range(n):
        for j in far:
            z_copy(c, j).wait_recv()
            x_copy(c, j).start()
            if c + 1 < n:
                z_copy(c + 1, j).start()
        if c + 2 < n:
            x_copy(c + 2, 0).start()
        if c < acts:
            a_copy(c, 0).wait_recv()
            a_copy(c, 2).start()
            a_copy(c, 4).start()
            a_copy(c, 1).wait_recv()
            a_copy(c, 5).start()
            if c + 1 < acts:
                act_begin(c + 1)
        if 1 <= c <= acts:
            a_copy(c - 1, 2).wait_recv()
            a_copy(c - 1, 6).start()
    for c in range(n):
        own_copy(c).wait()
        for j in range(half):
            if j:
                z_copy(c, j).wait_send()
            x_copy(c, j).wait()
    for a in range(acts):
        own_act(a).wait()
        for k in range(7):
            a_copy(a, k).wait_send()
            if k >= 3:
                a_copy(a, k).wait_recv()


def run_gather(half, chunks, acts):
    layout, shapes = [], []
    for mine, _, axis in chunks:
        layout.append((axis, mine.shape[axis]))
        shape = list(mine.shape)
        shape[axis] *= 2 * half
        shapes.append(jax.ShapeDtypeStruct(tuple(shape), mine.dtype))
    shapes += [jax.ShapeDtypeStruct((a.shape[0] * 8,) + a.shape[1:], a.dtype) for a in acts]
    n, m = len(chunks), len(acts)
    ins = [c[0] for c in chunks] + [c[1] for c in chunks] + acts
    ins += [flip_blocks(a, a.ndim - 1, 2 * half) for a in acts]
    anywhere = pl.BlockSpec(memory_space=pl.ANY)
    sem = pltpu.SemaphoreType.DMA
    return pl.pallas_call(
        functools.partial(gather_all, half, layout, m),
        out_shape=shapes,
        in_specs=[anywhere] * len(ins),
        out_specs=[anywhere] * len(shapes),
        scratch_shapes=[sem((n, half))] * 4 + [sem((m, 7))] * 2 + [sem((n + m,))],
        compiler_params=pltpu.CompilerParams(collective_id=0, has_side_effects=True),
        name="gather_all",
    )(*ins)


def flat(ref):
    value = ref[...]
    return value.reshape(-1, value.shape[-1])


def put(ref, value):
    ref[...] = value.astype(ref.dtype).reshape(ref.shape)


def blocked(shape, *index):
    return pl.BlockSpec(shape, lambda g: tuple(i(g) if callable(i) else i for i in index))


def step(offset=0):
    return lambda g: g + offset


def backward(half, by_columns, window, *refs):
    def take(count):
        nonlocal refs
        head, refs = refs[:count], refs[count:]
        return head

    cot, normed, packed, hidden, attended, turned = take(6)
    w_project, w_gate_up, w_down, w_output, tables, bias = take(6)
    d_packed, d_att, d_project = take(3)
    stage, x_in, z_out, z_in, mine = take(4), take(4), take(4), take(4), take(4)
    act_away, act_near, core_in, y_out, y_in, far_out, act_far, act_sum = [take(2) for _ in range(8)]
    x_send, x_recv, z_send, z_recv, a_send, a_recv = refs
    greet(group_places(half))

    spots, seqs, piece, _ = cot.shape
    units, heads = hidden.shape[-1], attended.shape[-1]
    groups = stage[0].shape[0]
    per = half // groups
    wide = D // (2 * groups)
    every = lambda ref: pl.BlockSpec(ref.shape, lambda g: (0,) * len(ref.shape))

    left = (cot, cot, normed, normed)
    right = (hidden, attended, d_packed, d_project)

    def product(c, left_ref, right_ref):
        value = dot_rows(flat(left_ref), flat(right_ref))
        return value.T if c < 2 and by_columns else value

    def columns_of(side, g=None):
        first = side * groups + (0 if g is None else g)
        return blocked((spots, seqs, piece, wide), 0, 0, 0, step(first) if g is None else first)

    def x_copy(c, g):
        return send_to(place(1, 0), stage[c].at[g], x_in[c].at[g], x_send.at[c, g], x_recv.at[c, g])

    def z_copy(c, j):
        source = z_out[c].at[j // per]
        if per > 1:
            rows = z_in[c].shape[1]
            source = source.at[pl.ds((j % per) * rows, rows)]
        return send_to(place(2 * j, 0), source, z_in[c].at[j], z_send.at[c, j], z_recv.at[c, j])

    def a_copy(a, s):
        source = (act_away[a], y_out[a], far_out[a])[s]
        target = (core_in[a], y_in[a], act_far[a])[s]
        there = (place(0, 1), place(0, 2), place(2, 0))[s]
        return send_to(there, source, target, a_send.at[a, s], a_recv.at[a, s])

    order = [(c, g) for c in range(4) for g in range(groups - 1, -1, -1)]
    started, served = [0], [0]

    def start_x(up_to):
        while started[0] < min(up_to, len(order)):
            x_copy(*order[started[0]]).start()
            started[0] += 1

    def away_products(chunks):
        def body(*refs):
            count = len(chunks)
            for k, c in enumerate(chunks):
                put(refs[1 + count + k], product(c, refs[0], refs[1 + k]))

        pltpu.emit_pipeline(
            body,
            grid=(groups,),
            in_specs=[columns_of(1)] + [every(right[c]) for c in chunks],
            out_specs=[blocked((1,) + stage[c].shape[1:], step(), 0, 0) for c in chunks],
        )(left[chunks[0]], *[right[c] for c in chunks], *[stage[c] for c in chunks])

    def own_product(c, g):
        out = mine[c] if g == 0 else z_out[c]

        def body(left_ref, right_ref, came_ref, *out_refs):
            total = product(c, left_ref, right_ref) + came_ref[0].astype(jnp.float32)
            for out_ref in out_refs:
                put(out_ref, total)

        outs = ([mine[c]] if g == 0 else []) + ([z_out[c]] if g > 0 or per > 1 else [])
        one = (1,) + stage[c].shape[1:]
        pltpu.emit_pipeline(
            body,
            grid=(1,),
            in_specs=[columns_of(0, g), every(right[c]), blocked(one, g, 0, 0)],
            out_specs=[blocked(one, 0 if out is mine[c] else g, 0, 0) for out in outs],
        )(left[c], right[c], x_in[c], *outs)

    def serve(count):
        for _ in range(count):
            c, g = order[served[0]]
            x_copy(c, g).wait_recv()
            served[0] += 1
            start_x(served[0] + window)
            own_product(c, g)
            for j in range(g * per, (g + 1) * per):
                if j:
                    z_copy(c, j).start()

    def units_step():
        tile = (1, seqs, piece)

        def body(cot_ref, down_ref, output_ref, packed_ref, d_packed_ref, d_att_ref):
            rows = flat(cot_ref)
            d_packed_ref[...] = units_back(rows, down_ref[...], flat(packed_ref)).reshape(d_packed_ref.shape)
            put(d_att_ref, dot_cols(rows, output_ref[...]))

        pltpu.emit_pipeline(
            body,
            grid=(spots,),
            in_specs=[
                blocked(tile + (D,), step(), 0, 0, 0),
                every(w_down),
                every(w_output),
                blocked(tile + (2 * units,), step(), 0, 0, 0),
            ],
            out_specs=[
                blocked(tile + (2 * units,), step(), 0, 0, 0),
                blocked(tile + (heads,), step(), 0, 0, 0),
            ],
        )(cot, w_down, w_output, packed, d_packed, d_att)

    def attention_step(first, count):
        block = lambda width: blocked((spots, 1, piece, width), 0, step(first), 0, 0)
        pltpu.emit_pipeline(
            attention_back,
            grid=(count,),
            in_specs=[block(3 * heads), block(heads), every(tables), every(bias)],
            out_specs=[block(3 * heads)],
        )(turned, d_att, tables, bias, d_project)

    def rows_of(width, core):
        return blocked((spots // 2, seqs, piece, width), core, 0, 0, 0)

    def normed_step(core):
        def body(d_project_ref, d_packed_ref, project_ref, gate_up_ref, out_ref):
            total = dot_cols(flat(d_project_ref), project_ref[...])
            put(out_ref, total + dot_cols(flat(d_packed_ref), gate_up_ref[...]))

        pltpu.emit_pipeline(
            body,
            grid=(D // 256,),
            in_specs=[
                rows_of(3 * heads, core),
                rows_of(2 * units, core),
                blocked((256, 3 * heads), step(), 0),
                blocked((256, 2 * units), step(), 0),
            ],
            out_specs=[blocked((spots // 2, seqs, piece, 256), 0, 0, 0, step())],
        )(d_project, d_packed, w_project, w_gate_up, (act_away if core else act_near)[0])

    def out_step(core):
        def body(attended_ref, hidden_ref, output_ref, down_ref, out_ref):
            total = dot_plain(flat(attended_ref), output_ref[...])
            put(out_ref, total + dot_plain(flat(hidden_ref), down_ref[...]))

        pltpu.emit_pipeline(
            body,
            grid=(D // 256,),
            in_specs=[
                rows_of(heads, core),
                rows_of(units, core),
                blocked((heads, 256), 0, step()),
                blocked((units, 256), 0, step()),
            ],
            out_specs=[blocked((spots // 2, seqs, piece, 256), 0, 0, 0, step())],
        )(attended, hidden, w_output, w_down, (act_away if core else act_near)[1])

    def add_terms(*refs):
        *terms, out_ref = refs
        put(out_ref, sum(flat(term).astype(jnp.float32) for term in terms))

    half_seqs = seqs // 2
    row = lambda *index: blocked((1, 1, piece, D), *index, 0, 0)
    line = lambda index: blocked((1, piece, D), index, 0, 0)

    def core_arrived(a):
        a_copy(a, 0).wait_recv()
        pltpu.emit_pipeline(
            add_terms,
            grid=(seqs,),
            in_specs=[row(1, step()), row(1, step())],
            out_specs=[line(step())],
        )(act_near[a], core_in[a], y_out[a])
        a_copy(a, 1).start()

    def y_arrived(a):
        a_copy(a, 1).wait_recv()
        for first, out in ((half_seqs, far_out[a]), (0, act_sum[a])):
            pltpu.emit_pipeline(
                add_terms,
                grid=(half_seqs,),
                in_specs=[row(0, step(first)), row(0, step(first)), line(step(first))],
                out_specs=[line(step())],
            )(act_near[a], core_in[a], y_in[a], out)
            if first:
                a_copy(a, 2).start()

    away_products((0, 1))
    start_x(window)
    units_step()
    away_products((2,))
    serve(1)
    attention_step(0, seqs // 2)
    serve(1)
    attention_step(seqs // 2, seqs - seqs // 2)
    away_products((3,))
    serve(2)
    normed_step(1)
    a_copy(0, 0).start()
    serve(2)
    normed_step(0)
    core_arrived(0)
    serve(2)
    out_step(1)
    a_copy(1, 0).start()
    out_step(0)
    serve(1)
    core_arrived(1)
    y_arrived(0)
    serve(1)
    y_arrived(1)
    serve(len(order) - served[0])
    for c in range(4):
        for j in range(1, half):
            z_copy(c, j).wait()
        for g in range(groups):
            x_copy(c, g).wait_send()
    for a in range(2):
        for s in range(3):
            a_copy(a, s).wait_send()
        a_copy(a, 2).wait_recv()


def run_backward(half, by_columns, rows, weights, tables, bias, window=3):
    cot, _, packed, hidden, attended, turned = rows
    low, full = jnp.bfloat16, jnp.float32
    spots, seqs, piece, _ = cot.shape
    each = D // (2 * half)
    groups = min(half, 4)
    wide = D // (2 * groups)
    widths = (hidden.shape[-1], attended.shape[-1], packed.shape[-1], turned.shape[-1])
    columns = [by_columns and c < 2 for c in range(4)]
    if by_columns and groups != half:
        columns = [False] * 4

    def shape_of(count, block, kind):
        return [
            jax.ShapeDtypeStruct((count, w, block) if flip else (count, block, w), kind)
            for w, flip in zip(widths, columns)
        ]

    def row_shape(*lead, kind=low):
        return [jax.ShapeDtypeStruct(lead + (piece, D), kind)] * 2

    shapes = [jax.ShapeDtypeStruct(r.shape, low) for r in (packed, attended, turned)]
    shapes += shape_of(groups, wide, low) * 3 + shape_of(half, each, low) + shape_of(1, wide, full)
    shapes += row_shape(spots // 2, seqs) * 3 + row_shape(seqs) * 2 + row_shape(seqs // 2) * 2
    shapes += row_shape(seqs // 2, kind=full)
    anywhere = pl.BlockSpec(memory_space=pl.ANY)
    ins = [*rows, *weights, tables, bias]
    sem = pltpu.SemaphoreType.DMA
    outs = pl.pallas_call(
        functools.partial(backward, half, columns[0], window),
        out_shape=shapes,
        in_specs=[anywhere] * len(ins),
        out_specs=[anywhere] * len(shapes),
        scratch_shapes=[sem((4, groups))] * 2 + [sem((4, half))] * 2 + [sem((2, 3))] * 2,
        compiler_params=pltpu.CompilerParams(
            collective_id=1, has_side_effects=True, vmem_limit_bytes=56 * 1024 * 1024
        ),
        name="backward",
    )(*ins)
    z_in, own = outs[15:19], outs[19:23]
    act_far, act_sum = outs[-4:-2], outs[-2:]
    pairs = []
    for c in range(4):
        came = [z_in[c][j].astype(full) for j in range(half)]
        first = own[c][0] if columns[c] else own[c][0, :each]
        pairs.append((first + sum(came[2::2]), sum(came[1::2])))
    totals = [near + flip_blocks(far.astype(full), 2, 2 * half) for near, far in zip(act_sum, act_far)]
    return pairs, totals


def sum_kernel(rounds, in_ref, out_ref, sent, came, send_sem, recv_sem):
    places = [place(*flips) for flips in rounds]
    greet(places)
    out_ref[...] = in_ref[...]
    for k, there in enumerate(places):
        sent[k] = out_ref[...]
        copy = send_to(there, sent.at[k], came.at[k], send_sem.at[k], recv_sem.at[k])
        copy.start()
        copy.wait()
        out_ref[...] = out_ref[...] + came[k]


def sum_everywhere(value):
    rounds = []
    for axis, size in enumerate((lax.axis_size("dp"), lax.axis_size("tensor"))):
        flip = 1
        while flip < size:
            rounds.append((0, flip) if axis else (flip, 0))
            flip *= 2
    vmem = pl.BlockSpec(memory_space=pltpu.VMEM)
    tile = (8, 128)
    sem = pltpu.SemaphoreType.DMA
    total = pl.pallas_call(
        functools.partial(sum_kernel, rounds),
        out_shape=jax.ShapeDtypeStruct(tile, jnp.float32),
        in_specs=[vmem],
        out_specs=vmem,
        scratch_shapes=[pltpu.VMEM((len(rounds),) + tile, jnp.float32)] * 2 + [sem((len(rounds),))] * 2,
        compiler_params=pltpu.CompilerParams(collective_id=2, has_side_effects=True),
        name="sum_everywhere",
    )(jnp.full(tile, value))
    return total[0, 0]


def dot_plain(a, b):
    return lax.dot_general(a, b, (((1,), (0,)), ((), ())), preferred_element_type=jnp.float32)


def dot_rows(a, b):
    return lax.dot_general(a, b, (((0,), (0,)), ((), ())), preferred_element_type=jnp.float32)


def dot_cols(a, b):
    return lax.dot_general(a, b, (((1,), (1,)), ((), ())), preferred_element_type=jnp.float32)


def turn(values, tables, direction):
    cosine, low_sine, high_sine = tables
    lanes = values.shape[1]
    half_rot = ROT // 2
    moved = pltpu.roll(values, lanes - half_rot, 1) * low_sine + pltpu.roll(values, half_rot, 1) * high_sine
    return values * cosine + direction * moved


def head_probabilities(query, key, bias):
    scores = dot_cols(query, key) * 0.125 + bias
    exponent = jnp.exp(scores - jnp.max(scores, axis=1, keepdims=True))
    return exponent / jnp.sum(exponent, axis=1, keepdims=True)


def attention_fore(projected_ref, tables_ref, bias_ref, turned_ref, attended_ref):
    spots, _, piece, width = projected_ref.shape
    rows, third = spots * piece, width // 3
    tables = [tables_ref[k] for k in range(3)]
    first = lax.broadcasted_iota(jnp.int32, (rows, 128), 1) < HEAD_DIM
    for pair in range(third // 128):
        span = [slice(k * third + pair * 128, k * third + pair * 128 + 128) for k in range(3)]
        query, key, value = [projected_ref[:, 0, :, s].reshape(rows, 128) for s in span]
        query = turn(query, tables, 1.0).astype(jnp.bfloat16)
        key = turn(key, tables, 1.0).astype(jnp.bfloat16)
        value = value.astype(jnp.bfloat16)
        for s, part in zip(span, (query, key, value)):
            turned_ref[:, 0, :, s] = part.reshape(spots, piece, 128)
        none = jnp.zeros_like(query)
        outs = [
            dot_plain(head_probabilities(q, key, bias_ref[...]).astype(jnp.bfloat16), value)
            for q in (jnp.where(first, query, none), jnp.where(first, none, query))
        ]
        attended_ref[:, 0, :, span[0]] = (
            jnp.where(first, outs[0], outs[1]).astype(jnp.bfloat16).reshape(spots, piece, 128)
        )


def attention_back(turned_ref, d_att_ref, tables_ref, bias_ref, d_project_ref):
    spots, _, piece, width = turned_ref.shape
    rows, third = spots * piece, width // 3
    tables = [tables_ref[k] for k in range(3)]
    first = lax.broadcasted_iota(jnp.int32, (rows, 128), 1) < HEAD_DIM
    for pair in range(third // 128):
        span = [slice(k * third + pair * 128, k * third + pair * 128 + 128) for k in range(3)]
        query, key, value = [turned_ref[:, 0, :, s].reshape(rows, 128) for s in span]
        d_att = d_att_ref[:, 0, :, span[0]].reshape(rows, 128)
        none = jnp.zeros_like(query)
        parts = []
        for head in range(2):
            keep = first if head == 0 else jnp.logical_not(first)
            one_query = jnp.where(keep, query, none)
            one_d_att = jnp.where(keep, d_att, none)
            prob = head_probabilities(one_query, key, bias_ref[...])
            d_value = dot_rows(prob.astype(jnp.bfloat16), d_att)
            d_prob = dot_cols(one_d_att, value)
            d_score = (prob * (d_prob - jnp.sum(d_prob * prob, axis=1, keepdims=True))).astype(
                jnp.bfloat16
            )
            parts.append((dot_plain(d_score, key), dot_rows(d_score, query), d_value))
        joined = [jnp.where(first, one, two) for one, two in zip(*parts)]
        done = (turn(0.125 * joined[0], tables, -1.0), turn(0.125 * joined[1], tables, -1.0), joined[2])
        for s, part in zip(span, done):
            d_project_ref[:, 0, :, s] = part.astype(jnp.bfloat16).reshape(spots, piece, 128)


def join_gate_up(packed, whole):
    last = packed[:, 2 * whole :]
    gate = jnp.concatenate([packed[:, :whole], last], axis=1)
    up = jnp.concatenate([packed[:, whole : 2 * whole], pltpu.roll(last, 64, 1)], axis=1)
    return gate, up


def units_fore(normed_ref, weight_ref, packed_ref, hidden_ref):
    packed = dot_plain(normed_ref[...], weight_ref[...])
    packed_ref[...] = packed
    units = hidden_ref.shape[1]
    gate, up = join_gate_up(packed, units - 64)
    hidden_ref[...] = (gate * jax.nn.sigmoid(gate) * up).astype(jnp.bfloat16)[:, :units]


def units_back(cot, down, packed):
    units = down.shape[0]
    whole = units - 64
    d_hid = dot_cols(cot, down).astype(jnp.bfloat16).astype(jnp.float32)
    d_hid = jnp.concatenate([d_hid, jnp.zeros((d_hid.shape[0], 64), jnp.float32)], axis=1)
    gate, up = join_gate_up(packed, whole)
    sigmoid_gate = jax.nn.sigmoid(gate)
    d_gate = d_hid * up * (sigmoid_gate * (1.0 + gate * (1.0 - sigmoid_gate)))
    d_up = d_hid * (gate * sigmoid_gate)
    first = lax.broadcasted_iota(jnp.int32, (gate.shape[0], 128), 1) < 64
    last = jnp.where(first, d_gate[:, whole:], pltpu.roll(d_up[:, whole:], 64, 1))
    parts = [d_gate[:, :whole], d_up[:, :whole], last]
    return jnp.concatenate([part.astype(jnp.bfloat16) for part in parts], axis=1)


def whole_block(shape):
    return pl.BlockSpec(shape, lambda *_: (0,) * len(shape))


KERNEL_PARAMS = pltpu.CompilerParams(vmem_limit_bytes=40 * 1024 * 1024)


def run_attention_fore(projected, tables, bias):
    spots, seqs, piece, width = projected.shape
    block = lambda w: pl.BlockSpec((spots, 1, piece, w), lambda s: (0, s, 0, 0))
    rows = spots * piece
    return pl.pallas_call(
        attention_fore,
        grid=(seqs,),
        in_specs=[block(width), whole_block(tables.shape), whole_block(bias.shape)],
        out_specs=[block(width), block(width // 3)],
        out_shape=[
            jax.ShapeDtypeStruct((spots, seqs, piece, width), jnp.bfloat16),
            jax.ShapeDtypeStruct((spots, seqs, piece, width // 3), jnp.bfloat16),
        ],
        compiler_params=KERNEL_PARAMS,
        cost_estimate=pl.CostEstimate(
            flops=seqs * rows * rows * width * 2, bytes_accessed=seqs * rows * width * 7, transcendentals=0
        ),
        name="attention_fore",
    )(projected, tables, bias)


def row_tile(rows):
    return 256 if rows % 256 == 0 else rows // 8


def run_units_fore(normed, weight):
    rows, units = normed.shape[0], weight.shape[1] // 2
    tile = row_tile(rows)
    block = lambda w: pl.BlockSpec((tile, w), lambda r: (r, 0))
    return pl.pallas_call(
        units_fore,
        grid=(rows // tile,),
        in_specs=[block(D), whole_block(weight.shape)],
        out_specs=[block(2 * units), block(units)],
        out_shape=[
            jax.ShapeDtypeStruct((rows, 2 * units), jnp.float32),
            jax.ShapeDtypeStruct((rows, units), jnp.bfloat16),
        ],
        compiler_params=KERNEL_PARAMS,
        cost_estimate=pl.CostEstimate(
            flops=rows * D * units * 4, bytes_accessed=rows * (D * 2 + units * 10), transcendentals=0
        ),
        name="units_fore",
    )(normed, weight)


def adam_update(weight_old, gradient, moment_old, square_old, factor, rate, decay):
    clipped = gradient * factor
    moment_new = BETA_ONE * moment_old + (1.0 - BETA_ONE) * clipped
    square_new = BETA_TWO * square_old + (1.0 - BETA_TWO) * clipped * clipped
    moment_hat = moment_new / (1.0 - BETA_ONE**STEP)
    square_hat = square_new / (1.0 - BETA_TWO**STEP)
    weight_new = weight_old - rate * (
        moment_hat / (jnp.sqrt(square_hat) + ADAM_EPS) + decay * weight_old
    )
    return (weight_new, moment_new, square_new)


def local(
    tokens,
    cotangent,
    project_weight,
    output_weight,
    gate_up_weight,
    down_weight,
    norm_params,
    first_project,
    first_output,
    first_gate_up,
    first_down,
    first_norm,
    second_project,
    second_output,
    second_gate_up,
    second_down,
    second_norm,
):
    count = lax.axis_size("dp")
    blocks_half = count // 2
    me = lax.axis_index("dp")
    side = (me // 2) % 2
    spot = lax.axis_index("tensor")
    spots = lax.axis_size("tensor")
    micro_count, piece = tokens.shape[0], tokens.shape[1]
    head_cols = project_weight.shape[2] // 2
    unit_cols = gate_up_weight.shape[2] // 2
    whole = unit_cols - 64
    rows_each = project_weight.shape[1]
    seqs = 2 * micro_count
    rows_all = spots * seqs * piece

    def halves(first, second):
        first, second = first.astype(jnp.bfloat16), second.astype(jnp.bfloat16)
        return jnp.where(side == 0, first, second), jnp.where(side == 0, second, first)

    def project_half(s):
        return jnp.concatenate(
            [project_weight[k, :, s * head_cols : (s + 1) * head_cols] for k in range(3)], axis=1
        )

    def unit_spans(s):
        return slice(s * whole, (s + 1) * whole), slice(2 * whole + 64 * s, 2 * whole + 64 * (s + 1))

    def gate_up_half(s):
        wide, narrow = unit_spans(s)
        return jnp.concatenate(
            [gate_up_weight[k, :, span] for span in (wide, narrow) for k in range(2)], axis=1
        )

    def output_half(s):
        return output_weight[s * head_cols : (s + 1) * head_cols]

    def down_half(s):
        return jnp.concatenate([down_weight[span] for span in unit_spans(s)], axis=0)

    by_columns = rows_each % 128 == 0

    norm_low = norm_params.astype(jnp.bfloat16)
    norm_full = gather_small(norm_low).astype(jnp.float32)
    gain, shift = norm_full[0], norm_full[1]

    tok_rows = relative(tokens, 2, me, count).astype(jnp.float32)
    row_mean = jnp.mean(tok_rows, axis=2, keepdims=True)
    centered = tok_rows - row_mean
    row_scale = lax.rsqrt(jnp.mean(centered * centered, axis=2, keepdims=True) + NORM_EPS)
    unit_rows = centered * row_scale
    normed = (unit_rows * gain + shift).astype(jnp.bfloat16)
    cot_low = relative(cotangent, 2, me, count)

    def chunk(half_of, columns):
        pair = halves(half_of(0), half_of(1))
        if columns and not by_columns:
            return (pair[0].T, pair[1].T, 0)
        return (*pair, int(columns))

    gathered = run_gather(
        blocks_half,
        [chunk(project_half, False), chunk(gate_up_half, False), chunk(down_half, True), chunk(output_half, True)],
        [normed, cot_low],
    )
    w_project, w_gate_up, w_down, w_output = gathered[:4]
    if not by_columns:
        w_down, w_output = w_down.T, w_output.T
    all_normed, all_cot = [rows.reshape(rows_all, D) for rows in gathered[4:]]

    order = jnp.array([0, 2, 1, 3])
    positions = ((spot ^ order)[:, None] * piece + jnp.arange(piece)[None, :]).reshape(-1)
    half_rot = ROT // 2
    inverse = 10000.0 ** (-2.0 * jnp.arange(half_rot, dtype=jnp.float32) / ROT)
    angles = positions.astype(jnp.float32)[:, None] * inverse[None, :]
    cosine, sine = jnp.cos(angles), jnp.sin(angles)
    none = jnp.zeros_like(sine)
    rest = jnp.zeros((angles.shape[0], HEAD_DIM - ROT), jnp.float32)
    tables = jnp.stack(
        [
            jnp.tile(jnp.concatenate(parts, axis=1), (1, 2))
            for parts in ((cosine, cosine, rest + 1.0), (-sine, none, rest), (none, sine, rest))
        ]
    )
    bias = jnp.where(positions[:, None] >= positions[None, :], 0.0, MASK_FILL)

    projected = dot_plain(all_normed, w_project).reshape(spots, seqs, piece, 3 * head_cols)
    turned, attended = run_attention_fore(projected, tables, bias)
    attended = attended.reshape(rows_all, head_cols)
    packed, hidden = run_units_fore(all_normed, w_gate_up)

    half_d = D // 2
    row_shape = (spots, seqs, piece, -1)
    rows = [values.reshape(row_shape) for values in (all_cot, all_normed, packed, hidden, attended, turned)]
    (grad_down, grad_output, grad_gate_up, grad_project), (d_normed, summed) = run_backward(
        blocks_half, by_columns, rows, (w_project, w_gate_up, w_down, w_output), tables, bias
    )
    if not by_columns:
        grad_down, grad_output = [tuple(g.T for g in pair) for pair in (grad_down, grad_output)]
    layer_out = from_relative((tok_rows + summed).astype(jnp.bfloat16), 2, me, count)

    d_unit = d_normed * gain
    d_input = row_scale * (
        d_unit
        - jnp.mean(d_unit, axis=2, keepdims=True)
        - unit_rows * jnp.mean(d_unit * unit_rows, axis=2, keepdims=True)
    )
    input_grad = from_relative((cot_low.astype(jnp.float32) + d_input).astype(jnp.bfloat16), 2, me, count)

    grad_norm = jnp.stack(
        [jnp.sum(d_normed * unit_rows, axis=(0, 1)), jnp.sum(d_normed, axis=(0, 1))]
    )
    grad_norm = grad_norm[:, :half_d] + swap(grad_norm[:, half_d:], 1, 0)
    grad_norm = grad_norm.reshape(2, blocks_half, rows_each)
    norm_grad = grad_norm[:, 0]
    for j in range(1, blocks_half):
        norm_grad = norm_grad + swap(grad_norm[:, j], 2 * j, 0)
    norm_grad = norm_grad + swap(norm_grad, 0, 2)
    norm_grad = norm_grad + swap(norm_grad, 0, 1)

    def in_order(pair):
        mine, other = pair
        return jnp.where(side == 0, mine, other), jnp.where(side == 0, other, mine)

    project_pair = in_order(grad_project)
    gate_up_pair = in_order(grad_gate_up)
    down_pair = in_order(grad_down)
    grads = (
        jnp.stack(
            [
                jnp.concatenate([g[:, k * head_cols : (k + 1) * head_cols] for g in project_pair], axis=1)
                for k in range(3)
            ]
        ),
        jnp.concatenate(in_order(grad_output), axis=0),
        jnp.stack(
            [
                jnp.concatenate(
                    [g[:, k * whole : (k + 1) * whole] for g in gate_up_pair]
                    + [g[:, 2 * whole + 64 * k : 2 * whole + 64 * (k + 1)] for g in gate_up_pair],
                    axis=1,
                )
                for k in range(2)
            ]
        ),
        jnp.concatenate([g[:whole] for g in down_pair] + [g[whole:] for g in down_pair], axis=0),
        norm_grad,
    )
    square_local = sum(jnp.sum(g * g) for g in grads[:4]) + jnp.sum(norm_grad * norm_grad) / spots
    norm_total = jnp.sqrt(sum_everywhere(square_local))
    limit = 0.03 * math.sqrt((4 * D * D + 3 * D * FF + 2 * D) * micro_count * count * SEQ)
    factor = jnp.minimum(1.0, limit / (norm_total + 1e-06))
    rates = (
        2.0 / math.sqrt(D),
        2.0 / math.sqrt(D // 32),
        2.0 / math.sqrt(D),
        2.0 / math.sqrt(FF),
        0.5,
    )
    decays = (0.1, 0.1, 0.1, 0.1, 0.0)
    masters = (project_weight, output_weight, gate_up_weight, down_weight, norm_params)
    firsts = (first_project, first_output, first_gate_up, first_down, first_norm)
    seconds = (second_project, second_output, second_gate_up, second_down, second_norm)
    updated = [
        adam_update(*parts) for parts in zip(masters, grads, firsts, seconds, [factor] * 5, rates, decays)
    ]
    return (
        layer_out,
        input_grad,
        *grads,
        norm_total,
        *[u[0] for u in updated],
        *[u[1] for u in updated],
        *[u[2] for u in updated],
    )


def solution(mesh):
    wide = P("dp", "tensor", None)
    stacked = P(None, "dp", "tensor")
    tall = P("tensor", "dp")
    params = (stacked, tall, stacked, tall, P(None, "dp"))
    return jax.shard_map(
        local,
        mesh=mesh,
        in_specs=(wide, wide, *params, *params, *params),
        out_specs=(wide, wide, *params, P(), *params, *params, *params),
        check_vma=False,
    )
```

```python
import functools
import math

import jax
import jax.numpy as jnp
from jax import lax
from jax.experimental import pallas as pl
from jax.experimental.pallas import tpu as pltpu
from jax.sharding import PartitionSpec as P

D = 2048
HEAD_DIM = 64
FF = 5632
SEQ = 320
STEP = 10
ROT = 16

BETA_ONE = 0.9
BETA_TWO = 0.999
ADAM_EPS = 1e-08
NORM_EPS = 1e-05
MASK_FILL = -1e30

BOTH = ("dp", "tensor")
MESH = pl.DeviceIdType.MESH


def swap(values, dp_flip, tensor_flip):
    dp_size, tensor_size = lax.axis_size("dp"), lax.axis_size("tensor")
    pairs = [
        (d * tensor_size + t, (d ^ dp_flip) * tensor_size + (t ^ tensor_flip))
        for d in range(dp_size)
        for t in range(tensor_size)
    ]
    return lax.ppermute(values, BOTH, pairs)


def block_order(count):
    return [2 * j + i for i in range(2) for j in range(count // 2)]


def relative(values, axis, me, count):
    width = values.shape[axis] // count
    return jnp.concatenate(
        [lax.dynamic_slice_in_dim(values, (me ^ r) * width, width, axis) for r in block_order(count)],
        axis=axis,
    )


def from_relative(values, axis, me, count):
    width = values.shape[axis] // count
    places = [((me ^ g) % 2) * (count // 2) + (me ^ g) // 2 for g in range(count)]
    return jnp.concatenate(
        [lax.dynamic_slice_in_dim(values, place * width, width, axis) for place in places],
        axis=axis,
    )


def flip_blocks(values, axis, count):
    width = values.shape[axis] // count
    return jnp.concatenate(
        [lax.slice_in_dim(values, (p ^ 1) * width, ((p ^ 1) + 1) * width, axis=axis) for p in range(count)],
        axis=axis,
    )


def gather_small(block):
    near = [block] + [swap(block, 2 * j, 0) for j in range(1, lax.axis_size("dp") // 2)]
    near = jnp.concatenate(near, axis=1)
    return jnp.concatenate([near, swap(near, 1, 0)], axis=1)


def place(dp_flip, tensor_flip):
    return (lax.axis_index("dp") ^ dp_flip, lax.axis_index("tensor") ^ tensor_flip)


def greet(places):
    barrier = pltpu.get_barrier_semaphore()
    for there in places:
        pl.semaphore_signal(barrier, inc=1, device_id=there, device_id_type=MESH)
    pl.semaphore_wait(barrier, len(places))


def send_to(there, source, target, send_sem, recv_sem):
    return pltpu.make_async_remote_copy(
        src_ref=source,
        dst_ref=target,
        send_sem=send_sem,
        recv_sem=recv_sem,
        device_id=there,
        device_id_type=MESH,
    )


def group_places(half):
    return [place(2 * j, 0) for j in range(1, half)] + [place(1, 0), place(0, 2), place(0, 1)]


def gather_all(half, layout, acts, *refs):
    n = len(layout)
    mine, other = refs[:n], refs[n : 2 * n]
    own_rows = refs[2 * n : 2 * n + acts]
    flipped_rows = refs[2 * n + acts : 2 * n + 2 * acts]
    outs = refs[2 * n + 2 * acts : 3 * n + 2 * acts]
    act_out = refs[3 * n + 2 * acts : 3 * n + 3 * acts]
    z_send, z_recv, x_send, x_recv, a_send, a_recv, own_sem = refs[3 * n + 3 * acts :]
    greet(group_places(half))

    def block(c, p):
        axis, width = layout[c]
        span = pl.ds(p * width, width)
        return outs[c].at[span] if axis == 0 else outs[c].at[:, span]

    def z_copy(c, j):
        source = (other if j % 2 else mine)[c]
        return send_to(place(2 * j, 0), source, block(c, j), z_send.at[c, j], z_recv.at[c, j])

    def x_copy(c, j):
        source = block(c, j) if j else mine[c]
        return send_to(place(1, 0), source, block(c, half + j), x_send.at[c, j], x_recv.at[c, j])

    def own_copy(c):
        return pltpu.make_async_copy(mine[c], block(c, 0), own_sem.at[c])

    def rows(a, index):
        each = act_out[a].shape[0] // 8
        return act_out[a].at[pl.ds(index * each, each)]

    def a_copy(a, k):
        source = (
            flipped_rows[a],
            own_rows[a],
            rows(a, 1),
            own_rows[a],
            rows(a, 1),
            rows(a, 2),
            rows(a, 3),
        )[k]
        there = place(2, 0) if k == 0 else place(0, 2) if k < 3 else place(0, 1)
        return send_to(there, source, rows(a, k + 1), a_send.at[a, k], a_recv.at[a, k])

    def own_act(a):
        return pltpu.make_async_copy(own_rows[a], rows(a, 0), own_sem.at[n + a])

    def act_begin(a):
        for k in (0, 1, 3):
            a_copy(a, k).start()

    far = range(1, half)
    for j in far:
        z_copy(0, j).start()
    for c in range(min(2, n)):
        x_copy(c, 0).start()
    act_begin(0)
    for a in range(acts):
        own_act(a).start()
    for c in range(n):
        own_copy(c).start()
    for c in range(n):
        for j in far:
            z_copy(c, j).wait_recv()
            x_copy(c, j).start()
            if c + 1 < n:
                z_copy(c + 1, j).start()
        if c + 2 < n:
            x_copy(c + 2, 0).start()
        if c < acts:
            a_copy(c, 0).wait_recv()
            a_copy(c, 2).start()
            a_copy(c, 4).start()
            a_copy(c, 1).wait_recv()
            a_copy(c, 5).start()
            if c + 1 < acts:
                act_begin(c + 1)
        if 1 <= c <= acts:
            a_copy(c - 1, 2).wait_recv()
            a_copy(c - 1, 6).start()
    for c in range(n):
        own_copy(c).wait()
        for j in range(half):
            if j:
                z_copy(c, j).wait_send()
            x_copy(c, j).wait()
    for a in range(acts):
        own_act(a).wait()
        for k in range(7):
            a_copy(a, k).wait_send()
            if k >= 3:
                a_copy(a, k).wait_recv()


def run_gather(half, chunks, acts):
    layout, shapes = [], []
    for mine, _, axis in chunks:
        layout.append((axis, mine.shape[axis]))
        shape = list(mine.shape)
        shape[axis] *= 2 * half
        shapes.append(jax.ShapeDtypeStruct(tuple(shape), mine.dtype))
    shapes += [jax.ShapeDtypeStruct((a.shape[0] * 8,) + a.shape[1:], a.dtype) for a in acts]
    n, m = len(chunks), len(acts)
    ins = [c[0] for c in chunks] + [c[1] for c in chunks] + acts
    ins += [flip_blocks(a, a.ndim - 1, 2 * half) for a in acts]
    anywhere = pl.BlockSpec(memory_space=pl.ANY)
    sem = pltpu.SemaphoreType.DMA
    return pl.pallas_call(
        functools.partial(gather_all, half, layout, m),
        out_shape=shapes,
        in_specs=[anywhere] * len(ins),
        out_specs=[anywhere] * len(shapes),
        scratch_shapes=[sem((n, half))] * 4 + [sem((m, 7))] * 2 + [sem((n + m,))],
        compiler_params=pltpu.CompilerParams(collective_id=0, has_side_effects=True),
        name="gather_all",
    )(*ins)


def flat(ref):
    value = ref[...]
    return value.reshape(-1, value.shape[-1])


def put(ref, value):
    ref[...] = value.astype(ref.dtype).reshape(ref.shape)


def blocked(shape, *index):
    return pl.BlockSpec(shape, lambda g: tuple(i(g) if callable(i) else i for i in index))


def step(offset=0):
    return lambda g: g + offset


def backward(half, by_columns, window, *refs):
    def take(count):
        nonlocal refs
        head, refs = refs[:count], refs[count:]
        return head

    cot, packed, hidden, attended, turned = take(5)
    normed_t, attended_t_all, hidden_t_all = take(3)
    w_project, w_gate_up, w_down, w_output, tables, bias = take(6)
    z_in, mine = take(4), take(4)
    act_away, act_near, core_in, y_out, y_in, far_out, act_far, act_sum = [take(2) for _ in range(8)]
    stage, x_in = take(4), take(4)
    d_packed, d_att, d_project, attended_t, hidden_t, normed_block, cot_block = take(7)
    x_send, x_recv, z_send, z_recv, a_send, a_recv, load_sem, block_sem = refs
    greet(group_places(half))

    spots, seqs, piece, _ = cot.shape
    units, heads = hidden.shape[-1], attended.shape[-1]
    groups = stage[0].shape[0]
    per = half // groups
    wide = D // (2 * groups)
    every = lambda ref: pl.BlockSpec(ref.shape, lambda g: (0,) * len(ref.shape))

    whole = (attended_t, hidden_t, d_packed, d_project)

    def product(c, block, whole_ref):
        if c >= 2:
            return dot_plain(block, flat(whole_ref))
        value = dot_plain(whole_ref[...], block)
        return value if by_columns else value.T

    def block_copy(index):
        c, g = order[index]
        span, slot = pl.ds(g * wide, wide), index % 2
        if c >= 2:
            source, target = normed_t.at[span], normed_block.at[slot]
        else:
            source, target = cot.at[:, :, :, span], cot_block.at[slot]
        return pltpu.make_async_copy(source, target, block_sem.at[slot])

    def x_copy(c, g):
        return send_to(place(1, 0), stage[c].at[g], x_in[c].at[g], x_send.at[c, g], x_recv.at[c, g])

    def z_copy(c, j):
        source = x_in[c].at[j // per]
        if per > 1:
            rows = z_in[c].shape[1]
            source = source.at[pl.ds((j % per) * rows, rows)]
        return send_to(place(2 * j, 0), source, z_in[c].at[j], z_send.at[c, j], z_recv.at[c, j])

    def a_copy(a, s):
        source = (act_away[a], y_out[a], far_out[a])[s]
        target = (core_in[a], y_in[a], act_far[a])[s]
        there = (place(0, 1), place(0, 2), place(2, 0))[s]
        return send_to(there, source, target, a_send.at[a, s], a_recv.at[a, s])

    order = [(0, 3), (0, 2), (1, 3), (1, 2), (1, 1), (0, 1)]
    order += [(c, g) for c in (2, 3) for g in (3, 2, 1)] + [(c, 0) for c in (2, 1, 3, 0)]
    started, served, ready = [0], [0], set()

    def start_x():
        while started[0] < min(served[0] + window, len(order)) and order[started[0]][0] in ready:
            x_copy(*order[started[0]]).start()
            started[0] += 1

    def away_products(chunks):
        def body(block_ref, *refs):
            count = len(chunks)
            for k, c in enumerate(chunks):
                put(refs[count + k], product(c, flat(block_ref), refs[k]))

        if chunks[0] >= 2:
            source, block = normed_t, blocked((wide, normed_t.shape[1]), step(groups), 0)
        else:
            source, block = cot, blocked((spots, seqs, piece, wide), 0, 0, 0, step(groups))
        pltpu.emit_pipeline(
            body,
            grid=(groups,),
            in_specs=[block] + [every(whole[c]) for c in chunks],
            out_specs=[blocked((1,) + stage[c].shape[1:], step(), 0, 0) for c in chunks],
        )(source, *[whole[c] for c in chunks], *[stage[c] for c in chunks])
        ready.update(chunks)
        start_x()

    def serve(count):
        for _ in range(count):
            index = served[0]
            c, g = order[index]
            served[0] += 1
            block_copy(index).wait()
            if served[0] < len(order):
                block_copy(served[0]).start()
            x_copy(c, g).wait_recv()
            start_x()
            block = flat((normed_block if c >= 2 else cot_block).at[index % 2])
            total = product(c, block, whole[c]) + x_in[c][g].astype(jnp.float32)
            if g == 0:
                mine[c][0] = total
            if g > 0 or per > 1:
                put(x_in[c].at[g], total)
            for j in range(g * per, (g + 1) * per):
                if j:
                    z_copy(c, j).start()

    def units_step():
        tile = (1, seqs, piece)

        def body(cot_ref, down_ref, output_ref, packed_ref, d_packed_ref, d_att_ref):
            rows = flat(cot_ref)
            d_packed_ref[...] = units_back(rows, down_ref[...], flat(packed_ref)).reshape(d_packed_ref.shape)
            put(d_att_ref, dot_cols(rows, output_ref[...]))

        pltpu.emit_pipeline(
            body,
            grid=(spots,),
            in_specs=[
                blocked(tile + (D,), step(), 0, 0, 0),
                every(w_down),
                every(w_output),
                blocked(tile + (2 * units,), step(), 0, 0, 0),
            ],
            out_specs=[
                blocked(tile + (2 * units,), step(), 0, 0, 0),
                blocked(tile + (heads,), step(), 0, 0, 0),
            ],
        )(cot, w_down, w_output, packed, d_packed, d_att)

    def attention_step(first, count):
        block = lambda width: blocked((spots, 1, piece, width), 0, step(first), 0, 0)
        pltpu.emit_pipeline(
            attention_back,
            grid=(count,),
            in_specs=[block(3 * heads), block(heads), every(tables), every(bias)],
            out_specs=[block(3 * heads)],
        )(turned, d_att, tables, bias, d_project)

    def two_cores(away_ref, near_ref, total):
        middle = total.shape[0] // 2
        put(near_ref, total[:middle])
        put(away_ref, total[middle:])

    core_block = blocked((spots // 2, seqs, piece, 256), 0, 0, 0, step())

    def normed_step():
        def body(d_project_ref, d_packed_ref, project_ref, gate_up_ref, away_ref, near_ref):
            total = dot_cols(flat(d_project_ref), project_ref[...])
            two_cores(away_ref, near_ref, total + dot_cols(flat(d_packed_ref), gate_up_ref[...]))

        pltpu.emit_pipeline(
            body,
            grid=(D // 256,),
            in_specs=[
                every(d_project),
                every(d_packed),
                blocked((256, 3 * heads), step(), 0),
                blocked((256, 2 * units), step(), 0),
            ],
            out_specs=[core_block, core_block],
        )(d_project, d_packed, w_project, w_gate_up, act_away[0], act_near[0])

    def out_step():
        def body(attended_ref, hidden_ref, output_ref, down_ref, away_ref, near_ref):
            total = dot_plain(flat(attended_ref), output_ref[...])
            two_cores(away_ref, near_ref, total + dot_plain(flat(hidden_ref), down_ref[...]))

        pltpu.emit_pipeline(
            body,
            grid=(D // 256,),
            in_specs=[
                every(attended),
                every(hidden),
                blocked((heads, 256), 0, step()),
                blocked((units, 256), 0, step()),
            ],
            out_specs=[core_block, core_block],
        )(attended, hidden, w_output, w_down, act_away[1], act_near[1])

    def add_terms(*refs):
        *terms, out_ref = refs
        put(out_ref, sum(flat(term).astype(jnp.float32) for term in terms))

    half_seqs = seqs // 2

    def core_arrived(a):
        a_copy(a, 0).wait_recv()
        rows = blocked((1, half_seqs, piece, D), 1, step(), 0, 0)
        pltpu.emit_pipeline(
            add_terms,
            grid=(2,),
            in_specs=[rows, rows],
            out_specs=[blocked((half_seqs, piece, D), step(), 0, 0)],
        )(act_near[a], core_in[a], y_out[a])
        a_copy(a, 1).start()

    def y_arrived(a):
        def body(*refs):
            add_terms(*refs[:3], refs[6])
            add_terms(*refs[3:6], refs[7])

        def both(shape, *lead):
            return [blocked(shape, *lead, step(first), 0, 0) for first in (half_seqs, 0)]

        rows, lines = both((1, 1, piece, D), 0), both((1, piece, D))
        a_copy(a, 1).wait_recv()
        pltpu.emit_pipeline(
            body,
            grid=(half_seqs,),
            in_specs=[rows[0], rows[0], lines[0], rows[1], rows[1], lines[1]],
            out_specs=[blocked((1, piece, D), step(), 0, 0)] * 2,
        )(*[act_near[a], core_in[a], y_in[a]] * 2, far_out[a], act_sum[a])
        a_copy(a, 2).start()

    loads = [
        pltpu.make_async_copy(attended_t_all, attended_t, load_sem.at[0]),
        pltpu.make_async_copy(hidden_t_all, hidden_t, load_sem.at[1]),
    ]
    for load in loads:
        load.start()
    block_copy(0).start()
    for load in loads:
        load.wait()
    away_products((0, 1))
    out_step()
    a_copy(1, 0).start()
    serve(2)
    units_step()
    core_arrived(1)
    away_products((2,))
    serve(2)
    attention_step(0, seqs // 2)
    serve(2)
    attention_step(seqs // 2, seqs - seqs // 2)
    away_products((3,))
    serve(1)
    y_arrived(1)
    normed_step()
    a_copy(0, 0).start()
    serve(1)
    core_arrived(0)
    serve(4)
    y_arrived(0)
    serve(len(order) - served[0])
    for c in range(4):
        for j in range(1, half):
            z_copy(c, j).wait()
        for g in range(groups):
            x_copy(c, g).wait_send()
    for a in range(2):
        for s in range(3):
            a_copy(a, s).wait_send()
        a_copy(a, 2).wait_recv()


def run_backward(half, by_columns, rows, transposed, weights, tables, bias, window=3):
    cot, packed, hidden, attended, turned = rows
    low, full = jnp.bfloat16, jnp.float32
    spots, seqs, piece, _ = cot.shape
    each = D // (2 * half)
    groups = min(half, 4)
    wide = D // (2 * groups)
    widths = (attended.shape[-1], hidden.shape[-1], packed.shape[-1], turned.shape[-1])
    columns = [by_columns and groups == half and c < 2 for c in range(4)]

    def shape_of(count, block):
        return [(count, w, block) if flip else (count, block, w) for w, flip in zip(widths, columns)]

    def row_shape(*lead, kind=low):
        return [jax.ShapeDtypeStruct(lead + (piece, D), kind)] * 2

    shapes = [jax.ShapeDtypeStruct(shape, low) for shape in shape_of(half, each)]
    shapes += [jax.ShapeDtypeStruct(shape, full) for shape in shape_of(1, wide)]
    shapes += row_shape(spots // 2, seqs) * 3 + row_shape(seqs) * 2 + row_shape(seqs // 2) * 2
    shapes += row_shape(seqs // 2, kind=full)
    anywhere = pl.BlockSpec(memory_space=pl.ANY)
    vmem = pl.BlockSpec(memory_space=pltpu.VMEM)
    ins = [*rows, *transposed, *weights, tables, bias]
    sem = pltpu.SemaphoreType.DMA
    rows_all = spots * seqs * piece
    scratch = [pltpu.VMEM(shape, low) for shape in shape_of(groups, wide)] * 2
    scratch += [pltpu.VMEM(r.shape, low) for r in (packed, attended, turned)]
    scratch += [pltpu.VMEM(t.shape, low) for t in transposed[1:]]
    scratch += [pltpu.VMEM((2, wide, rows_all), low), pltpu.VMEM((2, spots, seqs, piece, wide), low)]
    scratch += [sem((4, groups))] * 2 + [sem((4, half))] * 2 + [sem((2, 3))] * 2 + [sem((2,))] * 2
    outs = pl.pallas_call(
        functools.partial(backward, half, columns[0], window),
        out_shape=shapes,
        in_specs=[anywhere] * len(ins),
        out_specs=[anywhere] * 4 + [vmem] * 4 + [anywhere] * (len(shapes) - 8),
        scratch_shapes=scratch,
        compiler_params=pltpu.CompilerParams(
            collective_id=1, has_side_effects=True, vmem_limit_bytes=60 * 1024 * 1024
        ),
        name="backward",
    )(*ins)
    z_in, own = outs[:4], outs[4:8]
    act_far, act_sum = outs[-4:-2], outs[-2:]
    pairs = []
    for c in range(4):
        came = [z_in[c][j].astype(full) for j in range(half)]
        first = own[c][0] if columns[c] else own[c][0, :each]
        pairs.append((first + sum(came[2::2]), sum(came[1::2])))
    totals = [near + flip_blocks(far.astype(full), 2, 2 * half) for near, far in zip(act_sum, act_far)]
    return pairs, totals


def sum_kernel(rounds, in_ref, out_ref, sent, came, send_sem, recv_sem):
    places = [place(*flips) for flips in rounds]
    greet(places)
    out_ref[...] = in_ref[...]
    for k, there in enumerate(places):
        sent[k] = out_ref[...]
        copy = send_to(there, sent.at[k], came.at[k], send_sem.at[k], recv_sem.at[k])
        copy.start()
        copy.wait()
        out_ref[...] = out_ref[...] + came[k]


def sum_everywhere(value):
    rounds = []
    for axis, size in enumerate((lax.axis_size("dp"), lax.axis_size("tensor"))):
        flip = 1
        while flip < size:
            rounds.append((0, flip) if axis else (flip, 0))
            flip *= 2
    vmem = pl.BlockSpec(memory_space=pltpu.VMEM)
    tile = (8, 128)
    sem = pltpu.SemaphoreType.DMA
    total = pl.pallas_call(
        functools.partial(sum_kernel, rounds),
        out_shape=jax.ShapeDtypeStruct(tile, jnp.float32),
        in_specs=[vmem],
        out_specs=vmem,
        scratch_shapes=[pltpu.VMEM((len(rounds),) + tile, jnp.float32)] * 2 + [sem((len(rounds),))] * 2,
        compiler_params=pltpu.CompilerParams(collective_id=2, has_side_effects=True),
        name="sum_everywhere",
    )(jnp.full(tile, value))
    return total[0, 0]


def dot_plain(a, b):
    return lax.dot_general(a, b, (((1,), (0,)), ((), ())), preferred_element_type=jnp.float32)


def dot_rows(a, b):
    return lax.dot_general(a, b, (((0,), (0,)), ((), ())), preferred_element_type=jnp.float32)


def dot_cols(a, b):
    return lax.dot_general(a, b, (((1,), (1,)), ((), ())), preferred_element_type=jnp.float32)


def turn(values, tables, direction):
    cosine, low_sine, high_sine = tables
    lanes = values.shape[1]
    half_rot = ROT // 2
    moved = pltpu.roll(values, lanes - half_rot, 1) * low_sine + pltpu.roll(values, half_rot, 1) * high_sine
    return values * cosine + direction * moved


def head_probabilities(query, key, bias):
    scores = dot_cols(query, key) * 0.125 + bias
    exponent = jnp.exp(scores - jnp.max(scores, axis=1, keepdims=True))
    return exponent / jnp.sum(exponent, axis=1, keepdims=True)


def attention_fore(projected_ref, tables_ref, bias_ref, turned_ref, attended_ref):
    spots, _, piece, width = projected_ref.shape
    rows, third = spots * piece, width // 3
    tables = [tables_ref[k] for k in range(3)]
    first = lax.broadcasted_iota(jnp.int32, (rows, 128), 1) < HEAD_DIM
    for pair in range(third // 128):
        span = [slice(k * third + pair * 128, k * third + pair * 128 + 128) for k in range(3)]
        query, key, value = [projected_ref[:, 0, :, s].reshape(rows, 128) for s in span]
        query = turn(query, tables, 1.0).astype(jnp.bfloat16)
        key = turn(key, tables, 1.0).astype(jnp.bfloat16)
        value = value.astype(jnp.bfloat16)
        for s, part in zip(span, (query, key, value)):
            turned_ref[:, 0, :, s] = part.reshape(spots, piece, 128)
        none = jnp.zeros_like(query)
        outs = [
            dot_plain(head_probabilities(q, key, bias_ref[...]).astype(jnp.bfloat16), value)
            for q in (jnp.where(first, query, none), jnp.where(first, none, query))
        ]
        attended_ref[:, 0, :, span[0]] = (
            jnp.where(first, outs[0], outs[1]).astype(jnp.bfloat16).reshape(spots, piece, 128)
        )


def attention_back(turned_ref, d_att_ref, tables_ref, bias_ref, d_project_ref):
    spots, _, piece, width = turned_ref.shape
    rows, third = spots * piece, width // 3
    tables = [tables_ref[k] for k in range(3)]
    first = lax.broadcasted_iota(jnp.int32, (rows, 128), 1) < HEAD_DIM
    for pair in range(third // 128):
        span = [slice(k * third + pair * 128, k * third + pair * 128 + 128) for k in range(3)]
        query, key, value = [turned_ref[:, 0, :, s].reshape(rows, 128) for s in span]
        d_att = d_att_ref[:, 0, :, span[0]].reshape(rows, 128)
        none = jnp.zeros_like(query)
        parts = []
        for head in range(2):
            keep = first if head == 0 else jnp.logical_not(first)
            one_query = jnp.where(keep, query, none)
            one_d_att = jnp.where(keep, d_att, none)
            prob = head_probabilities(one_query, key, bias_ref[...])
            d_value = dot_rows(prob.astype(jnp.bfloat16), d_att)
            d_prob = dot_cols(one_d_att, value)
            d_score = (prob * (d_prob - jnp.sum(d_prob * prob, axis=1, keepdims=True))).astype(
                jnp.bfloat16
            )
            parts.append((dot_plain(d_score, key), dot_rows(d_score, query), d_value))
        joined = [jnp.where(first, one, two) for one, two in zip(*parts)]
        done = (turn(0.125 * joined[0], tables, -1.0), turn(0.125 * joined[1], tables, -1.0), joined[2])
        for s, part in zip(span, done):
            d_project_ref[:, 0, :, s] = part.astype(jnp.bfloat16).reshape(spots, piece, 128)


def join_gate_up(packed, whole):
    last = packed[:, 2 * whole :]
    gate = jnp.concatenate([packed[:, :whole], last], axis=1)
    up = jnp.concatenate([packed[:, whole : 2 * whole], pltpu.roll(last, 64, 1)], axis=1)
    return gate, up


def units_fore(normed_ref, weight_ref, packed_ref, hidden_ref):
    packed = dot_plain(normed_ref[...], weight_ref[...])
    packed_ref[...] = packed
    units = hidden_ref.shape[1]
    gate, up = join_gate_up(packed, units - 64)
    hidden_ref[...] = (gate * jax.nn.sigmoid(gate) * up).astype(jnp.bfloat16)[:, :units]


def units_back(cot, down, packed):
    units = down.shape[0]
    whole = units - 64
    d_hid = dot_cols(cot, down).astype(jnp.bfloat16).astype(jnp.float32)
    d_hid = jnp.concatenate([d_hid, jnp.zeros((d_hid.shape[0], 64), jnp.float32)], axis=1)
    gate, up = join_gate_up(packed, whole)
    sigmoid_gate = jax.nn.sigmoid(gate)
    d_gate = d_hid * up * (sigmoid_gate * (1.0 + gate * (1.0 - sigmoid_gate)))
    d_up = d_hid * (gate * sigmoid_gate)
    first = lax.broadcasted_iota(jnp.int32, (gate.shape[0], 128), 1) < 64
    last = jnp.where(first, d_gate[:, whole:], pltpu.roll(d_up[:, whole:], 64, 1))
    parts = [d_gate[:, :whole], d_up[:, :whole], last]
    return jnp.concatenate([part.astype(jnp.bfloat16) for part in parts], axis=1)


def whole_block(shape):
    return pl.BlockSpec(shape, lambda *_: (0,) * len(shape))


KERNEL_PARAMS = pltpu.CompilerParams(vmem_limit_bytes=40 * 1024 * 1024)


def run_attention_fore(projected, tables, bias):
    spots, seqs, piece, width = projected.shape
    block = lambda w: pl.BlockSpec((spots, 1, piece, w), lambda s: (0, s, 0, 0))
    rows = spots * piece
    return pl.pallas_call(
        attention_fore,
        grid=(seqs,),
        in_specs=[block(width), whole_block(tables.shape), whole_block(bias.shape)],
        out_specs=[block(width), block(width // 3)],
        out_shape=[
            jax.ShapeDtypeStruct((spots, seqs, piece, width), jnp.bfloat16),
            jax.ShapeDtypeStruct((spots, seqs, piece, width // 3), jnp.bfloat16),
        ],
        compiler_params=KERNEL_PARAMS,
        cost_estimate=pl.CostEstimate(
            flops=seqs * rows * rows * width * 2, bytes_accessed=seqs * rows * width * 7, transcendentals=0
        ),
        name="attention_fore",
    )(projected, tables, bias)


def row_tile(rows):
    return 256 if rows % 256 == 0 else rows // 8


def run_units_fore(normed, weight):
    rows, units = normed.shape[0], weight.shape[1] // 2
    tile = row_tile(rows)
    block = lambda w: pl.BlockSpec((tile, w), lambda r: (r, 0))
    return pl.pallas_call(
        units_fore,
        grid=(rows // tile,),
        in_specs=[block(D), whole_block(weight.shape)],
        out_specs=[block(2 * units), block(units)],
        out_shape=[
            jax.ShapeDtypeStruct((rows, 2 * units), jnp.float32),
            jax.ShapeDtypeStruct((rows, units), jnp.bfloat16),
        ],
        compiler_params=KERNEL_PARAMS,
        cost_estimate=pl.CostEstimate(
            flops=rows * D * units * 4, bytes_accessed=rows * (D * 2 + units * 10), transcendentals=0
        ),
        name="units_fore",
    )(normed, weight)


def adam_update(weight_old, gradient, moment_old, square_old, factor, rate, decay):
    clipped = gradient * factor
    moment_new = BETA_ONE * moment_old + (1.0 - BETA_ONE) * clipped
    square_new = BETA_TWO * square_old + (1.0 - BETA_TWO) * clipped * clipped
    moment_hat = moment_new / (1.0 - BETA_ONE**STEP)
    square_hat = square_new / (1.0 - BETA_TWO**STEP)
    weight_new = weight_old - rate * (
        moment_hat / (jnp.sqrt(square_hat) + ADAM_EPS) + decay * weight_old
    )
    return (weight_new, moment_new, square_new)


def local(
    tokens,
    cotangent,
    project_weight,
    output_weight,
    gate_up_weight,
    down_weight,
    norm_params,
    first_project,
    first_output,
    first_gate_up,
    first_down,
    first_norm,
    second_project,
    second_output,
    second_gate_up,
    second_down,
    second_norm,
):
    count = lax.axis_size("dp")
    blocks_half = count // 2
    me = lax.axis_index("dp")
    side = (me // 2) % 2
    spot = lax.axis_index("tensor")
    spots = lax.axis_size("tensor")
    micro_count, piece = tokens.shape[0], tokens.shape[1]
    head_cols = project_weight.shape[2] // 2
    unit_cols = gate_up_weight.shape[2] // 2
    whole = unit_cols - 64
    rows_each = project_weight.shape[1]
    seqs = 2 * micro_count
    rows_all = spots * seqs * piece

    def halves(first, second):
        first, second = first.astype(jnp.bfloat16), second.astype(jnp.bfloat16)
        return jnp.where(side == 0, first, second), jnp.where(side == 0, second, first)

    def project_half(s):
        return jnp.concatenate(
            [project_weight[k, :, s * head_cols : (s + 1) * head_cols] for k in range(3)], axis=1
        )

    def unit_spans(s):
        return slice(s * whole, (s + 1) * whole), slice(2 * whole + 64 * s, 2 * whole + 64 * (s + 1))

    def gate_up_half(s):
        wide, narrow = unit_spans(s)
        return jnp.concatenate(
            [gate_up_weight[k, :, span] for span in (wide, narrow) for k in range(2)], axis=1
        )

    def output_half(s):
        return output_weight[s * head_cols : (s + 1) * head_cols]

    def down_half(s):
        return jnp.concatenate([down_weight[span] for span in unit_spans(s)], axis=0)

    by_columns = rows_each % 128 == 0

    norm_low = norm_params.astype(jnp.bfloat16)
    norm_full = gather_small(norm_low).astype(jnp.float32)
    gain, shift = norm_full[0], norm_full[1]

    tok_rows = relative(tokens, 2, me, count).astype(jnp.float32)
    row_mean = jnp.mean(tok_rows, axis=2, keepdims=True)
    centered = tok_rows - row_mean
    row_scale = lax.rsqrt(jnp.mean(centered * centered, axis=2, keepdims=True) + NORM_EPS)
    unit_rows = centered * row_scale
    normed = (unit_rows * gain + shift).astype(jnp.bfloat16)
    cot_low = relative(cotangent, 2, me, count)

    def chunk(half_of, columns):
        pair = halves(half_of(0), half_of(1))
        if columns and not by_columns:
            return (pair[0].T, pair[1].T, 0)
        return (*pair, int(columns))

    gathered = run_gather(
        blocks_half,
        [chunk(project_half, False), chunk(gate_up_half, False), chunk(down_half, True), chunk(output_half, True)],
        [normed, cot_low],
    )
    w_project, w_gate_up, w_down, w_output = gathered[:4]
    if not by_columns:
        w_down, w_output = w_down.T, w_output.T
    all_normed, all_cot = [rows.reshape(rows_all, D) for rows in gathered[4:]]

    order = jnp.array([0, 2, 1, 3])
    positions = ((spot ^ order)[:, None] * piece + jnp.arange(piece)[None, :]).reshape(-1)
    half_rot = ROT // 2
    inverse = 10000.0 ** (-2.0 * jnp.arange(half_rot, dtype=jnp.float32) / ROT)
    angles = positions.astype(jnp.float32)[:, None] * inverse[None, :]
    cosine, sine = jnp.cos(angles), jnp.sin(angles)
    none = jnp.zeros_like(sine)
    rest = jnp.zeros((angles.shape[0], HEAD_DIM - ROT), jnp.float32)
    tables = jnp.stack(
        [
            jnp.tile(jnp.concatenate(parts, axis=1), (1, 2))
            for parts in ((cosine, cosine, rest + 1.0), (-sine, none, rest), (none, sine, rest))
        ]
    )
    bias = jnp.where(positions[:, None] >= positions[None, :], 0.0, MASK_FILL)

    projected = dot_plain(all_normed, w_project).reshape(spots, seqs, piece, 3 * head_cols)
    turned, attended = run_attention_fore(projected, tables, bias)
    attended = attended.reshape(rows_all, head_cols)
    packed, hidden = run_units_fore(all_normed, w_gate_up)

    half_d = D // 2
    row_shape = (spots, seqs, piece, -1)
    rows = [values.reshape(row_shape) for values in (all_cot, packed, hidden, attended, turned)]
    (grad_output, grad_down, grad_gate_up, grad_project), (d_normed, summed) = run_backward(
        blocks_half,
        by_columns,
        rows,
        (all_normed.T, attended.T, hidden.T),
        (w_project, w_gate_up, w_down, w_output),
        tables,
        bias,
    )
    if not by_columns:
        grad_down, grad_output = [tuple(g.T for g in pair) for pair in (grad_down, grad_output)]
    layer_out = from_relative((tok_rows + summed).astype(jnp.bfloat16), 2, me, count)

    d_unit = d_normed * gain
    d_input = row_scale * (
        d_unit
        - jnp.mean(d_unit, axis=2, keepdims=True)
        - unit_rows * jnp.mean(d_unit * unit_rows, axis=2, keepdims=True)
    )
    input_grad = from_relative((cot_low.astype(jnp.float32) + d_input).astype(jnp.bfloat16), 2, me, count)

    grad_norm = jnp.stack(
        [jnp.sum(d_normed * unit_rows, axis=(0, 1)), jnp.sum(d_normed, axis=(0, 1))]
    )
    grad_norm = grad_norm[:, :half_d] + swap(grad_norm[:, half_d:], 1, 0)
    grad_norm = grad_norm.reshape(2, blocks_half, rows_each)
    norm_grad = grad_norm[:, 0]
    for j in range(1, blocks_half):
        norm_grad = norm_grad + swap(grad_norm[:, j], 2 * j, 0)
    norm_grad = norm_grad + swap(norm_grad, 0, 2)
    norm_grad = norm_grad + swap(norm_grad, 0, 1)

    def in_order(pair):
        mine, other = pair
        return jnp.where(side == 0, mine, other), jnp.where(side == 0, other, mine)

    project_pair = in_order(grad_project)
    gate_up_pair = in_order(grad_gate_up)
    down_pair = in_order(grad_down)
    grads = (
        jnp.stack(
            [
                jnp.concatenate([g[:, k * head_cols : (k + 1) * head_cols] for g in project_pair], axis=1)
                for k in range(3)
            ]
        ),
        jnp.concatenate(in_order(grad_output), axis=0),
        jnp.stack(
            [
                jnp.concatenate(
                    [g[:, k * whole : (k + 1) * whole] for g in gate_up_pair]
                    + [g[:, 2 * whole + 64 * k : 2 * whole + 64 * (k + 1)] for g in gate_up_pair],
                    axis=1,
                )
                for k in range(2)
            ]
        ),
        jnp.concatenate([g[:whole] for g in down_pair] + [g[whole:] for g in down_pair], axis=0),
        norm_grad,
    )
    square_local = sum(jnp.sum(g * g) for g in grads[:4]) + jnp.sum(norm_grad * norm_grad) / spots
    norm_total = jnp.sqrt(sum_everywhere(square_local))
    limit = 0.03 * math.sqrt((4 * D * D + 3 * D * FF + 2 * D) * micro_count * count * SEQ)
    factor = jnp.minimum(1.0, limit / (norm_total + 1e-06))
    rates = (
        2.0 / math.sqrt(D),
        2.0 / math.sqrt(D // 32),
        2.0 / math.sqrt(D),
        2.0 / math.sqrt(FF),
        0.5,
    )
    decays = (0.1, 0.1, 0.1, 0.1, 0.0)
    masters = (project_weight, output_weight, gate_up_weight, down_weight, norm_params)
    firsts = (first_project, first_output, first_gate_up, first_down, first_norm)
    seconds = (second_project, second_output, second_gate_up, second_down, second_norm)
    updated = [
        adam_update(*parts) for parts in zip(masters, grads, firsts, seconds, [factor] * 5, rates, decays)
    ]
    return (
        layer_out,
        input_grad,
        *grads,
        norm_total,
        *[u[0] for u in updated],
        *[u[1] for u in updated],
        *[u[2] for u in updated],
    )


def solution(mesh):
    wide = P("dp", "tensor", None)
    stacked = P(None, "dp", "tensor")
    tall = P("tensor", "dp")
    params = (stacked, tall, stacked, tall, P(None, "dp"))
    return jax.shard_map(
        local,
        mesh=mesh,
        in_specs=(wide, wide, *params, *params, *params),
        out_specs=(wide, wide, *params, P(), *params, *params, *params),
        check_vma=False,
    )
```

```python
import functools
import math

import jax
import jax.numpy as jnp
from jax import lax
from jax.experimental import pallas as pl
from jax.experimental.pallas import tpu as pltpu
from jax.sharding import PartitionSpec as P

D = 2048
HEAD_DIM = 64
FF = 5632
SEQ = 320
STEP = 10
ROT = 16

BETA_ONE = 0.9
BETA_TWO = 0.999
ADAM_EPS = 1e-08
NORM_EPS = 1e-05
MASK_FILL = -1e30

BOTH = ("dp", "tensor")
MESH = pl.DeviceIdType.MESH


def swap(values, dp_flip, tensor_flip):
    dp_size, tensor_size = lax.axis_size("dp"), lax.axis_size("tensor")
    pairs = [
        (d * tensor_size + t, (d ^ dp_flip) * tensor_size + (t ^ tensor_flip))
        for d in range(dp_size)
        for t in range(tensor_size)
    ]
    return lax.ppermute(values, BOTH, pairs)


def block_order(count):
    return [2 * j + i for i in range(2) for j in range(count // 2)]


def relative(values, axis, me, count):
    width = values.shape[axis] // count
    return jnp.concatenate(
        [lax.dynamic_slice_in_dim(values, (me ^ r) * width, width, axis) for r in block_order(count)],
        axis=axis,
    )


def from_relative(values, axis, me, count):
    width = values.shape[axis] // count
    places = [((me ^ g) % 2) * (count // 2) + (me ^ g) // 2 for g in range(count)]
    return jnp.concatenate(
        [lax.dynamic_slice_in_dim(values, place * width, width, axis) for place in places],
        axis=axis,
    )


def flip_blocks(values, axis, count):
    width = values.shape[axis] // count
    return jnp.concatenate(
        [lax.slice_in_dim(values, (p ^ 1) * width, ((p ^ 1) + 1) * width, axis=axis) for p in range(count)],
        axis=axis,
    )


def gather_small(block):
    near = [block] + [swap(block, 2 * j, 0) for j in range(1, lax.axis_size("dp") // 2)]
    near = jnp.concatenate(near, axis=1)
    return jnp.concatenate([near, swap(near, 1, 0)], axis=1)


def place(dp_flip, tensor_flip):
    return (lax.axis_index("dp") ^ dp_flip, lax.axis_index("tensor") ^ tensor_flip)


def greet(places):
    barrier = pltpu.get_barrier_semaphore()
    for there in places:
        pl.semaphore_signal(barrier, inc=1, device_id=there, device_id_type=MESH)
    pl.semaphore_wait(barrier, len(places))


def send_to(there, source, target, send_sem, recv_sem):
    return pltpu.make_async_remote_copy(
        src_ref=source,
        dst_ref=target,
        send_sem=send_sem,
        recv_sem=recv_sem,
        device_id=there,
        device_id_type=MESH,
    )


def group_places(half):
    return [place(2 * j, 0) for j in range(1, half)] + [place(1, 0), place(0, 2), place(0, 1)]


def gather_all(half, layout, acts, *refs):
    n = len(layout)
    mine, other = refs[:n], refs[n : 2 * n]
    own_rows = refs[2 * n : 2 * n + acts]
    flipped_rows = refs[2 * n + acts : 2 * n + 2 * acts]
    outs = refs[2 * n + 2 * acts : 3 * n + 2 * acts]
    act_out = refs[3 * n + 2 * acts : 3 * n + 3 * acts]
    z_send, z_recv, x_send, x_recv, a_send, a_recv, own_sem = refs[3 * n + 3 * acts :]
    greet(group_places(half))

    def block(c, p):
        axis, width = layout[c]
        span = pl.ds(p * width, width)
        return outs[c].at[span] if axis == 0 else outs[c].at[:, span]

    def z_copy(c, j):
        source = (other if j % 2 else mine)[c]
        return send_to(place(2 * j, 0), source, block(c, j), z_send.at[c, j], z_recv.at[c, j])

    def x_copy(c, j):
        source = block(c, j) if j else mine[c]
        return send_to(place(1, 0), source, block(c, half + j), x_send.at[c, j], x_recv.at[c, j])

    def own_copy(c):
        return pltpu.make_async_copy(mine[c], block(c, 0), own_sem.at[c])

    def rows(a, index):
        each = act_out[a].shape[0] // 8
        return act_out[a].at[pl.ds(index * each, each)]

    def a_copy(a, k):
        source = (
            flipped_rows[a],
            own_rows[a],
            rows(a, 1),
            own_rows[a],
            rows(a, 1),
            rows(a, 2),
            rows(a, 3),
        )[k]
        there = place(2, 0) if k == 0 else place(0, 2) if k < 3 else place(0, 1)
        return send_to(there, source, rows(a, k + 1), a_send.at[a, k], a_recv.at[a, k])

    def own_act(a):
        return pltpu.make_async_copy(own_rows[a], rows(a, 0), own_sem.at[n + a])

    def act_begin(a):
        for k in (0, 1, 3):
            a_copy(a, k).start()

    far = range(1, half)
    for j in far:
        z_copy(0, j).start()
    for c in range(min(2, n)):
        x_copy(c, 0).start()
    act_begin(0)
    for a in range(acts):
        own_act(a).start()
    for c in range(n):
        own_copy(c).start()
    for c in range(n):
        for j in far:
            z_copy(c, j).wait_recv()
            x_copy(c, j).start()
            if c + 1 < n:
                z_copy(c + 1, j).start()
        if c + 2 < n:
            x_copy(c + 2, 0).start()
        if c < acts:
            a_copy(c, 0).wait_recv()
            a_copy(c, 2).start()
            a_copy(c, 4).start()
            a_copy(c, 1).wait_recv()
            a_copy(c, 5).start()
            if c + 1 < acts:
                act_begin(c + 1)
        if 1 <= c <= acts:
            a_copy(c - 1, 2).wait_recv()
            a_copy(c - 1, 6).start()
    for c in range(n):
        own_copy(c).wait()
        for j in range(half):
            if j:
                z_copy(c, j).wait_send()
            x_copy(c, j).wait()
    for a in range(acts):
        own_act(a).wait()
        for k in range(7):
            a_copy(a, k).wait_send()
            if k >= 3:
                a_copy(a, k).wait_recv()


def run_gather(half, chunks, acts):
    layout, shapes = [], []
    for mine, _, axis in chunks:
        layout.append((axis, mine.shape[axis]))
        shape = list(mine.shape)
        shape[axis] *= 2 * half
        shapes.append(jax.ShapeDtypeStruct(tuple(shape), mine.dtype))
    shapes += [jax.ShapeDtypeStruct((a.shape[0] * 8,) + a.shape[1:], a.dtype) for a in acts]
    n, m = len(chunks), len(acts)
    ins = [c[0] for c in chunks] + [c[1] for c in chunks] + acts
    ins += [flip_blocks(a, a.ndim - 1, 2 * half) for a in acts]
    anywhere = pl.BlockSpec(memory_space=pl.ANY)
    sem = pltpu.SemaphoreType.DMA
    return pl.pallas_call(
        functools.partial(gather_all, half, layout, m),
        out_shape=shapes,
        in_specs=[anywhere] * len(ins),
        out_specs=[anywhere] * len(shapes),
        scratch_shapes=[sem((n, half))] * 4 + [sem((m, 7))] * 2 + [sem((n + m,))],
        compiler_params=pltpu.CompilerParams(collective_id=0, has_side_effects=True),
        name="gather_all",
    )(*ins)


def flat(ref):
    value = ref[...]
    return value.reshape(-1, value.shape[-1])


def put(ref, value):
    ref[...] = value.astype(ref.dtype).reshape(ref.shape)


def blocked(shape, *index):
    return pl.BlockSpec(shape, lambda g: tuple(i(g) if callable(i) else i for i in index))


def step(offset=0):
    return lambda g: g + offset


def backward(half, by_columns, window, *refs):
    def take(count):
        nonlocal refs
        head, refs = refs[:count], refs[count:]
        return head

    cot, packed, hidden, attended, turned = take(5)
    normed_t, attended_t_all, hidden_t_all = take(3)
    w_project, w_gate_up, w_down, w_output, tables, bias = take(6)
    z_in, mine = take(4), take(4)
    act_away, act_near, core_in, y_out, y_in, far_out, act_far, act_sum = [take(2) for _ in range(8)]
    stage, x_in = take(4), take(4)
    d_packed, d_att, d_project, attended_t, hidden_t, normed_block, cot_block = take(7)
    x_send, x_recv, z_send, z_recv, a_send, a_recv, load_sem, block_sem = refs
    greet(group_places(half))

    spots, seqs, piece, _ = cot.shape
    units, heads = hidden.shape[-1], attended.shape[-1]
    groups = stage[0].shape[0]
    per = half // groups
    wide = D // (2 * groups)
    every = lambda ref: pl.BlockSpec(ref.shape, lambda g: (0,) * len(ref.shape))

    whole = (attended_t, hidden_t, d_packed, d_project)

    def product(c, block, whole_ref):
        if c >= 2:
            return dot_plain(block, flat(whole_ref))
        value = dot_plain(whole_ref[...], block)
        return value if by_columns else value.T

    def block_copy(index):
        c, g = order[index]
        span, slot = pl.ds(g * wide, wide), index % 2
        if c >= 2:
            source, target = normed_t.at[span], normed_block.at[slot]
        else:
            source, target = cot.at[:, :, :, span], cot_block.at[slot]
        return pltpu.make_async_copy(source, target, block_sem.at[slot])

    def x_copy(c, g):
        return send_to(place(1, 0), stage[c].at[g], x_in[c].at[g], x_send.at[c, g], x_recv.at[c, g])

    def z_copy(c, j):
        source = x_in[c].at[j // per]
        if per > 1:
            rows = z_in[c].shape[1]
            source = source.at[pl.ds((j % per) * rows, rows)]
        return send_to(place(2 * j, 0), source, z_in[c].at[j], z_send.at[c, j], z_recv.at[c, j])

    def a_copy(a, s):
        source = (act_away[a], y_out[a], far_out[a])[s]
        target = (core_in[a], y_in[a], act_far[a])[s]
        there = (place(0, 1), place(0, 2), place(2, 0))[s]
        return send_to(there, source, target, a_send.at[a, s], a_recv.at[a, s])

    order = [(0, 3), (0, 2), (1, 3), (1, 2), (1, 1), (0, 1)]
    order += [(c, g) for c in (2, 3) for g in (3, 2, 1)] + [(c, 0) for c in (2, 1, 3, 0)]
    started, served, ready = [0], [0], set()

    def start_x():
        while started[0] < min(served[0] + window, len(order)) and order[started[0]][0] in ready:
            x_copy(*order[started[0]]).start()
            started[0] += 1

    def away_products(chunks):
        def body(block_ref, *refs):
            count = len(chunks)
            for k, c in enumerate(chunks):
                put(refs[count + k], product(c, flat(block_ref), refs[k]))

        if chunks[0] >= 2:
            source, block = normed_t, blocked((wide, normed_t.shape[1]), step(groups), 0)
        else:
            source, block = cot, blocked((spots, seqs, piece, wide), 0, 0, 0, step(groups))
        pltpu.emit_pipeline(
            body,
            grid=(groups,),
            in_specs=[block] + [every(whole[c]) for c in chunks],
            out_specs=[blocked((1,) + stage[c].shape[1:], step(), 0, 0) for c in chunks],
        )(source, *[whole[c] for c in chunks], *[stage[c] for c in chunks])
        ready.update(chunks)
        start_x()

    def serve(count):
        for _ in range(count):
            index = served[0]
            c, g = order[index]
            served[0] += 1
            block_copy(index).wait()
            if served[0] < len(order):
                block_copy(served[0]).start()
            x_copy(c, g).wait_recv()
            start_x()
            block = flat((normed_block if c >= 2 else cot_block).at[index % 2])
            total = product(c, block, whole[c]) + x_in[c][g].astype(jnp.float32)
            if g == 0:
                mine[c][0] = total
            if g > 0 or per > 1:
                put(x_in[c].at[g], total)
            for j in range(g * per, (g + 1) * per):
                if j:
                    z_copy(c, j).start()

    def units_step():
        tile = (1, seqs, piece)

        def body(cot_ref, down_ref, output_ref, packed_ref, d_packed_ref, d_att_ref):
            rows = flat(cot_ref)
            d_packed_ref[...] = units_back(rows, down_ref[...], flat(packed_ref)).reshape(d_packed_ref.shape)
            put(d_att_ref, dot_cols(rows, output_ref[...]))

        pltpu.emit_pipeline(
            body,
            grid=(spots,),
            in_specs=[
                blocked(tile + (D,), step(), 0, 0, 0),
                every(w_down),
                every(w_output),
                blocked(tile + (2 * units,), step(), 0, 0, 0),
            ],
            out_specs=[
                blocked(tile + (2 * units,), step(), 0, 0, 0),
                blocked(tile + (heads,), step(), 0, 0, 0),
            ],
        )(cot, w_down, w_output, packed, d_packed, d_att)

    def attention_step(first, count):
        block = lambda width: blocked((spots, 1, piece, width), 0, step(first), 0, 0)
        pltpu.emit_pipeline(
            attention_back,
            grid=(count,),
            in_specs=[block(3 * heads), block(heads), every(tables), every(bias)],
            out_specs=[block(3 * heads)],
        )(turned, d_att, tables, bias, d_project)

    def two_cores(away_ref, near_ref, total):
        middle = total.shape[0] // 2
        put(near_ref, total[:middle])
        put(away_ref, total[middle:])

    core_block = blocked((spots // 2, seqs, piece, 256), 0, 0, 0, step())

    def normed_step():
        def body(d_project_ref, d_packed_ref, project_ref, gate_up_ref, away_ref, near_ref):
            total = dot_cols(flat(d_project_ref), project_ref[...])
            two_cores(away_ref, near_ref, total + dot_cols(flat(d_packed_ref), gate_up_ref[...]))

        pltpu.emit_pipeline(
            body,
            grid=(D // 256,),
            in_specs=[
                every(d_project),
                every(d_packed),
                blocked((256, 3 * heads), step(), 0),
                blocked((256, 2 * units), step(), 0),
            ],
            out_specs=[core_block, core_block],
        )(d_project, d_packed, w_project, w_gate_up, act_away[0], act_near[0])

    def out_step():
        def body(attended_ref, hidden_ref, output_ref, down_ref, away_ref, near_ref):
            total = dot_plain(flat(attended_ref), output_ref[...])
            two_cores(away_ref, near_ref, total + dot_plain(flat(hidden_ref), down_ref[...]))

        pltpu.emit_pipeline(
            body,
            grid=(D // 256,),
            in_specs=[
                every(attended),
                every(hidden),
                blocked((heads, 256), 0, step()),
                blocked((units, 256), 0, step()),
            ],
            out_specs=[core_block, core_block],
        )(attended, hidden, w_output, w_down, act_away[1], act_near[1])

    def add_terms(*refs):
        *terms, out_ref = refs
        put(out_ref, sum(flat(term).astype(jnp.float32) for term in terms))

    half_seqs = seqs // 2

    def core_arrived(a):
        a_copy(a, 0).wait_recv()
        rows = blocked((1, half_seqs, piece, D), 1, step(), 0, 0)
        pltpu.emit_pipeline(
            add_terms,
            grid=(2,),
            in_specs=[rows, rows],
            out_specs=[blocked((half_seqs, piece, D), step(), 0, 0)],
        )(act_near[a], core_in[a], y_out[a])
        a_copy(a, 1).start()

    def y_arrived(a):
        def body(*refs):
            add_terms(*refs[:3], refs[6])
            add_terms(*refs[3:6], refs[7])

        def both(shape, *lead):
            return [blocked(shape, *lead, step(first), 0, 0) for first in (half_seqs, 0)]

        rows, lines = both((1, 1, piece, D), 0), both((1, piece, D))
        a_copy(a, 1).wait_recv()
        pltpu.emit_pipeline(
            body,
            grid=(half_seqs,),
            in_specs=[rows[0], rows[0], lines[0], rows[1], rows[1], lines[1]],
            out_specs=[blocked((1, piece, D), step(), 0, 0)] * 2,
        )(*[act_near[a], core_in[a], y_in[a]] * 2, far_out[a], act_sum[a])
        a_copy(a, 2).start()

    loads = [
        pltpu.make_async_copy(attended_t_all, attended_t, load_sem.at[0]),
        pltpu.make_async_copy(hidden_t_all, hidden_t, load_sem.at[1]),
    ]
    for load in loads:
        load.start()
    block_copy(0).start()
    for load in loads:
        load.wait()
    away_products((0, 1))
    out_step()
    a_copy(1, 0).start()
    serve(2)
    units_step()
    core_arrived(1)
    away_products((2,))
    serve(2)
    attention_step(0, seqs // 2)
    serve(2)
    attention_step(seqs // 2, seqs - seqs // 2)
    away_products((3,))
    serve(1)
    y_arrived(1)
    normed_step()
    a_copy(0, 0).start()
    serve(1)
    core_arrived(0)
    serve(4)
    y_arrived(0)
    serve(len(order) - served[0])
    for c in range(4):
        for j in range(1, half):
            z_copy(c, j).wait()
        for g in range(groups):
            x_copy(c, g).wait_send()
    for a in range(2):
        for s in range(3):
            a_copy(a, s).wait_send()
        a_copy(a, 2).wait_recv()


def run_backward(half, by_columns, rows, transposed, weights, tables, bias, window=3):
    cot, packed, hidden, attended, turned = rows
    low, full = jnp.bfloat16, jnp.float32
    spots, seqs, piece, _ = cot.shape
    each = D // (2 * half)
    groups = min(half, 4)
    wide = D // (2 * groups)
    widths = (attended.shape[-1], hidden.shape[-1], packed.shape[-1], turned.shape[-1])
    columns = [by_columns and groups == half and c < 2 for c in range(4)]

    def shape_of(count, block):
        return [(count, w, block) if flip else (count, block, w) for w, flip in zip(widths, columns)]

    def row_shape(*lead, kind=low):
        return [jax.ShapeDtypeStruct(lead + (piece, D), kind)] * 2

    shapes = [jax.ShapeDtypeStruct(shape, low) for shape in shape_of(half, each)]
    shapes += [jax.ShapeDtypeStruct(shape, full) for shape in shape_of(1, wide)]
    shapes += row_shape(spots // 2, seqs) * 3 + row_shape(seqs) * 2 + row_shape(seqs // 2) * 2
    shapes += row_shape(seqs // 2, kind=full)
    anywhere = pl.BlockSpec(memory_space=pl.ANY)
    vmem = pl.BlockSpec(memory_space=pltpu.VMEM)
    ins = [*rows, *transposed, *weights, tables, bias]
    sem = pltpu.SemaphoreType.DMA
    rows_all = spots * seqs * piece
    scratch = [pltpu.VMEM(shape, low) for shape in shape_of(groups, wide)] * 2
    scratch += [pltpu.VMEM(r.shape, low) for r in (packed, attended, turned)]
    scratch += [pltpu.VMEM(t.shape, low) for t in transposed[1:]]
    scratch += [pltpu.VMEM((2, wide, rows_all), low), pltpu.VMEM((2, spots, seqs, piece, wide), low)]
    scratch += [sem((4, groups))] * 2 + [sem((4, half))] * 2 + [sem((2, 3))] * 2 + [sem((2,))] * 2
    outs = pl.pallas_call(
        functools.partial(backward, half, columns[0], window),
        out_shape=shapes,
        in_specs=[anywhere] * len(ins),
        out_specs=[anywhere] * 4 + [vmem] * 4 + [anywhere] * (len(shapes) - 8),
        scratch_shapes=scratch,
        compiler_params=pltpu.CompilerParams(
            collective_id=1, has_side_effects=True, vmem_limit_bytes=60 * 1024 * 1024
        ),
        name="backward",
    )(*ins)
    pairs = []
    for c in range(4):
        own = outs[4 + c][0] if columns[c] else outs[4 + c][0, :each]
        pairs.append((own, outs[c]))
    return pairs, outs[-4:]


def flip_lanes(values, width):
    lanes = values.shape[1]
    even = (lax.broadcasted_iota(jnp.int32, values.shape, 1) // width) % 2 == 0
    return jnp.where(even, pltpu.roll(values, lanes - width, 1), pltpu.roll(values, width, 1))


def norm_rows(tok_rows):
    centered = tok_rows - jnp.mean(tok_rows, axis=1, keepdims=True)
    row_scale = lax.rsqrt(jnp.mean(centered * centered, axis=1, keepdims=True) + NORM_EPS)
    return centered * row_scale, row_scale


def finish_rows(each, in_place, far_ref, far_out_ref, sum_ref, sum_out_ref, tok_ref, cot_ref, gain_ref, out_ref, input_ref, grad_ref):
    d_normed = flat(sum_ref) + flip_lanes(flat(far_ref).astype(jnp.float32), each)
    summed = flat(sum_out_ref) + flip_lanes(flat(far_out_ref).astype(jnp.float32), each)
    tok_rows, cot_rows = flat(tok_ref).astype(jnp.float32), flat(cot_ref).astype(jnp.float32)
    unit_rows, row_scale = norm_rows(tok_rows)
    d_unit = d_normed * gain_ref[0:1]
    d_input = row_scale * (
        d_unit
        - jnp.mean(d_unit, axis=1, keepdims=True)
        - unit_rows * jnp.mean(d_unit * unit_rows, axis=1, keepdims=True)
    )
    me = lax.axis_index("dp")
    for ref, value in ((out_ref, tok_rows + summed), (input_ref, cot_rows + d_input)):
        value = value.astype(jnp.bfloat16)
        if in_place:
            for p, r in enumerate(block_order(D // each)):
                span = pl.ds(pl.multiple_of((me ^ r) * each, each), each)
                ref[0, :, span] = value[:, p * each : (p + 1) * each]
        else:
            ref[0] = value
    share = jnp.concatenate(
        [
            jnp.sum(d_normed * unit_rows, axis=0, keepdims=True),
            jnp.sum(d_normed, axis=0, keepdims=True),
            jnp.zeros((6, D), jnp.float32),
        ],
        axis=0,
    )

    @pl.when(pl.program_id(0) == 0)
    def _():
        grad_ref[...] = share

    @pl.when(pl.program_id(0) > 0)
    def _():
        grad_ref[...] = grad_ref[...] + share


def run_finish_rows(each, totals, tokens, cot, gain):
    in_place = each % 128 == 0
    count, piece, _ = tokens.shape
    block = pl.BlockSpec((1, piece, D), lambda s: (s, 0, 0))
    fixed = pl.BlockSpec((8, D), lambda s: (0, 0))
    rows = jax.ShapeDtypeStruct(tokens.shape, jnp.bfloat16)
    return pl.pallas_call(
        functools.partial(finish_rows, each, in_place),
        grid=(count,),
        in_specs=[block] * 6 + [fixed],
        out_specs=[block, block, fixed],
        out_shape=[rows, rows, jax.ShapeDtypeStruct((8, D), jnp.float32)],
        compiler_params=KERNEL_PARAMS,
        name="finish_rows",
    )(*totals, tokens, cot, gain)


def join_grads(half, spans, *refs):
    own, came = refs[0:8:2], refs[1:8:2]
    output_ref, down_ref, gate_up_ref, project_ref, square_ref = refs[8:]
    side = (lax.axis_index("dp") // 2) % 2
    heads, whole = spans
    squares = jnp.float32(0.0)

    def halves(c, rows, columns):
        nonlocal squares
        pick = lambda j: came[c][j, rows, columns].astype(jnp.float32)
        mine = own[c][rows, columns] + sum(pick(j) for j in range(2, half, 2))
        other = sum(pick(j) for j in range(1, half, 2))
        squares = squares + jnp.sum(mine * mine) + jnp.sum(other * other)
        return mine, other

    def places(width, start=0):
        return [pl.ds(start + pl.multiple_of(s * width, width), width) for s in (side, 1 - side)]

    every = slice(None)
    for value, span in zip(halves(0, every, every), places(heads)):
        output_ref[span] = value
    for value, span in zip(halves(1, slice(0, whole), every), places(whole)):
        down_ref[span] = value
    for value, span in zip(halves(1, slice(whole, whole + 64), every), places(64, 2 * whole)):
        down_ref[span] = value
    for k in range(3):
        for value, span in zip(halves(3, every, slice(k * heads, (k + 1) * heads)), places(heads)):
            project_ref[k, :, span] = value
    for k in range(2):
        for value, span in zip(halves(2, every, slice(k * whole, (k + 1) * whole)), places(whole)):
            gate_up_ref[k, :, span] = value
    mine, other = halves(2, every, slice(2 * whole, 2 * whole + 128))
    zero, one = jnp.where(side == 0, mine, other), jnp.where(side == 0, other, mine)
    first = lax.broadcasted_iota(jnp.int32, zero.shape, 1) < 64
    gate_up_ref[0, :, 2 * whole :] = jnp.where(first, zero, pltpu.roll(one, 64, 1))
    gate_up_ref[1, :, 2 * whole :] = jnp.where(first, pltpu.roll(zero, 64, 1), one)
    square_ref[...] = jnp.full(square_ref.shape, squares)


def run_join_grads(half, pairs, shapes, spans):
    vmem = pl.BlockSpec(memory_space=pltpu.VMEM)
    return pl.pallas_call(
        functools.partial(join_grads, half, spans),
        in_specs=[vmem] * 8,
        out_specs=[vmem] * 5,
        out_shape=[jax.ShapeDtypeStruct(shape, jnp.float32) for shape in shapes + [(8, 128)]],
        compiler_params=pltpu.CompilerParams(vmem_limit_bytes=48 * 1024 * 1024),
        name="join_grads",
    )(*[part for pair in pairs for part in pair])


def sum_kernel(rounds, half, in_ref, out_ref, total_ref, sent, came, send_sem, recv_sem):
    places = [place(*flips) for flips in rounds]
    greet(places)
    count = in_ref.shape[0]
    out_ref[...] = in_ref[...]
    for k, (dp_flip, _) in enumerate(rounds):
        sent[k] = out_ref[...]
        copy = send_to(places[k], sent.at[k], came.at[k], send_sem.at[k], recv_sem.at[k])
        copy.start()
        copy.wait()
        move = (dp_flip % 2) * half + dp_flip // 2
        for p in range(count):
            out_ref[p] = out_ref[p] + came[k, p ^ move]
    rows, lanes = in_ref.shape[1:]
    me = lax.axis_index("dp")
    used = lax.broadcasted_iota(jnp.int32, (rows, lanes), 0) < rows - 1
    total = out_ref[0, rows - 1 :, :]
    for g in range(count):
        there = me ^ g
        value = out_ref[(there % 2) * half + there // 2]
        total = total + jnp.sum(jnp.where(used, value * value, 0.0))
    total_ref[...] = jnp.broadcast_to(total, total_ref.shape)


def sum_everywhere(shares, square):
    dp_size = lax.axis_size("dp")
    rounds = []
    for axis, size in enumerate((dp_size, lax.axis_size("tensor"))):
        flip = 1
        while flip < size:
            rounds.append((0, flip) if axis else (flip, 0))
            flip *= 2
    each = D // dp_size
    lanes = 128 if each % 128 == 0 else each
    used = 2 * each // lanes
    parts = shares.reshape(2, dp_size, each // lanes, lanes).transpose(1, 0, 2, 3).reshape(dp_size, used, lanes)
    filler = jnp.zeros((dp_size, 7 - used, lanes), jnp.float32)
    last = jnp.broadcast_to(square, (dp_size, 1, lanes))
    parts = jnp.concatenate([parts, filler, last], axis=1)
    vmem = pl.BlockSpec(memory_space=pltpu.VMEM)
    sem = pltpu.SemaphoreType.DMA
    summed, total = pl.pallas_call(
        functools.partial(sum_kernel, rounds, dp_size // 2),
        out_shape=[jax.ShapeDtypeStruct(shape, jnp.float32) for shape in (parts.shape, (8, lanes))],
        in_specs=[vmem],
        out_specs=[vmem, vmem],
        scratch_shapes=[pltpu.VMEM((len(rounds),) + parts.shape, jnp.float32)] * 2 + [sem((len(rounds),))] * 2,
        compiler_params=pltpu.CompilerParams(collective_id=2, has_side_effects=True),
        name="sum_everywhere",
    )(parts)
    return summed[0, :used].reshape(2, each), total[0, 0]


def dot_plain(a, b):
    return lax.dot_general(a, b, (((1,), (0,)), ((), ())), preferred_element_type=jnp.float32)


def dot_rows(a, b):
    return lax.dot_general(a, b, (((0,), (0,)), ((), ())), preferred_element_type=jnp.float32)


def dot_cols(a, b):
    return lax.dot_general(a, b, (((1,), (1,)), ((), ())), preferred_element_type=jnp.float32)


def turn(values, tables, direction):
    cosine, low_sine, high_sine = tables
    lanes = values.shape[1]
    half_rot = ROT // 2
    moved = pltpu.roll(values, lanes - half_rot, 1) * low_sine + pltpu.roll(values, half_rot, 1) * high_sine
    return values * cosine + direction * moved


def head_probabilities(query, key, bias):
    scores = dot_cols(query, key) * 0.125 + bias
    exponent = jnp.exp(scores - jnp.max(scores, axis=1, keepdims=True))
    return exponent / jnp.sum(exponent, axis=1, keepdims=True)


def attention_fore(projected_ref, tables_ref, bias_ref, turned_ref, attended_ref):
    spots, _, piece, width = projected_ref.shape
    rows, third = spots * piece, width // 3
    tables = [tables_ref[k] for k in range(3)]
    first = lax.broadcasted_iota(jnp.int32, (rows, 128), 1) < HEAD_DIM
    for pair in range(third // 128):
        span = [slice(k * third + pair * 128, k * third + pair * 128 + 128) for k in range(3)]
        query, key, value = [projected_ref[:, 0, :, s].reshape(rows, 128) for s in span]
        query = turn(query, tables, 1.0).astype(jnp.bfloat16)
        key = turn(key, tables, 1.0).astype(jnp.bfloat16)
        value = value.astype(jnp.bfloat16)
        for s, part in zip(span, (query, key, value)):
            turned_ref[:, 0, :, s] = part.reshape(spots, piece, 128)
        none = jnp.zeros_like(query)
        outs = [
            dot_plain(head_probabilities(q, key, bias_ref[...]).astype(jnp.bfloat16), value)
            for q in (jnp.where(first, query, none), jnp.where(first, none, query))
        ]
        attended_ref[:, 0, :, span[0]] = (
            jnp.where(first, outs[0], outs[1]).astype(jnp.bfloat16).reshape(spots, piece, 128)
        )


def attention_back(turned_ref, d_att_ref, tables_ref, bias_ref, d_project_ref):
    spots, _, piece, width = turned_ref.shape
    rows, third = spots * piece, width // 3
    tables = [tables_ref[k] for k in range(3)]
    first = lax.broadcasted_iota(jnp.int32, (rows, 128), 1) < HEAD_DIM
    for pair in range(third // 128):
        span = [slice(k * third + pair * 128, k * third + pair * 128 + 128) for k in range(3)]
        query, key, value = [turned_ref[:, 0, :, s].reshape(rows, 128) for s in span]
        d_att = d_att_ref[:, 0, :, span[0]].reshape(rows, 128)
        none = jnp.zeros_like(query)
        parts = []
        for head in range(2):
            keep = first if head == 0 else jnp.logical_not(first)
            one_query = jnp.where(keep, query, none)
            one_d_att = jnp.where(keep, d_att, none)
            prob = head_probabilities(one_query, key, bias_ref[...])
            d_value = dot_rows(prob.astype(jnp.bfloat16), d_att)
            d_prob = dot_cols(one_d_att, value)
            d_score = (prob * (d_prob - jnp.sum(d_prob * prob, axis=1, keepdims=True))).astype(
                jnp.bfloat16
            )
            parts.append((dot_plain(d_score, key), dot_rows(d_score, query), d_value))
        joined = [jnp.where(first, one, two) for one, two in zip(*parts)]
        done = (turn(0.125 * joined[0], tables, -1.0), turn(0.125 * joined[1], tables, -1.0), joined[2])
        for s, part in zip(span, done):
            d_project_ref[:, 0, :, s] = part.astype(jnp.bfloat16).reshape(spots, piece, 128)


def join_gate_up(packed, whole):
    last = packed[:, 2 * whole :]
    gate = jnp.concatenate([packed[:, :whole], last], axis=1)
    up = jnp.concatenate([packed[:, whole : 2 * whole], pltpu.roll(last, 64, 1)], axis=1)
    return gate, up


def units_fore(normed_ref, weight_ref, packed_ref, hidden_ref):
    packed = dot_plain(normed_ref[...], weight_ref[...])
    packed_ref[...] = packed
    units = hidden_ref.shape[1]
    gate, up = join_gate_up(packed, units - 64)
    hidden_ref[...] = (gate * jax.nn.sigmoid(gate) * up).astype(jnp.bfloat16)[:, :units]


def units_back(cot, down, packed):
    units = down.shape[0]
    whole = units - 64
    d_hid = dot_cols(cot, down).astype(jnp.bfloat16).astype(jnp.float32)
    d_hid = jnp.concatenate([d_hid, jnp.zeros((d_hid.shape[0], 64), jnp.float32)], axis=1)
    gate, up = join_gate_up(packed, whole)
    sigmoid_gate = jax.nn.sigmoid(gate)
    d_gate = d_hid * up * (sigmoid_gate * (1.0 + gate * (1.0 - sigmoid_gate)))
    d_up = d_hid * (gate * sigmoid_gate)
    first = lax.broadcasted_iota(jnp.int32, (gate.shape[0], 128), 1) < 64
    last = jnp.where(first, d_gate[:, whole:], pltpu.roll(d_up[:, whole:], 64, 1))
    parts = [d_gate[:, :whole], d_up[:, :whole], last]
    return jnp.concatenate([part.astype(jnp.bfloat16) for part in parts], axis=1)


def whole_block(shape):
    return pl.BlockSpec(shape, lambda *_: (0,) * len(shape))


KERNEL_PARAMS = pltpu.CompilerParams(vmem_limit_bytes=40 * 1024 * 1024)


def run_attention_fore(projected, tables, bias):
    spots, seqs, piece, width = projected.shape
    block = lambda w: pl.BlockSpec((spots, 1, piece, w), lambda s: (0, s, 0, 0))
    rows = spots * piece
    return pl.pallas_call(
        attention_fore,
        grid=(seqs,),
        in_specs=[block(width), whole_block(tables.shape), whole_block(bias.shape)],
        out_specs=[block(width), block(width // 3)],
        out_shape=[
            jax.ShapeDtypeStruct((spots, seqs, piece, width), jnp.bfloat16),
            jax.ShapeDtypeStruct((spots, seqs, piece, width // 3), jnp.bfloat16),
        ],
        compiler_params=KERNEL_PARAMS,
        cost_estimate=pl.CostEstimate(
            flops=seqs * rows * rows * width * 2, bytes_accessed=seqs * rows * width * 7, transcendentals=0
        ),
        name="attention_fore",
    )(projected, tables, bias)


def row_tile(rows):
    return 256 if rows % 256 == 0 else rows // 8


def run_units_fore(normed, weight):
    rows, units = normed.shape[0], weight.shape[1] // 2
    tile = row_tile(rows)
    block = lambda w: pl.BlockSpec((tile, w), lambda r: (r, 0))
    return pl.pallas_call(
        units_fore,
        grid=(rows // tile,),
        in_specs=[block(D), whole_block(weight.shape)],
        out_specs=[block(2 * units), block(units)],
        out_shape=[
            jax.ShapeDtypeStruct((rows, 2 * units), jnp.float32),
            jax.ShapeDtypeStruct((rows, units), jnp.bfloat16),
        ],
        compiler_params=KERNEL_PARAMS,
        cost_estimate=pl.CostEstimate(
            flops=rows * D * units * 4, bytes_accessed=rows * (D * 2 + units * 10), transcendentals=0
        ),
        name="units_fore",
    )(normed, weight)


def adam_update(weight_old, gradient, moment_old, square_old, factor, rate, decay):
    clipped = gradient * factor
    moment_new = BETA_ONE * moment_old + (1.0 - BETA_ONE) * clipped
    square_new = BETA_TWO * square_old + (1.0 - BETA_TWO) * clipped * clipped
    moment_hat = moment_new / (1.0 - BETA_ONE**STEP)
    square_hat = square_new / (1.0 - BETA_TWO**STEP)
    weight_new = weight_old - rate * (
        moment_hat / (jnp.sqrt(square_hat) + ADAM_EPS) + decay * weight_old
    )
    return (weight_new, moment_new, square_new)


def local(
    tokens,
    cotangent,
    project_weight,
    output_weight,
    gate_up_weight,
    down_weight,
    norm_params,
    first_project,
    first_output,
    first_gate_up,
    first_down,
    first_norm,
    second_project,
    second_output,
    second_gate_up,
    second_down,
    second_norm,
):
    count = lax.axis_size("dp")
    blocks_half = count // 2
    me = lax.axis_index("dp")
    side = (me // 2) % 2
    spot = lax.axis_index("tensor")
    spots = lax.axis_size("tensor")
    micro_count, piece = tokens.shape[0], tokens.shape[1]
    head_cols = project_weight.shape[2] // 2
    unit_cols = gate_up_weight.shape[2] // 2
    whole = unit_cols - 64
    rows_each = project_weight.shape[1]
    seqs = 2 * micro_count
    rows_all = spots * seqs * piece

    def halves(first, second):
        first, second = first.astype(jnp.bfloat16), second.astype(jnp.bfloat16)
        return jnp.where(side == 0, first, second), jnp.where(side == 0, second, first)

    def project_half(s):
        return jnp.concatenate(
            [project_weight[k, :, s * head_cols : (s + 1) * head_cols] for k in range(3)], axis=1
        )

    def unit_spans(s):
        return slice(s * whole, (s + 1) * whole), slice(2 * whole + 64 * s, 2 * whole + 64 * (s + 1))

    def gate_up_half(s):
        wide, narrow = unit_spans(s)
        return jnp.concatenate(
            [gate_up_weight[k, :, span] for span in (wide, narrow) for k in range(2)], axis=1
        )

    def output_half(s):
        return output_weight[s * head_cols : (s + 1) * head_cols]

    def down_half(s):
        return jnp.concatenate([down_weight[span] for span in unit_spans(s)], axis=0)

    by_columns = rows_each % 128 == 0

    norm_low = norm_params.astype(jnp.bfloat16)
    norm_full = gather_small(norm_low).astype(jnp.float32)
    gain, shift = norm_full[0], norm_full[1]

    tok_rel = relative(tokens, 2, me, count)
    cot_low = relative(cotangent, 2, me, count)
    unit_rows, _ = norm_rows(tok_rel.astype(jnp.float32).reshape(-1, D))
    normed = (unit_rows * gain + shift).astype(jnp.bfloat16).reshape(tokens.shape)

    def chunk(half_of, columns):
        pair = halves(half_of(0), half_of(1))
        if columns and not by_columns:
            return (pair[0].T, pair[1].T, 0)
        return (*pair, int(columns))

    gathered = run_gather(
        blocks_half,
        [chunk(project_half, False), chunk(gate_up_half, False), chunk(down_half, True), chunk(output_half, True)],
        [normed, cot_low],
    )
    w_project, w_gate_up, w_down, w_output = gathered[:4]
    if not by_columns:
        w_down, w_output = w_down.T, w_output.T
    all_normed, all_cot = [rows.reshape(rows_all, D) for rows in gathered[4:]]

    order = jnp.array([0, 2, 1, 3])
    positions = ((spot ^ order)[:, None] * piece + jnp.arange(piece)[None, :]).reshape(-1)
    half_rot = ROT // 2
    inverse = 10000.0 ** (-2.0 * jnp.arange(half_rot, dtype=jnp.float32) / ROT)
    angles = positions.astype(jnp.float32)[:, None] * inverse[None, :]
    cosine, sine = jnp.cos(angles), jnp.sin(angles)
    none = jnp.zeros_like(sine)
    rest = jnp.zeros((angles.shape[0], HEAD_DIM - ROT), jnp.float32)
    tables = jnp.stack(
        [
            jnp.tile(jnp.concatenate(parts, axis=1), (1, 2))
            for parts in ((cosine, cosine, rest + 1.0), (-sine, none, rest), (none, sine, rest))
        ]
    )
    bias = jnp.where(positions[:, None] >= positions[None, :], 0.0, MASK_FILL)

    projected = dot_plain(all_normed, w_project).reshape(spots, seqs, piece, 3 * head_cols)
    turned, attended = run_attention_fore(projected, tables, bias)
    attended = attended.reshape(rows_all, head_cols)
    packed, hidden = run_units_fore(all_normed, w_gate_up)

    row_shape = (spots, seqs, piece, -1)
    rows = [values.reshape(row_shape) for values in (all_cot, packed, hidden, attended, turned)]
    pairs, totals = run_backward(
        blocks_half,
        by_columns,
        rows,
        (all_normed.T, attended.T, hidden.T),
        (w_project, w_gate_up, w_down, w_output),
        tables,
        bias,
    )
    if not by_columns:
        pairs[:2] = [(own.T, came.swapaxes(1, 2)) for own, came in pairs[:2]]
    *weight_grads, squares = run_join_grads(
        blocks_half,
        pairs,
        [output_weight.shape, down_weight.shape, gate_up_weight.shape, project_weight.shape],
        (head_cols, whole),
    )
    layer_out, input_grad, shares = run_finish_rows(
        rows_each, totals, tok_rel, cot_low, jnp.broadcast_to(gain[None], (8, D))
    )
    if rows_each % 128:
        layer_out, input_grad = [from_relative(r, 2, me, count) for r in (layer_out, input_grad)]
    norm_grad, square_total = sum_everywhere(shares[:2], squares[0, 0])
    grads = (weight_grads[3], weight_grads[0], weight_grads[2], weight_grads[1], norm_grad)
    norm_total = jnp.sqrt(square_total)
    limit = 0.03 * math.sqrt((4 * D * D + 3 * D * FF + 2 * D) * micro_count * count * SEQ)
    factor = jnp.minimum(1.0, limit / (norm_total + 1e-06))
    rates = (
        2.0 / math.sqrt(D),
        2.0 / math.sqrt(D // 32),
        2.0 / math.sqrt(D),
        2.0 / math.sqrt(FF),
        0.5,
    )
    decays = (0.1, 0.1, 0.1, 0.1, 0.0)
    masters = (project_weight, output_weight, gate_up_weight, down_weight, norm_params)
    firsts = (first_project, first_output, first_gate_up, first_down, first_norm)
    seconds = (second_project, second_output, second_gate_up, second_down, second_norm)
    updated = [
        adam_update(*parts) for parts in zip(masters, grads, firsts, seconds, [factor] * 5, rates, decays)
    ]
    return (
        layer_out,
        input_grad,
        *grads,
        norm_total,
        *[u[0] for u in updated],
        *[u[1] for u in updated],
        *[u[2] for u in updated],
    )


def solution(mesh):
    wide = P("dp", "tensor", None)
    stacked = P(None, "dp", "tensor")
    tall = P("tensor", "dp")
    params = (stacked, tall, stacked, tall, P(None, "dp"))
    return jax.shard_map(
        local,
        mesh=mesh,
        in_specs=(wide, wide, *params, *params, *params),
        out_specs=(wide, wide, *params, P(), *params, *params, *params),
        check_vma=False,
    )
```

```python
import functools
import math

import jax
import jax.numpy as jnp
import numpy as np
from jax import lax
from jax.experimental import pallas as pl
from jax.experimental.pallas import tpu as pltpu
from jax.sharding import PartitionSpec as P

D = 2048
HEAD_DIM = 64
FF = 5632
SEQ = 320
STEP = 10
ROT = 16

BETA_ONE = 0.9
BETA_TWO = 0.999
ADAM_EPS = 1e-08
NORM_EPS = 1e-05
MASK_FILL = -1e30

BOTH = ("dp", "tensor")
MESH = pl.DeviceIdType.MESH


def block_order(count):
    return [2 * j + i for i in range(2) for j in range(count // 2)]


def relative(values, axis, me, count):
    width = values.shape[axis] // count
    return jnp.concatenate(
        [lax.dynamic_slice_in_dim(values, (me ^ r) * width, width, axis) for r in block_order(count)],
        axis=axis,
    )


def from_relative(values, axis, me, count):
    width = values.shape[axis] // count
    places = [((me ^ g) % 2) * (count // 2) + (me ^ g) // 2 for g in range(count)]
    return jnp.concatenate(
        [lax.dynamic_slice_in_dim(values, place * width, width, axis) for place in places],
        axis=axis,
    )


def flip_blocks(values, axis, count):
    width = values.shape[axis] // count
    return jnp.concatenate(
        [lax.slice_in_dim(values, (p ^ 1) * width, ((p ^ 1) + 1) * width, axis=axis) for p in range(count)],
        axis=axis,
    )


def place(dp_flip, tensor_flip):
    return (lax.axis_index("dp") ^ dp_flip, lax.axis_index("tensor") ^ tensor_flip)


def greet(places):
    barrier = pltpu.get_barrier_semaphore()
    for there in places:
        pl.semaphore_signal(barrier, inc=1, device_id=there, device_id_type=MESH)
    pl.semaphore_wait(barrier, len(places))


def send_to(there, source, target, send_sem, recv_sem):
    return pltpu.make_async_remote_copy(
        src_ref=source,
        dst_ref=target,
        send_sem=send_sem,
        recv_sem=recv_sem,
        device_id=there,
        device_id_type=MESH,
    )


def group_places(half):
    return [place(2 * j, 0) for j in range(1, half)] + [place(1, 0), place(0, 2), place(0, 1)]


def forward(half, by_columns, *refs):
    def take(count):
        nonlocal refs
        head, refs = refs[:count], refs[count:]
        return head

    project_pair, gate_up_pair, down_pair, output_pair = take(4)
    gains_own, unit_rows, cot_own, cot_flipped, tables, bias = take(6)
    w_project, w_gate_up, w_down, w_output, gains = take(5)
    normed, cot, normed_t, packed, hidden, attended, turned, hidden_t, attended_t = take(9)
    stage = take(2)
    normed_own, normed_flipped = take(2)
    z_send, z_recv, x_send, x_recv, a_send, a_recv, own_sem = refs
    greet(group_places(half))

    spots, seqs, piece, _ = cot.shape
    units, heads = hidden.shape[-1], attended.shape[-1]
    each = D // (2 * half)
    rows_all = spots * seqs * piece
    every = lambda ref: pl.BlockSpec(ref.shape, lambda *g: (0,) * len(ref.shape))

    def row_chunk(out, mine, other, share=0, shares=1):
        size = mine.shape[0] // shares
        rows = pl.ds(share * size, size)
        return mine.at[rows], other.at[rows], lambda p: out.at[pl.ds(p * mine.shape[0] + share * size, size)]

    def column_chunk(out, mine, other, share=0, shares=1):
        size = mine.shape[0] // shares
        rows, width = pl.ds(share * size, size), mine.shape[1]
        return mine.at[rows], other.at[rows], lambda p: out.at[rows, pl.ds(p * width, width)]

    out_chunk = column_chunk if by_columns else row_chunk
    pair = lambda ref: (ref.at[0], ref.at[1])
    chunks = [
        row_chunk(gains, gains_own, gains_own),
        row_chunk(w_project, *pair(project_pair)),
        row_chunk(w_gate_up, *pair(gate_up_pair), 0, 2),
        row_chunk(w_gate_up, *pair(gate_up_pair), 1, 2),
        out_chunk(w_down, *pair(down_pair), 0, 2),
        out_chunk(w_output, *pair(output_pair)),
        out_chunk(w_down, *pair(down_pair), 1, 2),
    ]
    GAINS, PROJECT, GATE_UP, DOWN, OUTPUT = 0, 1, 2, 4, 5
    n = len(chunks)
    far = range(1, half)

    def z_copy(c, j):
        mine, other, block = chunks[c]
        return send_to(place(2 * j, 0), other if j % 2 else mine, block(j), z_send.at[c, j], z_recv.at[c, j])

    def x_copy(c, j):
        mine, _, block = chunks[c]
        return send_to(place(1, 0), block(j) if j else mine, block(half + j), x_send.at[c, j], x_recv.at[c, j])

    def own_copy(c):
        return pltpu.make_async_copy(chunks[c][0], chunks[c][2](0), own_sem.at[c])

    def start_z(c):
        if c < n:
            for j in far:
                z_copy(c, j).start()

    def start_own(c):
        if c < n:
            x_copy(c, 0).start()
            own_copy(c).start()

    def serve(c):
        for j in far:
            z_copy(c, j).wait_recv()
            x_copy(c, j).start()
            if c + 1 < n and c != GAINS:
                z_copy(c + 1, j).start()
        if c > GAINS:
            start_own(c + 2)

    def have(*which):
        for c in which:
            own_copy(c).wait()
            for j in range(half):
                x_copy(c, j).wait_recv()

    act_own, act_flipped, act_out = (normed_own, cot_own), (normed_flipped, cot_flipped), (normed, cot)

    def rows(a, index):
        micro = seqs // 2
        return act_out[a].at[index // 2, pl.ds((index % 2) * micro, micro)]

    def a_copy(a, k):
        source = (act_flipped[a], act_own[a], rows(a, 1), act_own[a], rows(a, 1), rows(a, 2), rows(a, 3))[k]
        there = place(2, 0) if k == 0 else place(0, 2) if k < 3 else place(0, 1)
        return send_to(there, source, rows(a, k + 1), a_send.at[a, k], a_recv.at[a, k])

    def own_act(a):
        return pltpu.make_async_copy(act_own[a], rows(a, 0), own_sem.at[n + a])

    def act_begin(a):
        for k in (0, 1, 3):
            a_copy(a, k).start()
        own_act(a).start()

    def act_z(a):
        a_copy(a, 0).wait_recv()
        a_copy(a, 2).start()
        a_copy(a, 4).start()

    def act_y(a):
        a_copy(a, 1).wait_recv()
        a_copy(a, 5).start()
        a_copy(a, 2).wait_recv()
        a_copy(a, 6).start()

    def act_have(a):
        own_act(a).wait()
        for k in range(3, 7):
            a_copy(a, k).wait_recv()

    def norm_step():
        def body(unit_ref, gains_ref, out_ref, flipped_ref):
            gain, shift = [
                jnp.concatenate([gains_ref[p * 8 + k : p * 8 + k + 1] for p in range(2 * half)], axis=1)
                for k in range(2)
            ]
            value = unit_ref[0] * gain + shift
            put(out_ref, value)
            put(flipped_ref, flip_lanes(value, each))

        block = blocked((1, piece, D), step(), 0, 0)
        pltpu.emit_pipeline(
            body, grid=(seqs // 2,), in_specs=[block, every(gains)], out_specs=[block, block]
        )(unit_rows, gains, normed_own, normed_flipped)

    def attention_step(first, count):
        block = lambda width: blocked((spots, 1, piece, width), 0, step(first), 0, 0)

        def body(normed_ref, weight_ref, tables_ref, bias_ref, turned_ref, attended_ref):
            projected = dot_plain(flat(normed_ref), weight_ref[...])
            attention_fore(projected, tables_ref, bias_ref, turned_ref, attended_ref)

        pltpu.emit_pipeline(
            body,
            grid=(count,),
            in_specs=[block(D), every(w_project), every(tables), every(bias)],
            out_specs=[block(3 * heads), block(heads)],
        )(normed, w_project, tables, bias, turned, attended)

    def turn_over(source, out, in_block, out_block, steps):
        def body(ref, out_ref):
            put(out_ref, flat(ref).T)

        pltpu.emit_pipeline(body, grid=(steps,), in_specs=[in_block], out_specs=[out_block])(source, out)

    def units_step():
        tile = lambda width: blocked((1, seqs, piece, width), step(), 0, 0, 0)

        def body(normed_ref, weight_ref, packed_ref, hidden_ref):
            value, units_value = units_fore(flat(normed_ref), weight_ref[...])
            put(packed_ref, value)
            put(hidden_ref, units_value)

        pltpu.emit_pipeline(
            body,
            grid=(spots,),
            in_specs=[tile(D), every(w_gate_up)],
            out_specs=[tile(2 * units), tile(units)],
        )(normed, w_gate_up, packed, hidden)

    def grads_step():
        groups, wide = stage[0].shape[0], D // (2 * stage[0].shape[0])

        def body(cot_ref, attended_ref, hidden_ref, *out_refs):
            block = flat(cot_ref)
            for ref, out_ref in zip((attended_ref, hidden_ref), out_refs):
                value = dot_plain(ref[...], block)
                put(out_ref, value if by_columns else value.T)

        pltpu.emit_pipeline(
            body,
            grid=(groups,),
            in_specs=[
                blocked((spots, seqs, piece, wide), 0, 0, 0, step(groups)),
                every(attended_t),
                every(hidden_t),
            ],
            out_specs=[blocked((1,) + ref.shape[1:], step(), 0, 0) for ref in stage],
        )(cot, attended_t, hidden_t, *stage)

    start_z(GAINS)
    start_z(PROJECT)
    for c in (GAINS, PROJECT, GATE_UP):
        start_own(c)
    serve(GAINS)
    have(GAINS)
    norm_step()
    act_begin(0)
    act_z(0)
    serve(PROJECT)
    act_y(0)
    act_begin(1)
    act_have(0)
    have(PROJECT)
    attention_step(0, seqs // 2)
    serve(GATE_UP)
    act_z(1)
    attention_step(seqs // 2, seqs - seqs // 2)
    columns = lambda index: blocked((spots, seqs, piece, 256), 0, 0, 0, index)
    turn_over(normed, normed_t, columns(step()), blocked((256, rows_all), step(), 0), D // 256)
    turn_over(attended, attended_t, every(attended), every(attended_t), 1)
    serve(GATE_UP + 1)
    act_y(1)
    serve(DOWN)
    have(GATE_UP, GATE_UP + 1)
    units_step()
    serve(OUTPUT)
    turn_over(hidden, hidden_t, every(hidden), every(hidden_t), 1)
    act_have(1)
    serve(n - 1)
    grads_step()
    have(DOWN, OUTPUT, n - 1)
    for c in range(n):
        for j in range(half):
            if j:
                z_copy(c, j).wait_send()
            x_copy(c, j).wait_send()
    for a in range(2):
        for k in range(7):
            a_copy(a, k).wait_send()


def run_forward(half, by_columns, pairs, gains, unit_rows, cot, cot_flipped, tables, bias, group):
    low, full = jnp.bfloat16, jnp.float32
    each, heads, units = pairs[0].shape[1], pairs[0].shape[2] // 3, pairs[1].shape[2] // 2
    spots, seqs, piece = group
    rows_all = spots * seqs * piece
    groups = min(half, 4)
    wide = D // (2 * groups)
    widths = (heads, units)
    flat_stage = [(groups, w, wide) if by_columns else (groups, wide, w) for w in widths]
    across = [(w, D) if by_columns else (D, w) for w in (units, heads)]
    shapes = [
        ((D, 3 * heads), low),
        ((D, 2 * units), low),
        *[(shape, low) for shape in across],
        ((2 * half * 8, each), full),
        (group + (D,), low),
        (group + (D,), low),
        ((D, rows_all), low),
        (group + (2 * units,), full),
        (group + (units,), low),
        (group + (heads,), low),
        (group + (3 * heads,), low),
        ((units, rows_all), low),
        ((heads, rows_all), low),
        *[(shape, low) for shape in flat_stage],
        (cot.shape, low),
        (cot.shape, low),
    ]
    ins = [*pairs, gains, unit_rows, cot, cot_flipped, tables, bias]
    anywhere = pl.BlockSpec(memory_space=pl.ANY)
    sem = pltpu.SemaphoreType.DMA
    return pl.pallas_call(
        functools.partial(forward, half, by_columns),
        out_shape=[jax.ShapeDtypeStruct(*shape) for shape in shapes],
        in_specs=[anywhere] * len(ins),
        out_specs=[anywhere] * len(shapes),
        scratch_shapes=[sem((7, half))] * 4 + [sem((2, 7))] * 2 + [sem((9,))],
        compiler_params=pltpu.CompilerParams(
            collective_id=0, has_side_effects=True, vmem_limit_bytes=56 * 1024 * 1024
        ),
        name="forward",
    )(*ins)


def prepare(each, in_place, *refs):
    tokens, cot, project, gate_up, down, output = refs[:6]
    tok_ref, unit_ref, cot_ref, cot_flipped_ref, project_ref, gate_up_ref, down_ref, output_ref = refs[6:]
    me = lax.axis_index("dp")
    side = (me // 2) % 2
    blocks = block_order(D // each)
    if in_place:
        for p, r in enumerate(blocks):
            span, flipped = slice(p * each, (p + 1) * each), slice((p ^ 1) * each, ((p ^ 1) + 1) * each)
            there = pl.ds(pl.multiple_of((me ^ r) * each, each), each)
            tok_ref[:, :, span] = tokens[:, :, there]
            cot_ref[:, :, span] = cot[:, :, there]
            cot_flipped_ref[:, :, flipped] = cot[:, :, there]
    else:
        tok_ref[...] = tokens[...]
        cot_ref[...] = cot[...]
        for s in range(cot.shape[0]):
            put(cot_flipped_ref.at[s], flip_lanes(cot[s].astype(jnp.float32), each))
    for s in range(tokens.shape[0]):
        unit_ref[s], _ = norm_rows(tok_ref[s].astype(jnp.float32))
    heads, units = output.shape[0] // 2, down.shape[0] // 2
    whole = units - 64
    for h, s in enumerate((side, 1 - side)):
        part = lambda width, start=0: pl.ds(start + pl.multiple_of(s * width, width), width)
        for k in range(3):
            put(project_ref.at[h, :, pl.ds(k * heads, heads)], project[k, :, part(heads)])
        for k in range(2):
            put(gate_up_ref.at[h, :, pl.ds(k * whole, whole)], gate_up[k, :, part(whole)])
        put(output_ref.at[h], output[part(heads)])
        put(down_ref.at[h, pl.ds(0, whole)], down[part(whole)])
        put(down_ref.at[h, pl.ds(whole, 64)], down[part(64, 2 * whole)])
    gate, up = gate_up[0, :, 2 * whole :], gate_up[1, :, 2 * whole :]
    first = lax.broadcasted_iota(jnp.int32, gate.shape, 1) < 64
    zero = jnp.where(first, gate, pltpu.roll(up, 64, 1))
    one = jnp.where(first, pltpu.roll(gate, 64, 1), up)
    put(gate_up_ref.at[0, :, pl.ds(2 * whole, 128)], jnp.where(side == 0, zero, one))
    put(gate_up_ref.at[1, :, pl.ds(2 * whole, 128)], jnp.where(side == 0, one, zero))


def run_prepare(tokens, cot, weights):
    project, gate_up, down, output = weights
    each = project.shape[1]
    in_place = each % 128 == 0
    if not in_place:
        me, count = lax.axis_index("dp"), D // each
        tokens, cot = relative(tokens, 2, me, count), relative(cot, 2, me, count)
    low = jnp.bfloat16
    heads, units = output.shape[0] // 2, down.shape[0] // 2
    shapes = [(tokens.shape, low), (tokens.shape, jnp.float32), (cot.shape, low), (cot.shape, low)]
    shapes += [((2, each, 3 * heads), low), ((2, each, 2 * units), low)]
    shapes += [((2, units, each), low), ((2, heads, each), low)]
    vmem = pl.BlockSpec(memory_space=pltpu.VMEM)
    return pl.pallas_call(
        functools.partial(prepare, each, in_place),
        in_specs=[vmem] * 6,
        out_specs=[vmem] * 8,
        out_shape=[jax.ShapeDtypeStruct(*shape) for shape in shapes],
        compiler_params=KERNEL_PARAMS,
        name="prepare",
    )(tokens, cot, project, gate_up, down, output)


def flat(ref):
    value = ref[...]
    return value.reshape(-1, value.shape[-1])


def put(ref, value):
    ref[...] = value.astype(ref.dtype).reshape(ref.shape)


def blocked(shape, *index):
    return pl.BlockSpec(shape, lambda g: tuple(i(g) if callable(i) else i for i in index))


def step(offset=0):
    return lambda g: g + offset


def backward(half, by_columns, window, *refs):
    def take(count):
        nonlocal refs
        head, refs = refs[:count], refs[count:]
        return head

    cot, packed, hidden, attended, turned = take(5)
    normed_t, attended_t_all, hidden_t_all = take(3)
    w_project, w_gate_up, w_down, w_output, tables, bias = take(6)
    stage_out = take(2)
    z_in, mine = take(4), take(4)
    act_away, act_near, core_in, y_out, y_in, far_out, act_far, act_sum = [take(2) for _ in range(8)]
    stage, x_in = stage_out + take(2), take(4)
    d_packed, d_att, d_project, attended_t, hidden_t, normed_block, cot_block = take(7)
    x_send, x_recv, z_send, z_recv, a_send, a_recv, load_sem, block_sem = refs
    greet(group_places(half))

    spots, seqs, piece, _ = cot.shape
    units, heads = hidden.shape[-1], attended.shape[-1]
    groups = stage[0].shape[0]
    per = half // groups
    wide = D // (2 * groups)
    every = lambda ref: pl.BlockSpec(ref.shape, lambda g: (0,) * len(ref.shape))

    whole = (attended_t, hidden_t, d_packed, d_project)

    def product(c, block, whole_ref):
        if c >= 2:
            return dot_plain(block, flat(whole_ref))
        value = dot_plain(whole_ref[...], block)
        return value if by_columns else value.T

    def block_copy(index):
        c, g = order[index]
        span, slot = pl.ds(g * wide, wide), index % 2
        if c >= 2:
            source, target = normed_t.at[span], normed_block.at[slot]
        else:
            source, target = cot.at[:, :, :, span], cot_block.at[slot]
        return pltpu.make_async_copy(source, target, block_sem.at[slot])

    def x_copy(c, g):
        return send_to(place(1, 0), stage[c].at[g], x_in[c].at[g], x_send.at[c, g], x_recv.at[c, g])

    def z_copy(c, j):
        source = x_in[c].at[j // per]
        if per > 1:
            rows = z_in[c].shape[1]
            source = source.at[pl.ds((j % per) * rows, rows)]
        return send_to(place(2 * j, 0), source, z_in[c].at[j], z_send.at[c, j], z_recv.at[c, j])

    def a_copy(a, s):
        source = (act_away[a], y_out[a], far_out[a])[s]
        target = (core_in[a], y_in[a], act_far[a])[s]
        there = (place(0, 1), place(0, 2), place(2, 0))[s]
        return send_to(there, source, target, a_send.at[a, s], a_recv.at[a, s])

    order = [(0, 3), (0, 2), (1, 3), (1, 2), (1, 1), (0, 1)]
    order += [(c, g) for c in (2, 3) for g in (3, 2, 1)] + [(c, 0) for c in (2, 1, 3, 0)]
    started, served, ready = [0], [0], {0, 1}

    def start_x():
        while started[0] < min(served[0] + window, len(order)) and order[started[0]][0] in ready:
            x_copy(*order[started[0]]).start()
            started[0] += 1

    def away_product(c):
        def body(block_ref, whole_ref, out_ref):
            put(out_ref, product(c, block_ref[...], whole_ref))

        pltpu.emit_pipeline(
            body,
            grid=(groups,),
            in_specs=[blocked((wide, normed_t.shape[1]), step(groups), 0), every(whole[c])],
            out_specs=[blocked((1,) + stage[c].shape[1:], step(), 0, 0)],
        )(normed_t, whole[c], stage[c])
        ready.add(c)
        start_x()

    def serve(count):
        for _ in range(count):
            index = served[0]
            c, g = order[index]
            served[0] += 1
            block_copy(index).wait()
            if served[0] < len(order):
                block_copy(served[0]).start()
            x_copy(c, g).wait_recv()
            start_x()
            block = flat((normed_block if c >= 2 else cot_block).at[index % 2])
            total = product(c, block, whole[c]) + x_in[c][g].astype(jnp.float32)
            if g == 0:
                mine[c][0] = total
            if g > 0 or per > 1:
                put(x_in[c].at[g], total)
            for j in range(g * per, (g + 1) * per):
                if j:
                    z_copy(c, j).start()

    def units_step():
        tile = (1, seqs, piece)

        def body(cot_ref, down_ref, output_ref, packed_ref, d_packed_ref, d_att_ref):
            rows = flat(cot_ref)
            d_packed_ref[...] = units_back(rows, down_ref[...], flat(packed_ref)).reshape(d_packed_ref.shape)
            put(d_att_ref, dot_cols(rows, output_ref[...]))

        pltpu.emit_pipeline(
            body,
            grid=(spots,),
            in_specs=[
                blocked(tile + (D,), step(), 0, 0, 0),
                every(w_down),
                every(w_output),
                blocked(tile + (2 * units,), step(), 0, 0, 0),
            ],
            out_specs=[
                blocked(tile + (2 * units,), step(), 0, 0, 0),
                blocked(tile + (heads,), step(), 0, 0, 0),
            ],
        )(cot, w_down, w_output, packed, d_packed, d_att)

    def attention_step(first, count):
        block = lambda width: blocked((spots, 1, piece, width), 0, step(first), 0, 0)
        pltpu.emit_pipeline(
            attention_back,
            grid=(count,),
            in_specs=[block(3 * heads), block(heads), every(tables), every(bias)],
            out_specs=[block(3 * heads)],
        )(turned, d_att, tables, bias, d_project)

    def two_cores(away_ref, near_ref, total):
        middle = total.shape[0] // 2
        put(near_ref, total[:middle])
        put(away_ref, total[middle:])

    core_block = blocked((spots // 2, seqs, piece, 256), 0, 0, 0, step())

    def normed_step():
        def body(d_project_ref, d_packed_ref, project_ref, gate_up_ref, away_ref, near_ref):
            total = dot_cols(flat(d_project_ref), project_ref[...])
            two_cores(away_ref, near_ref, total + dot_cols(flat(d_packed_ref), gate_up_ref[...]))

        pltpu.emit_pipeline(
            body,
            grid=(D // 256,),
            in_specs=[
                every(d_project),
                every(d_packed),
                blocked((256, 3 * heads), step(), 0),
                blocked((256, 2 * units), step(), 0),
            ],
            out_specs=[core_block, core_block],
        )(d_project, d_packed, w_project, w_gate_up, act_away[0], act_near[0])

    def out_step():
        def body(attended_ref, hidden_ref, output_ref, down_ref, away_ref, near_ref):
            total = dot_plain(flat(attended_ref), output_ref[...])
            two_cores(away_ref, near_ref, total + dot_plain(flat(hidden_ref), down_ref[...]))

        pltpu.emit_pipeline(
            body,
            grid=(D // 256,),
            in_specs=[
                every(attended),
                every(hidden),
                blocked((heads, 256), 0, step()),
                blocked((units, 256), 0, step()),
            ],
            out_specs=[core_block, core_block],
        )(attended, hidden, w_output, w_down, act_away[1], act_near[1])

    def add_terms(*refs):
        *terms, out_ref = refs
        put(out_ref, sum(flat(term).astype(jnp.float32) for term in terms))

    half_seqs = seqs // 2

    def core_arrived(a):
        a_copy(a, 0).wait_recv()
        rows = blocked((1, half_seqs, piece, D), 1, step(), 0, 0)
        pltpu.emit_pipeline(
            add_terms,
            grid=(2,),
            in_specs=[rows, rows],
            out_specs=[blocked((half_seqs, piece, D), step(), 0, 0)],
        )(act_near[a], core_in[a], y_out[a])
        a_copy(a, 1).start()

    def y_arrived(a):
        def body(*refs):
            add_terms(*refs[:3], refs[6])
            add_terms(*refs[3:6], refs[7])

        def both(shape, *lead):
            return [blocked(shape, *lead, step(first), 0, 0) for first in (half_seqs, 0)]

        rows, lines = both((1, 1, piece, D), 0), both((1, piece, D))
        a_copy(a, 1).wait_recv()
        pltpu.emit_pipeline(
            body,
            grid=(half_seqs,),
            in_specs=[rows[0], rows[0], lines[0], rows[1], rows[1], lines[1]],
            out_specs=[blocked((1, piece, D), step(), 0, 0)] * 2,
        )(*[act_near[a], core_in[a], y_in[a]] * 2, far_out[a], act_sum[a])
        a_copy(a, 2).start()

    loads = [
        pltpu.make_async_copy(attended_t_all, attended_t, load_sem.at[0]),
        pltpu.make_async_copy(hidden_t_all, hidden_t, load_sem.at[1]),
    ]
    for load in loads:
        load.start()
    block_copy(0).start()
    start_x()
    for load in loads:
        load.wait()
    out_step()
    a_copy(1, 0).start()
    serve(2)
    units_step()
    core_arrived(1)
    away_product(2)
    serve(2)
    attention_step(0, seqs // 2)
    serve(2)
    attention_step(seqs // 2, seqs - seqs // 2)
    away_product(3)
    serve(1)
    y_arrived(1)
    normed_step()
    a_copy(0, 0).start()
    serve(1)
    core_arrived(0)
    serve(4)
    y_arrived(0)
    serve(len(order) - served[0])
    for c in range(4):
        for j in range(1, half):
            z_copy(c, j).wait()
        for g in range(groups):
            x_copy(c, g).wait_send()
    for a in range(2):
        for s in range(3):
            a_copy(a, s).wait_send()
        a_copy(a, 2).wait_recv()


def run_backward(half, by_columns, rows, transposed, weights, tables, bias, stage, window=3):
    cot, packed, hidden, attended, turned = rows
    low, full = jnp.bfloat16, jnp.float32
    spots, seqs, piece, _ = cot.shape
    each = D // (2 * half)
    groups = min(half, 4)
    wide = D // (2 * groups)
    widths = (attended.shape[-1], hidden.shape[-1], packed.shape[-1], turned.shape[-1])
    columns = [by_columns and groups == half and c < 2 for c in range(4)]

    def shape_of(count, block):
        return [(count, w, block) if flip else (count, block, w) for w, flip in zip(widths, columns)]

    def row_shape(*lead, kind=low):
        return [jax.ShapeDtypeStruct(lead + (piece, D), kind)] * 2

    shapes = [jax.ShapeDtypeStruct(shape, low) for shape in shape_of(half, each)]
    shapes += [jax.ShapeDtypeStruct(shape, full) for shape in shape_of(1, wide)]
    shapes += row_shape(spots // 2, seqs) * 3 + row_shape(seqs) * 2 + row_shape(seqs // 2) * 2
    shapes += row_shape(seqs // 2, kind=full)
    anywhere = pl.BlockSpec(memory_space=pl.ANY)
    vmem = pl.BlockSpec(memory_space=pltpu.VMEM)
    ins = [*rows, *transposed, *weights, tables, bias, *stage]
    sem = pltpu.SemaphoreType.DMA
    rows_all = spots * seqs * piece
    scratch = [pltpu.VMEM(shape, low) for shape in shape_of(groups, wide)[2:] + shape_of(groups, wide)]
    scratch += [pltpu.VMEM(r.shape, low) for r in (packed, attended, turned)]
    scratch += [pltpu.VMEM(t.shape, low) for t in transposed[1:]]
    scratch += [pltpu.VMEM((2, wide, rows_all), low), pltpu.VMEM((2, spots, seqs, piece, wide), low)]
    scratch += [sem((4, groups))] * 2 + [sem((4, half))] * 2 + [sem((2, 3))] * 2 + [sem((2,))] * 2
    outs = pl.pallas_call(
        functools.partial(backward, half, columns[0], window),
        out_shape=shapes,
        in_specs=[anywhere] * len(ins),
        out_specs=[anywhere] * 4 + [vmem] * 4 + [anywhere] * (len(shapes) - 8),
        scratch_shapes=scratch,
        compiler_params=pltpu.CompilerParams(
            collective_id=1, has_side_effects=True, vmem_limit_bytes=60 * 1024 * 1024
        ),
        name="backward",
    )(*ins)
    pairs = []
    for c in range(4):
        own = outs[4 + c][0] if columns[c] else outs[4 + c][0, :each]
        pairs.append((own, outs[c]))
    return pairs, outs[-4:]


def flip_lanes(values, width):
    lanes = values.shape[1]
    if width % 128 == 0:
        spans = [slice((p ^ 1) * width, ((p ^ 1) + 1) * width) for p in range(lanes // width)]
        return jnp.concatenate([values[:, span] for span in spans], axis=1)
    even = (lax.broadcasted_iota(jnp.int32, values.shape, 1) // width) % 2 == 0
    return jnp.where(even, pltpu.roll(values, lanes - width, 1), pltpu.roll(values, width, 1))


def norm_rows(tok_rows):
    centered = tok_rows - jnp.mean(tok_rows, axis=1, keepdims=True)
    row_scale = lax.rsqrt(jnp.mean(centered * centered, axis=1, keepdims=True) + NORM_EPS)
    return centered * row_scale, row_scale


def finish_rows(each, in_place, far_ref, far_out_ref, sum_ref, sum_out_ref, tok_ref, cot_ref, gain_ref, out_ref, input_ref, grad_ref):
    d_normed = flat(sum_ref) + flip_lanes(flat(far_ref).astype(jnp.float32), each)
    summed = flat(sum_out_ref) + flip_lanes(flat(far_out_ref).astype(jnp.float32), each)
    tok_rows, cot_rows = flat(tok_ref).astype(jnp.float32), flat(cot_ref).astype(jnp.float32)
    unit_rows, row_scale = norm_rows(tok_rows)
    d_unit = d_normed * gain_ref[0:1]
    d_input = row_scale * (
        d_unit
        - jnp.mean(d_unit, axis=1, keepdims=True)
        - unit_rows * jnp.mean(d_unit * unit_rows, axis=1, keepdims=True)
    )
    me = lax.axis_index("dp")
    for ref, value in ((out_ref, tok_rows + summed), (input_ref, cot_rows + d_input)):
        value = value.astype(jnp.bfloat16)
        if in_place:
            for p, r in enumerate(block_order(D // each)):
                span = pl.ds(pl.multiple_of((me ^ r) * each, each), each)
                ref[0, :, span] = value[:, p * each : (p + 1) * each]
        else:
            ref[0] = value
    share = jnp.concatenate(
        [
            jnp.sum(d_normed * unit_rows, axis=0, keepdims=True),
            jnp.sum(d_normed, axis=0, keepdims=True),
            jnp.zeros((6, D), jnp.float32),
        ],
        axis=0,
    )

    @pl.when(pl.program_id(0) == 0)
    def _():
        grad_ref[...] = share

    @pl.when(pl.program_id(0) > 0)
    def _():
        grad_ref[...] = grad_ref[...] + share


def run_finish_rows(each, totals, tokens, cot, gain):
    in_place = each % 128 == 0
    count, piece, _ = tokens.shape
    block = pl.BlockSpec((1, piece, D), lambda s: (s, 0, 0))
    fixed = pl.BlockSpec((8, D), lambda s: (0, 0))
    rows = jax.ShapeDtypeStruct(tokens.shape, jnp.bfloat16)
    return pl.pallas_call(
        functools.partial(finish_rows, each, in_place),
        grid=(count,),
        in_specs=[block] * 6 + [fixed],
        out_specs=[block, block, fixed],
        out_shape=[rows, rows, jax.ShapeDtypeStruct((8, D), jnp.float32)],
        compiler_params=KERNEL_PARAMS,
        name="finish_rows",
    )(*totals, tokens, cot, gain)


def join_grads(half, spans, *refs):
    own, came = refs[0:8:2], refs[1:8:2]
    output_ref, down_ref, gate_up_ref, project_ref, square_ref = refs[8:]
    side = (lax.axis_index("dp") // 2) % 2
    heads, whole = spans
    squares = jnp.float32(0.0)

    def halves(c, rows, columns):
        nonlocal squares
        pick = lambda j: came[c][j, rows, columns].astype(jnp.float32)
        mine = own[c][rows, columns] + sum(pick(j) for j in range(2, half, 2))
        other = sum(pick(j) for j in range(1, half, 2))
        squares = squares + jnp.sum(mine * mine) + jnp.sum(other * other)
        return mine, other

    def places(width, start=0):
        return [pl.ds(start + pl.multiple_of(s * width, width), width) for s in (side, 1 - side)]

    every = slice(None)
    for value, span in zip(halves(0, every, every), places(heads)):
        output_ref[span] = value
    for value, span in zip(halves(1, slice(0, whole), every), places(whole)):
        down_ref[span] = value
    for value, span in zip(halves(1, slice(whole, whole + 64), every), places(64, 2 * whole)):
        down_ref[span] = value
    for k in range(3):
        for value, span in zip(halves(3, every, slice(k * heads, (k + 1) * heads)), places(heads)):
            project_ref[k, :, span] = value
    for k in range(2):
        for value, span in zip(halves(2, every, slice(k * whole, (k + 1) * whole)), places(whole)):
            gate_up_ref[k, :, span] = value
    mine, other = halves(2, every, slice(2 * whole, 2 * whole + 128))
    zero, one = jnp.where(side == 0, mine, other), jnp.where(side == 0, other, mine)
    first = lax.broadcasted_iota(jnp.int32, zero.shape, 1) < 64
    gate_up_ref[0, :, 2 * whole :] = jnp.where(first, zero, pltpu.roll(one, 64, 1))
    gate_up_ref[1, :, 2 * whole :] = jnp.where(first, pltpu.roll(zero, 64, 1), one)
    square_ref[...] = jnp.full(square_ref.shape, squares)


def run_join_grads(half, pairs, shapes, spans):
    vmem = pl.BlockSpec(memory_space=pltpu.VMEM)
    return pl.pallas_call(
        functools.partial(join_grads, half, spans),
        in_specs=[vmem] * 8,
        out_specs=[vmem] * 5,
        out_shape=[jax.ShapeDtypeStruct(shape, jnp.float32) for shape in shapes + [(8, 128)]],
        compiler_params=pltpu.CompilerParams(vmem_limit_bytes=48 * 1024 * 1024),
        name="join_grads",
    )(*[part for pair in pairs for part in pair])


def sum_kernel(rounds, half, in_ref, out_ref, total_ref, sent, came, send_sem, recv_sem):
    places = [place(*flips) for flips in rounds]
    greet(places)
    count = in_ref.shape[0]
    out_ref[...] = in_ref[...]
    for k, (dp_flip, _) in enumerate(rounds):
        sent[k] = out_ref[...]
        copy = send_to(places[k], sent.at[k], came.at[k], send_sem.at[k], recv_sem.at[k])
        copy.start()
        copy.wait()
        move = (dp_flip % 2) * half + dp_flip // 2
        for p in range(count):
            out_ref[p] = out_ref[p] + came[k, p ^ move]
    rows, lanes = in_ref.shape[1:]
    me = lax.axis_index("dp")
    used = lax.broadcasted_iota(jnp.int32, (rows, lanes), 0) < rows - 1
    total = out_ref[0, rows - 1 :, :]
    for g in range(count):
        there = me ^ g
        value = out_ref[(there % 2) * half + there // 2]
        total = total + jnp.sum(jnp.where(used, value * value, 0.0))
    total_ref[...] = jnp.broadcast_to(total, total_ref.shape)


def sum_everywhere(shares, square):
    dp_size = lax.axis_size("dp")
    rounds = []
    for axis, size in enumerate((dp_size, lax.axis_size("tensor"))):
        flip = 1
        while flip < size:
            rounds.append((0, flip) if axis else (flip, 0))
            flip *= 2
    each = D // dp_size
    lanes = 128 if each % 128 == 0 else each
    used = 2 * each // lanes
    parts = shares.reshape(2, dp_size, each // lanes, lanes).transpose(1, 0, 2, 3).reshape(dp_size, used, lanes)
    filler = jnp.zeros((dp_size, 7 - used, lanes), jnp.float32)
    last = jnp.broadcast_to(square, (dp_size, 1, lanes))
    parts = jnp.concatenate([parts, filler, last], axis=1)
    vmem = pl.BlockSpec(memory_space=pltpu.VMEM)
    sem = pltpu.SemaphoreType.DMA
    summed, total = pl.pallas_call(
        functools.partial(sum_kernel, rounds, dp_size // 2),
        out_shape=[jax.ShapeDtypeStruct(shape, jnp.float32) for shape in (parts.shape, (8, lanes))],
        in_specs=[vmem],
        out_specs=[vmem, vmem],
        scratch_shapes=[pltpu.VMEM((len(rounds),) + parts.shape, jnp.float32)] * 2 + [sem((len(rounds),))] * 2,
        compiler_params=pltpu.CompilerParams(collective_id=2, has_side_effects=True),
        name="sum_everywhere",
    )(parts)
    return summed[0, :used].reshape(2, each), total[0, 0]


def dot_plain(a, b):
    return lax.dot_general(a, b, (((1,), (0,)), ((), ())), preferred_element_type=jnp.float32)


def dot_rows(a, b):
    return lax.dot_general(a, b, (((0,), (0,)), ((), ())), preferred_element_type=jnp.float32)


def dot_cols(a, b):
    return lax.dot_general(a, b, (((1,), (1,)), ((), ())), preferred_element_type=jnp.float32)


def turn(values, tables, direction):
    cosine, low_sine, high_sine = tables
    lanes = values.shape[1]
    half_rot = ROT // 2
    moved = pltpu.roll(values, lanes - half_rot, 1) * low_sine + pltpu.roll(values, half_rot, 1) * high_sine
    return values * cosine + direction * moved


def head_probabilities(query, key, bias):
    scores = dot_cols(query, key) * 0.125 + bias
    exponent = jnp.exp(scores - jnp.max(scores, axis=1, keepdims=True))
    return exponent / jnp.sum(exponent, axis=1, keepdims=True)


def attention_fore(projected, tables_ref, bias_ref, turned_ref, attended_ref):
    spots, _, piece, width = turned_ref.shape
    rows, third = spots * piece, width // 3
    tables = [tables_ref[k] for k in range(3)]
    first = lax.broadcasted_iota(jnp.int32, (rows, 128), 1) < HEAD_DIM
    for pair in range(third // 128):
        span = [slice(k * third + pair * 128, k * third + pair * 128 + 128) for k in range(3)]
        query, key, value = [projected[:, s] for s in span]
        query = turn(query, tables, 1.0).astype(jnp.bfloat16)
        key = turn(key, tables, 1.0).astype(jnp.bfloat16)
        value = value.astype(jnp.bfloat16)
        for s, part in zip(span, (query, key, value)):
            turned_ref[:, 0, :, s] = part.reshape(spots, piece, 128)
        none = jnp.zeros_like(query)
        outs = [
            dot_plain(head_probabilities(q, key, bias_ref[...]).astype(jnp.bfloat16), value)
            for q in (jnp.where(first, query, none), jnp.where(first, none, query))
        ]
        attended_ref[:, 0, :, span[0]] = (
            jnp.where(first, outs[0], outs[1]).astype(jnp.bfloat16).reshape(spots, piece, 128)
        )


def attention_back(turned_ref, d_att_ref, tables_ref, bias_ref, d_project_ref):
    spots, _, piece, width = turned_ref.shape
    rows, third = spots * piece, width // 3
    tables = [tables_ref[k] for k in range(3)]
    first = lax.broadcasted_iota(jnp.int32, (rows, 128), 1) < HEAD_DIM
    for pair in range(third // 128):
        span = [slice(k * third + pair * 128, k * third + pair * 128 + 128) for k in range(3)]
        query, key, value = [turned_ref[:, 0, :, s].reshape(rows, 128) for s in span]
        d_att = d_att_ref[:, 0, :, span[0]].reshape(rows, 128)
        none = jnp.zeros_like(query)
        parts = []
        for head in range(2):
            keep = first if head == 0 else jnp.logical_not(first)
            one_query = jnp.where(keep, query, none)
            one_d_att = jnp.where(keep, d_att, none)
            prob = head_probabilities(one_query, key, bias_ref[...])
            d_value = dot_rows(prob.astype(jnp.bfloat16), d_att)
            d_prob = dot_cols(one_d_att, value)
            d_score = (prob * (d_prob - jnp.sum(d_prob * prob, axis=1, keepdims=True))).astype(
                jnp.bfloat16
            )
            parts.append((dot_plain(d_score, key), dot_rows(d_score, query), d_value))
        joined = [jnp.where(first, one, two) for one, two in zip(*parts)]
        done = (turn(0.125 * joined[0], tables, -1.0), turn(0.125 * joined[1], tables, -1.0), joined[2])
        for s, part in zip(span, done):
            d_project_ref[:, 0, :, s] = part.astype(jnp.bfloat16).reshape(spots, piece, 128)


def join_gate_up(packed, whole):
    last = packed[:, 2 * whole :]
    gate = jnp.concatenate([packed[:, :whole], last], axis=1)
    up = jnp.concatenate([packed[:, whole : 2 * whole], pltpu.roll(last, 64, 1)], axis=1)
    return gate, up


def units_fore(normed, weight):
    packed = dot_plain(normed, weight)
    units = weight.shape[1] // 2
    gate, up = join_gate_up(packed, units - 64)
    return packed, (gate * jax.nn.sigmoid(gate) * up).astype(jnp.bfloat16)[:, :units]


def units_back(cot, down, packed):
    units = down.shape[0]
    whole = units - 64
    d_hid = dot_cols(cot, down).astype(jnp.bfloat16).astype(jnp.float32)
    d_hid = jnp.concatenate([d_hid, jnp.zeros((d_hid.shape[0], 64), jnp.float32)], axis=1)
    gate, up = join_gate_up(packed, whole)
    sigmoid_gate = jax.nn.sigmoid(gate)
    d_gate = d_hid * up * (sigmoid_gate * (1.0 + gate * (1.0 - sigmoid_gate)))
    d_up = d_hid * (gate * sigmoid_gate)
    first = lax.broadcasted_iota(jnp.int32, (gate.shape[0], 128), 1) < 64
    last = jnp.where(first, d_gate[:, whole:], pltpu.roll(d_up[:, whole:], 64, 1))
    parts = [d_gate[:, :whole], d_up[:, :whole], last]
    return jnp.concatenate([part.astype(jnp.bfloat16) for part in parts], axis=1)


KERNEL_PARAMS = pltpu.CompilerParams(vmem_limit_bytes=40 * 1024 * 1024)


def adam_update(weight_old, gradient, moment_old, square_old, factor, rate, decay):
    clipped = gradient * factor
    moment_new = BETA_ONE * moment_old + (1.0 - BETA_ONE) * clipped
    square_new = BETA_TWO * square_old + (1.0 - BETA_TWO) * clipped * clipped
    moment_hat = moment_new / (1.0 - BETA_ONE**STEP)
    square_hat = square_new / (1.0 - BETA_TWO**STEP)
    weight_new = weight_old - rate * (
        moment_hat / (jnp.sqrt(square_hat) + ADAM_EPS) + decay * weight_old
    )
    return (weight_new, moment_new, square_new)


def local(
    tokens,
    cotangent,
    project_weight,
    output_weight,
    gate_up_weight,
    down_weight,
    norm_params,
    first_project,
    first_output,
    first_gate_up,
    first_down,
    first_norm,
    second_project,
    second_output,
    second_gate_up,
    second_down,
    second_norm,
):
    count = lax.axis_size("dp")
    blocks_half = count // 2
    me = lax.axis_index("dp")
    side = (me // 2) % 2
    spot = lax.axis_index("tensor")
    spots = lax.axis_size("tensor")
    micro_count, piece = tokens.shape[0], tokens.shape[1]
    head_cols = project_weight.shape[2] // 2
    unit_cols = gate_up_weight.shape[2] // 2
    whole = unit_cols - 64
    rows_each = project_weight.shape[1]
    seqs = 2 * micro_count
    rows_all = spots * seqs * piece

    by_columns = rows_each % 128 == 0

    by_columns = rows_each % 128 == 0

    norm_low = norm_params.astype(jnp.bfloat16)
    tok_rel, unit_rows, cot_low, cot_flipped, *weight_pairs = run_prepare(
        tokens, cotangent, (project_weight, gate_up_weight, down_weight, output_weight)
    )
    if not by_columns:
        weight_pairs[2:] = [pair.swapaxes(1, 2) for pair in weight_pairs[2:]]

    order = [0, 2, 1, 3]
    half_rot = ROT // 2
    angles = np.arange(spots * piece)[:, None] * (10000.0 ** (-2.0 * np.arange(half_rot) / ROT))[None, :]
    cosine, sine = np.cos(angles), np.sin(angles)
    none = np.zeros_like(sine)
    rest = np.zeros((angles.shape[0], HEAD_DIM - ROT))
    in_order = np.stack(
        [
            np.tile(np.concatenate(parts, axis=1), (1, 2))
            for parts in ((cosine, cosine, rest + 1.0), (-sine, none, rest), (none, sine, rest))
        ]
    ).astype(np.float32)
    tables = jnp.concatenate(
        [lax.dynamic_slice_in_dim(jnp.asarray(in_order), (spot ^ k) * piece, piece, 1) for k in order], axis=1
    )
    positions = ((spot ^ jnp.array(order))[:, None] * piece + jnp.arange(piece)[None, :]).reshape(-1)
    bias = jnp.where(positions[:, None] >= positions[None, :], 0.0, MASK_FILL)

    own_gains = jnp.pad(norm_params.astype(jnp.bfloat16).astype(jnp.float32), ((0, 6), (0, 0)))
    (
        w_project,
        w_gate_up,
        w_down,
        w_output,
        gains,
        _,
        all_cot,
        normed_t,
        packed,
        hidden,
        attended,
        turned,
        hidden_t,
        attended_t,
        *stage,
    ) = run_forward(
        blocks_half,
        by_columns,
        weight_pairs,
        own_gains,
        unit_rows,
        cot_low,
        cot_flipped,
        tables,
        bias,
        (spots, seqs, piece),
    )
    gains = gains.reshape(count, 8, rows_each).transpose(1, 0, 2).reshape(8, D)
    if not by_columns:
        w_down, w_output = w_down.T, w_output.T
    pairs, totals = run_backward(
        blocks_half,
        by_columns,
        (all_cot, packed, hidden, attended, turned),
        (normed_t, attended_t, hidden_t),
        (w_project, w_gate_up, w_down, w_output),
        tables,
        bias,
        stage[:2],
    )
    if not by_columns:
        pairs[:2] = [(own.T, came.swapaxes(1, 2)) for own, came in pairs[:2]]
    *weight_grads, squares = run_join_grads(
        blocks_half,
        pairs,
        [output_weight.shape, down_weight.shape, gate_up_weight.shape, project_weight.shape],
        (head_cols, whole),
    )
    layer_out, input_grad, shares = run_finish_rows(
        rows_each, totals, tok_rel, cot_low, gains
    )
    if rows_each % 128:
        layer_out, input_grad = [from_relative(r, 2, me, count) for r in (layer_out, input_grad)]
    norm_grad, square_total = sum_everywhere(shares[:2], squares[0, 0])
    grads = (weight_grads[3], weight_grads[0], weight_grads[2], weight_grads[1], norm_grad)
    norm_total = jnp.sqrt(square_total)
    limit = 0.03 * math.sqrt((4 * D * D + 3 * D * FF + 2 * D) * micro_count * count * SEQ)
    factor = jnp.minimum(1.0, limit / (norm_total + 1e-06))
    rates = (
        2.0 / math.sqrt(D),
        2.0 / math.sqrt(D // 32),
        2.0 / math.sqrt(D),
        2.0 / math.sqrt(FF),
        0.5,
    )
    decays = (0.1, 0.1, 0.1, 0.1, 0.0)
    masters = (project_weight, output_weight, gate_up_weight, down_weight, norm_params)
    firsts = (first_project, first_output, first_gate_up, first_down, first_norm)
    seconds = (second_project, second_output, second_gate_up, second_down, second_norm)
    updated = [
        adam_update(*parts) for parts in zip(masters, grads, firsts, seconds, [factor] * 5, rates, decays)
    ]
    return (
        layer_out,
        input_grad,
        *grads,
        norm_total,
        *[u[0] for u in updated],
        *[u[1] for u in updated],
        *[u[2] for u in updated],
    )


def solution(mesh):
    wide = P("dp", "tensor", None)
    stacked = P(None, "dp", "tensor")
    tall = P("tensor", "dp")
    params = (stacked, tall, stacked, tall, P(None, "dp"))
    return jax.shard_map(
        local,
        mesh=mesh,
        in_specs=(wide, wide, *params, *params, *params),
        out_specs=(wide, wide, *params, P(), *params, *params, *params),
        check_vma=False,
    )
```

```python
import functools
import math

import jax
import jax.numpy as jnp
import numpy as np
from jax import lax
from jax.experimental import pallas as pl
from jax.experimental.pallas import tpu as pltpu
from jax.sharding import PartitionSpec as P

D = 2048
HEAD_DIM = 64
FF = 5632
SEQ = 320
STEP = 10
ROT = 16

BETA_ONE = 0.9
BETA_TWO = 0.999
ADAM_EPS = 1e-08
NORM_EPS = 1e-05
MASK_FILL = -1e30

BOTH = ("dp", "tensor")
MESH = pl.DeviceIdType.MESH


def block_order(count):
    return [2 * j + i for i in range(2) for j in range(count // 2)]


def relative(values, axis, me, count):
    width = values.shape[axis] // count
    return jnp.concatenate(
        [lax.dynamic_slice_in_dim(values, (me ^ r) * width, width, axis) for r in block_order(count)],
        axis=axis,
    )


def from_relative(values, axis, me, count):
    width = values.shape[axis] // count
    places = [((me ^ g) % 2) * (count // 2) + (me ^ g) // 2 for g in range(count)]
    return jnp.concatenate(
        [lax.dynamic_slice_in_dim(values, place * width, width, axis) for place in places],
        axis=axis,
    )


def flip_blocks(values, axis, count):
    width = values.shape[axis] // count
    return jnp.concatenate(
        [lax.slice_in_dim(values, (p ^ 1) * width, ((p ^ 1) + 1) * width, axis=axis) for p in range(count)],
        axis=axis,
    )


def place(dp_flip, tensor_flip):
    return (lax.axis_index("dp") ^ dp_flip, lax.axis_index("tensor") ^ tensor_flip)


def greet(places):
    barrier = pltpu.get_barrier_semaphore()
    for there in places:
        pl.semaphore_signal(barrier, inc=1, device_id=there, device_id_type=MESH)
    pl.semaphore_wait(barrier, len(places))


def send_to(there, source, target, send_sem, recv_sem):
    return pltpu.make_async_remote_copy(
        src_ref=source,
        dst_ref=target,
        send_sem=send_sem,
        recv_sem=recv_sem,
        device_id=there,
        device_id_type=MESH,
    )


def group_places(half):
    return [place(2 * j, 0) for j in range(1, half)] + [place(1, 0), place(0, 2), place(0, 1)]


def forward(half, by_columns, *refs):
    def take(count):
        nonlocal refs
        head, refs = refs[:count], refs[count:]
        return head

    project_pair, gate_up_pair, down_pair, output_pair = take(4)
    gains_own, unit_rows, cot_own, cot_flipped, tables, bias = take(6)
    w_project, w_gate_up, w_down, w_output, gains = take(5)
    normed, cot, normed_t, packed, hidden, attended, turned, hidden_t, attended_t = take(9)
    stage = take(2)
    normed_own, normed_flipped = take(2)
    z_send, z_recv, x_send, x_recv, a_send, a_recv = refs
    greet(group_places(half))

    spots, seqs, piece, _ = cot.shape
    units, heads = hidden.shape[-1], attended.shape[-1]
    each = D // (2 * half)
    rows_all = spots * seqs * piece
    every = lambda ref: pl.BlockSpec(ref.shape, lambda *g: (0,) * len(ref.shape))

    def row_chunk(out, mine, other, share=0, shares=1):
        size = mine.shape[0] // shares
        rows = pl.ds(share * size, size)
        return mine.at[rows], other.at[rows], lambda p: out.at[pl.ds(p * mine.shape[0] + share * size, size)]

    def column_chunk(out, mine, other, share=0, shares=1):
        size = mine.shape[0] // shares
        rows, width = pl.ds(share * size, size), mine.shape[1]
        return mine.at[rows], other.at[rows], lambda p: out.at[rows, pl.ds(p * width, width)]

    out_chunk = column_chunk if by_columns else row_chunk
    pair = lambda ref: (ref.at[0], ref.at[1])
    chunks = [
        row_chunk(gains, gains_own, gains_own),
        row_chunk(w_project, *pair(project_pair)),
        row_chunk(w_gate_up, *pair(gate_up_pair), 0, 2),
        row_chunk(w_gate_up, *pair(gate_up_pair), 1, 2),
        out_chunk(w_down, *pair(down_pair), 0, 2),
        out_chunk(w_output, *pair(output_pair)),
        out_chunk(w_down, *pair(down_pair), 1, 2),
    ]
    GAINS, PROJECT, GATE_UP, DOWN, OUTPUT = 0, 1, 2, 4, 5
    n = len(chunks)
    far = range(1, half)

    def z_copy(c, j):
        mine, other, block = chunks[c]
        return send_to(place(2 * j, 0), other if j % 2 else mine, block(j), z_send.at[c, j], z_recv.at[c, j])

    def x_copy(c, j):
        mine, _, block = chunks[c]
        return send_to(place(1, 0), block(j) if j else mine, block(half + j), x_send.at[c, j], x_recv.at[c, j])

    def start_z(c):
        if c < n:
            for j in far:
                z_copy(c, j).start()

    def start_own(c):
        if c < n:
            x_copy(c, 0).start()

    def keep(sources, outs, blocks, steps):
        def body(*refs):
            for ref, out_ref in zip(refs, refs[len(sources) :]):
                put(out_ref, ref[...])

        pltpu.emit_pipeline(
            body, grid=(steps,), in_specs=[block[0] for block in blocks], out_specs=[block[1] for block in blocks]
        )(*sources, *outs)

    def keep_weights():
        pairs = (project_pair, gate_up_pair, down_pair, output_pair)
        sizes = [(ref.shape[1] // 2, ref.shape[2]) for ref in pairs]
        blocks = [(blocked((1,) + size, 0, step(), 0), blocked(size, step(), 0)) for size in sizes]
        keep(pairs, (w_project, w_gate_up, w_down, w_output), blocks, 2)

    def keep_cot():
        lead = blocked((1, piece, D), step(), 0, 0)
        keep((cot_own,), (cot,), [(lead, blocked((1, 1, piece, D), 0, step(), 0, 0))], seqs // 2)

    def serve(c):
        for j in far:
            z_copy(c, j).wait_recv()
            x_copy(c, j).start()
            if c + 1 < n and c != GAINS:
                z_copy(c + 1, j).start()
        if c > GAINS:
            start_own(c + 2)

    def have(*which):
        for c in which:
            for j in range(half):
                x_copy(c, j).wait_recv()

    act_own, act_flipped, act_out = (normed_own, cot_own), (normed_flipped, cot_flipped), (normed, cot)

    def rows(a, index):
        micro = seqs // 2
        return act_out[a].at[index // 2, pl.ds((index % 2) * micro, micro)]

    def a_copy(a, k):
        source = (act_flipped[a], act_own[a], rows(a, 1), act_own[a], rows(a, 1), rows(a, 2), rows(a, 3))[k]
        there = place(2, 0) if k == 0 else place(0, 2) if k < 3 else place(0, 1)
        return send_to(there, source, rows(a, k + 1), a_send.at[a, k], a_recv.at[a, k])

    def act_begin(a):
        for k in (0, 1, 3):
            a_copy(a, k).start()

    def act_z(a):
        a_copy(a, 0).wait_recv()
        a_copy(a, 2).start()
        a_copy(a, 4).start()

    def act_y(a):
        a_copy(a, 1).wait_recv()
        a_copy(a, 5).start()
        a_copy(a, 2).wait_recv()
        a_copy(a, 6).start()

    def act_have(a):
        for k in range(3, 7):
            a_copy(a, k).wait_recv()

    def norm_step():
        def body(unit_ref, gains_ref, out_ref, flipped_ref, kept_ref):
            gain, shift = [
                jnp.concatenate([gains_ref[p * 8 + k : p * 8 + k + 1] for p in range(2 * half)], axis=1)
                for k in range(2)
            ]
            value = unit_ref[0] * gain + shift
            put(out_ref, value)
            put(flipped_ref, flip_lanes(value, each))
            put(kept_ref, value)

        block = blocked((1, piece, D), step(), 0, 0)
        kept = blocked((1, 1, piece, D), 0, step(), 0, 0)
        pltpu.emit_pipeline(
            body, grid=(seqs // 2,), in_specs=[block, every(gains)], out_specs=[block, block, kept]
        )(unit_rows, gains, normed_own, normed_flipped, normed)

    def attention_step(first, count):
        block = lambda width: blocked((spots, 1, piece, width), 0, step(first), 0, 0)

        def body(normed_ref, weight_ref, tables_ref, bias_ref, turned_ref, attended_ref):
            projected = dot_plain(flat(normed_ref), weight_ref[...])
            attention_fore(projected, tables_ref, bias_ref, turned_ref, attended_ref)

        pltpu.emit_pipeline(
            body,
            grid=(count,),
            in_specs=[block(D), every(w_project), every(tables), every(bias)],
            out_specs=[block(3 * heads), block(heads)],
        )(normed, w_project, tables, bias, turned, attended)

    def turn_over(source, out, in_block, out_block, steps):
        def body(ref, out_ref):
            put(out_ref, flat(ref).T)

        pltpu.emit_pipeline(body, grid=(steps,), in_specs=[in_block], out_specs=[out_block])(source, out)

    def units_step(first, count):
        tile = lambda width: blocked((1, seqs, piece, width), step(first), 0, 0, 0)

        def body(normed_ref, weight_ref, packed_ref, hidden_ref):
            value, units_value = units_fore(flat(normed_ref), weight_ref[...])
            put(packed_ref, value)
            put(hidden_ref, units_value)

        pltpu.emit_pipeline(
            body,
            grid=(count,),
            in_specs=[tile(D), every(w_gate_up)],
            out_specs=[tile(2 * units), tile(units)],
        )(normed, w_gate_up, packed, hidden)

    def grads_step():
        groups, wide = stage[0].shape[0], D // (2 * stage[0].shape[0])

        def body(cot_ref, attended_ref, hidden_ref, *out_refs):
            block = flat(cot_ref)
            for ref, out_ref in zip((attended_ref, hidden_ref), out_refs):
                value = dot_plain(ref[...], block)
                put(out_ref, value if by_columns else value.T)

        pltpu.emit_pipeline(
            body,
            grid=(groups,),
            in_specs=[
                blocked((spots, seqs, piece, wide), 0, 0, 0, step(groups)),
                every(attended_t),
                every(hidden_t),
            ],
            out_specs=[blocked((1,) + ref.shape[1:], step(), 0, 0) for ref in stage],
        )(cot, attended_t, hidden_t, *stage)

    start_z(GAINS)
    start_z(PROJECT)
    for c in (GAINS, PROJECT, GATE_UP):
        start_own(c)
    keep((gains_own,), (gains,), [(every(gains_own), blocked(gains_own.shape, 0, 0))], 1)
    serve(GAINS)
    have(GAINS)
    norm_step()
    act_begin(0)
    keep_weights()
    keep_cot()
    serve(PROJECT)
    act_z(0)
    act_y(0)
    act_begin(1)
    act_have(0)
    have(PROJECT)
    serve(GATE_UP)
    attention_step(0, seqs)
    act_z(1)
    turn_over(attended, attended_t, every(attended), every(attended_t), 1)
    serve(GATE_UP + 1)
    columns = lambda index: blocked((spots, seqs, piece, 256), 0, 0, 0, index)
    turn_over(normed, normed_t, columns(step()), blocked((256, rows_all), step(), 0), D // 256)
    act_y(1)
    serve(DOWN)
    have(GATE_UP, GATE_UP + 1)
    units_step(0, spots // 2)
    serve(OUTPUT)
    units_step(spots // 2, spots - spots // 2)
    turn_over(hidden, hidden_t, every(hidden), every(hidden_t), 1)
    act_have(1)
    serve(n - 1)
    grads_step()
    have(DOWN, OUTPUT, n - 1)
    for c in range(n):
        for j in range(half):
            if j:
                z_copy(c, j).wait_send()
            x_copy(c, j).wait_send()
    for a in range(2):
        for k in range(7):
            a_copy(a, k).wait_send()


def run_forward(half, by_columns, pairs, gains, unit_rows, cot, cot_flipped, tables, bias, group):
    low, full = jnp.bfloat16, jnp.float32
    each, heads, units = pairs[0].shape[1], pairs[0].shape[2] // 3, pairs[1].shape[2] // 2
    spots, seqs, piece = group
    rows_all = spots * seqs * piece
    groups = min(half, 4)
    wide = D // (2 * groups)
    widths = (heads, units)
    flat_stage = [(groups, w, wide) if by_columns else (groups, wide, w) for w in widths]
    across = [(w, D) if by_columns else (D, w) for w in (units, heads)]
    shapes = [
        ((D, 3 * heads), low),
        ((D, 2 * units), low),
        *[(shape, low) for shape in across],
        ((2 * half * 8, each), full),
        (group + (D,), low),
        (group + (D,), low),
        ((D, rows_all), low),
        (group + (2 * units,), full),
        (group + (units,), low),
        (group + (heads,), low),
        (group + (3 * heads,), low),
        ((units, rows_all), low),
        ((heads, rows_all), low),
        *[(shape, low) for shape in flat_stage],
        (cot.shape, low),
        (cot.shape, low),
    ]
    ins = [*pairs, gains, unit_rows, cot, cot_flipped, tables, bias]
    anywhere = pl.BlockSpec(memory_space=pl.ANY)
    sem = pltpu.SemaphoreType.DMA
    return pl.pallas_call(
        functools.partial(forward, half, by_columns),
        out_shape=[jax.ShapeDtypeStruct(*shape) for shape in shapes],
        in_specs=[anywhere] * len(ins),
        out_specs=[anywhere] * len(shapes),
        scratch_shapes=[sem((7, half))] * 4 + [sem((2, 7))] * 2,
        compiler_params=pltpu.CompilerParams(
            collective_id=0, has_side_effects=True, vmem_limit_bytes=56 * 1024 * 1024
        ),
        name="forward",
    )(*ins)


def prepare(each, in_place, *refs):
    tokens, cot, project, gate_up, down, output = refs[:6]
    tok_ref, unit_ref, cot_ref, cot_flipped_ref, project_ref, gate_up_ref, down_ref, output_ref = refs[6:]
    me = lax.axis_index("dp")
    side = (me // 2) % 2
    blocks = block_order(D // each)
    if in_place:
        for p, r in enumerate(blocks):
            span, flipped = slice(p * each, (p + 1) * each), slice((p ^ 1) * each, ((p ^ 1) + 1) * each)
            there = pl.ds(pl.multiple_of((me ^ r) * each, each), each)
            tok_ref[:, :, span] = tokens[:, :, there]
            cot_ref[:, :, span] = cot[:, :, there]
            cot_flipped_ref[:, :, flipped] = cot[:, :, there]
    else:
        tok_ref[...] = tokens[...]
        cot_ref[...] = cot[...]
        for s in range(cot.shape[0]):
            put(cot_flipped_ref.at[s], flip_lanes(cot[s].astype(jnp.float32), each))
    for s in range(tokens.shape[0]):
        unit_ref[s], _ = norm_rows(tok_ref[s].astype(jnp.float32))
    heads, units = output.shape[0] // 2, down.shape[0] // 2
    whole = units - 64
    for h, s in enumerate((side, 1 - side)):
        part = lambda width, start=0: pl.ds(start + pl.multiple_of(s * width, width), width)
        for k in range(3):
            put(project_ref.at[h, :, pl.ds(k * heads, heads)], project[k, :, part(heads)])
        for k in range(2):
            put(gate_up_ref.at[h, :, pl.ds(k * whole, whole)], gate_up[k, :, part(whole)])
        put(output_ref.at[h], output[part(heads)])
        put(down_ref.at[h, pl.ds(0, whole)], down[part(whole)])
        put(down_ref.at[h, pl.ds(whole, 64)], down[part(64, 2 * whole)])
    gate, up = gate_up[0, :, 2 * whole :], gate_up[1, :, 2 * whole :]
    first = lax.broadcasted_iota(jnp.int32, gate.shape, 1) < 64
    zero = jnp.where(first, gate, pltpu.roll(up, 64, 1))
    one = jnp.where(first, pltpu.roll(gate, 64, 1), up)
    put(gate_up_ref.at[0, :, pl.ds(2 * whole, 128)], jnp.where(side == 0, zero, one))
    put(gate_up_ref.at[1, :, pl.ds(2 * whole, 128)], jnp.where(side == 0, one, zero))


def whole_spec(shape):
    return pl.BlockSpec(shape, lambda *_: (0,) * len(shape))


def run_prepare(tokens, cot, weights):
    project, gate_up, down, output = weights
    each = project.shape[1]
    in_place = each % 128 == 0
    if not in_place:
        me, count = lax.axis_index("dp"), D // each
        tokens, cot = relative(tokens, 2, me, count), relative(cot, 2, me, count)
    low = jnp.bfloat16
    heads, units = output.shape[0] // 2, down.shape[0] // 2
    shapes = [(tokens.shape, low), (tokens.shape, jnp.float32), (cot.shape, low), (cot.shape, low)]
    shapes += [((2, each, 3 * heads), low), ((2, each, 2 * units), low)]
    shapes += [((2, units, each), low), ((2, heads, each), low)]
    ins = [tokens, cot, project, gate_up, down, output]
    return pl.pallas_call(
        functools.partial(prepare, each, in_place),
        grid=(1,),
        in_specs=[whole_spec(value.shape) for value in ins],
        out_specs=[whole_spec(shape) for shape, _ in shapes],
        out_shape=[jax.ShapeDtypeStruct(*shape) for shape in shapes],
        compiler_params=pltpu.CompilerParams(vmem_limit_bytes=60 * 1024 * 1024),
        name="prepare",
    )(*ins)


def flat(ref):
    value = ref[...]
    return value.reshape(-1, value.shape[-1])


def put(ref, value):
    ref[...] = value.astype(ref.dtype).reshape(ref.shape)


def blocked(shape, *index):
    return pl.BlockSpec(shape, lambda g: tuple(i(g) if callable(i) else i for i in index))


def step(offset=0):
    return lambda g: g + offset


def backward(half, by_columns, window, *refs):
    def take(count):
        nonlocal refs
        head, refs = refs[:count], refs[count:]
        return head

    cot, packed, hidden, attended, turned = take(5)
    normed_t, attended_t_all, hidden_t_all = take(3)
    w_project, w_gate_up, w_down, w_output, tables, bias = take(6)
    stage_out = take(2)
    z_in, mine = take(4), take(4)
    act_away, act_near, core_in, y_out, y_in, far_out = [take(2) for _ in range(6)]
    act_far, act_sum = take(1), take(2)
    stage, x_in = stage_out + take(2), take(4)
    d_packed, d_att, d_project, attended_t, hidden_t, normed_block, cot_block = take(7)
    x_send, x_recv, z_send, z_recv, a_send, a_recv, load_sem, block_sem = refs
    greet(group_places(half))

    spots, seqs, piece, _ = cot.shape
    units, heads = hidden.shape[-1], attended.shape[-1]
    groups = stage[0].shape[0]
    per = half // groups
    wide = D // (2 * groups)
    every = lambda ref: pl.BlockSpec(ref.shape, lambda g: (0,) * len(ref.shape))

    whole = (attended_t, hidden_t, d_packed, d_project)

    def product(c, block, whole_ref):
        if c >= 2:
            return dot_plain(block, flat(whole_ref))
        value = dot_plain(whole_ref[...], block)
        return value if by_columns else value.T

    def block_copy(index):
        c, g = order[index]
        span, slot = pl.ds(g * wide, wide), index % 2
        if c >= 2:
            source, target = normed_t.at[span], normed_block.at[slot]
        else:
            source, target = cot.at[:, :, :, span], cot_block.at[slot]
        return pltpu.make_async_copy(source, target, block_sem.at[slot])

    def x_copy(c, g):
        return send_to(place(1, 0), stage[c].at[g], x_in[c].at[g], x_send.at[c, g], x_recv.at[c, g])

    def z_copy(c, j):
        source = x_in[c].at[j // per]
        if per > 1:
            rows = z_in[c].shape[1]
            source = source.at[pl.ds((j % per) * rows, rows)]
        return send_to(place(2 * j, 0), source, z_in[c].at[j], z_send.at[c, j], z_recv.at[c, j])

    def a_copy(a, s):
        source = (act_away[a], y_out[a], far_out[a])[s]
        target = (core_in[a], y_in[a], act_far[0])[s]
        there = (place(0, 1), place(0, 2), place(2, 0))[s]
        return send_to(there, source, target, a_send.at[a, s], a_recv.at[a, s])

    order = [(0, 3), (0, 2), (1, 3), (1, 2), (1, 1), (0, 1)]
    order += [(c, g) for c in (2, 3) for g in (3, 2, 1)] + [(c, 0) for c in (2, 1, 3, 0)]
    started, served, ready = [0], [0], {0, 1}

    def start_x():
        while started[0] < min(served[0] + window, len(order)) and order[started[0]][0] in ready:
            x_copy(*order[started[0]]).start()
            started[0] += 1

    def away_product(c):
        def body(block_ref, whole_ref, out_ref):
            put(out_ref, product(c, block_ref[...], whole_ref))

        pltpu.emit_pipeline(
            body,
            grid=(groups,),
            in_specs=[blocked((wide, normed_t.shape[1]), step(groups), 0), every(whole[c])],
            out_specs=[blocked((1,) + stage[c].shape[1:], step(), 0, 0)],
        )(normed_t, whole[c], stage[c])
        ready.add(c)
        start_x()

    def serve(count):
        for _ in range(count):
            index = served[0]
            c, g = order[index]
            served[0] += 1
            block_copy(index).wait()
            if served[0] < len(order):
                block_copy(served[0]).start()
            x_copy(c, g).wait_recv()
            start_x()
            block = flat((normed_block if c >= 2 else cot_block).at[index % 2])
            total = product(c, block, whole[c]) + x_in[c][g].astype(jnp.float32)
            if g == 0:
                mine[c][0] = total
            if g > 0 or per > 1:
                put(x_in[c].at[g], total)
            for j in range(g * per, (g + 1) * per):
                if j:
                    z_copy(c, j).start()

    def units_step(first, count):
        tile = (1, seqs, piece)

        def body(cot_ref, down_ref, output_ref, packed_ref, d_packed_ref, d_att_ref):
            rows = flat(cot_ref)
            d_packed_ref[...] = units_back(rows, down_ref[...], flat(packed_ref)).reshape(d_packed_ref.shape)
            put(d_att_ref, dot_cols(rows, output_ref[...]))

        pltpu.emit_pipeline(
            body,
            grid=(count,),
            in_specs=[
                blocked(tile + (D,), step(first), 0, 0, 0),
                every(w_down),
                every(w_output),
                blocked(tile + (2 * units,), step(first), 0, 0, 0),
            ],
            out_specs=[
                blocked(tile + (2 * units,), step(first), 0, 0, 0),
                blocked(tile + (heads,), step(first), 0, 0, 0),
            ],
        )(cot, w_down, w_output, packed, d_packed, d_att)

    def attention_step(first, count):
        block = lambda width: blocked((spots, 1, piece, width), 0, step(first), 0, 0)
        pltpu.emit_pipeline(
            attention_back,
            grid=(count,),
            in_specs=[block(3 * heads), block(heads), every(tables), every(bias)],
            out_specs=[block(3 * heads)],
        )(turned, d_att, tables, bias, d_project)

    def two_cores(away_ref, near_ref, total):
        middle = total.shape[0] // 2
        put(near_ref, total[:middle])
        put(away_ref, total[middle:])

    def core_block(first):
        return blocked((spots // 2, seqs, piece, 256), 0, 0, 0, step(first))

    def normed_step():
        def body(d_project_ref, d_packed_ref, project_ref, gate_up_ref, away_ref, near_ref):
            total = dot_cols(flat(d_project_ref), project_ref[...])
            two_cores(away_ref, near_ref, total + dot_cols(flat(d_packed_ref), gate_up_ref[...]))

        pltpu.emit_pipeline(
            body,
            grid=(D // 256,),
            in_specs=[
                every(d_project),
                every(d_packed),
                blocked((256, 3 * heads), step(), 0),
                blocked((256, 2 * units), step(), 0),
            ],
            out_specs=[core_block(0)] * 2,
        )(d_project, d_packed, w_project, w_gate_up, act_away[0], act_near[0])

    def out_step(first, count):
        def body(attended_ref, hidden_ref, output_ref, down_ref, away_ref, near_ref):
            total = dot_plain(flat(attended_ref), output_ref[...])
            two_cores(away_ref, near_ref, total + dot_plain(flat(hidden_ref), down_ref[...]))

        pltpu.emit_pipeline(
            body,
            grid=(count,),
            in_specs=[
                every(attended),
                every(hidden),
                blocked((heads, 256), 0, step(first)),
                blocked((units, 256), 0, step(first)),
            ],
            out_specs=[core_block(first)] * 2,
        )(attended, hidden, w_output, w_down, act_away[1], act_near[1])

    def add_terms(*refs):
        *terms, out_ref = refs
        put(out_ref, sum(flat(term).astype(jnp.float32) for term in terms))

    half_seqs = seqs // 2

    def core_arrived(a):
        a_copy(a, 0).wait_recv()
        rows = blocked((1, half_seqs, piece, D), 1, step(), 0, 0)
        pltpu.emit_pipeline(
            add_terms,
            grid=(2,),
            in_specs=[rows, rows],
            out_specs=[blocked((half_seqs, piece, D), step(), 0, 0)],
        )(act_near[a], core_in[a], y_out[a])
        a_copy(a, 1).start()

    def y_arrived(a):
        def body(*refs):
            add_terms(*refs[:3], refs[6])
            add_terms(*refs[3:6], refs[7])

        def both(shape, *lead):
            return [blocked(shape, *lead, step(first), 0, 0) for first in (half_seqs, 0)]

        rows, lines = both((1, 1, piece, D), 0), both((1, piece, D))
        a_copy(a, 1).wait_recv()
        pltpu.emit_pipeline(
            body,
            grid=(half_seqs,),
            in_specs=[rows[0], rows[0], lines[0], rows[1], rows[1], lines[1]],
            out_specs=[blocked((1, piece, D), step(), 0, 0)] * 2,
        )(*[act_near[a], core_in[a], y_in[a]] * 2, far_out[a], act_sum[a])
        if a == 0:
            a_copy(a, 2).start()

    loads = [
        pltpu.make_async_copy(attended_t_all, attended_t, load_sem.at[0]),
        pltpu.make_async_copy(hidden_t_all, hidden_t, load_sem.at[1]),
    ]
    for load in loads:
        load.start()
    block_copy(0).start()
    start_x()
    for load in loads:
        load.wait()
    steps = D // 256
    units_step(0, spots)
    serve(2)
    away_product(2)
    serve(2)
    attention_step(0, seqs // 2)
    serve(1)
    attention_step(seqs // 2, seqs - seqs // 2)
    away_product(3)
    serve(1)
    normed_step()
    a_copy(0, 0).start()
    serve(1)
    out_step(0, steps // 2)
    core_arrived(0)
    serve(1)
    out_step(steps // 2, steps - steps // 2)
    a_copy(1, 0).start()
    serve(2)
    core_arrived(1)
    y_arrived(0)
    serve(len(order) - served[0])
    y_arrived(1)
    for c in range(4):
        for j in range(1, half):
            z_copy(c, j).wait()
        for g in range(groups):
            x_copy(c, g).wait_send()
    for a in range(2):
        for s in range(2):
            a_copy(a, s).wait_send()
    a_copy(0, 2).wait()


def run_backward(half, by_columns, rows, transposed, weights, tables, bias, stage, window=3):
    cot, packed, hidden, attended, turned = rows
    low, full = jnp.bfloat16, jnp.float32
    spots, seqs, piece, _ = cot.shape
    each = D // (2 * half)
    groups = min(half, 4)
    wide = D // (2 * groups)
    widths = (attended.shape[-1], hidden.shape[-1], packed.shape[-1], turned.shape[-1])
    columns = [by_columns and groups == half and c < 2 for c in range(4)]

    def shape_of(count, block):
        return [(count, w, block) if flip else (count, block, w) for w, flip in zip(widths, columns)]

    def row_shape(*lead, kind=low):
        return [jax.ShapeDtypeStruct(lead + (piece, D), kind)] * 2

    shapes = [jax.ShapeDtypeStruct(shape, low) for shape in shape_of(half, each)]
    shapes += [jax.ShapeDtypeStruct(shape, full) for shape in shape_of(1, wide)]
    shapes += row_shape(spots // 2, seqs) * 3 + row_shape(seqs) * 2 + row_shape(seqs // 2)
    shapes += row_shape(seqs // 2)[:1] + row_shape(seqs // 2, kind=full)
    anywhere = pl.BlockSpec(memory_space=pl.ANY)
    vmem = pl.BlockSpec(memory_space=pltpu.VMEM)
    ins = [*rows, *transposed, *weights, tables, bias, *stage]
    sem = pltpu.SemaphoreType.DMA
    rows_all = spots * seqs * piece
    scratch = [pltpu.VMEM(shape, low) for shape in shape_of(groups, wide)[2:] + shape_of(groups, wide)]
    scratch += [pltpu.VMEM(r.shape, low) for r in (packed, attended, turned)]
    scratch += [pltpu.VMEM(t.shape, low) for t in transposed[1:]]
    scratch += [pltpu.VMEM((2, wide, rows_all), low), pltpu.VMEM((2, spots, seqs, piece, wide), low)]
    scratch += [sem((4, groups))] * 2 + [sem((4, half))] * 2 + [sem((2, 3))] * 2 + [sem((2,))] * 2
    outs = pl.pallas_call(
        functools.partial(backward, half, columns[0], window),
        out_shape=shapes,
        in_specs=[anywhere] * len(ins),
        out_specs=[anywhere] * 4 + [vmem] * 4 + [anywhere] * (len(shapes) - 8),
        scratch_shapes=scratch,
        compiler_params=pltpu.CompilerParams(
            collective_id=1, has_side_effects=True, vmem_limit_bytes=60 * 1024 * 1024
        ),
        name="backward",
    )(*ins)
    pairs = []
    for c in range(4):
        own = outs[4 + c][0] if columns[c] else outs[4 + c][0, :each]
        pairs.append((own, outs[c]))
    *_, out_far, normed_far, normed_sum, out_sum = outs
    dp_size, tensor_size = lax.axis_size("dp"), lax.axis_size("tensor")
    partners = [
        (d * tensor_size + t, (d ^ 2) * tensor_size + t) for d in range(dp_size) for t in range(tensor_size)
    ]
    out_far = lax.ppermute(out_far, ("dp", "tensor"), partners)
    return pairs, (normed_far, normed_sum), (out_far, out_sum)


def flip_lanes(values, width):
    lanes = values.shape[1]
    if width % 128 == 0:
        spans = [slice((p ^ 1) * width, ((p ^ 1) + 1) * width) for p in range(lanes // width)]
        return jnp.concatenate([values[:, span] for span in spans], axis=1)
    even = (lax.broadcasted_iota(jnp.int32, values.shape, 1) // width) % 2 == 0
    return jnp.where(even, pltpu.roll(values, lanes - width, 1), pltpu.roll(values, width, 1))


def norm_rows(tok_rows):
    centered = tok_rows - jnp.mean(tok_rows, axis=1, keepdims=True)
    row_scale = lax.rsqrt(jnp.mean(centered * centered, axis=1, keepdims=True) + NORM_EPS)
    return centered * row_scale, row_scale


def put_rows(ref, value, each, in_place):
    value = value.astype(jnp.bfloat16)
    if not in_place:
        ref[0] = value
        return
    me = lax.axis_index("dp")
    for p, r in enumerate(block_order(D // each)):
        span = pl.ds(pl.multiple_of((me ^ r) * each, each), each)
        ref[0, :, span] = value[:, p * each : (p + 1) * each]


def finish_out(each, in_place, far_ref, sum_ref, tok_ref, out_ref):
    summed = flat(sum_ref) + flip_lanes(flat(far_ref).astype(jnp.float32), each)
    put_rows(out_ref, flat(tok_ref).astype(jnp.float32) + summed, each, in_place)


def finish_rows(each, in_place, far_ref, sum_ref, tok_ref, cot_ref, gain_ref, input_ref, grad_ref):
    d_normed = flat(sum_ref) + flip_lanes(flat(far_ref).astype(jnp.float32), each)
    unit_rows, row_scale = norm_rows(flat(tok_ref).astype(jnp.float32))
    d_unit = d_normed * gain_ref[0:1]
    d_input = row_scale * (
        d_unit
        - jnp.mean(d_unit, axis=1, keepdims=True)
        - unit_rows * jnp.mean(d_unit * unit_rows, axis=1, keepdims=True)
    )
    put_rows(input_ref, flat(cot_ref).astype(jnp.float32) + d_input, each, in_place)
    share = jnp.concatenate(
        [
            jnp.sum(d_normed * unit_rows, axis=0, keepdims=True),
            jnp.sum(d_normed, axis=0, keepdims=True),
            jnp.zeros((6, D), jnp.float32),
        ],
        axis=0,
    )

    @pl.when(pl.program_id(0) == 0)
    def _():
        grad_ref[...] = share

    @pl.when(pl.program_id(0) > 0)
    def _():
        grad_ref[...] = grad_ref[...] + share


def run_finish(kernel, each, rows, fixed_in, fixed_out):
    in_place = each % 128 == 0
    count, piece, _ = rows[-1].shape
    block = pl.BlockSpec((1, piece, D), lambda s: (s, 0, 0))
    fixed = pl.BlockSpec((8, D), lambda s: (0, 0))
    done, *others = pl.pallas_call(
        functools.partial(kernel, each, in_place),
        grid=(count,),
        in_specs=[block] * len(rows) + [fixed] * len(fixed_in),
        out_specs=[block] + [fixed] * fixed_out,
        out_shape=[jax.ShapeDtypeStruct(rows[-1].shape, jnp.bfloat16)]
        + [jax.ShapeDtypeStruct((8, D), jnp.float32)] * fixed_out,
        compiler_params=KERNEL_PARAMS,
        name=kernel.__name__,
    )(*rows, *fixed_in)
    if not in_place:
        done = from_relative(done, 2, lax.axis_index("dp"), D // each)
    return done, *others


def join_grads(half, spans, *refs):
    own, came = refs[0:8:2], refs[1:8:2]
    output_ref, down_ref, gate_up_ref, project_ref, square_ref = refs[8:]
    side = (lax.axis_index("dp") // 2) % 2
    heads, whole = spans
    squares = jnp.float32(0.0)

    def halves(c, rows, columns):
        nonlocal squares
        pick = lambda j: came[c][j, rows, columns].astype(jnp.float32)
        mine = own[c][rows, columns] + sum(pick(j) for j in range(2, half, 2))
        other = sum(pick(j) for j in range(1, half, 2))
        squares = squares + jnp.sum(mine * mine) + jnp.sum(other * other)
        return mine, other

    def places(width, start=0):
        return [pl.ds(start + pl.multiple_of(s * width, width), width) for s in (side, 1 - side)]

    every = slice(None)
    for value, span in zip(halves(0, every, every), places(heads)):
        output_ref[span] = value
    for value, span in zip(halves(1, slice(0, whole), every), places(whole)):
        down_ref[span] = value
    for value, span in zip(halves(1, slice(whole, whole + 64), every), places(64, 2 * whole)):
        down_ref[span] = value
    for k in range(3):
        for value, span in zip(halves(3, every, slice(k * heads, (k + 1) * heads)), places(heads)):
            project_ref[k, :, span] = value
    for k in range(2):
        for value, span in zip(halves(2, every, slice(k * whole, (k + 1) * whole)), places(whole)):
            gate_up_ref[k, :, span] = value
    mine, other = halves(2, every, slice(2 * whole, 2 * whole + 128))
    zero, one = jnp.where(side == 0, mine, other), jnp.where(side == 0, other, mine)
    first = lax.broadcasted_iota(jnp.int32, zero.shape, 1) < 64
    gate_up_ref[0, :, 2 * whole :] = jnp.where(first, zero, pltpu.roll(one, 64, 1))
    gate_up_ref[1, :, 2 * whole :] = jnp.where(first, pltpu.roll(zero, 64, 1), one)
    square_ref[...] = jnp.full(square_ref.shape, squares)


def run_join_grads(half, pairs, shapes, spans):
    ins = [part for pair in pairs for part in pair]
    shapes = shapes + [(8, 128)]
    return pl.pallas_call(
        functools.partial(join_grads, half, spans),
        grid=(1,),
        in_specs=[whole_spec(value.shape) for value in ins],
        out_specs=[whole_spec(shape) for shape in shapes],
        out_shape=[jax.ShapeDtypeStruct(shape, jnp.float32) for shape in shapes],
        compiler_params=pltpu.CompilerParams(vmem_limit_bytes=56 * 1024 * 1024),
        name="join_grads",
    )(*ins)


def sum_kernel(rounds, half, in_ref, out_ref, total_ref, sent, came, send_sem, recv_sem):
    places = [place(*flips) for flips in rounds]
    greet(places)
    count = in_ref.shape[0]
    out_ref[...] = in_ref[...]
    for k, (dp_flip, _) in enumerate(rounds):
        sent[k] = out_ref[...]
        copy = send_to(places[k], sent.at[k], came.at[k], send_sem.at[k], recv_sem.at[k])
        copy.start()
        copy.wait()
        move = (dp_flip % 2) * half + dp_flip // 2
        for p in range(count):
            out_ref[p] = out_ref[p] + came[k, p ^ move]
    rows, lanes = in_ref.shape[1:]
    me = lax.axis_index("dp")
    used = lax.broadcasted_iota(jnp.int32, (rows, lanes), 0) < rows - 1
    total = out_ref[0, rows - 1 :, :]
    for g in range(count):
        there = me ^ g
        value = out_ref[(there % 2) * half + there // 2]
        total = total + jnp.sum(jnp.where(used, value * value, 0.0))
    total_ref[...] = jnp.broadcast_to(total, total_ref.shape)


def sum_everywhere(shares, square):
    dp_size = lax.axis_size("dp")
    rounds = []
    for axis, size in enumerate((dp_size, lax.axis_size("tensor"))):
        flip = 1
        while flip < size:
            rounds.append((0, flip) if axis else (flip, 0))
            flip *= 2
    each = D // dp_size
    lanes = 128 if each % 128 == 0 else each
    used = 2 * each // lanes
    parts = shares.reshape(2, dp_size, each // lanes, lanes).transpose(1, 0, 2, 3).reshape(dp_size, used, lanes)
    filler = jnp.zeros((dp_size, 7 - used, lanes), jnp.float32)
    last = jnp.broadcast_to(square, (dp_size, 1, lanes))
    parts = jnp.concatenate([parts, filler, last], axis=1)
    vmem = pl.BlockSpec(memory_space=pltpu.VMEM)
    sem = pltpu.SemaphoreType.DMA
    summed, total = pl.pallas_call(
        functools.partial(sum_kernel, rounds, dp_size // 2),
        out_shape=[jax.ShapeDtypeStruct(shape, jnp.float32) for shape in (parts.shape, (8, lanes))],
        in_specs=[vmem],
        out_specs=[vmem, vmem],
        scratch_shapes=[pltpu.VMEM((len(rounds),) + parts.shape, jnp.float32)] * 2 + [sem((len(rounds),))] * 2,
        compiler_params=pltpu.CompilerParams(collective_id=2, has_side_effects=True),
        name="sum_everywhere",
    )(parts)
    return summed[0, :used].reshape(2, each), total[0, 0]


def dot_plain(a, b):
    return lax.dot_general(a, b, (((1,), (0,)), ((), ())), preferred_element_type=jnp.float32)


def dot_rows(a, b):
    return lax.dot_general(a, b, (((0,), (0,)), ((), ())), preferred_element_type=jnp.float32)


def dot_cols(a, b):
    return lax.dot_general(a, b, (((1,), (1,)), ((), ())), preferred_element_type=jnp.float32)


def turn(values, tables, direction):
    cosine, low_sine, high_sine = tables
    lanes = values.shape[1]
    half_rot = ROT // 2
    moved = pltpu.roll(values, lanes - half_rot, 1) * low_sine + pltpu.roll(values, half_rot, 1) * high_sine
    return values * cosine + direction * moved


def head_probabilities(query, key, bias):
    scores = dot_cols(query, key) * 0.125 + bias
    exponent = jnp.exp(scores - jnp.max(scores, axis=1, keepdims=True))
    return exponent / jnp.sum(exponent, axis=1, keepdims=True)


def attention_fore(projected, tables_ref, bias_ref, turned_ref, attended_ref):
    spots, _, piece, width = turned_ref.shape
    rows, third = spots * piece, width // 3
    tables = [tables_ref[k] for k in range(3)]
    first = lax.broadcasted_iota(jnp.int32, (rows, 128), 1) < HEAD_DIM
    for pair in range(third // 128):
        span = [slice(k * third + pair * 128, k * third + pair * 128 + 128) for k in range(3)]
        query, key, value = [projected[:, s] for s in span]
        query = turn(query, tables, 1.0).astype(jnp.bfloat16)
        key = turn(key, tables, 1.0).astype(jnp.bfloat16)
        value = value.astype(jnp.bfloat16)
        for s, part in zip(span, (query, key, value)):
            turned_ref[:, 0, :, s] = part.reshape(spots, piece, 128)
        none = jnp.zeros_like(query)
        outs = [
            dot_plain(head_probabilities(q, key, bias_ref[...]).astype(jnp.bfloat16), value)
            for q in (jnp.where(first, query, none), jnp.where(first, none, query))
        ]
        attended_ref[:, 0, :, span[0]] = (
            jnp.where(first, outs[0], outs[1]).astype(jnp.bfloat16).reshape(spots, piece, 128)
        )


def attention_back(turned_ref, d_att_ref, tables_ref, bias_ref, d_project_ref):
    spots, _, piece, width = turned_ref.shape
    rows, third = spots * piece, width // 3
    tables = [tables_ref[k] for k in range(3)]
    first = lax.broadcasted_iota(jnp.int32, (rows, 128), 1) < HEAD_DIM
    for pair in range(third // 128):
        span = [slice(k * third + pair * 128, k * third + pair * 128 + 128) for k in range(3)]
        query, key, value = [turned_ref[:, 0, :, s].reshape(rows, 128) for s in span]
        d_att = d_att_ref[:, 0, :, span[0]].reshape(rows, 128)
        none = jnp.zeros_like(query)
        parts = []
        for head in range(2):
            keep = first if head == 0 else jnp.logical_not(first)
            one_query = jnp.where(keep, query, none)
            one_d_att = jnp.where(keep, d_att, none)
            prob = head_probabilities(one_query, key, bias_ref[...])
            d_value = dot_rows(prob.astype(jnp.bfloat16), d_att)
            d_prob = dot_cols(one_d_att, value)
            d_score = (prob * (d_prob - jnp.sum(d_prob * prob, axis=1, keepdims=True))).astype(
                jnp.bfloat16
            )
            parts.append((dot_plain(d_score, key), dot_rows(d_score, query), d_value))
        joined = [jnp.where(first, one, two) for one, two in zip(*parts)]
        done = (turn(0.125 * joined[0], tables, -1.0), turn(0.125 * joined[1], tables, -1.0), joined[2])
        for s, part in zip(span, done):
            d_project_ref[:, 0, :, s] = part.astype(jnp.bfloat16).reshape(spots, piece, 128)


def join_gate_up(packed, whole):
    last = packed[:, 2 * whole :]
    gate = jnp.concatenate([packed[:, :whole], last], axis=1)
    up = jnp.concatenate([packed[:, whole : 2 * whole], pltpu.roll(last, 64, 1)], axis=1)
    return gate, up


def units_fore(normed, weight):
    packed = dot_plain(normed, weight)
    units = weight.shape[1] // 2
    gate, up = join_gate_up(packed, units - 64)
    return packed, (gate * jax.nn.sigmoid(gate) * up).astype(jnp.bfloat16)[:, :units]


def units_back(cot, down, packed):
    units = down.shape[0]
    whole = units - 64
    d_hid = dot_cols(cot, down).astype(jnp.bfloat16).astype(jnp.float32)
    d_hid = jnp.concatenate([d_hid, jnp.zeros((d_hid.shape[0], 64), jnp.float32)], axis=1)
    gate, up = join_gate_up(packed, whole)
    sigmoid_gate = jax.nn.sigmoid(gate)
    d_gate = d_hid * up * (sigmoid_gate * (1.0 + gate * (1.0 - sigmoid_gate)))
    d_up = d_hid * (gate * sigmoid_gate)
    first = lax.broadcasted_iota(jnp.int32, (gate.shape[0], 128), 1) < 64
    last = jnp.where(first, d_gate[:, whole:], pltpu.roll(d_up[:, whole:], 64, 1))
    parts = [d_gate[:, :whole], d_up[:, :whole], last]
    return jnp.concatenate([part.astype(jnp.bfloat16) for part in parts], axis=1)


KERNEL_PARAMS = pltpu.CompilerParams(vmem_limit_bytes=40 * 1024 * 1024)


def adam_update(weight_old, gradient, moment_old, square_old, factor, rate, decay):
    clipped = gradient * factor
    moment_new = BETA_ONE * moment_old + (1.0 - BETA_ONE) * clipped
    square_new = BETA_TWO * square_old + (1.0 - BETA_TWO) * clipped * clipped
    moment_hat = moment_new / (1.0 - BETA_ONE**STEP)
    square_hat = square_new / (1.0 - BETA_TWO**STEP)
    weight_new = weight_old - rate * (
        moment_hat / (jnp.sqrt(square_hat) + ADAM_EPS) + decay * weight_old
    )
    return (weight_new, moment_new, square_new)


def local(
    tokens,
    cotangent,
    project_weight,
    output_weight,
    gate_up_weight,
    down_weight,
    norm_params,
    first_project,
    first_output,
    first_gate_up,
    first_down,
    first_norm,
    second_project,
    second_output,
    second_gate_up,
    second_down,
    second_norm,
):
    count = lax.axis_size("dp")
    blocks_half = count // 2
    me = lax.axis_index("dp")
    side = (me // 2) % 2
    spot = lax.axis_index("tensor")
    spots = lax.axis_size("tensor")
    micro_count, piece = tokens.shape[0], tokens.shape[1]
    head_cols = project_weight.shape[2] // 2
    unit_cols = gate_up_weight.shape[2] // 2
    whole = unit_cols - 64
    rows_each = project_weight.shape[1]
    seqs = 2 * micro_count
    rows_all = spots * seqs * piece

    by_columns = rows_each % 128 == 0

    by_columns = rows_each % 128 == 0

    norm_low = norm_params.astype(jnp.bfloat16)
    tok_rel, unit_rows, cot_low, cot_flipped, *weight_pairs = run_prepare(
        tokens, cotangent, (project_weight, gate_up_weight, down_weight, output_weight)
    )
    if not by_columns:
        weight_pairs[2:] = [pair.swapaxes(1, 2) for pair in weight_pairs[2:]]

    order = [0, 2, 1, 3]
    half_rot = ROT // 2
    angles = np.arange(spots * piece)[:, None] * (10000.0 ** (-2.0 * np.arange(half_rot) / ROT))[None, :]
    cosine, sine = np.cos(angles), np.sin(angles)
    none = np.zeros_like(sine)
    rest = np.zeros((angles.shape[0], HEAD_DIM - ROT))
    in_order = np.stack(
        [
            np.tile(np.concatenate(parts, axis=1), (1, 2))
            for parts in ((cosine, cosine, rest + 1.0), (-sine, none, rest), (none, sine, rest))
        ]
    ).astype(np.float32)
    tables = jnp.concatenate(
        [lax.dynamic_slice_in_dim(jnp.asarray(in_order), (spot ^ k) * piece, piece, 1) for k in order], axis=1
    )
    positions = ((spot ^ jnp.array(order))[:, None] * piece + jnp.arange(piece)[None, :]).reshape(-1)
    bias = jnp.where(positions[:, None] >= positions[None, :], 0.0, MASK_FILL)

    own_gains = jnp.pad(norm_params.astype(jnp.bfloat16).astype(jnp.float32), ((0, 6), (0, 0)))
    (
        w_project,
        w_gate_up,
        w_down,
        w_output,
        gains,
        _,
        all_cot,
        normed_t,
        packed,
        hidden,
        attended,
        turned,
        hidden_t,
        attended_t,
        *stage,
    ) = run_forward(
        blocks_half,
        by_columns,
        weight_pairs,
        own_gains,
        unit_rows,
        cot_low,
        cot_flipped,
        tables,
        bias,
        (spots, seqs, piece),
    )
    gains = gains.reshape(count, 8, rows_each).transpose(1, 0, 2).reshape(8, D)
    if not by_columns:
        w_down, w_output = w_down.T, w_output.T
    pairs, normed_parts, out_parts = run_backward(
        blocks_half,
        by_columns,
        (all_cot, packed, hidden, attended, turned),
        (normed_t, attended_t, hidden_t),
        (w_project, w_gate_up, w_down, w_output),
        tables,
        bias,
        stage[:2],
    )
    if not by_columns:
        pairs[:2] = [(own.T, came.swapaxes(1, 2)) for own, came in pairs[:2]]
    *weight_grads, squares = run_join_grads(
        blocks_half,
        pairs,
        [output_weight.shape, down_weight.shape, gate_up_weight.shape, project_weight.shape],
        (head_cols, whole),
    )
    input_grad, shares = run_finish(finish_rows, rows_each, [*normed_parts, tok_rel, cot_low], [gains], 1)
    norm_grad, square_total = sum_everywhere(shares[:2], squares[0, 0])
    grads = (weight_grads[3], weight_grads[0], weight_grads[2], weight_grads[1], norm_grad)
    norm_total = jnp.sqrt(square_total)
    (layer_out,) = run_finish(finish_out, rows_each, [*out_parts, tok_rel], [], 0)
    limit = 0.03 * math.sqrt((4 * D * D + 3 * D * FF + 2 * D) * micro_count * count * SEQ)
    factor = jnp.minimum(1.0, limit / (norm_total + 1e-06))
    rates = (
        2.0 / math.sqrt(D),
        2.0 / math.sqrt(D // 32),
        2.0 / math.sqrt(D),
        2.0 / math.sqrt(FF),
        0.5,
    )
    decays = (0.1, 0.1, 0.1, 0.1, 0.0)
    masters = (project_weight, output_weight, gate_up_weight, down_weight, norm_params)
    firsts = (first_project, first_output, first_gate_up, first_down, first_norm)
    seconds = (second_project, second_output, second_gate_up, second_down, second_norm)
    updated = [
        adam_update(*parts) for parts in zip(masters, grads, firsts, seconds, [factor] * 5, rates, decays)
    ]
    return (
        layer_out,
        input_grad,
        *grads,
        norm_total,
        *[u[0] for u in updated],
        *[u[1] for u in updated],
        *[u[2] for u in updated],
    )


def solution(mesh):
    wide = P("dp", "tensor", None)
    stacked = P(None, "dp", "tensor")
    tall = P("tensor", "dp")
    params = (stacked, tall, stacked, tall, P(None, "dp"))
    return jax.shard_map(
        local,
        mesh=mesh,
        in_specs=(wide, wide, *params, *params, *params),
        out_specs=(wide, wide, *params, P(), *params, *params, *params),
        check_vma=False,
    )
```

```python
import functools
import math

import jax
import jax.numpy as jnp
import numpy as np
from jax import lax
from jax.experimental import pallas as pl
from jax.experimental.pallas import tpu as pltpu
from jax.sharding import PartitionSpec as P

D = 2048
HEAD_DIM = 64
FF = 5632
SEQ = 320
STEP = 10
ROT = 16

BETA_ONE = 0.9
BETA_TWO = 0.999
ADAM_EPS = 1e-08
NORM_EPS = 1e-05
MASK_FILL = -1e30

BOTH = ("dp", "tensor")
MESH = pl.DeviceIdType.MESH


def block_order(count):
    return [2 * j + i for i in range(2) for j in range(count // 2)]


def relative(values, axis, me, count):
    width = values.shape[axis] // count
    return jnp.concatenate(
        [lax.dynamic_slice_in_dim(values, (me ^ r) * width, width, axis) for r in block_order(count)],
        axis=axis,
    )


def from_relative(values, axis, me, count):
    width = values.shape[axis] // count
    places = [((me ^ g) % 2) * (count // 2) + (me ^ g) // 2 for g in range(count)]
    return jnp.concatenate(
        [lax.dynamic_slice_in_dim(values, place * width, width, axis) for place in places],
        axis=axis,
    )


def place(dp_flip, tensor_flip):
    return (lax.axis_index("dp") ^ dp_flip, lax.axis_index("tensor") ^ tensor_flip)


def greet(places):
    barrier = pltpu.get_barrier_semaphore()
    for there in places:
        pl.semaphore_signal(barrier, inc=1, device_id=there, device_id_type=MESH)
    pl.semaphore_wait(barrier, len(places))


def send_to(there, source, target, send_sem, recv_sem):
    return pltpu.make_async_remote_copy(
        src_ref=source,
        dst_ref=target,
        send_sem=send_sem,
        recv_sem=recv_sem,
        device_id=there,
        device_id_type=MESH,
    )


def group_places(half):
    return [place(2 * j, 0) for j in range(1, half)] + [place(1, 0), place(0, 2), place(0, 1)]


def forward(half, by_columns, *refs):
    def take(count):
        nonlocal refs
        head, refs = refs[:count], refs[count:]
        return head

    project_pair, gate_up_pair, down_pair, output_pair = take(4)
    gains_own, unit_rows, cot_own, cot_flipped, tables, bias = take(6)
    w_project, w_gate_up, w_down, w_output, gains = take(5)
    normed, cot, normed_t, packed, hidden, attended, turned, hidden_t, attended_t = take(9)
    stage = take(2)
    normed_own, normed_flipped = take(2)
    z_send, z_recv, x_send, x_recv, a_send, a_recv = refs
    greet(group_places(half))

    spots, seqs, piece, _ = cot.shape
    units, heads = hidden.shape[-1], attended.shape[-1]
    each = D // (2 * half)
    rows_all = spots * seqs * piece
    every = lambda ref: pl.BlockSpec(ref.shape, lambda *g: (0,) * len(ref.shape))

    def row_chunk(out, mine, other, share=0, shares=1):
        size = mine.shape[0] // shares
        rows = pl.ds(share * size, size)
        return mine.at[rows], other.at[rows], lambda p: out.at[pl.ds(p * mine.shape[0] + share * size, size)]

    def column_chunk(out, mine, other, share=0, shares=1):
        size = mine.shape[0] // shares
        rows, width = pl.ds(share * size, size), mine.shape[1]
        return mine.at[rows], other.at[rows], lambda p: out.at[rows, pl.ds(p * width, width)]

    out_chunk = column_chunk if by_columns else row_chunk
    pair = lambda ref: (ref.at[0], ref.at[1])
    chunks = [
        row_chunk(gains, gains_own, gains_own),
        row_chunk(w_project, *pair(project_pair)),
        row_chunk(w_gate_up, *pair(gate_up_pair), 0, 2),
        row_chunk(w_gate_up, *pair(gate_up_pair), 1, 2),
        out_chunk(w_down, *pair(down_pair), 0, 2),
        out_chunk(w_output, *pair(output_pair)),
        out_chunk(w_down, *pair(down_pair), 1, 2),
    ]
    GAINS, PROJECT, GATE_UP, DOWN, OUTPUT = 0, 1, 2, 4, 5
    n = len(chunks)
    far = range(1, half)

    def z_copy(c, j):
        mine, other, block = chunks[c]
        return send_to(place(2 * j, 0), other if j % 2 else mine, block(j), z_send.at[c, j], z_recv.at[c, j])

    def x_copy(c, j):
        mine, _, block = chunks[c]
        return send_to(place(1, 0), block(j) if j else mine, block(half + j), x_send.at[c, j], x_recv.at[c, j])

    def start_z(c):
        if c < n:
            for j in far:
                z_copy(c, j).start()

    def start_own(c):
        if c < n:
            x_copy(c, 0).start()

    def keep(sources, outs, blocks, steps):
        def body(*refs):
            for ref, out_ref in zip(refs, refs[len(sources) :]):
                put(out_ref, ref[...])

        pltpu.emit_pipeline(
            body, grid=(steps,), in_specs=[block[0] for block in blocks], out_specs=[block[1] for block in blocks]
        )(*sources, *outs)

    def keep_weights():
        pairs = (project_pair, gate_up_pair, down_pair, output_pair)
        sizes = [(ref.shape[1] // 2, ref.shape[2]) for ref in pairs]
        blocks = [(blocked((1,) + size, 0, step(), 0), blocked(size, step(), 0)) for size in sizes]
        keep(pairs, (w_project, w_gate_up, w_down, w_output), blocks, 2)

    def keep_cot():
        lead = blocked((1, piece, D), step(), 0, 0)
        keep((cot_own,), (cot,), [(lead, blocked((1, 1, piece, D), 0, step(), 0, 0))], seqs // 2)

    def serve(c):
        for j in far:
            z_copy(c, j).wait_recv()
            x_copy(c, j).start()
            if c + 1 < n and c != GAINS:
                z_copy(c + 1, j).start()
        if c > GAINS:
            start_own(c + 2)

    def have(*which):
        for c in which:
            for j in range(half):
                x_copy(c, j).wait_recv()

    act_own, act_flipped, act_out = (normed_own, cot_own), (normed_flipped, cot_flipped), (normed, cot)

    def rows(a, index):
        micro = seqs // 2
        return act_out[a].at[index // 2, pl.ds((index % 2) * micro, micro)]

    def a_copy(a, k):
        source = (act_flipped[a], act_own[a], rows(a, 1), act_own[a], rows(a, 1), rows(a, 2), rows(a, 3))[k]
        there = place(2, 0) if k == 0 else place(0, 2) if k < 3 else place(0, 1)
        return send_to(there, source, rows(a, k + 1), a_send.at[a, k], a_recv.at[a, k])

    def act_begin(a):
        for k in (0, 1, 3):
            a_copy(a, k).start()

    def act_z(a):
        a_copy(a, 0).wait_recv()
        a_copy(a, 2).start()
        a_copy(a, 4).start()

    def act_y(a):
        a_copy(a, 1).wait_recv()
        a_copy(a, 5).start()
        a_copy(a, 2).wait_recv()
        a_copy(a, 6).start()

    def act_have(a):
        for k in range(3, 7):
            a_copy(a, k).wait_recv()

    def norm_step():
        def body(unit_ref, gains_ref, out_ref, flipped_ref, kept_ref):
            gain, shift = [
                jnp.concatenate([gains_ref[p * 8 + k : p * 8 + k + 1] for p in range(2 * half)], axis=1)
                for k in range(2)
            ]
            value = unit_ref[0] * gain + shift
            put(out_ref, value)
            put(flipped_ref, flip_lanes(value, each))
            put(kept_ref, value)

        block = blocked((1, piece, D), step(), 0, 0)
        kept = blocked((1, 1, piece, D), 0, step(), 0, 0)
        pltpu.emit_pipeline(
            body, grid=(seqs // 2,), in_specs=[block, every(gains)], out_specs=[block, block, kept]
        )(unit_rows, gains, normed_own, normed_flipped, normed)

    def attention_step(first, count):
        block = lambda width: blocked((spots, 1, piece, width), 0, step(first), 0, 0)

        def body(normed_ref, weight_ref, tables_ref, bias_ref, turned_ref, attended_ref):
            projected = dot_plain(flat(normed_ref), weight_ref[...])
            attention_fore(projected, tables_ref, bias_ref, turned_ref, attended_ref)

        pltpu.emit_pipeline(
            body,
            grid=(count,),
            in_specs=[block(D), every(w_project), every(tables), every(bias)],
            out_specs=[block(3 * heads), block(heads)],
        )(normed, w_project, tables, bias, turned, attended)

    def turn_over(source, out, in_block, out_block, steps):
        def body(ref, out_ref):
            put(out_ref, flat(ref).T)

        pltpu.emit_pipeline(body, grid=(steps,), in_specs=[in_block], out_specs=[out_block])(source, out)

    def units_step(first, count):
        tile = lambda width: blocked((1, seqs, piece, width), step(first), 0, 0, 0)

        def body(normed_ref, weight_ref, packed_ref, hidden_ref):
            value, units_value = units_fore(flat(normed_ref), weight_ref[...])
            put(packed_ref, value)
            put(hidden_ref, units_value)

        pltpu.emit_pipeline(
            body,
            grid=(count,),
            in_specs=[tile(D), every(w_gate_up)],
            out_specs=[tile(2 * units), tile(units)],
        )(normed, w_gate_up, packed, hidden)

    def grads_step():
        groups, wide = stage[0].shape[0], D // (2 * stage[0].shape[0])

        def body(cot_ref, attended_ref, hidden_ref, *out_refs):
            block = flat(cot_ref)
            for ref, out_ref in zip((attended_ref, hidden_ref), out_refs):
                value = dot_plain(ref[...], block)
                put(out_ref, value if by_columns else value.T)

        pltpu.emit_pipeline(
            body,
            grid=(groups,),
            in_specs=[
                blocked((spots, seqs, piece, wide), 0, 0, 0, step(groups)),
                every(attended_t),
                every(hidden_t),
            ],
            out_specs=[blocked((1,) + ref.shape[1:], step(), 0, 0) for ref in stage],
        )(cot, attended_t, hidden_t, *stage)

    start_z(GAINS)
    start_z(PROJECT)
    for c in (GAINS, PROJECT, GATE_UP):
        start_own(c)
    keep((gains_own,), (gains,), [(every(gains_own), blocked(gains_own.shape, 0, 0))], 1)
    serve(GAINS)
    have(GAINS)
    norm_step()
    act_begin(0)
    keep_weights()
    keep_cot()
    serve(PROJECT)
    act_z(0)
    act_y(0)
    act_begin(1)
    act_have(0)
    have(PROJECT)
    serve(GATE_UP)
    attention_step(0, seqs)
    act_z(1)
    turn_over(attended, attended_t, every(attended), every(attended_t), 1)
    serve(GATE_UP + 1)
    columns = lambda index: blocked((spots, seqs, piece, 256), 0, 0, 0, index)
    turn_over(normed, normed_t, columns(step()), blocked((256, rows_all), step(), 0), D // 256)
    act_y(1)
    serve(DOWN)
    have(GATE_UP, GATE_UP + 1)
    units_step(0, spots // 2)
    serve(OUTPUT)
    units_step(spots // 2, spots - spots // 2)
    turn_over(hidden, hidden_t, every(hidden), every(hidden_t), 1)
    act_have(1)
    serve(n - 1)
    grads_step()
    have(DOWN, OUTPUT, n - 1)
    for c in range(n):
        for j in range(half):
            if j:
                z_copy(c, j).wait_send()
            x_copy(c, j).wait_send()
    for a in range(2):
        for k in range(7):
            a_copy(a, k).wait_send()


def run_forward(half, by_columns, pairs, gains, unit_rows, cot, cot_flipped, tables, bias, group):
    low, full = jnp.bfloat16, jnp.float32
    each, heads, units = pairs[0].shape[1], pairs[0].shape[2] // 3, pairs[1].shape[2] // 2
    spots, seqs, piece = group
    rows_all = spots * seqs * piece
    groups = min(half, 4)
    wide = D // (2 * groups)
    widths = (heads, units)
    flat_stage = [(groups, w, wide) if by_columns else (groups, wide, w) for w in widths]
    across = [(w, D) if by_columns else (D, w) for w in (units, heads)]
    shapes = [
        ((D, 3 * heads), low),
        ((D, 2 * units), low),
        *[(shape, low) for shape in across],
        ((2 * half * 8, each), full),
        (group + (D,), low),
        (group + (D,), low),
        ((D, rows_all), low),
        (group + (2 * units,), full),
        (group + (units,), low),
        (group + (heads,), low),
        (group + (3 * heads,), low),
        ((units, rows_all), low),
        ((heads, rows_all), low),
        *[(shape, low) for shape in flat_stage],
        (cot.shape, low),
        (cot.shape, low),
    ]
    ins = [*pairs, gains, unit_rows, cot, cot_flipped, tables, bias]
    anywhere = pl.BlockSpec(memory_space=pl.ANY)
    sem = pltpu.SemaphoreType.DMA
    return pl.pallas_call(
        functools.partial(forward, half, by_columns),
        out_shape=[jax.ShapeDtypeStruct(*shape) for shape in shapes],
        in_specs=[anywhere] * len(ins),
        out_specs=[anywhere] * len(shapes),
        scratch_shapes=[sem((7, half))] * 4 + [sem((2, 7))] * 2,
        compiler_params=pltpu.CompilerParams(
            collective_id=0, has_side_effects=True, vmem_limit_bytes=56 * 1024 * 1024
        ),
        name="forward",
    )(*ins)


def angle_tables(length):
    half_rot = ROT // 2
    angles = np.arange(length)[:, None] * (10000.0 ** (-2.0 * np.arange(half_rot) / ROT))[None, :]
    cosine, sine = np.cos(angles), np.sin(angles)
    none = np.zeros_like(sine)
    rest = np.zeros((length, HEAD_DIM - ROT))
    rows = ((cosine, cosine, rest + 1.0), (-sine, none, rest), (none, sine, rest))
    return np.stack([np.tile(np.concatenate(parts, axis=1), (1, 2)) for parts in rows]).astype(np.float32)


def prepare(each, in_place, *refs):
    tokens, cot, project, gate_up, down, output, params, angles = refs[:8]
    tok_ref, unit_ref, cot_ref, cot_flipped_ref, project_ref, gate_up_ref, down_ref, output_ref = refs[8:16]
    gains_ref, tables_ref, bias_ref = refs[16:]
    me = lax.axis_index("dp")
    gains_ref[...] = jnp.zeros_like(gains_ref)
    gains_ref[0:2] = params[...].astype(jnp.bfloat16).astype(jnp.float32)
    piece, shape = tokens.shape[1], bias_ref.shape
    places = [lax.broadcasted_iota(jnp.int32, shape, axis) for axis in range(2)]
    positions = list(places)
    for k, flip in enumerate((0, 2, 1, 3)):
        spot = lax.axis_index("tensor") ^ flip
        tables_ref[:, k * piece : (k + 1) * piece] = angles[:, pl.ds(pl.multiple_of(spot * piece, piece), piece)]
        for axis, value in enumerate(places):
            inside = jnp.logical_and(value >= k * piece, value < (k + 1) * piece)
            positions[axis] = jnp.where(inside, value + (spot - k) * piece, positions[axis])
    bias_ref[...] = jnp.where(positions[0] >= positions[1], 0.0, MASK_FILL)
    side = (me // 2) % 2
    blocks = block_order(D // each)
    if in_place:
        for p, r in enumerate(blocks):
            span, flipped = slice(p * each, (p + 1) * each), slice((p ^ 1) * each, ((p ^ 1) + 1) * each)
            there = pl.ds(pl.multiple_of((me ^ r) * each, each), each)
            tok_ref[:, :, span] = tokens[:, :, there]
            cot_ref[:, :, span] = cot[:, :, there]
            cot_flipped_ref[:, :, flipped] = cot[:, :, there]
    else:
        tok_ref[...] = tokens[...]
        cot_ref[...] = cot[...]
        for s in range(cot.shape[0]):
            put(cot_flipped_ref.at[s], flip_lanes(cot[s].astype(jnp.float32), each))
    for s in range(tokens.shape[0]):
        unit_ref[s], _ = norm_rows(tok_ref[s].astype(jnp.float32))
    heads, units = output.shape[0] // 2, down.shape[0] // 2
    whole = units - 64
    for h, s in enumerate((side, 1 - side)):
        part = lambda width, start=0: pl.ds(start + pl.multiple_of(s * width, width), width)
        for k in range(3):
            put(project_ref.at[h, :, pl.ds(k * heads, heads)], project[k, :, part(heads)])
        for k in range(2):
            put(gate_up_ref.at[h, :, pl.ds(k * whole, whole)], gate_up[k, :, part(whole)])
        put(output_ref.at[h], output[part(heads)])
        put(down_ref.at[h, pl.ds(0, whole)], down[part(whole)])
        put(down_ref.at[h, pl.ds(whole, 64)], down[part(64, 2 * whole)])
    gate, up = gate_up[0, :, 2 * whole :], gate_up[1, :, 2 * whole :]
    first = lax.broadcasted_iota(jnp.int32, gate.shape, 1) < 64
    zero = jnp.where(first, gate, pltpu.roll(up, 64, 1))
    one = jnp.where(first, pltpu.roll(gate, 64, 1), up)
    put(gate_up_ref.at[0, :, pl.ds(2 * whole, 128)], jnp.where(side == 0, zero, one))
    put(gate_up_ref.at[1, :, pl.ds(2 * whole, 128)], jnp.where(side == 0, one, zero))


def whole_spec(shape):
    return pl.BlockSpec(shape, lambda *_: (0,) * len(shape))


def run_prepare(tokens, cot, weights, params, angles):
    project, gate_up, down, output = weights
    each = project.shape[1]
    in_place = each % 128 == 0
    if not in_place:
        me, count = lax.axis_index("dp"), D // each
        tokens, cot = relative(tokens, 2, me, count), relative(cot, 2, me, count)
    low = jnp.bfloat16
    heads, units = output.shape[0] // 2, down.shape[0] // 2
    shapes = [(tokens.shape, low), (tokens.shape, jnp.float32), (cot.shape, low), (cot.shape, low)]
    shapes += [((2, each, 3 * heads), low), ((2, each, 2 * units), low)]
    shapes += [((2, units, each), low), ((2, heads, each), low)]
    length = angles.shape[1]
    shapes += [((8, each), jnp.float32), (angles.shape, jnp.float32), ((length, length), jnp.float32)]
    ins = [tokens, cot, project, gate_up, down, output, params, angles]
    return pl.pallas_call(
        functools.partial(prepare, each, in_place),
        grid=(1,),
        in_specs=[whole_spec(value.shape) for value in ins],
        out_specs=[whole_spec(shape) for shape, _ in shapes],
        out_shape=[jax.ShapeDtypeStruct(*shape) for shape in shapes],
        compiler_params=pltpu.CompilerParams(vmem_limit_bytes=60 * 1024 * 1024),
        name="prepare",
    )(*ins)


def flat(ref):
    value = ref[...]
    return value.reshape(-1, value.shape[-1])


def put(ref, value):
    ref[...] = value.astype(ref.dtype).reshape(ref.shape)


def blocked(shape, *index):
    return pl.BlockSpec(shape, lambda g: tuple(i(g) if callable(i) else i for i in index))


def step(offset=0):
    return lambda g: g + offset


def backward(half, by_columns, window, *refs):
    def take(count):
        nonlocal refs
        head, refs = refs[:count], refs[count:]
        return head

    cot, packed, hidden, attended, turned = take(5)
    normed_t, attended_t_all, hidden_t_all = take(3)
    w_project, w_gate_up, w_down, w_output, tables, bias = take(6)
    stage_out = take(2)
    z_in, mine = take(4), take(4)
    act_away, act_near, core_in, y_out, y_in, far_out = [take(2) for _ in range(6)]
    act_far, act_sum = take(1), take(2)
    stage, x_in = stage_out + take(2), take(4)
    d_packed, d_att, d_project, attended_t, hidden_t, normed_block, cot_block = take(7)
    x_send, x_recv, z_send, z_recv, a_send, a_recv, load_sem, block_sem = refs
    greet(group_places(half))

    spots, seqs, piece, _ = cot.shape
    units, heads = hidden.shape[-1], attended.shape[-1]
    groups = stage[0].shape[0]
    per = half // groups
    wide = D // (2 * groups)
    every = lambda ref: pl.BlockSpec(ref.shape, lambda g: (0,) * len(ref.shape))

    whole = (attended_t, hidden_t, d_packed, d_project)

    def product(c, block, whole_ref):
        if c >= 2:
            return dot_plain(block, flat(whole_ref))
        value = dot_plain(whole_ref[...], block)
        return value if by_columns else value.T

    def block_copy(index):
        c, g = order[index]
        span, slot = pl.ds(g * wide, wide), index % 2
        if c >= 2:
            source, target = normed_t.at[span], normed_block.at[slot]
        else:
            source, target = cot.at[:, :, :, span], cot_block.at[slot]
        return pltpu.make_async_copy(source, target, block_sem.at[slot])

    def x_copy(c, g):
        return send_to(place(1, 0), stage[c].at[g], x_in[c].at[g], x_send.at[c, g], x_recv.at[c, g])

    def z_copy(c, j):
        source = x_in[c].at[j // per]
        if per > 1:
            rows = z_in[c].shape[1]
            source = source.at[pl.ds((j % per) * rows, rows)]
        return send_to(place(2 * j, 0), source, z_in[c].at[j], z_send.at[c, j], z_recv.at[c, j])

    def a_copy(a, s):
        source = (act_away[a], y_out[a], far_out[a])[s]
        target = (core_in[a], y_in[a], act_far[0])[s]
        there = (place(0, 1), place(0, 2), place(2, 0))[s]
        return send_to(there, source, target, a_send.at[a, s], a_recv.at[a, s])

    order = [(0, 3), (0, 2), (1, 3), (1, 2), (1, 1), (0, 1)]
    order += [(c, g) for c in (2, 3) for g in (3, 2, 1)] + [(c, 0) for c in (2, 1, 3, 0)]
    started, served, ready = [0], [0], {0, 1}

    def start_x():
        while started[0] < min(served[0] + window, len(order)) and order[started[0]][0] in ready:
            x_copy(*order[started[0]]).start()
            started[0] += 1

    def away_product(c):
        def body(block_ref, whole_ref, out_ref):
            put(out_ref, product(c, block_ref[...], whole_ref))

        pltpu.emit_pipeline(
            body,
            grid=(groups,),
            in_specs=[blocked((wide, normed_t.shape[1]), step(groups), 0), every(whole[c])],
            out_specs=[blocked((1,) + stage[c].shape[1:], step(), 0, 0)],
        )(normed_t, whole[c], stage[c])
        ready.add(c)
        start_x()

    def serve(count):
        for _ in range(count):
            index = served[0]
            c, g = order[index]
            served[0] += 1
            block_copy(index).wait()
            if served[0] < len(order):
                block_copy(served[0]).start()
            x_copy(c, g).wait_recv()
            start_x()
            block = flat((normed_block if c >= 2 else cot_block).at[index % 2])
            total = product(c, block, whole[c]) + x_in[c][g].astype(jnp.float32)
            if g == 0:
                mine[c][0] = total
            if g > 0 or per > 1:
                put(x_in[c].at[g], total)
            for j in range(g * per, (g + 1) * per):
                if j:
                    z_copy(c, j).start()

    def units_step(first, count):
        tile = (1, seqs, piece)

        def body(cot_ref, down_ref, output_ref, packed_ref, d_packed_ref, d_att_ref):
            rows = flat(cot_ref)
            d_packed_ref[...] = units_back(rows, down_ref[...], flat(packed_ref)).reshape(d_packed_ref.shape)
            put(d_att_ref, dot_cols(rows, output_ref[...]))

        pltpu.emit_pipeline(
            body,
            grid=(count,),
            in_specs=[
                blocked(tile + (D,), step(first), 0, 0, 0),
                every(w_down),
                every(w_output),
                blocked(tile + (2 * units,), step(first), 0, 0, 0),
            ],
            out_specs=[
                blocked(tile + (2 * units,), step(first), 0, 0, 0),
                blocked(tile + (heads,), step(first), 0, 0, 0),
            ],
        )(cot, w_down, w_output, packed, d_packed, d_att)

    def attention_step(first, count):
        block = lambda width: blocked((spots, 1, piece, width), 0, step(first), 0, 0)
        pltpu.emit_pipeline(
            attention_back,
            grid=(count,),
            in_specs=[block(3 * heads), block(heads), every(tables), every(bias)],
            out_specs=[block(3 * heads)],
        )(turned, d_att, tables, bias, d_project)

    def two_cores(away_ref, near_ref, total):
        middle = total.shape[0] // 2
        put(near_ref, total[:middle])
        put(away_ref, total[middle:])

    def core_block(first):
        return blocked((spots // 2, seqs, piece, 512), 0, 0, 0, step(first))

    def normed_step():
        def body(d_project_ref, d_packed_ref, project_ref, gate_up_ref, away_ref, near_ref):
            total = dot_cols(flat(d_project_ref), project_ref[...])
            two_cores(away_ref, near_ref, total + dot_cols(flat(d_packed_ref), gate_up_ref[...]))

        pltpu.emit_pipeline(
            body,
            grid=(D // 512,),
            in_specs=[
                every(d_project),
                every(d_packed),
                blocked((512, 3 * heads), step(), 0),
                blocked((512, 2 * units), step(), 0),
            ],
            out_specs=[core_block(0)] * 2,
        )(d_project, d_packed, w_project, w_gate_up, act_away[0], act_near[0])

    def out_step(first, count):
        def body(attended_ref, hidden_ref, output_ref, down_ref, away_ref, near_ref):
            total = dot_plain(flat(attended_ref), output_ref[...])
            two_cores(away_ref, near_ref, total + dot_plain(flat(hidden_ref), down_ref[...]))

        pltpu.emit_pipeline(
            body,
            grid=(count,),
            in_specs=[
                every(attended),
                every(hidden),
                blocked((heads, 512), 0, step(first)),
                blocked((units, 512), 0, step(first)),
            ],
            out_specs=[core_block(first)] * 2,
        )(attended, hidden, w_output, w_down, act_away[1], act_near[1])

    def add_terms(*refs):
        *terms, out_ref = refs
        put(out_ref, sum(flat(term).astype(jnp.float32) for term in terms))

    half_seqs = seqs // 2

    def core_arrived(a):
        a_copy(a, 0).wait_recv()
        rows = blocked((1, half_seqs, piece, D), 1, step(), 0, 0)
        pltpu.emit_pipeline(
            add_terms,
            grid=(2,),
            in_specs=[rows, rows],
            out_specs=[blocked((half_seqs, piece, D), step(), 0, 0)],
        )(act_near[a], core_in[a], y_out[a])
        a_copy(a, 1).start()

    def y_arrived(a):
        def body(*refs):
            add_terms(*refs[:3], refs[6])
            add_terms(*refs[3:6], refs[7])

        def both(shape, *lead):
            return [blocked(shape, *lead, step(first), 0, 0) for first in (half_seqs, 0)]

        rows, lines = both((1, 1, piece, D), 0), both((1, piece, D))
        a_copy(a, 1).wait_recv()
        pltpu.emit_pipeline(
            body,
            grid=(half_seqs,),
            in_specs=[rows[0], rows[0], lines[0], rows[1], rows[1], lines[1]],
            out_specs=[blocked((1, piece, D), step(), 0, 0)] * 2,
        )(*[act_near[a], core_in[a], y_in[a]] * 2, far_out[a], act_sum[a])
        if a == 0:
            a_copy(a, 2).start()

    loads = [
        pltpu.make_async_copy(attended_t_all, attended_t, load_sem.at[0]),
        pltpu.make_async_copy(hidden_t_all, hidden_t, load_sem.at[1]),
    ]
    for load in loads:
        load.start()
    block_copy(0).start()
    start_x()
    for load in loads:
        load.wait()
    steps = D // 512
    units_step(0, spots)
    serve(2)
    away_product(2)
    serve(2)
    attention_step(0, seqs // 2)
    serve(1)
    attention_step(seqs // 2, seqs - seqs // 2)
    away_product(3)
    serve(1)
    normed_step()
    a_copy(0, 0).start()
    serve(1)
    out_step(0, steps // 2)
    core_arrived(0)
    serve(1)
    out_step(steps // 2, steps - steps // 2)
    a_copy(1, 0).start()
    serve(2)
    core_arrived(1)
    y_arrived(0)
    serve(len(order) - served[0])
    y_arrived(1)
    for c in range(4):
        for j in range(1, half):
            z_copy(c, j).wait()
        for g in range(groups):
            x_copy(c, g).wait_send()
    for a in range(2):
        for s in range(2):
            a_copy(a, s).wait_send()
    a_copy(0, 2).wait()


def run_backward(half, by_columns, rows, transposed, weights, tables, bias, stage, window=3):
    cot, packed, hidden, attended, turned = rows
    low, full = jnp.bfloat16, jnp.float32
    spots, seqs, piece, _ = cot.shape
    each = D // (2 * half)
    groups = min(half, 4)
    wide = D // (2 * groups)
    widths = (attended.shape[-1], hidden.shape[-1], packed.shape[-1], turned.shape[-1])
    columns = [by_columns and groups == half and c < 2 for c in range(4)]

    def shape_of(count, block):
        return [(count, w, block) if flip else (count, block, w) for w, flip in zip(widths, columns)]

    def row_shape(*lead, kind=low):
        return [jax.ShapeDtypeStruct(lead + (piece, D), kind)] * 2

    shapes = [jax.ShapeDtypeStruct(shape, low) for shape in shape_of(half, each)]
    shapes += [jax.ShapeDtypeStruct(shape, full) for shape in shape_of(1, wide)]
    shapes += row_shape(spots // 2, seqs) * 3 + row_shape(seqs) * 2 + row_shape(seqs // 2)
    shapes += row_shape(seqs // 2)[:1] + row_shape(seqs // 2, kind=full)
    anywhere = pl.BlockSpec(memory_space=pl.ANY)
    vmem = pl.BlockSpec(memory_space=pltpu.VMEM)
    ins = [*rows, *transposed, *weights, tables, bias, *stage]
    sem = pltpu.SemaphoreType.DMA
    rows_all = spots * seqs * piece
    scratch = [pltpu.VMEM(shape, low) for shape in shape_of(groups, wide)[2:] + shape_of(groups, wide)]
    scratch += [pltpu.VMEM(r.shape, low) for r in (packed, attended, turned)]
    scratch += [pltpu.VMEM(t.shape, low) for t in transposed[1:]]
    scratch += [pltpu.VMEM((2, wide, rows_all), low), pltpu.VMEM((2, spots, seqs, piece, wide), low)]
    scratch += [sem((4, groups))] * 2 + [sem((4, half))] * 2 + [sem((2, 3))] * 2 + [sem((2,))] * 2
    outs = pl.pallas_call(
        functools.partial(backward, half, columns[0], window),
        out_shape=shapes,
        in_specs=[anywhere] * len(ins),
        out_specs=[anywhere] * 4 + [vmem] * 4 + [anywhere] * (len(shapes) - 8),
        scratch_shapes=scratch,
        compiler_params=pltpu.CompilerParams(
            collective_id=1, has_side_effects=True, vmem_limit_bytes=60 * 1024 * 1024
        ),
        name="backward",
    )(*ins)
    pairs = []
    for c in range(4):
        own = outs[4 + c][0] if columns[c] else outs[4 + c][0, :each]
        pairs.append((own, outs[c]))
    *_, out_far, normed_far, normed_sum, out_sum = outs
    dp_size, tensor_size = lax.axis_size("dp"), lax.axis_size("tensor")
    partners = [
        (d * tensor_size + t, (d ^ 2) * tensor_size + t) for d in range(dp_size) for t in range(tensor_size)
    ]
    out_far = lax.ppermute(out_far, ("dp", "tensor"), partners)
    return pairs, (normed_far, normed_sum), (out_far, out_sum)


def flip_lanes(values, width):
    lanes = values.shape[1]
    if width % 128 == 0:
        spans = [slice((p ^ 1) * width, ((p ^ 1) + 1) * width) for p in range(lanes // width)]
        return jnp.concatenate([values[:, span] for span in spans], axis=1)
    even = (lax.broadcasted_iota(jnp.int32, values.shape, 1) // width) % 2 == 0
    return jnp.where(even, pltpu.roll(values, lanes - width, 1), pltpu.roll(values, width, 1))


def norm_rows(tok_rows):
    centered = tok_rows - jnp.mean(tok_rows, axis=1, keepdims=True)
    row_scale = lax.rsqrt(jnp.mean(centered * centered, axis=1, keepdims=True) + NORM_EPS)
    return centered * row_scale, row_scale


def put_rows(ref, value, each, in_place):
    value = value.astype(jnp.bfloat16)
    if not in_place:
        ref[0] = value
        return
    me = lax.axis_index("dp")
    for p, r in enumerate(block_order(D // each)):
        span = pl.ds(pl.multiple_of((me ^ r) * each, each), each)
        ref[0, :, span] = value[:, p * each : (p + 1) * each]


def finish_out(each, in_place, far_ref, sum_ref, tok_ref, out_ref):
    summed = flat(sum_ref) + flip_lanes(flat(far_ref).astype(jnp.float32), each)
    put_rows(out_ref, flat(tok_ref).astype(jnp.float32) + summed, each, in_place)


def finish_rows(each, in_place, far_ref, sum_ref, tok_ref, cot_ref, gain, input_ref):
    d_normed = flat(sum_ref) + flip_lanes(flat(far_ref).astype(jnp.float32), each)
    unit_rows, row_scale = norm_rows(flat(tok_ref).astype(jnp.float32))
    d_unit = d_normed * gain
    d_input = row_scale * (
        d_unit
        - jnp.mean(d_unit, axis=1, keepdims=True)
        - unit_rows * jnp.mean(d_unit * unit_rows, axis=1, keepdims=True)
    )
    put_rows(input_ref, flat(cot_ref).astype(jnp.float32) + d_input, each, in_place)
    return jnp.sum(d_normed * unit_rows, axis=0, keepdims=True), jnp.sum(d_normed, axis=0, keepdims=True)


def run_finish(kernel, each, rows, fixed_in, fixed_out):
    in_place = each % 128 == 0
    count, piece, _ = rows[-1].shape
    block = pl.BlockSpec((1, piece, D), lambda s: (s, 0, 0))
    fixed = pl.BlockSpec((8, D), lambda s: (0, 0))
    done, *others = pl.pallas_call(
        functools.partial(kernel, each, in_place),
        grid=(count,),
        in_specs=[block] * len(rows) + [fixed] * len(fixed_in),
        out_specs=[block] + [fixed] * fixed_out,
        out_shape=[jax.ShapeDtypeStruct(rows[-1].shape, jnp.bfloat16)]
        + [jax.ShapeDtypeStruct((8, D), jnp.float32)] * fixed_out,
        compiler_params=KERNEL_PARAMS,
        name=kernel.__name__,
    )(*rows, *fixed_in)
    if not in_place:
        done = from_relative(done, 2, lax.axis_index("dp"), D // each)
    return done, *others


def join_grads(half, spans, *refs):
    own, came = refs[0:8:2], refs[1:8:2]
    far, close, tok, cot, gains = refs[8:13]
    output_ref, down_ref, gate_up_ref, project_ref, input_ref, shares_ref = refs[13:]
    each = D // (2 * half)
    in_place = each % 128 == 0
    parts = [
        finish_rows(each, in_place, *[r.at[pl.ds(k, 1)] for r in (far, close, tok, cot)], gains[0:1], input_ref.at[pl.ds(k, 1)])
        for k in range(tok.shape[0])
    ]
    shares = [sum(values) for values in zip(*parts)]
    side = (lax.axis_index("dp") // 2) % 2
    heads, whole = spans
    squares = jnp.float32(0.0)

    def halves(c, rows, columns):
        nonlocal squares
        pick = lambda j: came[c][j, rows, columns].astype(jnp.float32)
        mine = own[c][rows, columns] + sum(pick(j) for j in range(2, half, 2))
        other = sum(pick(j) for j in range(1, half, 2))
        squares = squares + jnp.sum(mine * mine) + jnp.sum(other * other)
        return mine, other

    def places(width, start=0):
        return [pl.ds(start + pl.multiple_of(s * width, width), width) for s in (side, 1 - side)]

    every = slice(None)
    for value, span in zip(halves(0, every, every), places(heads)):
        output_ref[span] = value
    for value, span in zip(halves(1, slice(0, whole), every), places(whole)):
        down_ref[span] = value
    for value, span in zip(halves(1, slice(whole, whole + 64), every), places(64, 2 * whole)):
        down_ref[span] = value
    for k in range(3):
        for value, span in zip(halves(3, every, slice(k * heads, (k + 1) * heads)), places(heads)):
            project_ref[k, :, span] = value
    for k in range(2):
        for value, span in zip(halves(2, every, slice(k * whole, (k + 1) * whole)), places(whole)):
            gate_up_ref[k, :, span] = value
    mine, other = halves(2, every, slice(2 * whole, 2 * whole + 128))
    zero, one = jnp.where(side == 0, mine, other), jnp.where(side == 0, other, mine)
    first = lax.broadcasted_iota(jnp.int32, zero.shape, 1) < 64
    gate_up_ref[0, :, 2 * whole :] = jnp.where(first, zero, pltpu.roll(one, 64, 1))
    gate_up_ref[1, :, 2 * whole :] = jnp.where(first, pltpu.roll(zero, 64, 1), one)
    if in_place:
        shares_ref[...] = jnp.zeros_like(shares_ref)
        per = each // 128
        for p in range(2 * half):
            for k, share in enumerate(shares):
                for q in range(per):
                    first = p * each + q * 128
                    shares_ref[p, k * per + q : k * per + q + 1] = share[:, first : first + 128]
            shares_ref[p, 7:8] = jnp.full((1, 128), squares)
    else:
        shares_ref[...] = jnp.concatenate(shares + [jnp.full((6, D), squares)], axis=0)


def run_join_grads(half, pairs, rows, shapes, spans):
    each = D // (2 * half)
    in_place = each % 128 == 0
    ins = [part for pair in pairs for part in pair] + rows
    kinds = [(shape, jnp.float32) for shape in shapes] + [(rows[2].shape, jnp.bfloat16)]
    kinds += [((2 * half, 8, 128) if in_place else (8, D), jnp.float32)]
    *grads, input_grad, shares = pl.pallas_call(
        functools.partial(join_grads, half, spans),
        grid=(1,),
        in_specs=[whole_spec(value.shape) for value in ins],
        out_specs=[whole_spec(shape) for shape, _ in kinds],
        out_shape=[jax.ShapeDtypeStruct(*kind) for kind in kinds],
        compiler_params=pltpu.CompilerParams(vmem_limit_bytes=60 * 1024 * 1024),
        name="join_grads",
    )(*ins)
    if not in_place:
        input_grad = from_relative(input_grad, 2, lax.axis_index("dp"), 2 * half)
        blocks = shares.reshape(8, 2 * half, each).transpose(1, 0, 2)
        shares = jnp.concatenate([blocks[:, :2], jnp.zeros_like(blocks[:, :5]), blocks[:, 2:3]], axis=1)
    return grads, input_grad, shares


def sum_kernel(half, spots, in_ref, out_ref, total_ref, first, second, send_sem, recv_sem):
    me, spot = lax.axis_index("dp"), lax.axis_index("tensor")
    z_places = [place(2 * j, 0) for j in range(half)]
    rest = [(i, t) for i in range(2) for t in range(spots)]
    rest_places = [place(i, t) for i, t in rest]
    greet(z_places[1:] + rest_places[1:])
    count = in_ref.shape[0]

    def exchange(places, slots, base):
        copies = [
            send_to(places[k], slots.at[0], slots.at[k], send_sem.at[base + k], recv_sem.at[base + k])
            for k in range(1, len(places))
        ]
        for copy in copies:
            copy.start()
        for copy in copies:
            copy.wait()

    first[0] = in_ref[...]
    exchange(z_places, first, 0)
    for p in range(count):
        i, j = p // half, p % half
        total = jnp.zeros(in_ref.shape[1:], jnp.float32)
        for g in range(half):
            k = g ^ (me // 2)
            total = total + first[k, i * half + (j ^ k)]
        second[0, p] = total
    exchange(rest_places, second, half)
    for p in range(count):
        i, j = p // half, p % half
        total = jnp.zeros(in_ref.shape[1:], jnp.float32)
        for x in range(2):
            for t in range(spots):
                flip = x ^ (me % 2)
                total = total + second[flip * spots + (t ^ spot), (i ^ flip) * half + j]
        out_ref[p] = total
    rows, lanes = in_ref.shape[1:]
    used = lax.broadcasted_iota(jnp.int32, (rows, lanes), 0) < rows - 1
    total = out_ref[0, rows - 1 :, :]
    for g in range(count):
        there = me ^ g
        value = out_ref[(there % 2) * half + there // 2]
        total = total + jnp.sum(jnp.where(used, value * value, 0.0))
    total_ref[...] = jnp.broadcast_to(total, total_ref.shape)


def sum_everywhere(parts):
    half, spots = lax.axis_size("dp") // 2, lax.axis_size("tensor")
    each, lanes = D // (2 * half), parts.shape[2]
    vmem = pl.BlockSpec(memory_space=pltpu.VMEM)
    sem = pltpu.SemaphoreType.DMA
    summed, total = pl.pallas_call(
        functools.partial(sum_kernel, half, spots),
        out_shape=[jax.ShapeDtypeStruct(shape, jnp.float32) for shape in (parts.shape, (8, lanes))],
        in_specs=[vmem],
        out_specs=[vmem, vmem],
        scratch_shapes=[
            pltpu.VMEM((half,) + parts.shape, jnp.float32),
            pltpu.VMEM((2 * spots,) + parts.shape, jnp.float32),
            sem((half + 2 * spots,)),
            sem((half + 2 * spots,)),
        ],
        compiler_params=pltpu.CompilerParams(collective_id=2, has_side_effects=True),
        name="sum_everywhere",
    )(parts)
    return summed[0, : 2 * each // lanes].reshape(2, each), total[0, 0]


def dot_plain(a, b):
    return lax.dot_general(a, b, (((1,), (0,)), ((), ())), preferred_element_type=jnp.float32)


def dot_rows(a, b):
    return lax.dot_general(a, b, (((0,), (0,)), ((), ())), preferred_element_type=jnp.float32)


def dot_cols(a, b):
    return lax.dot_general(a, b, (((1,), (1,)), ((), ())), preferred_element_type=jnp.float32)


def turn(values, tables, direction):
    cosine, low_sine, high_sine = tables
    lanes = values.shape[1]
    half_rot = ROT // 2
    moved = pltpu.roll(values, lanes - half_rot, 1) * low_sine + pltpu.roll(values, half_rot, 1) * high_sine
    return values * cosine + direction * moved


def head_probabilities(query, key, bias):
    scores = dot_cols(query, key) * 0.125 + bias
    exponent = jnp.exp(scores - jnp.max(scores, axis=1, keepdims=True))
    return exponent / jnp.sum(exponent, axis=1, keepdims=True)


def attention_fore(projected, tables_ref, bias_ref, turned_ref, attended_ref):
    spots, _, piece, width = turned_ref.shape
    rows, third = spots * piece, width // 3
    tables = [tables_ref[k] for k in range(3)]
    first = lax.broadcasted_iota(jnp.int32, (rows, 128), 1) < HEAD_DIM
    for pair in range(third // 128):
        span = [slice(k * third + pair * 128, k * third + pair * 128 + 128) for k in range(3)]
        query, key, value = [projected[:, s] for s in span]
        query = turn(query, tables, 1.0).astype(jnp.bfloat16)
        key = turn(key, tables, 1.0).astype(jnp.bfloat16)
        value = value.astype(jnp.bfloat16)
        for s, part in zip(span, (query, key, value)):
            turned_ref[:, 0, :, s] = part.reshape(spots, piece, 128)
        none = jnp.zeros_like(query)
        outs = [
            dot_plain(head_probabilities(q, key, bias_ref[...]).astype(jnp.bfloat16), value)
            for q in (jnp.where(first, query, none), jnp.where(first, none, query))
        ]
        attended_ref[:, 0, :, span[0]] = (
            jnp.where(first, outs[0], outs[1]).astype(jnp.bfloat16).reshape(spots, piece, 128)
        )


def attention_back(turned_ref, d_att_ref, tables_ref, bias_ref, d_project_ref):
    spots, _, piece, width = turned_ref.shape
    rows, third = spots * piece, width // 3
    tables = [tables_ref[k] for k in range(3)]
    first = lax.broadcasted_iota(jnp.int32, (rows, 128), 1) < HEAD_DIM
    for pair in range(third // 128):
        span = [slice(k * third + pair * 128, k * third + pair * 128 + 128) for k in range(3)]
        query, key, value = [turned_ref[:, 0, :, s].reshape(rows, 128) for s in span]
        d_att = d_att_ref[:, 0, :, span[0]].reshape(rows, 128)
        none = jnp.zeros_like(query)
        parts = []
        for head in range(2):
            keep = first if head == 0 else jnp.logical_not(first)
            one_query = jnp.where(keep, query, none)
            one_d_att = jnp.where(keep, d_att, none)
            prob = head_probabilities(one_query, key, bias_ref[...])
            d_value = dot_rows(prob.astype(jnp.bfloat16), d_att)
            d_prob = dot_cols(one_d_att, value)
            d_score = (prob * (d_prob - jnp.sum(d_prob * prob, axis=1, keepdims=True))).astype(
                jnp.bfloat16
            )
            parts.append((dot_plain(d_score, key), dot_rows(d_score, query), d_value))
        joined = [jnp.where(first, one, two) for one, two in zip(*parts)]
        done = (turn(0.125 * joined[0], tables, -1.0), turn(0.125 * joined[1], tables, -1.0), joined[2])
        for s, part in zip(span, done):
            d_project_ref[:, 0, :, s] = part.astype(jnp.bfloat16).reshape(spots, piece, 128)


def join_gate_up(packed, whole):
    last = packed[:, 2 * whole :]
    gate = jnp.concatenate([packed[:, :whole], last], axis=1)
    up = jnp.concatenate([packed[:, whole : 2 * whole], pltpu.roll(last, 64, 1)], axis=1)
    return gate, up


def units_fore(normed, weight):
    packed = dot_plain(normed, weight)
    units = weight.shape[1] // 2
    gate, up = join_gate_up(packed, units - 64)
    return packed, (gate * jax.nn.sigmoid(gate) * up).astype(jnp.bfloat16)[:, :units]


def units_back(cot, down, packed):
    units = down.shape[0]
    whole = units - 64
    d_hid = dot_cols(cot, down).astype(jnp.bfloat16).astype(jnp.float32)
    d_hid = jnp.concatenate([d_hid, jnp.zeros((d_hid.shape[0], 64), jnp.float32)], axis=1)
    gate, up = join_gate_up(packed, whole)
    sigmoid_gate = jax.nn.sigmoid(gate)
    d_gate = d_hid * up * (sigmoid_gate * (1.0 + gate * (1.0 - sigmoid_gate)))
    d_up = d_hid * (gate * sigmoid_gate)
    first = lax.broadcasted_iota(jnp.int32, (gate.shape[0], 128), 1) < 64
    last = jnp.where(first, d_gate[:, whole:], pltpu.roll(d_up[:, whole:], 64, 1))
    parts = [d_gate[:, :whole], d_up[:, :whole], last]
    return jnp.concatenate([part.astype(jnp.bfloat16) for part in parts], axis=1)


KERNEL_PARAMS = pltpu.CompilerParams(vmem_limit_bytes=40 * 1024 * 1024)


def adam_update(weight_old, gradient, moment_old, square_old, factor, rate, decay):
    clipped = gradient * factor
    moment_new = BETA_ONE * moment_old + (1.0 - BETA_ONE) * clipped
    square_new = BETA_TWO * square_old + (1.0 - BETA_TWO) * clipped * clipped
    moment_hat = moment_new / (1.0 - BETA_ONE**STEP)
    square_hat = square_new / (1.0 - BETA_TWO**STEP)
    weight_new = weight_old - rate * (
        moment_hat / (jnp.sqrt(square_hat) + ADAM_EPS) + decay * weight_old
    )
    return (weight_new, moment_new, square_new)


def local(
    tokens,
    cotangent,
    project_weight,
    output_weight,
    gate_up_weight,
    down_weight,
    norm_params,
    first_project,
    first_output,
    first_gate_up,
    first_down,
    first_norm,
    second_project,
    second_output,
    second_gate_up,
    second_down,
    second_norm,
):
    count = lax.axis_size("dp")
    blocks_half = count // 2
    me = lax.axis_index("dp")
    side = (me // 2) % 2
    spot = lax.axis_index("tensor")
    spots = lax.axis_size("tensor")
    micro_count, piece = tokens.shape[0], tokens.shape[1]
    head_cols = project_weight.shape[2] // 2
    unit_cols = gate_up_weight.shape[2] // 2
    whole = unit_cols - 64
    rows_each = project_weight.shape[1]
    seqs = 2 * micro_count
    rows_all = spots * seqs * piece

    by_columns = rows_each % 128 == 0

    by_columns = rows_each % 128 == 0

    norm_low = norm_params.astype(jnp.bfloat16)
    tok_rel, unit_rows, cot_low, cot_flipped, *weight_pairs, own_gains, tables, bias = run_prepare(
        tokens,
        cotangent,
        (project_weight, gate_up_weight, down_weight, output_weight),
        norm_params,
        jnp.asarray(angle_tables(spots * piece)),
    )
    if not by_columns:
        weight_pairs[2:] = [pair.swapaxes(1, 2) for pair in weight_pairs[2:]]

    (
        w_project,
        w_gate_up,
        w_down,
        w_output,
        gains,
        _,
        all_cot,
        normed_t,
        packed,
        hidden,
        attended,
        turned,
        hidden_t,
        attended_t,
        *stage,
    ) = run_forward(
        blocks_half,
        by_columns,
        weight_pairs,
        own_gains,
        unit_rows,
        cot_low,
        cot_flipped,
        tables,
        bias,
        (spots, seqs, piece),
    )
    gains = gains.reshape(count, 8, rows_each).transpose(1, 0, 2).reshape(8, D)
    if not by_columns:
        w_down, w_output = w_down.T, w_output.T
    pairs, normed_parts, out_parts = run_backward(
        blocks_half,
        by_columns,
        (all_cot, packed, hidden, attended, turned),
        (normed_t, attended_t, hidden_t),
        (w_project, w_gate_up, w_down, w_output),
        tables,
        bias,
        stage[:2],
    )
    if not by_columns:
        pairs[:2] = [(own.T, came.swapaxes(1, 2)) for own, came in pairs[:2]]
    weight_grads, input_grad, shares = run_join_grads(
        blocks_half,
        pairs,
        [*normed_parts, tok_rel, cot_low, gains],
        [output_weight.shape, down_weight.shape, gate_up_weight.shape, project_weight.shape],
        (head_cols, whole),
    )
    norm_grad, square_total = sum_everywhere(shares)
    grads = (weight_grads[3], weight_grads[0], weight_grads[2], weight_grads[1], norm_grad)
    norm_total = jnp.sqrt(square_total)
    (layer_out,) = run_finish(finish_out, rows_each, [*out_parts, tok_rel], [], 0)
    limit = 0.03 * math.sqrt((4 * D * D + 3 * D * FF + 2 * D) * micro_count * count * SEQ)
    factor = jnp.minimum(1.0, limit / (norm_total + 1e-06))
    rates = (
        2.0 / math.sqrt(D),
        2.0 / math.sqrt(D // 32),
        2.0 / math.sqrt(D),
        2.0 / math.sqrt(FF),
        0.5,
    )
    decays = (0.1, 0.1, 0.1, 0.1, 0.0)
    masters = (project_weight, output_weight, gate_up_weight, down_weight, norm_params)
    firsts = (first_project, first_output, first_gate_up, first_down, first_norm)
    seconds = (second_project, second_output, second_gate_up, second_down, second_norm)
    updated = [
        adam_update(*parts) for parts in zip(masters, grads, firsts, seconds, [factor] * 5, rates, decays)
    ]
    return (
        layer_out,
        input_grad,
        *grads,
        norm_total,
        *[u[0] for u in updated],
        *[u[1] for u in updated],
        *[u[2] for u in updated],
    )


def solution(mesh):
    wide = P("dp", "tensor", None)
    stacked = P(None, "dp", "tensor")
    tall = P("tensor", "dp")
    params = (stacked, tall, stacked, tall, P(None, "dp"))
    return jax.shard_map(
        local,
        mesh=mesh,
        in_specs=(wide, wide, *params, *params, *params),
        out_specs=(wide, wide, *params, P(), *params, *params, *params),
        check_vma=False,
    )
```

```python
import functools
import math

import jax
import jax.numpy as jnp
import numpy as np
from jax import lax
from jax.experimental import pallas as pl
from jax.experimental.pallas import tpu as pltpu
from jax.sharding import PartitionSpec as P

D = 2048
HEAD_DIM = 64
FF = 5632
SEQ = 320
STEP = 10
ROT = 16

BETA_ONE = 0.9
BETA_TWO = 0.999
ADAM_EPS = 1e-08
NORM_EPS = 1e-05
MASK_FILL = -1e30

BOTH = ("dp", "tensor")
MESH = pl.DeviceIdType.MESH


def block_order(count):
    return [2 * j + i for i in range(2) for j in range(count // 2)]


def relative(values, axis, me, count):
    width = values.shape[axis] // count
    return jnp.concatenate(
        [lax.dynamic_slice_in_dim(values, (me ^ r) * width, width, axis) for r in block_order(count)],
        axis=axis,
    )


def from_relative(values, axis, me, count):
    width = values.shape[axis] // count
    places = [((me ^ g) % 2) * (count // 2) + (me ^ g) // 2 for g in range(count)]
    return jnp.concatenate(
        [lax.dynamic_slice_in_dim(values, place * width, width, axis) for place in places],
        axis=axis,
    )


def place(dp_flip, tensor_flip):
    return (lax.axis_index("dp") ^ dp_flip, lax.axis_index("tensor") ^ tensor_flip)


def greet(places):
    barrier = pltpu.get_barrier_semaphore()
    for there in places:
        pl.semaphore_signal(barrier, inc=1, device_id=there, device_id_type=MESH)
    pl.semaphore_wait(barrier, len(places))


def send_to(there, source, target, send_sem, recv_sem):
    return pltpu.make_async_remote_copy(
        src_ref=source,
        dst_ref=target,
        send_sem=send_sem,
        recv_sem=recv_sem,
        device_id=there,
        device_id_type=MESH,
    )


def group_places(half):
    return [place(2 * j, 0) for j in range(1, half)] + [place(1, 0), place(0, 2), place(0, 1)]


def forward(half, by_columns, *refs):
    def take(count):
        nonlocal refs
        head, refs = refs[:count], refs[count:]
        return head

    project_pair, gate_up_pair, down_pair, output_pair = take(4)
    gains_own, unit_rows, cot_own, cot_flipped, tables, bias = take(6)
    w_project, w_gate_up, w_down, w_output, gains = take(5)
    normed, cot, normed_t, packed, hidden, attended, turned, logs, hidden_t, attended_t = take(10)
    stage = take(2)
    normed_own, normed_flipped = take(2)
    z_send, z_recv, x_send, x_recv, a_send, a_recv = refs
    greet(group_places(half))

    spots, seqs, piece, _ = cot.shape
    units, heads = hidden.shape[-1], attended.shape[-1]
    each = D // (2 * half)
    rows_all = spots * seqs * piece
    every = lambda ref: pl.BlockSpec(ref.shape, lambda *g: (0,) * len(ref.shape))

    def row_chunk(out, mine, other, share=0, shares=1):
        size = mine.shape[0] // shares
        rows = pl.ds(share * size, size)
        return mine.at[rows], other.at[rows], lambda p: out.at[pl.ds(p * mine.shape[0] + share * size, size)]

    def column_chunk(out, mine, other, share=0, shares=1):
        size = mine.shape[0] // shares
        rows, width = pl.ds(share * size, size), mine.shape[1]
        return mine.at[rows], other.at[rows], lambda p: out.at[rows, pl.ds(p * width, width)]

    out_chunk = column_chunk if by_columns else row_chunk
    pair = lambda ref: (ref.at[0], ref.at[1])
    chunks = [
        row_chunk(gains, gains_own, gains_own),
        row_chunk(w_project, *pair(project_pair)),
        row_chunk(w_gate_up, *pair(gate_up_pair), 0, 2),
        row_chunk(w_gate_up, *pair(gate_up_pair), 1, 2),
        out_chunk(w_down, *pair(down_pair), 0, 2),
        out_chunk(w_output, *pair(output_pair)),
        out_chunk(w_down, *pair(down_pair), 1, 2),
    ]
    GAINS, PROJECT, GATE_UP, DOWN, OUTPUT = 0, 1, 2, 4, 5
    n = len(chunks)
    far = range(1, half)

    def z_copy(c, j):
        mine, other, block = chunks[c]
        return send_to(place(2 * j, 0), other if j % 2 else mine, block(j), z_send.at[c, j], z_recv.at[c, j])

    def x_copy(c, j):
        mine, _, block = chunks[c]
        return send_to(place(1, 0), block(j) if j else mine, block(half + j), x_send.at[c, j], x_recv.at[c, j])

    def start_z(c):
        if c < n:
            for j in far:
                z_copy(c, j).start()

    def start_own(c):
        if c < n:
            x_copy(c, 0).start()

    def keep(sources, outs, blocks, steps):
        def body(*refs):
            for ref, out_ref in zip(refs, refs[len(sources) :]):
                put(out_ref, ref[...])

        pltpu.emit_pipeline(
            body, grid=(steps,), in_specs=[block[0] for block in blocks], out_specs=[block[1] for block in blocks]
        )(*sources, *outs)

    def keep_weights():
        pairs = (project_pair, gate_up_pair, down_pair, output_pair)
        sizes = [(ref.shape[1] // 2, ref.shape[2]) for ref in pairs]
        blocks = [(blocked((1,) + size, 0, step(), 0), blocked(size, step(), 0)) for size in sizes]
        keep(pairs, (w_project, w_gate_up, w_down, w_output), blocks, 2)

    def keep_cot():
        lead = blocked((1, piece, D), step(), 0, 0)
        keep((cot_own,), (cot,), [(lead, blocked((1, 1, piece, D), 0, step(), 0, 0))], seqs // 2)

    def serve(c):
        for j in far:
            z_copy(c, j).wait_recv()
            x_copy(c, j).start()
            if c + 1 < n and c != GAINS:
                z_copy(c + 1, j).start()
        if c > GAINS:
            start_own(c + 2)

    def have(*which):
        for c in which:
            for j in range(half):
                x_copy(c, j).wait_recv()

    act_own, act_flipped, act_out = (normed_own, cot_own), (normed_flipped, cot_flipped), (normed, cot)

    def rows(a, index):
        micro = seqs // 2
        return act_out[a].at[index // 2, pl.ds((index % 2) * micro, micro)]

    def a_copy(a, k):
        source = (act_flipped[a], act_own[a], rows(a, 1), act_own[a], rows(a, 1), rows(a, 2), rows(a, 3))[k]
        there = place(2, 0) if k == 0 else place(0, 2) if k < 3 else place(0, 1)
        return send_to(there, source, rows(a, k + 1), a_send.at[a, k], a_recv.at[a, k])

    def act_begin(a):
        for k in (0, 1, 3):
            a_copy(a, k).start()

    def act_z(a):
        a_copy(a, 0).wait_recv()
        a_copy(a, 2).start()
        a_copy(a, 4).start()

    def act_y(a):
        a_copy(a, 1).wait_recv()
        a_copy(a, 5).start()
        a_copy(a, 2).wait_recv()
        a_copy(a, 6).start()

    def act_have(a):
        for k in range(3, 7):
            a_copy(a, k).wait_recv()

    def norm_step():
        def body(unit_ref, gains_ref, out_ref, flipped_ref, kept_ref):
            gain, shift = [
                jnp.concatenate([gains_ref[p * 8 + k : p * 8 + k + 1] for p in range(2 * half)], axis=1)
                for k in range(2)
            ]
            value = unit_ref[0] * gain + shift
            put(out_ref, value)
            put(flipped_ref, flip_lanes(value, each))
            put(kept_ref, value)

        block = blocked((1, piece, D), step(), 0, 0)
        kept = blocked((1, 1, piece, D), 0, step(), 0, 0)
        pltpu.emit_pipeline(
            body, grid=(seqs // 2,), in_specs=[block, every(gains)], out_specs=[block, block, kept]
        )(unit_rows, gains, normed_own, normed_flipped, normed)

    def attention_step(first, count):
        block = lambda width: blocked((spots, 1, piece, width), 0, step(first), 0, 0)

        def body(normed_ref, weight_ref, *refs):
            attention_fore(dot_plain(flat(normed_ref), weight_ref[...]), *refs)

        pltpu.emit_pipeline(
            body,
            grid=(count,),
            in_specs=[block(D), every(w_project), every(tables), every(bias)],
            out_specs=[block(3 * heads), block(heads), block(128)],
        )(normed, w_project, tables, bias, turned, attended, logs)

    def turn_over(source, out, in_block, out_block, steps):
        def body(ref, out_ref):
            put(out_ref, flat(ref).T)

        pltpu.emit_pipeline(body, grid=(steps,), in_specs=[in_block], out_specs=[out_block])(source, out)

    def units_step(first, count):
        tile = lambda width: blocked((1, seqs, piece, width), step(first), 0, 0, 0)

        def body(normed_ref, weight_ref, packed_ref, hidden_ref):
            value, units_value = units_fore(flat(normed_ref), weight_ref[...])
            put(packed_ref, value)
            put(hidden_ref, units_value)

        pltpu.emit_pipeline(
            body,
            grid=(count,),
            in_specs=[tile(D), every(w_gate_up)],
            out_specs=[tile(2 * units), tile(units)],
        )(normed, w_gate_up, packed, hidden)

    def grads_step():
        groups, wide = stage[0].shape[0], D // (2 * stage[0].shape[0])

        def body(cot_ref, attended_ref, hidden_ref, *out_refs):
            block = flat(cot_ref)
            for ref, out_ref in zip((attended_ref, hidden_ref), out_refs):
                value = dot_plain(ref[...], block)
                put(out_ref, value if by_columns else value.T)

        pltpu.emit_pipeline(
            body,
            grid=(groups,),
            in_specs=[
                blocked((spots, seqs, piece, wide), 0, 0, 0, step(groups)),
                every(attended_t),
                every(hidden_t),
            ],
            out_specs=[blocked((1,) + ref.shape[1:], step(), 0, 0) for ref in stage],
        )(cot, attended_t, hidden_t, *stage)

    start_z(GAINS)
    start_z(PROJECT)
    start_own(GAINS)
    keep((gains_own,), (gains,), [(every(gains_own), blocked(gains_own.shape, 0, 0))], 1)
    serve(GAINS)
    have(GAINS)
    start_own(PROJECT)
    start_own(GATE_UP)
    norm_step()
    act_begin(0)
    keep_weights()
    keep_cot()
    serve(PROJECT)
    act_z(0)
    act_y(0)
    act_begin(1)
    act_have(0)
    have(PROJECT)
    serve(GATE_UP)
    attention_step(0, seqs)
    act_z(1)
    turn_over(attended, attended_t, every(attended), every(attended_t), 1)
    serve(GATE_UP + 1)
    columns = lambda index: blocked((spots, seqs, piece, 256), 0, 0, 0, index)
    turn_over(normed, normed_t, columns(step()), blocked((256, rows_all), step(), 0), D // 256)
    act_y(1)
    serve(DOWN)
    have(GATE_UP, GATE_UP + 1)
    units_step(0, spots // 2)
    serve(OUTPUT)
    units_step(spots // 2, spots - spots // 2)
    serve(n - 1)
    turn_over(hidden, hidden_t, every(hidden), every(hidden_t), 1)
    act_have(1)
    grads_step()
    have(DOWN, OUTPUT, n - 1)
    for c in range(n):
        for j in range(half):
            if j:
                z_copy(c, j).wait_send()
            x_copy(c, j).wait_send()
    for a in range(2):
        for k in range(7):
            a_copy(a, k).wait_send()


def run_forward(half, by_columns, pairs, gains, unit_rows, cot, cot_flipped, tables, bias, group):
    low, full = jnp.bfloat16, jnp.float32
    each, heads, units = pairs[0].shape[1], pairs[0].shape[2] // 3, pairs[1].shape[2] // 2
    spots, seqs, piece = group
    rows_all = spots * seqs * piece
    groups = min(half, 4)
    wide = D // (2 * groups)
    widths = (heads, units)
    flat_stage = [(groups, w, wide) if by_columns else (groups, wide, w) for w in widths]
    across = [(w, D) if by_columns else (D, w) for w in (units, heads)]
    shapes = [
        ((D, 3 * heads), low),
        ((D, 2 * units), low),
        *[(shape, low) for shape in across],
        ((2 * half * 8, each), full),
        (group + (D,), low),
        (group + (D,), low),
        ((D, rows_all), low),
        (group + (2 * units,), full),
        (group + (units,), low),
        (group + (heads,), low),
        (group + (3 * heads,), low),
        (group + (128,), full),
        ((units, rows_all), low),
        ((heads, rows_all), low),
        *[(shape, low) for shape in flat_stage],
        (cot.shape, low),
        (cot.shape, low),
    ]
    ins = [*pairs, gains, unit_rows, cot, cot_flipped, tables, bias]
    anywhere = pl.BlockSpec(memory_space=pl.ANY)
    sem = pltpu.SemaphoreType.DMA
    return pl.pallas_call(
        functools.partial(forward, half, by_columns),
        out_shape=[jax.ShapeDtypeStruct(*shape) for shape in shapes],
        in_specs=[anywhere] * len(ins),
        out_specs=[anywhere] * len(shapes),
        scratch_shapes=[sem((7, half))] * 4 + [sem((2, 7))] * 2,
        compiler_params=pltpu.CompilerParams(
            collective_id=0, has_side_effects=True, vmem_limit_bytes=56 * 1024 * 1024
        ),
        name="forward",
    )(*ins)


def angle_tables(length):
    half_rot = ROT // 2
    angles = np.arange(length)[:, None] * (10000.0 ** (-2.0 * np.arange(half_rot) / ROT))[None, :]
    cosine, sine = np.cos(angles), np.sin(angles)
    none = np.zeros_like(sine)
    rest = np.zeros((length, HEAD_DIM - ROT))
    rows = ((cosine, cosine, rest + 1.0), (-sine, none, rest), (none, sine, rest))
    return np.stack([np.tile(np.concatenate(parts, axis=1), (1, 2)) for parts in rows]).astype(np.float32)


def prepare(each, in_place, *refs):
    tokens, cot, project, gate_up, down, output, params, angles = refs[:8]
    tok_ref, unit_ref, cot_ref, cot_flipped_ref, project_ref, gate_up_ref, down_ref, output_ref = refs[8:16]
    gains_ref, tables_ref, bias_ref = refs[16:]
    me = lax.axis_index("dp")
    gains_ref[...] = jnp.zeros_like(gains_ref)
    gains_ref[0:2] = params[...].astype(jnp.bfloat16).astype(jnp.float32)
    piece, shape = tokens.shape[1], bias_ref.shape
    places = [lax.broadcasted_iota(jnp.int32, shape, axis) for axis in range(2)]
    positions = list(places)
    for k, flip in enumerate((0, 2, 1, 3)):
        spot = lax.axis_index("tensor") ^ flip
        tables_ref[:, k * piece : (k + 1) * piece] = angles[:, pl.ds(pl.multiple_of(spot * piece, piece), piece)]
        for axis, value in enumerate(places):
            inside = jnp.logical_and(value >= k * piece, value < (k + 1) * piece)
            positions[axis] = jnp.where(inside, value + (spot - k) * piece, positions[axis])
    bias_ref[...] = jnp.where(positions[0] >= positions[1], 0.0, MASK_FILL)
    side = (me // 2) % 2
    blocks = block_order(D // each)
    if in_place:
        for p, r in enumerate(blocks):
            span, flipped = slice(p * each, (p + 1) * each), slice((p ^ 1) * each, ((p ^ 1) + 1) * each)
            there = pl.ds(pl.multiple_of((me ^ r) * each, each), each)
            tok_ref[:, :, span] = tokens[:, :, there]
            cot_ref[:, :, span] = cot[:, :, there]
            cot_flipped_ref[:, :, flipped] = cot[:, :, there]
    else:
        tok_ref[...] = tokens[...]
        cot_ref[...] = cot[...]
        for s in range(cot.shape[0]):
            put(cot_flipped_ref.at[s], flip_lanes(cot[s].astype(jnp.float32), each))
    for s in range(tokens.shape[0]):
        unit_ref[s], _ = norm_rows(tok_ref[s].astype(jnp.float32))
    heads, units = output.shape[0] // 2, down.shape[0] // 2
    whole = units - 64
    for h, s in enumerate((side, 1 - side)):
        part = lambda width, start=0: pl.ds(start + pl.multiple_of(s * width, width), width)
        for k in range(3):
            put(project_ref.at[h, :, pl.ds(k * heads, heads)], project[k, :, part(heads)])
        for k in range(2):
            put(gate_up_ref.at[h, :, pl.ds(k * whole, whole)], gate_up[k, :, part(whole)])
        put(output_ref.at[h], output[part(heads)])
        put(down_ref.at[h, pl.ds(0, whole)], down[part(whole)])
        put(down_ref.at[h, pl.ds(whole, 64)], down[part(64, 2 * whole)])
    gate, up = gate_up[0, :, 2 * whole :], gate_up[1, :, 2 * whole :]
    first = lax.broadcasted_iota(jnp.int32, gate.shape, 1) < 64
    zero = jnp.where(first, gate, pltpu.roll(up, 64, 1))
    one = jnp.where(first, pltpu.roll(gate, 64, 1), up)
    put(gate_up_ref.at[0, :, pl.ds(2 * whole, 128)], jnp.where(side == 0, zero, one))
    put(gate_up_ref.at[1, :, pl.ds(2 * whole, 128)], jnp.where(side == 0, one, zero))


def whole_spec(shape):
    return pl.BlockSpec(shape, lambda *_: (0,) * len(shape))


def run_prepare(tokens, cot, weights, params, angles):
    project, gate_up, down, output = weights
    each = project.shape[1]
    in_place = each % 128 == 0
    if not in_place:
        me, count = lax.axis_index("dp"), D // each
        tokens, cot = relative(tokens, 2, me, count), relative(cot, 2, me, count)
    low = jnp.bfloat16
    heads, units = output.shape[0] // 2, down.shape[0] // 2
    shapes = [(tokens.shape, low), (tokens.shape, jnp.float32), (cot.shape, low), (cot.shape, low)]
    shapes += [((2, each, 3 * heads), low), ((2, each, 2 * units), low)]
    shapes += [((2, units, each), low), ((2, heads, each), low)]
    length = angles.shape[1]
    shapes += [((8, each), jnp.float32), (angles.shape, jnp.float32), ((length, length), jnp.float32)]
    ins = [tokens, cot, project, gate_up, down, output, params, angles]
    return pl.pallas_call(
        functools.partial(prepare, each, in_place),
        grid=(1,),
        in_specs=[whole_spec(value.shape) for value in ins],
        out_specs=[whole_spec(shape) for shape, _ in shapes],
        out_shape=[jax.ShapeDtypeStruct(*shape) for shape in shapes],
        compiler_params=pltpu.CompilerParams(vmem_limit_bytes=60 * 1024 * 1024),
        name="prepare",
    )(*ins)


def flat(ref):
    value = ref[...]
    return value.reshape(-1, value.shape[-1])


def put(ref, value):
    ref[...] = value.astype(ref.dtype).reshape(ref.shape)


def blocked(shape, *index):
    return pl.BlockSpec(shape, lambda g: tuple(i(g) if callable(i) else i for i in index))


def step(offset=0):
    return lambda g: g + offset


def backward(half, by_columns, window, *refs):
    def take(count):
        nonlocal refs
        head, refs = refs[:count], refs[count:]
        return head

    cot, packed, hidden, attended, turned, logs = take(6)
    normed_t, attended_t_all, hidden_t_all = take(3)
    w_project, w_gate_up, w_down, w_output, tables, bias = take(6)
    stage_out = take(2)
    z_in, mine = take(4), take(4)
    act_away, act_near, core_in, y_out, y_in, far_out = [take(2) for _ in range(6)]
    act_far, act_sum = take(1), take(2)
    stage, x_in = stage_out + take(2), take(4)
    d_packed, d_att, d_project, attended_t, hidden_t, normed_block, cot_block = take(7)
    x_send, x_recv, z_send, z_recv, a_send, a_recv, load_sem, block_sem = refs
    greet(group_places(half))

    spots, seqs, piece, _ = cot.shape
    units, heads = hidden.shape[-1], attended.shape[-1]
    groups = stage[0].shape[0]
    per = half // groups
    wide = D // (2 * groups)
    every = lambda ref: pl.BlockSpec(ref.shape, lambda g: (0,) * len(ref.shape))

    whole = (attended_t, hidden_t, d_packed, d_project)

    def product(c, block, whole_ref):
        if c >= 2:
            return dot_plain(block, flat(whole_ref))
        value = dot_plain(whole_ref[...], block)
        return value if by_columns else value.T

    def block_copy(index):
        c, g = order[index]
        span, slot = pl.ds(g * wide, wide), index % 2
        if c >= 2:
            source, target = normed_t.at[span], normed_block.at[slot]
        else:
            source, target = cot.at[:, :, :, span], cot_block.at[slot]
        return pltpu.make_async_copy(source, target, block_sem.at[slot])

    def x_copy(c, g):
        return send_to(place(1, 0), stage[c].at[g], x_in[c].at[g], x_send.at[c, g], x_recv.at[c, g])

    def z_copy(c, j):
        source = x_in[c].at[j // per]
        if per > 1:
            rows = z_in[c].shape[1]
            source = source.at[pl.ds((j % per) * rows, rows)]
        return send_to(place(2 * j, 0), source, z_in[c].at[j], z_send.at[c, j], z_recv.at[c, j])

    def a_copy(a, s):
        source = (act_away[a], y_out[a], far_out[a])[s]
        target = (core_in[a], y_in[a], act_far[0])[s]
        there = (place(0, 1), place(0, 2), place(2, 0))[s]
        return send_to(there, source, target, a_send.at[a, s], a_recv.at[a, s])

    order = [(0, 3), (0, 2), (1, 3), (1, 2), (2, 3), (1, 1), (0, 1), (2, 2), (2, 1)]
    order += [(3, g) for g in (3, 2, 1)] + [(c, 0) for c in (2, 1, 3, 0)]
    started, served, ready = [0], [0], {0, 1}

    def start_x():
        while started[0] < min(served[0] + window, len(order)) and order[started[0]][0] in ready:
            x_copy(*order[started[0]]).start()
            started[0] += 1

    def away_product(c):
        def body(block_ref, whole_ref, out_ref):
            put(out_ref, product(c, block_ref[...], whole_ref))

        pltpu.emit_pipeline(
            body,
            grid=(groups,),
            in_specs=[blocked((wide, normed_t.shape[1]), step(groups), 0), every(whole[c])],
            out_specs=[blocked((1,) + stage[c].shape[1:], step(), 0, 0)],
        )(normed_t, whole[c], stage[c])
        ready.add(c)
        start_x()

    def serve(count):
        for _ in range(count):
            index = served[0]
            c, g = order[index]
            served[0] += 1
            block_copy(index).wait()
            if served[0] < len(order):
                block_copy(served[0]).start()
            x_copy(c, g).wait_recv()
            start_x()
            block = flat((normed_block if c >= 2 else cot_block).at[index % 2])
            total = product(c, block, whole[c]) + x_in[c][g].astype(jnp.float32)
            if g == 0:
                mine[c][0] = total
            if g > 0 or per > 1:
                put(x_in[c].at[g], total)
            for j in range(g * per, (g + 1) * per):
                if j:
                    z_copy(c, j).start()

    def units_step(first, count):
        tile = (1, seqs, piece)

        def body(cot_ref, down_ref, output_ref, packed_ref, d_packed_ref, d_att_ref):
            rows = flat(cot_ref)
            d_packed_ref[...] = units_back(rows, down_ref[...], flat(packed_ref)).reshape(d_packed_ref.shape)
            put(d_att_ref, dot_cols(rows, output_ref[...]))

        pltpu.emit_pipeline(
            body,
            grid=(count,),
            in_specs=[
                blocked(tile + (D,), step(first), 0, 0, 0),
                every(w_down),
                every(w_output),
                blocked(tile + (2 * units,), step(first), 0, 0, 0),
            ],
            out_specs=[
                blocked(tile + (2 * units,), step(first), 0, 0, 0),
                blocked(tile + (heads,), step(first), 0, 0, 0),
            ],
        )(cot, w_down, w_output, packed, d_packed, d_att)

    def attention_step(first, count):
        block = lambda width: blocked((spots, 1, piece, width), 0, step(first), 0, 0)
        pltpu.emit_pipeline(
            attention_back,
            grid=(count,),
            in_specs=[block(3 * heads), block(heads), block(128), every(tables), every(bias)],
            out_specs=[block(3 * heads)],
        )(turned, d_att, logs, tables, bias, d_project)

    def two_cores(away_ref, near_ref, total):
        middle = total.shape[0] // 2
        put(near_ref, total[:middle])
        put(away_ref, total[middle:])

    def core_block(first):
        return blocked((spots // 2, seqs, piece, 512), 0, 0, 0, step(first))

    def normed_step():
        def body(d_project_ref, d_packed_ref, project_ref, gate_up_ref, away_ref, near_ref):
            total = dot_cols(flat(d_project_ref), project_ref[...])
            two_cores(away_ref, near_ref, total + dot_cols(flat(d_packed_ref), gate_up_ref[...]))

        pltpu.emit_pipeline(
            body,
            grid=(D // 512,),
            in_specs=[
                every(d_project),
                every(d_packed),
                blocked((512, 3 * heads), step(), 0),
                blocked((512, 2 * units), step(), 0),
            ],
            out_specs=[core_block(0)] * 2,
        )(d_project, d_packed, w_project, w_gate_up, act_away[0], act_near[0])

    def out_step(first, count):
        def body(attended_ref, hidden_ref, output_ref, down_ref, away_ref, near_ref):
            total = dot_plain(flat(attended_ref), output_ref[...])
            two_cores(away_ref, near_ref, total + dot_plain(flat(hidden_ref), down_ref[...]))

        pltpu.emit_pipeline(
            body,
            grid=(count,),
            in_specs=[
                every(attended),
                every(hidden),
                blocked((heads, 512), 0, step(first)),
                blocked((units, 512), 0, step(first)),
            ],
            out_specs=[core_block(first)] * 2,
        )(attended, hidden, w_output, w_down, act_away[1], act_near[1])

    def add_terms(*refs):
        *terms, out_ref = refs
        put(out_ref, sum(flat(term).astype(jnp.float32) for term in terms))

    half_seqs = seqs // 2

    def core_arrived(a):
        a_copy(a, 0).wait_recv()
        rows = blocked((1, half_seqs, piece, D), 1, step(), 0, 0)
        pltpu.emit_pipeline(
            add_terms,
            grid=(2,),
            in_specs=[rows, rows],
            out_specs=[blocked((half_seqs, piece, D), step(), 0, 0)],
        )(act_near[a], core_in[a], y_out[a])
        a_copy(a, 1).start()

    def y_arrived(a):
        def body(*refs):
            add_terms(*refs[:3], refs[6])
            add_terms(*refs[3:6], refs[7])

        def both(shape, *lead):
            return [blocked(shape, *lead, step(first), 0, 0) for first in (half_seqs, 0)]

        rows, lines = both((1, 1, piece, D), 0), both((1, piece, D))
        a_copy(a, 1).wait_recv()
        pltpu.emit_pipeline(
            body,
            grid=(half_seqs,),
            in_specs=[rows[0], rows[0], lines[0], rows[1], rows[1], lines[1]],
            out_specs=[blocked((1, piece, D), step(), 0, 0)] * 2,
        )(*[act_near[a], core_in[a], y_in[a]] * 2, far_out[a], act_sum[a])
        if a == 0:
            a_copy(a, 2).start()

    loads = [
        pltpu.make_async_copy(attended_t_all, attended_t, load_sem.at[0]),
        pltpu.make_async_copy(hidden_t_all, hidden_t, load_sem.at[1]),
    ]
    for load in loads:
        load.start()
    block_copy(0).start()
    start_x()
    for load in loads:
        load.wait()
    steps = D // 512
    units_step(0, spots // 2)
    serve(2)
    units_step(spots // 2, spots - spots // 2)
    serve(1)
    away_product(2)
    serve(1)
    attention_step(0, seqs)
    away_product(3)
    serve(3)
    normed_step()
    a_copy(0, 0).start()
    serve(1)
    out_step(0, steps // 2)
    core_arrived(0)
    serve(1)
    out_step(steps // 2, steps - steps // 2)
    a_copy(1, 0).start()
    serve(1)
    core_arrived(1)
    serve(2)
    y_arrived(0)
    serve(len(order) - served[0])
    y_arrived(1)
    for c in range(4):
        for j in range(1, half):
            z_copy(c, j).wait()
        for g in range(groups):
            x_copy(c, g).wait_send()
    for a in range(2):
        for s in range(2):
            a_copy(a, s).wait_send()
    a_copy(0, 2).wait()


def run_backward(half, by_columns, rows, transposed, weights, tables, bias, stage, window=2):
    cot, packed, hidden, attended, turned, _ = rows
    low, full = jnp.bfloat16, jnp.float32
    spots, seqs, piece, _ = cot.shape
    each = D // (2 * half)
    groups = min(half, 4)
    wide = D // (2 * groups)
    widths = (attended.shape[-1], hidden.shape[-1], packed.shape[-1], turned.shape[-1])
    columns = [by_columns and groups == half and c < 2 for c in range(4)]

    def shape_of(count, block):
        return [(count, w, block) if flip else (count, block, w) for w, flip in zip(widths, columns)]

    def row_shape(*lead, kind=low):
        return [jax.ShapeDtypeStruct(lead + (piece, D), kind)] * 2

    shapes = [jax.ShapeDtypeStruct(shape, low) for shape in shape_of(half, each)]
    shapes += [jax.ShapeDtypeStruct(shape, full) for shape in shape_of(1, wide)]
    shapes += row_shape(spots // 2, seqs) * 3 + row_shape(seqs) * 2 + row_shape(seqs // 2)
    shapes += row_shape(seqs // 2)[:1] + row_shape(seqs // 2, kind=full)
    anywhere = pl.BlockSpec(memory_space=pl.ANY)
    vmem = pl.BlockSpec(memory_space=pltpu.VMEM)
    ins = [*rows, *transposed, *weights, tables, bias, *stage]
    sem = pltpu.SemaphoreType.DMA
    rows_all = spots * seqs * piece
    scratch = [pltpu.VMEM(shape, low) for shape in shape_of(groups, wide)[2:] + shape_of(groups, wide)]
    scratch += [pltpu.VMEM(r.shape, low) for r in (packed, attended, turned)]
    scratch += [pltpu.VMEM(t.shape, low) for t in transposed[1:]]
    scratch += [pltpu.VMEM((2, wide, rows_all), low), pltpu.VMEM((2, spots, seqs, piece, wide), low)]
    scratch += [sem((4, groups))] * 2 + [sem((4, half))] * 2 + [sem((2, 3))] * 2 + [sem((2,))] * 2
    outs = pl.pallas_call(
        functools.partial(backward, half, columns[0], window),
        out_shape=shapes,
        in_specs=[anywhere] * len(ins),
        out_specs=[anywhere] * 4 + [vmem] * 4 + [anywhere] * (len(shapes) - 8),
        scratch_shapes=scratch,
        compiler_params=pltpu.CompilerParams(
            collective_id=1, has_side_effects=True, vmem_limit_bytes=60 * 1024 * 1024
        ),
        name="backward",
    )(*ins)
    pairs = []
    for c in range(4):
        own = outs[4 + c][0] if columns[c] else outs[4 + c][0, :each]
        pairs.append((own, outs[c]))
    *_, out_far, normed_far, normed_sum, out_sum = outs
    dp_size, tensor_size = lax.axis_size("dp"), lax.axis_size("tensor")
    partners = [
        (d * tensor_size + t, (d ^ 2) * tensor_size + t) for d in range(dp_size) for t in range(tensor_size)
    ]
    out_far = lax.ppermute(out_far, ("dp", "tensor"), partners)
    return pairs, (normed_far, normed_sum), (out_far, out_sum)


def flip_lanes(values, width):
    lanes = values.shape[1]
    if width % 128 == 0:
        spans = [slice((p ^ 1) * width, ((p ^ 1) + 1) * width) for p in range(lanes // width)]
        return jnp.concatenate([values[:, span] for span in spans], axis=1)
    even = (lax.broadcasted_iota(jnp.int32, values.shape, 1) // width) % 2 == 0
    return jnp.where(even, pltpu.roll(values, lanes - width, 1), pltpu.roll(values, width, 1))


def norm_rows(tok_rows):
    centered = tok_rows - jnp.mean(tok_rows, axis=1, keepdims=True)
    row_scale = lax.rsqrt(jnp.mean(centered * centered, axis=1, keepdims=True) + NORM_EPS)
    return centered * row_scale, row_scale


def put_rows(ref, value, each, in_place):
    value = value.astype(jnp.bfloat16)
    if not in_place:
        ref[0] = value
        return
    me = lax.axis_index("dp")
    for p, r in enumerate(block_order(D // each)):
        span = pl.ds(pl.multiple_of((me ^ r) * each, each), each)
        ref[0, :, span] = value[:, p * each : (p + 1) * each]


def finish_out(each, in_place, far_ref, sum_ref, tok_ref, out_ref):
    summed = flat(sum_ref) + flip_lanes(flat(far_ref).astype(jnp.float32), each)
    put_rows(out_ref, flat(tok_ref).astype(jnp.float32) + summed, each, in_place)


def finish_rows(each, in_place, far_ref, sum_ref, tok_ref, cot_ref, gain, input_ref):
    d_normed = flat(sum_ref) + flip_lanes(flat(far_ref).astype(jnp.float32), each)
    unit_rows, row_scale = norm_rows(flat(tok_ref).astype(jnp.float32))
    d_unit = d_normed * gain
    d_input = row_scale * (
        d_unit
        - jnp.mean(d_unit, axis=1, keepdims=True)
        - unit_rows * jnp.mean(d_unit * unit_rows, axis=1, keepdims=True)
    )
    put_rows(input_ref, flat(cot_ref).astype(jnp.float32) + d_input, each, in_place)
    return jnp.sum(d_normed * unit_rows, axis=0, keepdims=True), jnp.sum(d_normed, axis=0, keepdims=True)


def run_finish(kernel, each, rows, fixed_in, fixed_out):
    in_place = each % 128 == 0
    count, piece, _ = rows[-1].shape
    block = pl.BlockSpec((1, piece, D), lambda s: (s, 0, 0))
    fixed = pl.BlockSpec((8, D), lambda s: (0, 0))
    done, *others = pl.pallas_call(
        functools.partial(kernel, each, in_place),
        grid=(count,),
        in_specs=[block] * len(rows) + [fixed] * len(fixed_in),
        out_specs=[block] + [fixed] * fixed_out,
        out_shape=[jax.ShapeDtypeStruct(rows[-1].shape, jnp.bfloat16)]
        + [jax.ShapeDtypeStruct((8, D), jnp.float32)] * fixed_out,
        compiler_params=KERNEL_PARAMS,
        name=kernel.__name__,
    )(*rows, *fixed_in)
    if not in_place:
        done = from_relative(done, 2, lax.axis_index("dp"), D // each)
    return done, *others


def join_grads(half, spans, *refs):
    own, came = refs[0:8:2], refs[1:8:2]
    far, close, tok, cot, gains = refs[8:13]
    output_ref, down_ref, gate_up_ref, project_ref, input_ref, shares_ref = refs[13:]
    each = D // (2 * half)
    in_place = each % 128 == 0
    parts = [
        finish_rows(each, in_place, *[r.at[pl.ds(k, 1)] for r in (far, close, tok, cot)], gains[0:1], input_ref.at[pl.ds(k, 1)])
        for k in range(tok.shape[0])
    ]
    shares = [sum(values) for values in zip(*parts)]
    side = (lax.axis_index("dp") // 2) % 2
    heads, whole = spans
    squares = jnp.float32(0.0)

    def halves(c, rows, columns):
        nonlocal squares
        pick = lambda j: came[c][j, rows, columns].astype(jnp.float32)
        mine = own[c][rows, columns] + sum(pick(j) for j in range(2, half, 2))
        other = sum(pick(j) for j in range(1, half, 2))
        squares = squares + jnp.sum(mine * mine) + jnp.sum(other * other)
        return mine, other

    def places(width, start=0):
        return [pl.ds(start + pl.multiple_of(s * width, width), width) for s in (side, 1 - side)]

    every = slice(None)
    for value, span in zip(halves(0, every, every), places(heads)):
        output_ref[span] = value
    for value, span in zip(halves(1, slice(0, whole), every), places(whole)):
        down_ref[span] = value
    for value, span in zip(halves(1, slice(whole, whole + 64), every), places(64, 2 * whole)):
        down_ref[span] = value
    for k in range(3):
        for value, span in zip(halves(3, every, slice(k * heads, (k + 1) * heads)), places(heads)):
            project_ref[k, :, span] = value
    for k in range(2):
        for value, span in zip(halves(2, every, slice(k * whole, (k + 1) * whole)), places(whole)):
            gate_up_ref[k, :, span] = value
    mine, other = halves(2, every, slice(2 * whole, 2 * whole + 128))
    zero, one = jnp.where(side == 0, mine, other), jnp.where(side == 0, other, mine)
    first = lax.broadcasted_iota(jnp.int32, zero.shape, 1) < 64
    gate_up_ref[0, :, 2 * whole :] = jnp.where(first, zero, pltpu.roll(one, 64, 1))
    gate_up_ref[1, :, 2 * whole :] = jnp.where(first, pltpu.roll(zero, 64, 1), one)
    if in_place:
        shares_ref[...] = jnp.zeros_like(shares_ref)
        per = each // 128
        for p in range(2 * half):
            for k, share in enumerate(shares):
                for q in range(per):
                    first = p * each + q * 128
                    shares_ref[p, k * per + q : k * per + q + 1] = share[:, first : first + 128]
            shares_ref[p, 7:8] = jnp.full((1, 128), squares)
    else:
        shares_ref[...] = jnp.concatenate(shares + [jnp.full((6, D), squares)], axis=0)


def run_join_grads(half, pairs, rows, shapes, spans):
    each = D // (2 * half)
    in_place = each % 128 == 0
    ins = [part for pair in pairs for part in pair] + rows
    kinds = [(shape, jnp.float32) for shape in shapes] + [(rows[2].shape, jnp.bfloat16)]
    kinds += [((2 * half, 8, 128) if in_place else (8, D), jnp.float32)]
    *grads, input_grad, shares = pl.pallas_call(
        functools.partial(join_grads, half, spans),
        grid=(1,),
        in_specs=[whole_spec(value.shape) for value in ins],
        out_specs=[whole_spec(shape) for shape, _ in kinds],
        out_shape=[jax.ShapeDtypeStruct(*kind) for kind in kinds],
        compiler_params=pltpu.CompilerParams(vmem_limit_bytes=60 * 1024 * 1024),
        name="join_grads",
    )(*ins)
    if not in_place:
        input_grad = from_relative(input_grad, 2, lax.axis_index("dp"), 2 * half)
        blocks = shares.reshape(8, 2 * half, each).transpose(1, 0, 2)
        shares = jnp.concatenate([blocks[:, :2], jnp.zeros_like(blocks[:, :5]), blocks[:, 2:3]], axis=1)
    return grads, input_grad, shares


def sum_kernel(half, spots, in_ref, out_ref, total_ref, first, second, send_sem, recv_sem):
    me, spot = lax.axis_index("dp"), lax.axis_index("tensor")
    z_places = [place(2 * j, 0) for j in range(half)]
    rest = [(i, t) for i in range(2) for t in range(spots)]
    rest_places = [place(i, t) for i, t in rest]
    greet(z_places[1:] + rest_places[1:])
    count = in_ref.shape[0]

    def exchange(places, slots, base):
        copies = [
            send_to(places[k], slots.at[0], slots.at[k], send_sem.at[base + k], recv_sem.at[base + k])
            for k in range(1, len(places))
        ]
        for copy in copies:
            copy.start()
        for copy in copies:
            copy.wait()

    first[0] = in_ref[...]
    exchange(z_places, first, 0)
    for p in range(count):
        i, j = p // half, p % half
        total = jnp.zeros(in_ref.shape[1:], jnp.float32)
        for g in range(half):
            k = g ^ (me // 2)
            total = total + first[k, i * half + (j ^ k)]
        second[0, p] = total
    exchange(rest_places, second, half)
    for p in range(count):
        i, j = p // half, p % half
        total = jnp.zeros(in_ref.shape[1:], jnp.float32)
        for x in range(2):
            for t in range(spots):
                flip = x ^ (me % 2)
                total = total + second[flip * spots + (t ^ spot), (i ^ flip) * half + j]
        out_ref[p] = total
    rows, lanes = in_ref.shape[1:]
    used = lax.broadcasted_iota(jnp.int32, (rows, lanes), 0) < rows - 1
    total = out_ref[0, rows - 1 :, :]
    for g in range(count):
        there = me ^ g
        value = out_ref[(there % 2) * half + there // 2]
        total = total + jnp.sum(jnp.where(used, value * value, 0.0))
    total_ref[...] = jnp.broadcast_to(total, total_ref.shape)


def sum_everywhere(parts):
    half, spots = lax.axis_size("dp") // 2, lax.axis_size("tensor")
    each, lanes = D // (2 * half), parts.shape[2]
    vmem = pl.BlockSpec(memory_space=pltpu.VMEM)
    sem = pltpu.SemaphoreType.DMA
    summed, total = pl.pallas_call(
        functools.partial(sum_kernel, half, spots),
        out_shape=[jax.ShapeDtypeStruct(shape, jnp.float32) for shape in (parts.shape, (8, lanes))],
        in_specs=[vmem],
        out_specs=[vmem, vmem],
        scratch_shapes=[
            pltpu.VMEM((half,) + parts.shape, jnp.float32),
            pltpu.VMEM((2 * spots,) + parts.shape, jnp.float32),
            sem((half + 2 * spots,)),
            sem((half + 2 * spots,)),
        ],
        compiler_params=pltpu.CompilerParams(collective_id=2, has_side_effects=True),
        name="sum_everywhere",
    )(parts)
    return summed[0, : 2 * each // lanes].reshape(2, each), total[0, 0]


def dot_plain(a, b):
    return lax.dot_general(a, b, (((1,), (0,)), ((), ())), preferred_element_type=jnp.float32)


def dot_rows(a, b):
    return lax.dot_general(a, b, (((0,), (0,)), ((), ())), preferred_element_type=jnp.float32)


def dot_cols(a, b):
    return lax.dot_general(a, b, (((1,), (1,)), ((), ())), preferred_element_type=jnp.float32)


def turn(values, tables, direction):
    cosine, low_sine, high_sine = tables
    lanes = values.shape[1]
    half_rot = ROT // 2
    moved = pltpu.roll(values, lanes - half_rot, 1) * low_sine + pltpu.roll(values, half_rot, 1) * high_sine
    return values * cosine + direction * moved


def head_scores(query, key, bias):
    return dot_cols(query, key) * 0.125 + bias


def attention_fore(projected, tables_ref, bias_ref, turned_ref, attended_ref, logs_ref):
    spots, _, piece, width = turned_ref.shape
    rows, third = spots * piece, width // 3
    tables = [tables_ref[k] for k in range(3)]
    lane = lax.broadcasted_iota(jnp.int32, (rows, 128), 1)
    first, logs = lane < HEAD_DIM, jnp.zeros((rows, 128), jnp.float32)
    for pair in range(third // 128):
        span = [slice(k * third + pair * 128, k * third + pair * 128 + 128) for k in range(3)]
        query, key, value = [projected[:, s] for s in span]
        query = turn(query, tables, 1.0).astype(jnp.bfloat16)
        key = turn(key, tables, 1.0).astype(jnp.bfloat16)
        value = value.astype(jnp.bfloat16)
        for s, part in zip(span, (query, key, value)):
            turned_ref[:, 0, :, s] = part.reshape(spots, piece, 128)
        none = jnp.zeros_like(query)
        outs = []
        for head, one in enumerate((jnp.where(first, query, none), jnp.where(first, none, query))):
            scores = head_scores(one, key, bias_ref[...])
            top = jnp.max(scores, axis=1, keepdims=True)
            exponent = jnp.exp(scores - top)
            total = jnp.sum(exponent, axis=1, keepdims=True)
            outs.append(dot_plain((exponent * (1.0 / total)).astype(jnp.bfloat16), value))
            logs = jnp.where(lane == 2 * pair + head, top + jnp.log(total), logs)
        attended_ref[:, 0, :, span[0]] = (
            jnp.where(first, outs[0], outs[1]).astype(jnp.bfloat16).reshape(spots, piece, 128)
        )
    put(logs_ref, logs)


def attention_back(turned_ref, d_att_ref, logs_ref, tables_ref, bias_ref, d_project_ref):
    spots, _, piece, width = turned_ref.shape
    rows, third = spots * piece, width // 3
    tables = [tables_ref[k] for k in range(3)]
    first = lax.broadcasted_iota(jnp.int32, (rows, 128), 1) < HEAD_DIM
    logs = flat(logs_ref)
    for pair in range(third // 128):
        span = [slice(k * third + pair * 128, k * third + pair * 128 + 128) for k in range(3)]
        query, key, value = [turned_ref[:, 0, :, s].reshape(rows, 128) for s in span]
        d_att = d_att_ref[:, 0, :, span[0]].reshape(rows, 128)
        none = jnp.zeros_like(query)
        parts = []
        for head in range(2):
            keep = first if head == 0 else jnp.logical_not(first)
            one_query = jnp.where(keep, query, none)
            one_d_att = jnp.where(keep, d_att, none)
            log = logs[:, 2 * pair + head : 2 * pair + head + 1]
            prob = jnp.exp(head_scores(one_query, key, bias_ref[...]) - log)
            d_value = dot_rows(prob.astype(jnp.bfloat16), d_att)
            d_prob = dot_cols(one_d_att, value)
            d_score = (prob * (d_prob - jnp.sum(d_prob * prob, axis=1, keepdims=True))).astype(
                jnp.bfloat16
            )
            parts.append((dot_plain(d_score, key), dot_rows(d_score, query), d_value))
        joined = [jnp.where(first, one, two) for one, two in zip(*parts)]
        done = (turn(0.125 * joined[0], tables, -1.0), turn(0.125 * joined[1], tables, -1.0), joined[2])
        for s, part in zip(span, done):
            d_project_ref[:, 0, :, s] = part.astype(jnp.bfloat16).reshape(spots, piece, 128)


def join_gate_up(packed, whole):
    last = packed[:, 2 * whole :]
    gate = jnp.concatenate([packed[:, :whole], last], axis=1)
    up = jnp.concatenate([packed[:, whole : 2 * whole], pltpu.roll(last, 64, 1)], axis=1)
    return gate, up


def units_fore(normed, weight):
    packed = dot_plain(normed, weight)
    units = weight.shape[1] // 2
    gate, up = join_gate_up(packed, units - 64)
    return packed, (gate * jax.nn.sigmoid(gate) * up).astype(jnp.bfloat16)[:, :units]


def units_back(cot, down, packed):
    units = down.shape[0]
    whole = units - 64
    d_hid = dot_cols(cot, down).astype(jnp.bfloat16).astype(jnp.float32)
    d_hid = jnp.concatenate([d_hid, jnp.zeros((d_hid.shape[0], 64), jnp.float32)], axis=1)
    gate, up = join_gate_up(packed, whole)
    sigmoid_gate = jax.nn.sigmoid(gate)
    d_gate = d_hid * up * (sigmoid_gate * (1.0 + gate * (1.0 - sigmoid_gate)))
    d_up = d_hid * (gate * sigmoid_gate)
    first = lax.broadcasted_iota(jnp.int32, (gate.shape[0], 128), 1) < 64
    last = jnp.where(first, d_gate[:, whole:], pltpu.roll(d_up[:, whole:], 64, 1))
    parts = [d_gate[:, :whole], d_up[:, :whole], last]
    return jnp.concatenate([part.astype(jnp.bfloat16) for part in parts], axis=1)


KERNEL_PARAMS = pltpu.CompilerParams(vmem_limit_bytes=40 * 1024 * 1024)


def adam_update(weight_old, gradient, moment_old, square_old, factor, rate, decay):
    clipped = gradient * factor
    moment_new = BETA_ONE * moment_old + (1.0 - BETA_ONE) * clipped
    square_new = BETA_TWO * square_old + (1.0 - BETA_TWO) * clipped * clipped
    moment_hat = moment_new / (1.0 - BETA_ONE**STEP)
    square_hat = square_new / (1.0 - BETA_TWO**STEP)
    weight_new = weight_old - rate * (
        moment_hat / (jnp.sqrt(square_hat) + ADAM_EPS) + decay * weight_old
    )
    return (weight_new, moment_new, square_new)


def local(
    tokens,
    cotangent,
    project_weight,
    output_weight,
    gate_up_weight,
    down_weight,
    norm_params,
    first_project,
    first_output,
    first_gate_up,
    first_down,
    first_norm,
    second_project,
    second_output,
    second_gate_up,
    second_down,
    second_norm,
):
    count = lax.axis_size("dp")
    blocks_half = count // 2
    me = lax.axis_index("dp")
    side = (me // 2) % 2
    spot = lax.axis_index("tensor")
    spots = lax.axis_size("tensor")
    micro_count, piece = tokens.shape[0], tokens.shape[1]
    head_cols = project_weight.shape[2] // 2
    unit_cols = gate_up_weight.shape[2] // 2
    whole = unit_cols - 64
    rows_each = project_weight.shape[1]
    seqs = 2 * micro_count
    rows_all = spots * seqs * piece

    by_columns = rows_each % 128 == 0

    by_columns = rows_each % 128 == 0

    norm_low = norm_params.astype(jnp.bfloat16)
    tok_rel, unit_rows, cot_low, cot_flipped, *weight_pairs, own_gains, tables, bias = run_prepare(
        tokens,
        cotangent,
        (project_weight, gate_up_weight, down_weight, output_weight),
        norm_params,
        jnp.asarray(angle_tables(spots * piece)),
    )
    if not by_columns:
        weight_pairs[2:] = [pair.swapaxes(1, 2) for pair in weight_pairs[2:]]

    (
        w_project,
        w_gate_up,
        w_down,
        w_output,
        gains,
        _,
        all_cot,
        normed_t,
        packed,
        hidden,
        attended,
        turned,
        logs,
        hidden_t,
        attended_t,
        *stage,
    ) = run_forward(
        blocks_half,
        by_columns,
        weight_pairs,
        own_gains,
        unit_rows,
        cot_low,
        cot_flipped,
        tables,
        bias,
        (spots, seqs, piece),
    )
    gains = gains.reshape(count, 8, rows_each).transpose(1, 0, 2).reshape(8, D)
    if not by_columns:
        w_down, w_output = w_down.T, w_output.T
    pairs, normed_parts, out_parts = run_backward(
        blocks_half,
        by_columns,
        (all_cot, packed, hidden, attended, turned, logs),
        (normed_t, attended_t, hidden_t),
        (w_project, w_gate_up, w_down, w_output),
        tables,
        bias,
        stage[:2],
    )
    if not by_columns:
        pairs[:2] = [(own.T, came.swapaxes(1, 2)) for own, came in pairs[:2]]
    weight_grads, input_grad, shares = run_join_grads(
        blocks_half,
        pairs,
        [*normed_parts, tok_rel, cot_low, gains],
        [output_weight.shape, down_weight.shape, gate_up_weight.shape, project_weight.shape],
        (head_cols, whole),
    )
    norm_grad, square_total = sum_everywhere(shares)
    grads = (weight_grads[3], weight_grads[0], weight_grads[2], weight_grads[1], norm_grad)
    norm_total = jnp.sqrt(square_total)
    (layer_out,) = run_finish(finish_out, rows_each, [*out_parts, tok_rel], [], 0)
    limit = 0.03 * math.sqrt((4 * D * D + 3 * D * FF + 2 * D) * micro_count * count * SEQ)
    factor = jnp.minimum(1.0, limit / (norm_total + 1e-06))
    rates = (
        2.0 / math.sqrt(D),
        2.0 / math.sqrt(D // 32),
        2.0 / math.sqrt(D),
        2.0 / math.sqrt(FF),
        0.5,
    )
    decays = (0.1, 0.1, 0.1, 0.1, 0.0)
    masters = (project_weight, output_weight, gate_up_weight, down_weight, norm_params)
    firsts = (first_project, first_output, first_gate_up, first_down, first_norm)
    seconds = (second_project, second_output, second_gate_up, second_down, second_norm)
    updated = [
        adam_update(*parts) for parts in zip(masters, grads, firsts, seconds, [factor] * 5, rates, decays)
    ]
    return (
        layer_out,
        input_grad,
        *grads,
        norm_total,
        *[u[0] for u in updated],
        *[u[1] for u in updated],
        *[u[2] for u in updated],
    )


def solution(mesh):
    wide = P("dp", "tensor", None)
    stacked = P(None, "dp", "tensor")
    tall = P("tensor", "dp")
    params = (stacked, tall, stacked, tall, P(None, "dp"))
    return jax.shard_map(
        local,
        mesh=mesh,
        in_specs=(wide, wide, *params, *params, *params),
        out_specs=(wide, wide, *params, P(), *params, *params, *params),
        check_vma=False,
    )
```

```python
import functools
import math

import jax
import jax.numpy as jnp
import numpy as np
from jax import lax
from jax.experimental import pallas as pl
from jax.experimental.pallas import tpu as pltpu
from jax.sharding import PartitionSpec as P

D = 2048
HEAD_DIM = 64
FF = 5632
SEQ = 320
STEP = 10
ROT = 16

BETA_ONE = 0.9
BETA_TWO = 0.999
ADAM_EPS = 1e-08
NORM_EPS = 1e-05
MASK_FILL = -1e30

BOTH = ("dp", "tensor")
MESH = pl.DeviceIdType.MESH


def block_order(count):
    return [2 * j + i for i in range(2) for j in range(count // 2)]


def relative(values, axis, me, count):
    width = values.shape[axis] // count
    return jnp.concatenate(
        [lax.dynamic_slice_in_dim(values, (me ^ r) * width, width, axis) for r in block_order(count)],
        axis=axis,
    )


def from_relative(values, axis, me, count):
    width = values.shape[axis] // count
    places = [((me ^ g) % 2) * (count // 2) + (me ^ g) // 2 for g in range(count)]
    return jnp.concatenate(
        [lax.dynamic_slice_in_dim(values, place * width, width, axis) for place in places],
        axis=axis,
    )


def place(dp_flip, tensor_flip):
    return (lax.axis_index("dp") ^ dp_flip, lax.axis_index("tensor") ^ tensor_flip)


def greet(places):
    barrier = pltpu.get_barrier_semaphore()
    for there in places:
        pl.semaphore_signal(barrier, inc=1, device_id=there, device_id_type=MESH)
    pl.semaphore_wait(barrier, len(places))


def send_to(there, source, target, send_sem, recv_sem):
    return pltpu.make_async_remote_copy(
        src_ref=source,
        dst_ref=target,
        send_sem=send_sem,
        recv_sem=recv_sem,
        device_id=there,
        device_id_type=MESH,
    )


def group_places(half):
    return [place(2 * j, 0) for j in range(1, half)] + [place(1, 0), place(0, 2), place(0, 1)]


def forward(half, by_columns, *refs):
    def take(count):
        nonlocal refs
        head, refs = refs[:count], refs[count:]
        return head

    project_pair, gate_up_pair, down_pair, output_pair = take(4)
    gains_own, unit_rows, cot_own, cot_flipped, tables, bias = take(6)
    w_project, w_gate_up, w_down, w_output, gains = take(5)
    normed, cot, normed_t, packed, hidden, attended, turned, logs, hidden_t, attended_t = take(10)
    stage = take(2)
    normed_own, normed_flipped = take(2)
    z_send, z_recv, x_send, x_recv, a_send, a_recv = refs
    greet(group_places(half))

    spots, seqs, piece, _ = cot.shape
    units, heads = hidden.shape[-1], attended.shape[-1]
    each = D // (2 * half)
    rows_all = spots * seqs * piece
    every = lambda ref: pl.BlockSpec(ref.shape, lambda *g: (0,) * len(ref.shape))

    def row_chunk(out, mine, other, share=0, shares=1):
        size = mine.shape[0] // shares
        rows = pl.ds(share * size, size)
        return mine.at[rows], other.at[rows], lambda p: out.at[pl.ds(p * mine.shape[0] + share * size, size)]

    def column_chunk(out, mine, other, share=0, shares=1):
        size = mine.shape[0] // shares
        rows, width = pl.ds(share * size, size), mine.shape[1]
        return mine.at[rows], other.at[rows], lambda p: out.at[rows, pl.ds(p * width, width)]

    out_chunk = column_chunk if by_columns else row_chunk
    pair = lambda ref: (ref.at[0], ref.at[1])
    chunks = [
        row_chunk(gains, gains_own, gains_own),
        row_chunk(w_project, *pair(project_pair)),
        row_chunk(w_gate_up, *pair(gate_up_pair), 0, 2),
        row_chunk(w_gate_up, *pair(gate_up_pair), 1, 2),
        out_chunk(w_down, *pair(down_pair), 0, 2),
        out_chunk(w_output, *pair(output_pair)),
        out_chunk(w_down, *pair(down_pair), 1, 2),
    ]
    GAINS, PROJECT, GATE_UP, DOWN, OUTPUT = 0, 1, 2, 4, 5
    n = len(chunks)
    far = range(half - 1, 0, -1)

    def z_copy(c, j):
        mine, other, block = chunks[c]
        return send_to(place(2 * j, 0), other if j % 2 else mine, block(j), z_send.at[c, j], z_recv.at[c, j])

    def x_copy(c, j):
        mine, _, block = chunks[c]
        return send_to(place(1, 0), block(j) if j else mine, block(half + j), x_send.at[c, j], x_recv.at[c, j])

    def start_z(c):
        if c < n:
            for j in far:
                z_copy(c, j).start()

    def start_own(c):
        if c < n:
            x_copy(c, 0).start()

    def keep(sources, outs, blocks, steps):
        def body(*refs):
            for ref, out_ref in zip(refs, refs[len(sources) :]):
                put(out_ref, ref[...])

        pltpu.emit_pipeline(
            body, grid=(steps,), in_specs=[block[0] for block in blocks], out_specs=[block[1] for block in blocks]
        )(*sources, *outs)

    def keep_weights():
        pairs = (project_pair, gate_up_pair, down_pair, output_pair)
        sizes = [(ref.shape[1] // 2, ref.shape[2]) for ref in pairs]
        blocks = [(blocked((1,) + size, 0, step(), 0), blocked(size, step(), 0)) for size in sizes]
        keep(pairs, (w_project, w_gate_up, w_down, w_output), blocks, 2)

    def keep_cot():
        lead = blocked((1, piece, D), step(), 0, 0)
        keep((cot_own,), (cot,), [(lead, blocked((1, 1, piece, D), 0, step(), 0, 0))], seqs // 2)

    def serve(c):
        for j in far:
            z_copy(c, j).wait_recv()
            x_copy(c, j).start()
            if c + 1 < n and c != GAINS:
                z_copy(c + 1, j).start()
        if c > GAINS:
            start_own(c + 2)

    def have(*which):
        for c in which:
            for j in range(half):
                x_copy(c, j).wait_recv()

    act_own, act_flipped, act_out = (normed_own, cot_own), (normed_flipped, cot_flipped), (normed, cot)

    def rows(a, index):
        micro = seqs // 2
        return act_out[a].at[index // 2, pl.ds((index % 2) * micro, micro)]

    def a_copy(a, k):
        source = (act_flipped[a], act_own[a], rows(a, 1), act_own[a], rows(a, 1), rows(a, 2), rows(a, 3))[k]
        there = place(2, 0) if k == 0 else place(0, 2) if k < 3 else place(0, 1)
        return send_to(there, source, rows(a, k + 1), a_send.at[a, k], a_recv.at[a, k])

    def act_begin(a):
        for k in (0, 1, 3):
            a_copy(a, k).start()

    def act_z(a):
        a_copy(a, 0).wait_recv()
        a_copy(a, 2).start()
        a_copy(a, 4).start()

    def act_y(a):
        a_copy(a, 1).wait_recv()
        a_copy(a, 5).start()
        a_copy(a, 2).wait_recv()
        a_copy(a, 6).start()

    def act_have(a):
        for k in range(3, 7):
            a_copy(a, k).wait_recv()

    def norm_step():
        def body(unit_ref, gains_ref, out_ref, flipped_ref, kept_ref):
            gain, shift = [
                jnp.concatenate([gains_ref[p * 8 + k : p * 8 + k + 1] for p in range(2 * half)], axis=1)
                for k in range(2)
            ]
            value = unit_ref[0] * gain + shift
            put(out_ref, value)
            put(flipped_ref, flip_lanes(value, each))
            put(kept_ref, value)

        block = blocked((1, piece, D), step(), 0, 0)
        kept = blocked((1, 1, piece, D), 0, step(), 0, 0)
        pltpu.emit_pipeline(
            body, grid=(seqs // 2,), in_specs=[block, every(gains)], out_specs=[block, block, kept]
        )(unit_rows, gains, normed_own, normed_flipped, normed)

    def attention_step(first, count):
        block = lambda width: blocked((spots, 1, piece, width), 0, step(first), 0, 0)

        def body(normed_ref, weight_ref, *refs):
            attention_fore(dot_plain(flat(normed_ref), weight_ref[...]), *refs)

        pltpu.emit_pipeline(
            body,
            grid=(count,),
            in_specs=[block(D), every(w_project), every(tables), every(bias)],
            out_specs=[block(3 * heads), block(heads), block(128)],
        )(normed, w_project, tables, bias, turned, attended, logs)

    def turn_over(source, out, in_block, out_block, steps):
        def body(ref, out_ref):
            put(out_ref, flat(ref).T)

        pltpu.emit_pipeline(body, grid=(steps,), in_specs=[in_block], out_specs=[out_block])(source, out)

    def units_step(first, count):
        tile = lambda width: blocked((1, seqs, piece, width), step(first), 0, 0, 0)

        def body(normed_ref, weight_ref, packed_ref, hidden_ref):
            value, units_value = units_fore(flat(normed_ref), weight_ref[...])
            put(packed_ref, value)
            put(hidden_ref, units_value)

        pltpu.emit_pipeline(
            body,
            grid=(count,),
            in_specs=[tile(D), every(w_gate_up)],
            out_specs=[tile(2 * units), tile(units)],
        )(normed, w_gate_up, packed, hidden)

    def grads_step():
        groups, wide = stage[0].shape[0], D // (2 * stage[0].shape[0])

        def body(cot_ref, attended_ref, hidden_ref, *out_refs):
            block = flat(cot_ref)
            for ref, out_ref in zip((attended_ref, hidden_ref), out_refs):
                value = dot_plain(ref[...], block)
                put(out_ref, value if by_columns else value.T)

        pltpu.emit_pipeline(
            body,
            grid=(groups,),
            in_specs=[
                blocked((spots, seqs, piece, wide), 0, 0, 0, step(groups)),
                every(attended_t),
                every(hidden_t),
            ],
            out_specs=[blocked((1,) + ref.shape[1:], step(), 0, 0) for ref in stage],
        )(cot, attended_t, hidden_t, *stage)

    start_z(GAINS)
    start_z(PROJECT)
    start_own(GAINS)
    keep((gains_own,), (gains,), [(every(gains_own), blocked(gains_own.shape, 0, 0))], 1)
    serve(GAINS)
    have(GAINS)
    start_own(PROJECT)
    start_own(GATE_UP)
    norm_step()
    act_begin(0)
    keep_weights()
    keep_cot()
    serve(PROJECT)
    act_z(0)
    act_y(0)
    act_begin(1)
    act_have(0)
    have(PROJECT)
    serve(GATE_UP)
    attention_step(0, seqs)
    act_z(1)
    turn_over(attended, attended_t, every(attended), every(attended_t), 1)
    serve(GATE_UP + 1)
    columns = lambda index: blocked((spots, seqs, piece, 256), 0, 0, 0, index)
    turn_over(normed, normed_t, columns(step()), blocked((256, rows_all), step(), 0), D // 256)
    act_y(1)
    serve(DOWN)
    have(GATE_UP, GATE_UP + 1)
    units_step(0, spots // 2)
    serve(OUTPUT)
    units_step(spots // 2, spots - spots // 2)
    serve(n - 1)
    turn_over(hidden, hidden_t, every(hidden), every(hidden_t), 1)
    act_have(1)
    grads_step()
    have(DOWN, OUTPUT, n - 1)
    for c in range(n):
        for j in range(half):
            if j:
                z_copy(c, j).wait_send()
            x_copy(c, j).wait_send()
    for a in range(2):
        for k in range(7):
            a_copy(a, k).wait_send()


def run_forward(half, by_columns, pairs, gains, unit_rows, cot, cot_flipped, tables, bias, group):
    low, full = jnp.bfloat16, jnp.float32
    each, heads, units = pairs[0].shape[1], pairs[0].shape[2] // 3, pairs[1].shape[2] // 2
    spots, seqs, piece = group
    rows_all = spots * seqs * piece
    groups = min(half, 4)
    wide = D // (2 * groups)
    widths = (heads, units)
    flat_stage = [(groups, w, wide) if by_columns else (groups, wide, w) for w in widths]
    across = [(w, D) if by_columns else (D, w) for w in (units, heads)]
    shapes = [
        ((D, 3 * heads), low),
        ((D, 2 * units), low),
        *[(shape, low) for shape in across],
        ((2 * half * 8, each), full),
        (group + (D,), low),
        (group + (D,), low),
        ((D, rows_all), low),
        (group + (2 * units,), full),
        (group + (units,), low),
        (group + (heads,), low),
        (group + (3 * heads,), low),
        (group + (128,), full),
        ((units, rows_all), low),
        ((heads, rows_all), low),
        *[(shape, low) for shape in flat_stage],
        (cot.shape, low),
        (cot.shape, low),
    ]
    ins = [*pairs, gains, unit_rows, cot, cot_flipped, tables, bias]
    anywhere = pl.BlockSpec(memory_space=pl.ANY)
    sem = pltpu.SemaphoreType.DMA
    return pl.pallas_call(
        functools.partial(forward, half, by_columns),
        out_shape=[jax.ShapeDtypeStruct(*shape) for shape in shapes],
        in_specs=[anywhere] * len(ins),
        out_specs=[anywhere] * len(shapes),
        scratch_shapes=[sem((7, half))] * 4 + [sem((2, 7))] * 2,
        compiler_params=pltpu.CompilerParams(
            collective_id=0, has_side_effects=True, vmem_limit_bytes=56 * 1024 * 1024
        ),
        name="forward",
    )(*ins)


def angle_tables(length):
    half_rot = ROT // 2
    angles = np.arange(length)[:, None] * (10000.0 ** (-2.0 * np.arange(half_rot) / ROT))[None, :]
    cosine, sine = np.cos(angles), np.sin(angles)
    none = np.zeros_like(sine)
    rest = np.zeros((length, HEAD_DIM - ROT))
    rows = ((cosine, cosine, rest + 1.0), (-sine, none, rest), (none, sine, rest))
    return np.stack([np.tile(np.concatenate(parts, axis=1), (1, 2)) for parts in rows]).astype(np.float32)


def prepare(each, in_place, *refs):
    tokens, cot, project, gate_up, down, output, params, angles = refs[:8]
    tok_ref, unit_ref, cot_ref, cot_flipped_ref, project_ref, gate_up_ref, down_ref, output_ref = refs[8:16]
    gains_ref, tables_ref, bias_ref = refs[16:]
    me = lax.axis_index("dp")
    gains_ref[...] = jnp.zeros_like(gains_ref)
    gains_ref[0:2] = params[...].astype(jnp.bfloat16).astype(jnp.float32)
    piece, shape = tokens.shape[1], bias_ref.shape
    places = [lax.broadcasted_iota(jnp.int32, shape, axis) for axis in range(2)]
    positions = list(places)
    for k, flip in enumerate((0, 2, 1, 3)):
        spot = lax.axis_index("tensor") ^ flip
        tables_ref[:, k * piece : (k + 1) * piece] = angles[:, pl.ds(pl.multiple_of(spot * piece, piece), piece)]
        for axis, value in enumerate(places):
            inside = jnp.logical_and(value >= k * piece, value < (k + 1) * piece)
            positions[axis] = jnp.where(inside, value + (spot - k) * piece, positions[axis])
    bias_ref[...] = jnp.where(positions[0] >= positions[1], 0.0, MASK_FILL)
    side = (me // 2) % 2
    blocks = block_order(D // each)
    if in_place:
        for p, r in enumerate(blocks):
            span, flipped = slice(p * each, (p + 1) * each), slice((p ^ 1) * each, ((p ^ 1) + 1) * each)
            there = pl.ds(pl.multiple_of((me ^ r) * each, each), each)
            tok_ref[:, :, span] = tokens[:, :, there]
            cot_ref[:, :, span] = cot[:, :, there]
            cot_flipped_ref[:, :, flipped] = cot[:, :, there]
    else:
        tok_ref[...] = tokens[...]
        cot_ref[...] = cot[...]
        for s in range(cot.shape[0]):
            put(cot_flipped_ref.at[s], flip_lanes(cot[s].astype(jnp.float32), each))
    for s in range(tokens.shape[0]):
        unit_ref[s], _ = norm_rows(tok_ref[s].astype(jnp.float32))
    heads, units = output.shape[0] // 2, down.shape[0] // 2
    whole = units - 64
    for h, s in enumerate((side, 1 - side)):
        part = lambda width, start=0: pl.ds(start + pl.multiple_of(s * width, width), width)
        for k in range(3):
            put(project_ref.at[h, :, pl.ds(k * heads, heads)], project[k, :, part(heads)])
        for k in range(2):
            put(gate_up_ref.at[h, :, pl.ds(k * whole, whole)], gate_up[k, :, part(whole)])
        put(output_ref.at[h], output[part(heads)])
        put(down_ref.at[h, pl.ds(0, whole)], down[part(whole)])
        put(down_ref.at[h, pl.ds(whole, 64)], down[part(64, 2 * whole)])
    gate, up = gate_up[0, :, 2 * whole :], gate_up[1, :, 2 * whole :]
    first = lax.broadcasted_iota(jnp.int32, gate.shape, 1) < 64
    zero = jnp.where(first, gate, pltpu.roll(up, 64, 1))
    one = jnp.where(first, pltpu.roll(gate, 64, 1), up)
    put(gate_up_ref.at[0, :, pl.ds(2 * whole, 128)], jnp.where(side == 0, zero, one))
    put(gate_up_ref.at[1, :, pl.ds(2 * whole, 128)], jnp.where(side == 0, one, zero))


def whole_spec(shape):
    return pl.BlockSpec(shape, lambda *_: (0,) * len(shape))


def run_prepare(tokens, cot, weights, params, angles):
    project, gate_up, down, output = weights
    each = project.shape[1]
    in_place = each % 128 == 0
    if not in_place:
        me, count = lax.axis_index("dp"), D // each
        tokens, cot = relative(tokens, 2, me, count), relative(cot, 2, me, count)
    low = jnp.bfloat16
    heads, units = output.shape[0] // 2, down.shape[0] // 2
    shapes = [(tokens.shape, low), (tokens.shape, jnp.float32), (cot.shape, low), (cot.shape, low)]
    shapes += [((2, each, 3 * heads), low), ((2, each, 2 * units), low)]
    shapes += [((2, units, each), low), ((2, heads, each), low)]
    length = angles.shape[1]
    shapes += [((8, each), jnp.float32), (angles.shape, jnp.float32), ((length, length), jnp.float32)]
    ins = [tokens, cot, project, gate_up, down, output, params, angles]
    return pl.pallas_call(
        functools.partial(prepare, each, in_place),
        grid=(1,),
        in_specs=[whole_spec(value.shape) for value in ins],
        out_specs=[whole_spec(shape) for shape, _ in shapes],
        out_shape=[jax.ShapeDtypeStruct(*shape) for shape in shapes],
        compiler_params=pltpu.CompilerParams(vmem_limit_bytes=60 * 1024 * 1024),
        name="prepare",
    )(*ins)


def flat(ref):
    value = ref[...]
    return value.reshape(-1, value.shape[-1])


def put(ref, value):
    ref[...] = value.astype(ref.dtype).reshape(ref.shape)


def blocked(shape, *index):
    return pl.BlockSpec(shape, lambda g: tuple(i(g) if callable(i) else i for i in index))


def step(offset=0):
    return lambda g: g + offset


def backward(half, by_columns, window, *refs):
    def take(count):
        nonlocal refs
        head, refs = refs[:count], refs[count:]
        return head

    cot, packed, hidden, attended, turned, logs = take(6)
    normed_t, attended_t_all, hidden_t_all = take(3)
    w_project, w_gate_up, w_down, w_output, tables, bias = take(6)
    stage_out = take(2)
    z_in, mine = take(4), take(4)
    act_away, act_near, core_in, y_out, y_in, far_out = [take(2) for _ in range(6)]
    act_far, act_sum = take(1), take(2)
    stage, x_in = stage_out + take(2), take(4)
    d_packed, d_att, d_project, attended_t, hidden_t, normed_block, cot_block = take(7)
    x_send, x_recv, z_send, z_recv, a_send, a_recv, load_sem, block_sem = refs
    greet(group_places(half))

    spots, seqs, piece, _ = cot.shape
    units, heads = hidden.shape[-1], attended.shape[-1]
    groups = stage[0].shape[0]
    per = half // groups
    wide = D // (2 * groups)
    every = lambda ref: pl.BlockSpec(ref.shape, lambda g: (0,) * len(ref.shape))

    whole = (attended_t, hidden_t, d_packed, d_project)

    def product(c, block, whole_ref):
        if c >= 2:
            return dot_plain(block, flat(whole_ref))
        value = dot_plain(whole_ref[...], block)
        return value if by_columns else value.T

    def block_copy(index):
        c, g = order[index]
        span, slot = pl.ds(g * wide, wide), index % 2
        if c >= 2:
            source, target = normed_t.at[span], normed_block.at[slot]
        else:
            source, target = cot.at[:, :, :, span], cot_block.at[slot]
        return pltpu.make_async_copy(source, target, block_sem.at[slot])

    def x_copy(c, g):
        return send_to(place(1, 0), stage[c].at[g], x_in[c].at[g], x_send.at[c, g], x_recv.at[c, g])

    def z_copy(c, j):
        source = x_in[c].at[j // per]
        if per > 1:
            rows = z_in[c].shape[1]
            source = source.at[pl.ds((j % per) * rows, rows)]
        return send_to(place(2 * j, 0), source, z_in[c].at[j], z_send.at[c, j], z_recv.at[c, j])

    def a_copy(a, s):
        source = (act_away[a], y_out[a], far_out[a])[s]
        target = (core_in[a], y_in[a], act_far[0])[s]
        there = (place(0, 1), place(0, 2), place(2, 0))[s]
        return send_to(there, source, target, a_send.at[a, s], a_recv.at[a, s])

    order = [(0, 3), (0, 2), (1, 3), (1, 2), (2, 3), (1, 1), (0, 1), (2, 2), (2, 1)]
    order += [(3, g) for g in (3, 2, 1)] + [(c, 0) for c in (2, 1, 3, 0)]
    started, served, ready = [0], [0], {0, 1}

    def start_x():
        while started[0] < min(served[0] + window, len(order)) and order[started[0]][0] in ready:
            x_copy(*order[started[0]]).start()
            started[0] += 1

    def away_product(c):
        def body(block_ref, whole_ref, out_ref):
            put(out_ref, product(c, block_ref[...], whole_ref))

        pltpu.emit_pipeline(
            body,
            grid=(groups,),
            in_specs=[blocked((wide, normed_t.shape[1]), step(groups), 0), every(whole[c])],
            out_specs=[blocked((1,) + stage[c].shape[1:], step(), 0, 0)],
        )(normed_t, whole[c], stage[c])
        ready.add(c)
        start_x()

    def serve(count):
        for _ in range(count):
            index = served[0]
            c, g = order[index]
            served[0] += 1
            block_copy(index).wait()
            if served[0] < len(order):
                block_copy(served[0]).start()
            x_copy(c, g).wait_recv()
            start_x()
            block = flat((normed_block if c >= 2 else cot_block).at[index % 2])
            total = product(c, block, whole[c]) + x_in[c][g].astype(jnp.float32)
            if g == 0:
                mine[c][0] = total
            if g > 0 or per > 1:
                put(x_in[c].at[g], total)
            for j in range(g * per, (g + 1) * per):
                if j:
                    z_copy(c, j).start()

    def units_step(first, count):
        tile = (1, seqs, piece)

        def body(cot_ref, down_ref, output_ref, packed_ref, d_packed_ref, d_att_ref):
            rows = flat(cot_ref)
            d_packed_ref[...] = units_back(rows, down_ref[...], flat(packed_ref)).reshape(d_packed_ref.shape)
            put(d_att_ref, dot_cols(rows, output_ref[...]))

        pltpu.emit_pipeline(
            body,
            grid=(count,),
            in_specs=[
                blocked(tile + (D,), step(first), 0, 0, 0),
                every(w_down),
                every(w_output),
                blocked(tile + (2 * units,), step(first), 0, 0, 0),
            ],
            out_specs=[
                blocked(tile + (2 * units,), step(first), 0, 0, 0),
                blocked(tile + (heads,), step(first), 0, 0, 0),
            ],
        )(cot, w_down, w_output, packed, d_packed, d_att)

    def attention_step(first, count):
        block = lambda width: blocked((spots, 1, piece, width), 0, step(first), 0, 0)
        pltpu.emit_pipeline(
            attention_back,
            grid=(count,),
            in_specs=[block(3 * heads), block(heads), block(128), every(tables), every(bias)],
            out_specs=[block(3 * heads)],
        )(turned, d_att, logs, tables, bias, d_project)

    def two_cores(away_ref, near_ref, total):
        middle = total.shape[0] // 2
        put(near_ref, total[:middle])
        put(away_ref, total[middle:])

    def core_block(first):
        return blocked((spots // 2, seqs, piece, 512), 0, 0, 0, step(first))

    def normed_step():
        def body(d_project_ref, d_packed_ref, project_ref, gate_up_ref, away_ref, near_ref):
            total = dot_cols(flat(d_project_ref), project_ref[...])
            two_cores(away_ref, near_ref, total + dot_cols(flat(d_packed_ref), gate_up_ref[...]))

        pltpu.emit_pipeline(
            body,
            grid=(D // 512,),
            in_specs=[
                every(d_project),
                every(d_packed),
                blocked((512, 3 * heads), step(), 0),
                blocked((512, 2 * units), step(), 0),
            ],
            out_specs=[core_block(0)] * 2,
        )(d_project, d_packed, w_project, w_gate_up, act_away[0], act_near[0])

    def out_step(first, count):
        def body(attended_ref, hidden_ref, output_ref, down_ref, away_ref, near_ref):
            total = dot_plain(flat(attended_ref), output_ref[...])
            two_cores(away_ref, near_ref, total + dot_plain(flat(hidden_ref), down_ref[...]))

        pltpu.emit_pipeline(
            body,
            grid=(count,),
            in_specs=[
                every(attended),
                every(hidden),
                blocked((heads, 512), 0, step(first)),
                blocked((units, 512), 0, step(first)),
            ],
            out_specs=[core_block(first)] * 2,
        )(attended, hidden, w_output, w_down, act_away[1], act_near[1])

    def add_terms(*refs):
        *terms, out_ref = refs
        put(out_ref, sum(flat(term).astype(jnp.float32) for term in terms))

    half_seqs = seqs // 2

    def core_arrived(a):
        a_copy(a, 0).wait_recv()
        rows = blocked((1, half_seqs, piece, D), 1, step(), 0, 0)
        pltpu.emit_pipeline(
            add_terms,
            grid=(2,),
            in_specs=[rows, rows],
            out_specs=[blocked((half_seqs, piece, D), step(), 0, 0)],
        )(act_near[a], core_in[a], y_out[a])
        a_copy(a, 1).start()

    def y_arrived(a):
        def body(*refs):
            add_terms(*refs[:3], refs[6])
            add_terms(*refs[3:6], refs[7])

        def both(shape, *lead):
            return [blocked(shape, *lead, step(first), 0, 0) for first in (half_seqs, 0)]

        rows, lines = both((1, 1, piece, D), 0), both((1, piece, D))
        a_copy(a, 1).wait_recv()
        pltpu.emit_pipeline(
            body,
            grid=(half_seqs,),
            in_specs=[rows[0], rows[0], lines[0], rows[1], rows[1], lines[1]],
            out_specs=[blocked((1, piece, D), step(), 0, 0)] * 2,
        )(*[act_near[a], core_in[a], y_in[a]] * 2, far_out[a], act_sum[a])
        if a == 0:
            a_copy(a, 2).start()

    loads = [
        pltpu.make_async_copy(attended_t_all, attended_t, load_sem.at[0]),
        pltpu.make_async_copy(hidden_t_all, hidden_t, load_sem.at[1]),
    ]
    for load in loads:
        load.start()
    block_copy(0).start()
    start_x()
    for load in loads:
        load.wait()
    steps = D // 512
    units_step(0, spots // 2)
    serve(2)
    units_step(spots // 2, spots - spots // 2)
    serve(1)
    away_product(2)
    serve(1)
    attention_step(0, seqs)
    away_product(3)
    serve(3)
    normed_step()
    a_copy(0, 0).start()
    serve(1)
    out_step(0, steps // 2)
    core_arrived(0)
    serve(1)
    out_step(steps // 2, steps - steps // 2)
    a_copy(1, 0).start()
    serve(1)
    core_arrived(1)
    serve(2)
    y_arrived(0)
    serve(len(order) - served[0])
    y_arrived(1)
    for c in range(4):
        for j in range(1, half):
            z_copy(c, j).wait()
        for g in range(groups):
            x_copy(c, g).wait_send()
    for a in range(2):
        for s in range(2):
            a_copy(a, s).wait_send()
    a_copy(0, 2).wait()


def run_backward(half, by_columns, rows, transposed, weights, tables, bias, stage, window=2):
    cot, packed, hidden, attended, turned, _ = rows
    low, full = jnp.bfloat16, jnp.float32
    spots, seqs, piece, _ = cot.shape
    each = D // (2 * half)
    groups = min(half, 4)
    wide = D // (2 * groups)
    widths = (attended.shape[-1], hidden.shape[-1], packed.shape[-1], turned.shape[-1])
    columns = [by_columns and groups == half and c < 2 for c in range(4)]

    def shape_of(count, block):
        return [(count, w, block) if flip else (count, block, w) for w, flip in zip(widths, columns)]

    def row_shape(*lead, kind=low):
        return [jax.ShapeDtypeStruct(lead + (piece, D), kind)] * 2

    shapes = [jax.ShapeDtypeStruct(shape, low) for shape in shape_of(half, each)]
    shapes += [jax.ShapeDtypeStruct(shape, full) for shape in shape_of(1, wide)]
    shapes += row_shape(spots // 2, seqs) * 3 + row_shape(seqs) * 2 + row_shape(seqs // 2)
    shapes += row_shape(seqs // 2)[:1] + row_shape(seqs // 2, kind=full)
    anywhere = pl.BlockSpec(memory_space=pl.ANY)
    vmem = pl.BlockSpec(memory_space=pltpu.VMEM)
    ins = [*rows, *transposed, *weights, tables, bias, *stage]
    sem = pltpu.SemaphoreType.DMA
    rows_all = spots * seqs * piece
    scratch = [pltpu.VMEM(shape, low) for shape in shape_of(groups, wide)[2:] + shape_of(groups, wide)]
    scratch += [pltpu.VMEM(r.shape, low) for r in (packed, attended, turned)]
    scratch += [pltpu.VMEM(t.shape, low) for t in transposed[1:]]
    scratch += [pltpu.VMEM((2, wide, rows_all), low), pltpu.VMEM((2, spots, seqs, piece, wide), low)]
    scratch += [sem((4, groups))] * 2 + [sem((4, half))] * 2 + [sem((2, 3))] * 2 + [sem((2,))] * 2
    outs = pl.pallas_call(
        functools.partial(backward, half, columns[0], window),
        out_shape=shapes,
        in_specs=[anywhere] * len(ins),
        out_specs=[anywhere] * 4 + [vmem] * 4 + [anywhere] * (len(shapes) - 8),
        scratch_shapes=scratch,
        compiler_params=pltpu.CompilerParams(
            collective_id=1, has_side_effects=True, vmem_limit_bytes=60 * 1024 * 1024
        ),
        name="backward",
    )(*ins)
    pairs = []
    for c in range(4):
        own = outs[4 + c][0] if columns[c] else outs[4 + c][0, :each]
        pairs.append((own, outs[c]))
    *_, out_far, normed_far, normed_sum, out_sum = outs
    dp_size, tensor_size = lax.axis_size("dp"), lax.axis_size("tensor")
    partners = [
        (d * tensor_size + t, (d ^ 2) * tensor_size + t) for d in range(dp_size) for t in range(tensor_size)
    ]
    out_far = lax.ppermute(out_far, ("dp", "tensor"), partners)
    return pairs, (normed_far, normed_sum), (out_far, out_sum)


def flip_lanes(values, width):
    lanes = values.shape[1]
    if width % 128 == 0:
        spans = [slice((p ^ 1) * width, ((p ^ 1) + 1) * width) for p in range(lanes // width)]
        return jnp.concatenate([values[:, span] for span in spans], axis=1)
    even = (lax.broadcasted_iota(jnp.int32, values.shape, 1) // width) % 2 == 0
    return jnp.where(even, pltpu.roll(values, lanes - width, 1), pltpu.roll(values, width, 1))


def norm_rows(tok_rows):
    centered = tok_rows - jnp.mean(tok_rows, axis=1, keepdims=True)
    row_scale = lax.rsqrt(jnp.mean(centered * centered, axis=1, keepdims=True) + NORM_EPS)
    return centered * row_scale, row_scale


def put_rows(ref, value, each, in_place):
    value = value.astype(jnp.bfloat16)
    if not in_place:
        ref[0] = value
        return
    me = lax.axis_index("dp")
    for p, r in enumerate(block_order(D // each)):
        span = pl.ds(pl.multiple_of((me ^ r) * each, each), each)
        ref[0, :, span] = value[:, p * each : (p + 1) * each]


def finish_out(each, in_place, far_ref, sum_ref, tok_ref, out_ref):
    summed = flat(sum_ref) + flip_lanes(flat(far_ref).astype(jnp.float32), each)
    put_rows(out_ref, flat(tok_ref).astype(jnp.float32) + summed, each, in_place)


def finish_rows(each, in_place, far_ref, sum_ref, tok_ref, cot_ref, gain, input_ref):
    d_normed = flat(sum_ref) + flip_lanes(flat(far_ref).astype(jnp.float32), each)
    unit_rows, row_scale = norm_rows(flat(tok_ref).astype(jnp.float32))
    d_unit = d_normed * gain
    d_input = row_scale * (
        d_unit
        - jnp.mean(d_unit, axis=1, keepdims=True)
        - unit_rows * jnp.mean(d_unit * unit_rows, axis=1, keepdims=True)
    )
    put_rows(input_ref, flat(cot_ref).astype(jnp.float32) + d_input, each, in_place)
    return jnp.sum(d_normed * unit_rows, axis=0, keepdims=True), jnp.sum(d_normed, axis=0, keepdims=True)


def run_finish(kernel, each, rows, fixed_in, fixed_out):
    in_place = each % 128 == 0
    count, piece, _ = rows[-1].shape
    block = pl.BlockSpec((1, piece, D), lambda s: (s, 0, 0))
    fixed = pl.BlockSpec((8, D), lambda s: (0, 0))
    done, *others = pl.pallas_call(
        functools.partial(kernel, each, in_place),
        grid=(count,),
        in_specs=[block] * len(rows) + [fixed] * len(fixed_in),
        out_specs=[block] + [fixed] * fixed_out,
        out_shape=[jax.ShapeDtypeStruct(rows[-1].shape, jnp.bfloat16)]
        + [jax.ShapeDtypeStruct((8, D), jnp.float32)] * fixed_out,
        compiler_params=KERNEL_PARAMS,
        name=kernel.__name__,
    )(*rows, *fixed_in)
    if not in_place:
        done = from_relative(done, 2, lax.axis_index("dp"), D // each)
    return done, *others


def join_grads(half, spans, *refs):
    own, came = refs[0:8:2], refs[1:8:2]
    far, close, tok, cot, gains = refs[8:13]
    output_ref, down_ref, gate_up_ref, project_ref, input_ref, shares_ref = refs[13:]
    each = D // (2 * half)
    in_place = each % 128 == 0
    parts = [
        finish_rows(each, in_place, *[r.at[pl.ds(k, 1)] for r in (far, close, tok, cot)], gains[0:1], input_ref.at[pl.ds(k, 1)])
        for k in range(tok.shape[0])
    ]
    shares = [sum(values) for values in zip(*parts)]
    side = (lax.axis_index("dp") // 2) % 2
    heads, whole = spans
    squares = jnp.float32(0.0)

    def halves(c, rows, columns):
        nonlocal squares
        pick = lambda j: came[c][j, rows, columns].astype(jnp.float32)
        mine = own[c][rows, columns] + sum(pick(j) for j in range(2, half, 2))
        other = sum(pick(j) for j in range(1, half, 2))
        squares = squares + jnp.sum(mine * mine) + jnp.sum(other * other)
        return mine, other

    def places(width, start=0):
        return [pl.ds(start + pl.multiple_of(s * width, width), width) for s in (side, 1 - side)]

    every = slice(None)
    for value, span in zip(halves(0, every, every), places(heads)):
        output_ref[span] = value
    for value, span in zip(halves(1, slice(0, whole), every), places(whole)):
        down_ref[span] = value
    for value, span in zip(halves(1, slice(whole, whole + 64), every), places(64, 2 * whole)):
        down_ref[span] = value
    for k in range(3):
        for value, span in zip(halves(3, every, slice(k * heads, (k + 1) * heads)), places(heads)):
            project_ref[k, :, span] = value
    for k in range(2):
        for value, span in zip(halves(2, every, slice(k * whole, (k + 1) * whole)), places(whole)):
            gate_up_ref[k, :, span] = value
    mine, other = halves(2, every, slice(2 * whole, 2 * whole + 128))
    zero, one = jnp.where(side == 0, mine, other), jnp.where(side == 0, other, mine)
    first = lax.broadcasted_iota(jnp.int32, zero.shape, 1) < 64
    gate_up_ref[0, :, 2 * whole :] = jnp.where(first, zero, pltpu.roll(one, 64, 1))
    gate_up_ref[1, :, 2 * whole :] = jnp.where(first, pltpu.roll(zero, 64, 1), one)
    if in_place:
        shares_ref[...] = jnp.zeros_like(shares_ref)
        per = each // 128
        for p in range(2 * half):
            for k, share in enumerate(shares):
                for q in range(per):
                    first = p * each + q * 128
                    shares_ref[p, k * per + q : k * per + q + 1] = share[:, first : first + 128]
            shares_ref[p, 7:8] = jnp.full((1, 128), squares)
    else:
        shares_ref[...] = jnp.concatenate(shares + [jnp.full((6, D), squares)], axis=0)


def run_join_grads(half, pairs, rows, shapes, spans):
    each = D // (2 * half)
    in_place = each % 128 == 0
    ins = [part for pair in pairs for part in pair] + rows
    kinds = [(shape, jnp.float32) for shape in shapes] + [(rows[2].shape, jnp.bfloat16)]
    kinds += [((2 * half, 8, 128) if in_place else (8, D), jnp.float32)]
    *grads, input_grad, shares = pl.pallas_call(
        functools.partial(join_grads, half, spans),
        grid=(1,),
        in_specs=[whole_spec(value.shape) for value in ins],
        out_specs=[whole_spec(shape) for shape, _ in kinds],
        out_shape=[jax.ShapeDtypeStruct(*kind) for kind in kinds],
        compiler_params=pltpu.CompilerParams(vmem_limit_bytes=60 * 1024 * 1024),
        name="join_grads",
    )(*ins)
    if not in_place:
        input_grad = from_relative(input_grad, 2, lax.axis_index("dp"), 2 * half)
        blocks = shares.reshape(8, 2 * half, each).transpose(1, 0, 2)
        shares = jnp.concatenate([blocks[:, :2], jnp.zeros_like(blocks[:, :5]), blocks[:, 2:3]], axis=1)
    return grads, input_grad, shares


def sum_kernel(half, spots, in_ref, out_ref, total_ref, first, second, send_sem, recv_sem):
    me, spot = lax.axis_index("dp"), lax.axis_index("tensor")
    z_places = [place(2 * j, 0) for j in range(half)]
    rest = [(i, t) for i in range(2) for t in range(spots)]
    rest_places = [place(i, t) for i, t in rest]
    greet(z_places[1:] + rest_places[1:])
    count = in_ref.shape[0]

    def exchange(places, slots, base):
        copies = [
            send_to(places[k], slots.at[0], slots.at[k], send_sem.at[base + k], recv_sem.at[base + k])
            for k in range(1, len(places))
        ]
        for copy in copies:
            copy.start()
        for copy in copies:
            copy.wait()

    first[0] = in_ref[...]
    exchange(z_places, first, 0)
    for p in range(count):
        i, j = p // half, p % half
        total = jnp.zeros(in_ref.shape[1:], jnp.float32)
        for g in range(half):
            k = g ^ (me // 2)
            total = total + first[k, i * half + (j ^ k)]
        second[0, p] = total
    exchange(rest_places, second, half)
    for p in range(count):
        i, j = p // half, p % half
        total = jnp.zeros(in_ref.shape[1:], jnp.float32)
        for x in range(2):
            for t in range(spots):
                flip = x ^ (me % 2)
                total = total + second[flip * spots + (t ^ spot), (i ^ flip) * half + j]
        out_ref[p] = total
    rows, lanes = in_ref.shape[1:]
    used = lax.broadcasted_iota(jnp.int32, (rows, lanes), 0) < rows - 1
    total = out_ref[0, rows - 1 :, :]
    for g in range(count):
        there = me ^ g
        value = out_ref[(there % 2) * half + there // 2]
        total = total + jnp.sum(jnp.where(used, value * value, 0.0))
    total_ref[...] = jnp.broadcast_to(total, total_ref.shape)


def sum_everywhere(parts):
    half, spots = lax.axis_size("dp") // 2, lax.axis_size("tensor")
    each, lanes = D // (2 * half), parts.shape[2]
    vmem = pl.BlockSpec(memory_space=pltpu.VMEM)
    sem = pltpu.SemaphoreType.DMA
    summed, total = pl.pallas_call(
        functools.partial(sum_kernel, half, spots),
        out_shape=[jax.ShapeDtypeStruct(shape, jnp.float32) for shape in (parts.shape, (8, lanes))],
        in_specs=[vmem],
        out_specs=[vmem, vmem],
        scratch_shapes=[
            pltpu.VMEM((half,) + parts.shape, jnp.float32),
            pltpu.VMEM((2 * spots,) + parts.shape, jnp.float32),
            sem((half + 2 * spots,)),
            sem((half + 2 * spots,)),
        ],
        compiler_params=pltpu.CompilerParams(collective_id=2, has_side_effects=True),
        name="sum_everywhere",
    )(parts)
    return summed[0, : 2 * each // lanes].reshape(2, each), total[0, 0]


def dot_plain(a, b):
    return lax.dot_general(a, b, (((1,), (0,)), ((), ())), preferred_element_type=jnp.float32)


def dot_rows(a, b):
    return lax.dot_general(a, b, (((0,), (0,)), ((), ())), preferred_element_type=jnp.float32)


def dot_cols(a, b):
    return lax.dot_general(a, b, (((1,), (1,)), ((), ())), preferred_element_type=jnp.float32)


def turn(values, tables, direction):
    cosine, low_sine, high_sine = tables
    lanes = values.shape[1]
    half_rot = ROT // 2
    moved = pltpu.roll(values, lanes - half_rot, 1) * low_sine + pltpu.roll(values, half_rot, 1) * high_sine
    return values * cosine + direction * moved


def head_scores(query, key, bias):
    return dot_cols(query, key) * 0.125 + bias


def attention_fore(projected, tables_ref, bias_ref, turned_ref, attended_ref, logs_ref):
    spots, _, piece, width = turned_ref.shape
    rows, third = spots * piece, width // 3
    tables = [tables_ref[k] for k in range(3)]
    lane = lax.broadcasted_iota(jnp.int32, (rows, 128), 1)
    first, logs = lane < HEAD_DIM, jnp.zeros((rows, 128), jnp.float32)
    for pair in range(third // 128):
        span = [slice(k * third + pair * 128, k * third + pair * 128 + 128) for k in range(3)]
        query, key, value = [projected[:, s] for s in span]
        query = turn(query, tables, 1.0).astype(jnp.bfloat16)
        key = turn(key, tables, 1.0).astype(jnp.bfloat16)
        value = value.astype(jnp.bfloat16)
        for s, part in zip(span, (query, key, value)):
            turned_ref[:, 0, :, s] = part.reshape(spots, piece, 128)
        none = jnp.zeros_like(query)
        outs = []
        for head, one in enumerate((jnp.where(first, query, none), jnp.where(first, none, query))):
            scores = head_scores(one, key, bias_ref[...])
            top = jnp.max(scores, axis=1, keepdims=True)
            exponent = jnp.exp(scores - top)
            total = jnp.sum(exponent, axis=1, keepdims=True)
            outs.append(dot_plain((exponent * (1.0 / total)).astype(jnp.bfloat16), value))
            logs = jnp.where(lane == 2 * pair + head, top + jnp.log(total), logs)
        attended_ref[:, 0, :, span[0]] = (
            jnp.where(first, outs[0], outs[1]).astype(jnp.bfloat16).reshape(spots, piece, 128)
        )
    put(logs_ref, logs)


def attention_back(turned_ref, d_att_ref, logs_ref, tables_ref, bias_ref, d_project_ref):
    spots, _, piece, width = turned_ref.shape
    rows, third = spots * piece, width // 3
    tables = [tables_ref[k] for k in range(3)]
    first = lax.broadcasted_iota(jnp.int32, (rows, 128), 1) < HEAD_DIM
    logs = flat(logs_ref)
    for pair in range(third // 128):
        span = [slice(k * third + pair * 128, k * third + pair * 128 + 128) for k in range(3)]
        query, key, value = [turned_ref[:, 0, :, s].reshape(rows, 128) for s in span]
        d_att = d_att_ref[:, 0, :, span[0]].reshape(rows, 128)
        none = jnp.zeros_like(query)
        parts = []
        for head in range(2):
            keep = first if head == 0 else jnp.logical_not(first)
            one_query = jnp.where(keep, query, none)
            one_d_att = jnp.where(keep, d_att, none)
            log = logs[:, 2 * pair + head : 2 * pair + head + 1]
            prob = jnp.exp(head_scores(one_query, key, bias_ref[...]) - log)
            d_value = dot_rows(prob.astype(jnp.bfloat16), d_att)
            d_prob = dot_cols(one_d_att, value)
            d_score = (prob * (d_prob - jnp.sum(d_prob * prob, axis=1, keepdims=True))).astype(
                jnp.bfloat16
            )
            parts.append((dot_plain(d_score, key), dot_rows(d_score, query), d_value))
        joined = [jnp.where(first, one, two) for one, two in zip(*parts)]
        done = (turn(0.125 * joined[0], tables, -1.0), turn(0.125 * joined[1], tables, -1.0), joined[2])
        for s, part in zip(span, done):
            d_project_ref[:, 0, :, s] = part.astype(jnp.bfloat16).reshape(spots, piece, 128)


def join_gate_up(packed, whole):
    last = packed[:, 2 * whole :]
    gate = jnp.concatenate([packed[:, :whole], last], axis=1)
    up = jnp.concatenate([packed[:, whole : 2 * whole], pltpu.roll(last, 64, 1)], axis=1)
    return gate, up


def units_fore(normed, weight):
    packed = dot_plain(normed, weight)
    units = weight.shape[1] // 2
    gate, up = join_gate_up(packed, units - 64)
    return packed, (gate * jax.nn.sigmoid(gate) * up).astype(jnp.bfloat16)[:, :units]


def units_back(cot, down, packed):
    units = down.shape[0]
    whole = units - 64
    d_hid = dot_cols(cot, down).astype(jnp.bfloat16).astype(jnp.float32)
    d_hid = jnp.concatenate([d_hid, jnp.zeros((d_hid.shape[0], 64), jnp.float32)], axis=1)
    gate, up = join_gate_up(packed, whole)
    sigmoid_gate = jax.nn.sigmoid(gate)
    d_gate = d_hid * up * (sigmoid_gate * (1.0 + gate * (1.0 - sigmoid_gate)))
    d_up = d_hid * (gate * sigmoid_gate)
    first = lax.broadcasted_iota(jnp.int32, (gate.shape[0], 128), 1) < 64
    last = jnp.where(first, d_gate[:, whole:], pltpu.roll(d_up[:, whole:], 64, 1))
    parts = [d_gate[:, :whole], d_up[:, :whole], last]
    return jnp.concatenate([part.astype(jnp.bfloat16) for part in parts], axis=1)


KERNEL_PARAMS = pltpu.CompilerParams(vmem_limit_bytes=40 * 1024 * 1024)


def adam_update(weight_old, gradient, moment_old, square_old, factor, rate, decay):
    clipped = gradient * factor
    moment_new = BETA_ONE * moment_old + (1.0 - BETA_ONE) * clipped
    square_new = BETA_TWO * square_old + (1.0 - BETA_TWO) * clipped * clipped
    moment_hat = moment_new / (1.0 - BETA_ONE**STEP)
    square_hat = square_new / (1.0 - BETA_TWO**STEP)
    weight_new = weight_old - rate * (
        moment_hat / (jnp.sqrt(square_hat) + ADAM_EPS) + decay * weight_old
    )
    return (weight_new, moment_new, square_new)


def local(
    tokens,
    cotangent,
    project_weight,
    output_weight,
    gate_up_weight,
    down_weight,
    norm_params,
    first_project,
    first_output,
    first_gate_up,
    first_down,
    first_norm,
    second_project,
    second_output,
    second_gate_up,
    second_down,
    second_norm,
):
    count = lax.axis_size("dp")
    blocks_half = count // 2
    me = lax.axis_index("dp")
    side = (me // 2) % 2
    spot = lax.axis_index("tensor")
    spots = lax.axis_size("tensor")
    micro_count, piece = tokens.shape[0], tokens.shape[1]
    head_cols = project_weight.shape[2] // 2
    unit_cols = gate_up_weight.shape[2] // 2
    whole = unit_cols - 64
    rows_each = project_weight.shape[1]
    seqs = 2 * micro_count
    rows_all = spots * seqs * piece

    by_columns = rows_each % 128 == 0

    by_columns = rows_each % 128 == 0

    norm_low = norm_params.astype(jnp.bfloat16)
    tok_rel, unit_rows, cot_low, cot_flipped, *weight_pairs, own_gains, tables, bias = run_prepare(
        tokens,
        cotangent,
        (project_weight, gate_up_weight, down_weight, output_weight),
        norm_params,
        jnp.asarray(angle_tables(spots * piece)),
    )
    if not by_columns:
        weight_pairs[2:] = [pair.swapaxes(1, 2) for pair in weight_pairs[2:]]

    (
        w_project,
        w_gate_up,
        w_down,
        w_output,
        gains,
        _,
        all_cot,
        normed_t,
        packed,
        hidden,
        attended,
        turned,
        logs,
        hidden_t,
        attended_t,
        *stage,
    ) = run_forward(
        blocks_half,
        by_columns,
        weight_pairs,
        own_gains,
        unit_rows,
        cot_low,
        cot_flipped,
        tables,
        bias,
        (spots, seqs, piece),
    )
    gains = gains.reshape(count, 8, rows_each).transpose(1, 0, 2).reshape(8, D)
    if not by_columns:
        w_down, w_output = w_down.T, w_output.T
    pairs, normed_parts, out_parts = run_backward(
        blocks_half,
        by_columns,
        (all_cot, packed, hidden, attended, turned, logs),
        (normed_t, attended_t, hidden_t),
        (w_project, w_gate_up, w_down, w_output),
        tables,
        bias,
        stage[:2],
    )
    if not by_columns:
        pairs[:2] = [(own.T, came.swapaxes(1, 2)) for own, came in pairs[:2]]
    weight_grads, input_grad, shares = run_join_grads(
        blocks_half,
        pairs,
        [*normed_parts, tok_rel, cot_low, gains],
        [output_weight.shape, down_weight.shape, gate_up_weight.shape, project_weight.shape],
        (head_cols, whole),
    )
    norm_grad, square_total = sum_everywhere(shares)
    grads = (weight_grads[3], weight_grads[0], weight_grads[2], weight_grads[1], norm_grad)
    norm_total = jnp.sqrt(square_total)
    (layer_out,) = run_finish(finish_out, rows_each, [*out_parts, tok_rel], [], 0)
    limit = 0.03 * math.sqrt((4 * D * D + 3 * D * FF + 2 * D) * micro_count * count * SEQ)
    factor = jnp.minimum(1.0, limit / (norm_total + 1e-06))
    rates = (
        2.0 / math.sqrt(D),
        2.0 / math.sqrt(D // 32),
        2.0 / math.sqrt(D),
        2.0 / math.sqrt(FF),
        0.5,
    )
    decays = (0.1, 0.1, 0.1, 0.1, 0.0)
    masters = (project_weight, output_weight, gate_up_weight, down_weight, norm_params)
    firsts = (first_project, first_output, first_gate_up, first_down, first_norm)
    seconds = (second_project, second_output, second_gate_up, second_down, second_norm)
    updated = [
        adam_update(*parts) for parts in zip(masters, grads, firsts, seconds, [factor] * 5, rates, decays)
    ]
    return (
        layer_out,
        input_grad,
        *grads,
        norm_total,
        *[u[0] for u in updated],
        *[u[1] for u in updated],
        *[u[2] for u in updated],
    )


def solution(mesh):
    wide = P("dp", "tensor", None)
    stacked = P(None, "dp", "tensor")
    tall = P("tensor", "dp")
    params = (stacked, tall, stacked, tall, P(None, "dp"))
    return jax.shard_map(
        local,
        mesh=mesh,
        in_specs=(wide, wide, *params, *params, *params),
        out_specs=(wide, wide, *params, P(), *params, *params, *params),
        check_vma=False,
    )
```
